32 devices in a mesh: seq: 8 (over y, x, core), head: 4 (over z).
Axes of the slice: x: 2, y: 2, z: 4, core: 2. Of those that a mesh axis runs over, the one named last changes fastest.
Arguments:
- layer_input: bfloat16 [2, 2048, 1536], P(None, ('seq', 'head')), may hold values from -6 to 6
- segments: int32 [2, 2048], replicated, may hold values from 0 to 2, as said below
- routes: int32 [2, 2048, 8], P(None, ('seq', 'head')), may hold values from 0 to 39, all different within a row
- pair_rank: int32 [2, 2048, 8], P(None, ('seq', 'head')), may hold values from 0 to 1023, as said below
- query_key_value_weight: bfloat16 [1536, 2560], P(('seq', 'head')), may hold values from -0.15625 to 0.15625
- output_weight: bfloat16 [1536, 1536], P(('seq', 'head')), may hold values from -2 to 2
- router_weight: bfloat16 [1536, 40], P(('seq', 'head')), may hold values from -0.078125 to 0.078125
- norm_attn: bfloat16 [1536], P(('seq', 'head')), may hold values from 0.5 to 1.5
- norm_ffn: bfloat16 [1536], P(('seq', 'head')), may hold values from 0.5 to 1.5
- w_gate_up: bfloat16 [40, 1536, 1024], P('head', 'seq'), may hold values from -0.15625 to 0.15625
- w_down: bfloat16 [40, 512, 1536], P('head', 'seq'), may hold values from -1.5 to 1.5
- cotangent: bfloat16 [2, 2048, 1536], P(None, ('seq', 'head')), may hold values from -6 to 6
Outputs:
- mixed_out: bfloat16 [2, 2048, 1536], P(None, ('seq', 'head'))
- d_x: float32 [2, 2048, 1536], P(None, ('seq', 'head'))
- d_w_qkv: float32 [1536, 2560], P(('seq', 'head'))
- d_w_out: float32 [1536, 1536], P(('seq', 'head'))
- d_w_router: float32 [1536, 40], P(('seq', 'head'))
- d_norm_attn: float32 [1536], P(('seq', 'head'))
- d_norm_ffn: float32 [1536], P(('seq', 'head'))
- d_w_gate_up: float32 [40, 1536, 1024], P('head', 'seq')
- d_w_down: float32 [40, 512, 1536], P('head', 'seq')
The draws below stay inside these ranges and needn't reach their ends.
Inputs may be any that keep to these rules, and one draw needn't show every extreme that they name: `segments`: segment numbers start at 0 and never fall along a sequence. In one sequence, drawn from the seed, all tokens share segment 0; the other holds 3 documents, each of 200 to 2000 tokens. `pair_rank`: over the pairs of one group (positions b * 64 to (b + 1) * 64 - 1 of every sequence, all 8 routes) the ranks are each number of 0 to 1023 once.
All inputs are finite; a program needn't handle non-finite values.
Results may differ from the reference program's by a relative error of at most 0.025.
Values may be sent and summed in bfloat16 or wider, within the bound.
A program may use at most 192 MiB of HBM per device.

```python
import jax
import jax.numpy as jnp
from jax import lax

MODEL_WIDTH = 1536
QUERY_HEADS = 24
KEY_VALUE_HEADS = 8
HEAD_WIDTH = 64
EXPERTS = 40
TOPK = 8
FF = 512
SEQUENCE_COUNT = 2
TB = 64
DOC_MIN = 200
DOC_MAX = 2000
SEQUENCE_LENGTH = 2048
CAP = 25


def draw_segments(key, part):
    key = jax.random.fold_in(key, 11)
    key_pick, key_sizes = jax.random.split(key)
    whole = jax.random.randint(key_pick, (), 0, SEQUENCE_COUNT)
    doc_count = SEQUENCE_LENGTH // DOC_MAX + 2
    spare_tokens = SEQUENCE_LENGTH - doc_count * DOC_MIN
    even_share = spare_tokens // doc_count
    leftover = spare_tokens - doc_count * even_share
    headroom = DOC_MAX - DOC_MIN - even_share - doc_count
    jitter_most = max(0, min(even_share, headroom))
    wobble = jax.random.randint(key_sizes, (SEQUENCE_COUNT, doc_count), 0, jitter_most + 1)
    jitter = wobble - jnp.roll(wobble, -1, axis=1)
    last_extra = (jnp.arange(doc_count, dtype=jnp.int32) == doc_count - 1).astype(jnp.int32) * leftover
    sizes = DOC_MIN + even_share + jitter + last_extra[None, :]
    ends = jnp.cumsum(sizes, axis=1)
    token_positions = jnp.arange(SEQUENCE_LENGTH, dtype=jnp.int32)
    numbers = jnp.sum((ends[:, None, :] <= token_positions[None, :, None]).astype(jnp.int32), axis=2)
    single = jnp.arange(SEQUENCE_COUNT, dtype=jnp.int32)[:, None] == whole
    return jnp.where(single, 0, numbers).astype(jnp.int32)


def shuffled(key):
    return jax.random.permutation(key, SEQUENCE_COUNT * TB * TOPK)


def draw_pair_rank(key, part):
    key = jax.random.fold_in(key, 23)
    blocks = SEQUENCE_LENGTH // TB
    keys = jax.random.split(key, blocks)
    ranks = jax.vmap(shuffled)(keys).astype(jnp.int32)
    return ranks.reshape(blocks, SEQUENCE_COUNT, TB, TOPK).transpose(1, 0, 2, 3).reshape(SEQUENCE_COUNT, SEQUENCE_LENGTH, TOPK)


def shard_levels(rng, extent, shards, smallest, largest):
    factor_of = 1.0
    for position, parts in shards:
        heights = jax.random.uniform(jax.random.fold_in(jax.random.fold_in(rng, 6), position), (parts,), jnp.float32, smallest / len(shards), largest / len(shards))
        factor_of = factor_of * jnp.repeat(jnp.exp(heights), extent[position] // parts).reshape((-1,) + (1,) * (len(extent) - 1 - position))
    return factor_of


def distinct(rng, rows, number_of, top, lift):
    order = jax.random.permutation(jax.random.fold_in(rng, 1), number_of)
    boost = order
    for power in range(3):
        boost = boost * boost // number_of
    boost = boost * lift // number_of
    chance = jax.random.randint(jax.random.fold_in(rng, 2), (rows, number_of), 0, 4096) + boost
    fixed_rows = jax.random.permutation(jax.random.fold_in(rng, 3), rows)[jnp.arange(number_of) % rows]
    chance = jnp.where(jnp.arange(rows)[:, None] == fixed_rows[None, :], 1 << 14, chance)
    score = chance * number_of + jnp.arange(number_of)
    return lax.top_k(score.astype(jnp.int32), top)[1].astype(jnp.int32)


def noise(stream_key, dims, spread, bound, cuts=(), held_as=jnp.bfloat16):
    values = spread * jax.random.normal(stream_key, dims, jnp.float32)
    if cuts:
        values = values * shard_levels(stream_key, dims, cuts, -0.22, 0.18)
    return jnp.clip(values, -bound, bound).astype(held_as)


def setup_inputs(seed: int = 0) -> dict:
    key_list = jax.random.split(jax.random.key(seed), 13)
    return {
        "layer_input": noise(key_list[0], (SEQUENCE_COUNT, SEQUENCE_LENGTH, MODEL_WIDTH), 1.0, 6.0, ((1, 32),)),
        "segments": draw_segments(jax.random.fold_in(key_list[12], 71), 0),
        "routes": distinct(key_list[2], SEQUENCE_COUNT * SEQUENCE_LENGTH, EXPERTS, TOPK, 1638).reshape((SEQUENCE_COUNT, SEQUENCE_LENGTH, TOPK)),
        "pair_rank": draw_pair_rank(jax.random.fold_in(key_list[12], 71), 0),
        "query_key_value_weight": noise(key_list[4], (MODEL_WIDTH, KEY_VALUE_HEADS * (QUERY_HEADS // KEY_VALUE_HEADS + 2) * HEAD_WIDTH), MODEL_WIDTH ** -0.5, 0.15625, ((0, 32),)),
        "output_weight": noise(key_list[5], (QUERY_HEADS * HEAD_WIDTH, MODEL_WIDTH), 8 ** -0.5, 2.0, ((0, 32),)),
        "router_weight": noise(key_list[6], (MODEL_WIDTH, EXPERTS), (4 * MODEL_WIDTH) ** -0.5, 0.078125, ((0, 32),)),
        "norm_attn": jnp.clip(1.0 + 0.1 * jax.random.normal(key_list[7], (MODEL_WIDTH,), jnp.float32), 0.5, 1.5).astype(jnp.bfloat16),
        "norm_ffn": jnp.clip(1.0 + 0.1 * jax.random.normal(key_list[8], (MODEL_WIDTH,), jnp.float32), 0.5, 1.5).astype(jnp.bfloat16),
        "w_gate_up": noise(key_list[9], (EXPERTS, MODEL_WIDTH, 2 * FF), MODEL_WIDTH ** -0.5, 0.15625, ((0, 4), (1, 8))),
        "w_down": noise(key_list[10], (EXPERTS, FF, MODEL_WIDTH), 16 ** -0.5, 1.5, ((0, 4), (1, 8))),
        "cotangent": noise(key_list[11], (SEQUENCE_COUNT, SEQUENCE_LENGTH, MODEL_WIDTH), 1.0, 6.0, ((1, 32),)),
    }


@jax.custom_vjp
def low(v):
    return lax.optimization_barrier(v.astype(jnp.bfloat16)).astype(jnp.float32)

@jax.custom_vjp
def low_back(v):
    return v

def low_keep(v):
    return (low(v), None)

def low_pass(kept, grad):
    return (grad,)

def back_keep(v):
    return (v, None)

def back_low(kept, grad):
    return (low(grad),)
low.defvjp(low_keep, low_pass)
low_back.defvjp(back_keep, back_low)
epsilon = 1e-06
negative = -1e+30
theta = 10000.0
HIGH_PRECISION = lax.Precision.HIGHEST

def rms_scale(value, gain):
    return value * lax.rsqrt(lax.optimization_barrier(jnp.mean(value * value, axis=-1, keepdims=True)) + epsilon) * gain

def rotate(value, cosine, sine):
    half = value.shape[-1] // 2
    first = value[..., :half]
    second = value[..., half:]
    return jnp.concatenate([first * cosine - second * sine, second * cosine + first * sine], axis=-1)

def rope_tables(token_count):
    half = HEAD_WIDTH // 2
    freq = theta ** (-jnp.arange(half, dtype=jnp.float32) / half)
    angle = jnp.arange(token_count, dtype=jnp.float32)[:, None] * freq[None, :]
    return (jnp.cos(angle), jnp.sin(angle))

def attend(query_rows, keys, values, segments):
    block_width = min(512, SEQUENCE_LENGTH)
    token_count = SEQUENCE_LENGTH // block_width
    query_group = QUERY_HEADS // KEY_VALUE_HEADS
    token_positions = jnp.arange(SEQUENCE_LENGTH, dtype=jnp.int32)

    def single_block(args):
        q_block, seg_block, pos_block = args
        scores = low_back(jnp.einsum('qhgd,khd->hgqk', q_block, keys, precision=HIGH_PRECISION) * HEAD_WIDTH ** (-0.5))
        mask = (seg_block[:, None] == segments[None, :]) & (token_positions[None, :] <= pos_block[:, None])
        scores = jnp.where(mask, scores, negative)
        probs = low(jax.nn.softmax(scores, axis=-1))
        return jnp.einsum('hgqk,khd->qhgd', probs, values, precision=HIGH_PRECISION)
    layer_result = lax.map(jax.checkpoint(single_block), (query_rows.reshape(token_count, block_width, KEY_VALUE_HEADS, query_group, HEAD_WIDTH), segments.reshape(token_count, block_width), token_positions.reshape(token_count, block_width)))
    return layer_result.reshape(SEQUENCE_LENGTH, KEY_VALUE_HEADS, query_group, HEAD_WIDTH)

def placement(routes, pair_rank):
    blocks = SEQUENCE_LENGTH // TB
    per_block = SEQUENCE_COUNT * TB * TOPK

    def arrange(values):
        return values.reshape(SEQUENCE_COUNT, blocks, TB, TOPK).transpose(1, 0, 2, 3).reshape(blocks, per_block)

    def one_group(expert_of, rank):
        order = jnp.zeros((per_block,), jnp.int32).at[rank].set(jnp.arange(per_block, dtype=jnp.int32))
        flags = (expert_of[order][:, None] == jnp.arange(EXPERTS, dtype=jnp.int32)[None, :]).astype(jnp.int32)
        before = jnp.cumsum(flags, axis=0) - flags
        return lax.optimization_barrier(jnp.sum(before * flags, axis=1))[rank]
    slot = jax.vmap(one_group)(arrange(routes), arrange(pair_rank))
    slot = slot.reshape(blocks, SEQUENCE_COUNT, TB, TOPK).transpose(1, 0, 2, 3).reshape(SEQUENCE_COUNT, SEQUENCE_LENGTH, TOPK)
    kept = slot < CAP
    spare = EXPERTS * blocks * CAP
    block_of = (jnp.arange(SEQUENCE_LENGTH, dtype=jnp.int32) // TB)[None, :, None]
    target = jnp.where(kept, routes * (blocks * CAP) + block_of * CAP + slot, spare).astype(jnp.int32)
    token = jnp.arange(SEQUENCE_COUNT, dtype=jnp.int32)[:, None, None] * SEQUENCE_LENGTH + jnp.arange(SEQUENCE_LENGTH, dtype=jnp.int32)[None, :, None] + 0 * routes
    source = jnp.full((spare + 1,), SEQUENCE_COUNT * SEQUENCE_LENGTH, jnp.int32).at[target.reshape(-1)].set(token.reshape(-1).astype(jnp.int32))
    return (target, source[:spare], kept)

def layer(layer_input, query_key_value_weight, output_weight, router_weight, gain_attn, gain_ffn, w_gate_up, w_down, segments, routes, target, source, kept):
    query_group = QUERY_HEADS // KEY_VALUE_HEADS
    blocks = SEQUENCE_LENGTH // TB
    first_input = low(rms_scale(layer_input, gain_attn))
    projected_rows = low_back(jnp.einsum('kja,at->kjt', first_input, query_key_value_weight, precision=HIGH_PRECISION)).reshape(SEQUENCE_COUNT, SEQUENCE_LENGTH, KEY_VALUE_HEADS, query_group + 2, HEAD_WIDTH)
    cosine, sine = rope_tables(SEQUENCE_LENGTH)
    cosine = cosine[None, :, None, None, :]
    sine = sine[None, :, None, None, :]
    turned = rotate(projected_rows[:, :, :, :query_group + 1], cosine, sine)
    query_rows = low(low_back(turned[:, :, :, :query_group]))
    keys = low(low_back(turned[:, :, :, query_group]))
    values = low(low_back(projected_rows[:, :, :, query_group + 1]))

    def one_sequence(args):
        return attend(args[0], args[1], args[2], args[3])
    attended = lax.map(one_sequence, (query_rows, keys, values, segments))
    head_values = low(low_back(attended.reshape(SEQUENCE_COUNT, SEQUENCE_LENGTH, QUERY_HEADS * HEAD_WIDTH)))
    attention_output = low_back(jnp.einsum('hnq,qa->hna', head_values, output_weight, precision=HIGH_PRECISION))
    middle = layer_input + attention_output
    second_input = low(rms_scale(middle, gain_ffn))
    router_logits = jnp.einsum('nxr,rf->nxf', second_input, router_weight, precision=HIGH_PRECISION)
    gates = jax.nn.softmax(jnp.take_along_axis(router_logits, routes, axis=2), axis=-1)
    flat = jnp.concatenate([second_input.reshape(SEQUENCE_COUNT * SEQUENCE_LENGTH, MODEL_WIDTH), jnp.zeros((1, MODEL_WIDTH), jnp.float32)], axis=0)
    token_rows = low_back(flat[source]).reshape(EXPERTS, blocks * CAP, MODEL_WIDTH)

    def one_expert(args):
        rows_in, up_weight, down_weight = args
        gate_up = low_back(jnp.dot(rows_in, up_weight, precision=HIGH_PRECISION))
        act = low(jax.nn.silu(gate_up[:, :FF]) * gate_up[:, FF:])
        return low(low_back(jnp.dot(act, down_weight, precision=HIGH_PRECISION)))
    outputs = lax.map(jax.checkpoint(one_expert), (token_rows, w_gate_up, w_down))
    padded = jnp.concatenate([outputs.reshape(EXPERTS * blocks * CAP, MODEL_WIDTH), jnp.zeros((1, MODEL_WIDTH), jnp.float32)], axis=0)
    picked = padded[target]
    weights = gates * kept.astype(jnp.float32)
    moe = lax.optimization_barrier(jnp.sum(picked * weights[..., None], axis=2))
    return middle + moe

def reference(layer_input, segments, routes, pair_rank, query_key_value_weight, output_weight, router_weight, norm_attn, norm_ffn, w_gate_up, w_down, cotangent):
    target, source, kept = placement(routes, pair_rank)

    def forward(input_value, qkv_in, out_in, router_in, attn_gain, ffn_gain, up_in, down_in):
        return layer(input_value, qkv_in, out_in, router_in, attn_gain, ffn_gain, up_in, down_in, segments, routes, target, source, kept)
    primals = (layer_input, query_key_value_weight, output_weight, router_weight, norm_attn, norm_ffn, w_gate_up, w_down)
    layer_result, pull = jax.vjp(forward, *[value.astype(jnp.float32) for value in primals])
    grads = pull(cotangent.astype(jnp.float32))
    return (layer_result.astype(jnp.bfloat16), grads[0], grads[1], grads[2], grads[3], grads[4], grads[5], grads[6], grads[7])
```

```python
import functools

import jax
import jax.numpy as jnp
from jax import lax
from jax.experimental import pallas as pl
from jax.experimental.pallas import tpu as pltpu
from jax.sharding import Mesh, PartitionSpec as P

MODEL_WIDTH = 1536
QUERY_HEADS = 24
KEY_VALUE_HEADS = 8
HEAD_WIDTH = 64
EXPERTS = 40
FF = 512
CAP = 25
LANES = 128
LOW = 64

epsilon = 1e-06
negative = -1e30
theta = 10000.0
HIGH_PRECISION = lax.Precision.HIGHEST
MESH = pl.DeviceIdType.MESH
f32 = jnp.float32
bf16 = jnp.bfloat16
ANY = pl.BlockSpec(memory_space=pl.ANY)
WHOLE = pl.BlockSpec(memory_space=pltpu.VMEM)
DMA = pltpu.SemaphoreType.DMA


def rope_tables(token_positions, head_size):
    half = head_size // 2
    freq = theta ** (-jnp.arange(half, dtype=jnp.float32) / half)
    angle = token_positions.astype(jnp.float32)[:, None] * freq[None, :]
    return (jnp.cos(angle)[None, :, None, None, :], jnp.sin(angle)[None, :, None, None, :])


def rotate(value, cosine, sine):
    half = value.shape[-1] // 2
    first = value[..., :half]
    second = value[..., half:]
    return jnp.concatenate(
        [first * cosine - second * sine, second * cosine + first * sine], axis=-1
    )


def digits(count):
    number = count.bit_length() - 1
    assert 1 << number == count
    return number


def flip(index, mask):
    out = index
    bit = 0
    while (1 << bit) <= mask:
        if (mask >> bit) & 1:
            out = out + (1 - 2 * ((index // (1 << bit)) % 2)) * (1 << bit)
        bit += 1
    return out


def subsets(bits):
    out = [0]
    for bit in bits:
        out = out + [mask | (1 << bit) for mask in out]
    return out


def near(count):
    return sorted(range(1, count), key=lambda step: min(step, count - step))


def meet(peers):
    sem = pltpu.get_barrier_semaphore()
    for peer in peers:
        pl.semaphore_signal(sem, inc=1, device_id=peer, device_id_type=MESH)
    pl.semaphore_wait(sem, len(peers))


class Cube:
    def __init__(self, chips, with_core):
        self.chips = chips
        self.chip_digits = digits(chips)
        self.number = self.chip_digits + int(with_core)
        self.with_core = with_core
        up = tuple(range(self.chip_digits))
        core = (self.chip_digits,) if with_core else ()
        self.gather_orders = (up + core, up[::-1] + core)
        self.scatter_orders = (core + up, core + up[::-1])

    def place(self, mask):
        chip = flip(lax.axis_index("chip"), mask & (self.chips - 1))
        if not self.with_core:
            return (chip,)
        return (chip, flip(lax.axis_index("core"), mask >> self.chip_digits))

    def peer(self, digit):
        if digit < self.chip_digits:
            return {"chip": flip(lax.axis_index("chip"), 1 << digit)}
        return {"core": flip(lax.axis_index("core"), 1)}


def gather_kernel(cube, heads, in_ref, out_ref, local, line_send, line_recv, send, recv):
    hz = lax.axis_index("head")
    rows = in_ref.shape[0]
    half = rows // 2
    others = near(heads) if heads > 1 else []
    meet(
        [cube.peer(digit) for digit in range(cube.number)]
        + [{"head": (hz + d) % heads} for d in others]
    )

    def at(mask, d):
        index = cube.place(mask)
        return index + ((hz + heads - d) % heads,) if heads > 1 else index

    own = pltpu.make_async_copy(in_ref, out_ref.at[at(0, 0)], local)
    own.start()
    line = {}
    for d in others:
        line[d] = pltpu.make_async_remote_copy(
            src_ref=in_ref,
            dst_ref=out_ref.at[at(0, 0)],
            send_sem=line_send.at[d - 1],
            recv_sem=line_recv.at[d - 1],
            device_id={"head": (hz + d) % heads},
            device_id_type=MESH,
        )
        line[d].start()
    copies = {}

    def forward(side, mask, d):
        order = cube.gather_orders[side]
        last = max([k for k in range(cube.number) if (mask >> order[k]) & 1], default=-1)
        for k in range(last + 1, cube.number):
            later = mask | (1 << order[k])
            part = pl.ds(side * half, half)
            place = out_ref.at[at(mask, d) + (part,)]
            copy = pltpu.make_async_remote_copy(
                src_ref=in_ref.at[part] if mask == 0 and d == 0 else place,
                dst_ref=place,
                send_sem=send.at[side, later, d],
                recv_sem=recv.at[side, later, d],
                device_id=cube.peer(order[k]),
                device_id_type=MESH,
            )
            copy.start()
            copies[(side, later, d)] = copy

    for side in range(2):
        forward(side, 0, 0)
    for d in others:
        line[d].wait_recv()
        for side in range(2):
            forward(side, 0, d)
    for mask in sorted(range(1, 1 << cube.number), key=lambda m: bin(m).count("1")):
        for d in [0] + others:
            for side in range(2):
                copies[(side, mask, d)].wait_recv()
                forward(side, mask, d)
    own.wait()
    for copy in list(line.values()) + list(copies.values()):
        copy.wait_send()


def gather(value, chips, heads, with_core, number):
    rows, columns = value.shape
    cube = Cube(chips, with_core)
    lead = (chips,) + ((2,) if with_core else ()) + ((heads,) if heads > 1 else ())
    steps = max(heads - 1, 1)
    return pl.pallas_call(
        functools.partial(gather_kernel, cube, heads),
        out_shape=jax.ShapeDtypeStruct(lead + (rows, columns), value.dtype),
        in_specs=[ANY],
        out_specs=ANY,
        scratch_shapes=[
            DMA,
            DMA((steps,)),
            DMA((steps,)),
            DMA((2, 1 << cube.number, heads)),
            DMA((2, 1 << cube.number, heads)),
        ],
        compiler_params=pltpu.CompilerParams(collective_id=number, has_side_effects=True),
        name="gather",
    )(value)


def scatter_kernel(cube, heads, in_ref, out_ref, *refs):
    count = cube.number
    arrived, parts = refs[:count], refs[count : 2 * count - 1]
    line_out, line_in, line_send, line_recv, send, recv = refs[2 * count - 1 :]
    hz = lax.axis_index("head")
    half = in_ref.shape[-2] // 2
    others = near(heads) if heads > 1 else []
    order_of_lines = others[::-1] + [0]
    meet(
        [cube.peer(digit) for digit in range(count)] + [{"head": (hz + d) % heads} for d in others]
    )
    copies = {}

    def slot(side, k, mask):
        return subsets(cube.scatter_orders[side][k + 1 :]).index(mask)

    def mine(side, mask, d):
        index = cube.place(mask)
        if heads > 1:
            index = index + ((hz + d) % heads,)
        return in_ref.at[index + (pl.ds(side * half, half),)]

    def pass_on(side, k, mask, d, source):
        where = slot(side, k, mask)
        copy = pltpu.make_async_remote_copy(
            src_ref=source,
            dst_ref=arrived[k].at[side, where, d],
            send_sem=send.at[side, k, where, d],
            recv_sem=recv.at[side, k, where, d],
            device_id=cube.peer(cube.scatter_orders[side][k]),
            device_id_type=MESH,
        )
        copy.start()
        copies[(side, k, mask, d)] = copy

    def total(side, steps, mask, d):
        value = mine(side, mask, d)[...].astype(f32)
        for j in range(steps):
            copies[(side, j, mask, d)].wait_recv()
            value = value + arrived[j][side, slot(side, j, mask), d].astype(f32)
        return value

    for k in range(count):
        for d in order_of_lines:
            for side in range(2):
                order = cube.scatter_orders[side]
                for mask in subsets(order[k + 1 :])[::-1]:
                    full = mask | (1 << order[k])
                    if k == 0:
                        source = mine(side, full, d)
                    else:
                        source = parts[k - 1].at[side, slot(side, k, mask), d]
                        source[...] = total(side, k, full, d).astype(bf16)
                    pass_on(side, k, mask, d, source)
    line = {}
    for d in order_of_lines:
        for side in range(2):
            value = total(side, count, 0, d)
            if d:
                line_out[d - 1, pl.ds(side * half, half)] = value.astype(bf16)
            else:
                out_ref[pl.ds(side * half, half)] = value
        if d:
            line[d] = pltpu.make_async_remote_copy(
                src_ref=line_out.at[d - 1],
                dst_ref=line_in.at[d - 1],
                send_sem=line_send.at[d - 1],
                recv_sem=line_recv.at[d - 1],
                device_id={"head": (hz + d) % heads},
                device_id_type=MESH,
            )
            line[d].start()
    for d in others:
        line[d].wait_recv()
        out_ref[...] += line_in[d - 1].astype(f32)
    for copy in list(line.values()) + list(copies.values()):
        copy.wait_send()


def scatter_sum(value, chips, heads, with_core, number):
    rows, columns = value.shape[-2:]
    cube = Cube(chips, with_core)
    half = rows // 2
    steps = max(heads - 1, 1)
    line_rows = rows if heads > 1 else 16
    slots = [(1 << cube.number) >> (k + 1) for k in range(cube.number)]
    if 2 * value.size + 4 * heads * half * columns * (sum(slots) + sum(slots[1:])) > 40 << 20:
        names = ("chip", "core") if with_core else ("chip",)
        names = names + (("head",) if heads > 1 else ())
        flat = value.reshape(-1, columns)
        return lax.psum_scatter(flat, names, scatter_dimension=0, tiled=True).astype(f32)
    return pl.pallas_call(
        functools.partial(scatter_kernel, cube, heads),
        out_shape=jax.ShapeDtypeStruct((rows, columns), f32),
        in_specs=[WHOLE],
        out_specs=WHOLE,
        scratch_shapes=[pltpu.VMEM((2, s, heads, half, columns), bf16) for s in slots]
        + [pltpu.VMEM((2, s, heads, half, columns), bf16) for s in slots[1:]]
        + [
            pltpu.VMEM((steps, line_rows, columns), bf16),
            pltpu.VMEM((steps, line_rows, columns), bf16),
            DMA((steps,)),
            DMA((steps,)),
            DMA((2, cube.number, slots[0], heads)),
            DMA((2, cube.number, slots[0], heads)),
        ],
        compiler_params=pltpu.CompilerParams(
            collective_id=number, has_side_effects=True, vmem_limit_bytes=56 << 20
        ),
        name="scatter_sum",
    )(value)


def line_kernel(heads, same, in_ref, out_ref, local, send, recv):
    hz = lax.axis_index("head")
    others = near(heads)[::-1]
    meet([{"head": (hz + d) % heads} for d in others])

    def source(place):
        return in_ref if same else in_ref.at[place]

    own = pltpu.make_async_copy(source(hz), out_ref.at[hz], local)
    own.start()
    copies = []
    for d in others:
        place = (hz + d) % heads
        copy = pltpu.make_async_remote_copy(
            src_ref=source(place),
            dst_ref=out_ref.at[hz],
            send_sem=send.at[d - 1],
            recv_sem=recv.at[d - 1],
            device_id={"head": place},
            device_id_type=MESH,
        )
        copy.start()
        copies.append(copy)
    own.wait()
    for copy in copies:
        copy.wait()


def line_exchange(value, heads, number, same=False):
    return pl.pallas_call(
        functools.partial(line_kernel, heads, same),
        out_shape=jax.ShapeDtypeStruct((heads,) + value.shape if same else value.shape, value.dtype),
        in_specs=[ANY],
        out_specs=ANY,
        scratch_shapes=[DMA, DMA((heads - 1,)), DMA((heads - 1,))],
        compiler_params=pltpu.CompilerParams(collective_id=number, has_side_effects=True),
        name="line_exchange",
    )(value)


NT = (((1,), (1,)), ((), ()))


def experts_kernel(
    tile,
    hidden,
    x_ref,
    c_ref,
    gate_hbm,
    up_hbm,
    down_hbm,
    moe_ref,
    back_ref,
    d_gate_hbm,
    d_up_hbm,
    d_down_hbm,
    w_gate,
    w_up,
    w_down,
    d_gate_w,
    d_up_w,
    d_down_w,
    acts,
    back_gate,
    back_up,
    stage_wide,
    stage_down,
    load,
    store,
):
    step = pl.program_id(0)
    width, total = w_gate.shape

    @pl.when(step == 0)
    def _():
        loads = [
            pltpu.make_async_copy(gate_hbm, w_gate, load.at[0]),
            pltpu.make_async_copy(up_hbm, w_up, load.at[1]),
            pltpu.make_async_copy(down_hbm, w_down, load.at[2]),
        ]
        for copy in loads:
            copy.start()
        d_gate_w[...] = jnp.zeros_like(d_gate_w)
        d_up_w[...] = jnp.zeros_like(d_up_w)
        d_down_w[...] = jnp.zeros_like(d_down_w)
        for copy in loads:
            copy.wait()

    x = x_ref[:, :width]
    c = c_ref[...]
    routed = x_ref[:, width:]
    first_expert = lax.axis_index("head") * (total // hidden)
    d_gates = jnp.zeros((x.shape[0], LANES), f32)
    for begin in range(0, total, tile):
        js = pl.ds(begin, tile)
        column = begin + lax.broadcasted_iota(jnp.int32, (LANES, tile), 1)
        line = lax.broadcasted_iota(jnp.int32, (LANES, tile), 0)
        expert = first_expert + column // hidden
        here = (line == expert).astype(f32)
        both = (here + (line == expert + LOW).astype(f32)).astype(bf16)
        weight = jnp.dot(routed, both, preferred_element_type=f32)
        gate = jnp.dot(x, w_gate[:, js], preferred_element_type=f32)
        up = jnp.dot(x, w_up[:, js], preferred_element_type=f32)
        d_act = lax.dot_general(c, w_down[js, :], NT, preferred_element_type=f32)
        sigma = 1.0 / (1.0 + jnp.exp(-gate))
        silu = gate * sigma
        act = (silu * up).astype(bf16).astype(f32)
        d_gates = d_gates + lax.dot_general(
            (act * d_act).astype(bf16), here.astype(bf16), NT, preferred_element_type=f32
        )
        acts[:, js] = (act * weight).astype(bf16)
        d_act = d_act * weight
        back_up[:, js] = (d_act * silu).astype(bf16)
        back_gate[:, js] = (d_act * up * sigma * (1.0 + gate * (1.0 - sigma))).astype(bf16)
    back_ref[:, width:] = d_gates.astype(bf16)
    x_turned = x.T
    for begin in range(0, total, tile):
        js = pl.ds(begin, tile)
        d_gate_w[:, js] += jnp.dot(x_turned, back_gate[:, js], preferred_element_type=f32)
        d_up_w[:, js] += jnp.dot(x_turned, back_up[:, js], preferred_element_type=f32)
        d_down_w[js, :] += jnp.dot(acts[:, js].T, c, preferred_element_type=f32)
    for begin in range(0, width, 512):
        cs = pl.ds(begin, 512)
        moe_ref[:, cs] = jnp.dot(acts[...], w_down[:, cs], preferred_element_type=f32).astype(bf16)
        back_ref[:, cs] = (
            lax.dot_general(back_gate[...], w_gate[cs, :], NT, preferred_element_type=f32)
            + lax.dot_general(back_up[...], w_up[cs, :], NT, preferred_element_type=f32)
        ).astype(bf16)

    @pl.when(step == pl.num_programs(0) - 1)
    def _():
        rows = stage_wide.shape[1]
        jobs = [
            (source, target, stage, begin)
            for source, target, stage in (
                (d_gate_w, d_gate_hbm, stage_wide),
                (d_up_w, d_up_hbm, stage_wide),
                (d_down_w, d_down_hbm, stage_down),
            )
            for begin in range(0, source.shape[0], rows)
        ]
        flight = {}
        for index, (source, target, stage, begin) in enumerate(jobs):
            now = index % 2
            if now in flight:
                flight[now].wait()
            stage[now] = source[pl.ds(begin, rows), :].astype(bf16)
            flight[now] = pltpu.make_async_copy(
                stage.at[now], target.at[pl.ds(begin, rows), :], store.at[now]
            )
            flight[now].start()
        for copy in flight.values():
            copy.wait()


def experts(x, c, w_gate, w_up, w_down, hidden):
    tokens, columns = x.shape
    width, total = w_gate.shape
    block = min(256, tokens)
    tile = 256 if total % 256 == 0 else hidden
    return pl.pallas_call(
        functools.partial(experts_kernel, tile, hidden),
        grid=(tokens // block,),
        out_shape=(
            jax.ShapeDtypeStruct((tokens, width), bf16),
            jax.ShapeDtypeStruct((tokens, columns), bf16),
            jax.ShapeDtypeStruct((width, total), bf16),
            jax.ShapeDtypeStruct((width, total), bf16),
            jax.ShapeDtypeStruct((total, width), bf16),
        ),
        in_specs=[
            pl.BlockSpec((block, columns), lambda i: (i, 0)),
            pl.BlockSpec((block, width), lambda i: (i, 0)),
            ANY,
            ANY,
            ANY,
        ],
        out_specs=(
            pl.BlockSpec((block, width), lambda i: (i, 0)),
            pl.BlockSpec((block, columns), lambda i: (i, 0)),
            ANY,
            ANY,
            ANY,
        ),
        scratch_shapes=[
            pltpu.VMEM((width, total), bf16),
            pltpu.VMEM((width, total), bf16),
            pltpu.VMEM((total, width), bf16),
            pltpu.VMEM((width, total), f32),
            pltpu.VMEM((width, total), f32),
            pltpu.VMEM((total, width), f32),
            pltpu.VMEM((block, total), bf16),
            pltpu.VMEM((block, total), bf16),
            pltpu.VMEM((block, total), bf16),
            pltpu.VMEM((2, 64, total), bf16),
            pltpu.VMEM((2, 64, width), bf16),
            DMA((3,)),
            DMA((2,)),
        ],
        compiler_params=pltpu.CompilerParams(vmem_limit_bytes=60 << 20),
        name="experts",
    )(x, c, w_gate, w_up, w_down)


def across(value, chips, mask):
    if mask == 0:
        return value
    return lax.ppermute(value, "chip", [(i, i ^ mask) for i in range(chips)])


def sibling(value):
    return lax.ppermute(value, "core", [(0, 1), (1, 0)])


def per_device(
    layer_input,
    segments,
    routes,
    pair_rank,
    query_key_value_weight,
    output_weight,
    router_weight,
    norm_attn,
    norm_ffn,
    w_gate_up,
    w_down,
    cotangent,
):
    chips = lax.axis_size("chip")
    head_number = lax.axis_size("head")
    sequence_batch, token_rows, width = layer_input.shape
    length = segments.shape[1]
    blk = token_rows * head_number
    query_group = QUERY_HEADS // KEY_VALUE_HEADS
    key_value_location = KEY_VALUE_HEADS // head_number
    loc_experts, slice_rows = w_gate_up.shape[:2]
    top = routes.shape[2]
    tokens_present = sequence_batch * token_rows
    pairs = tokens_present * top
    line_tokens = tokens_present * head_number
    scale = HEAD_WIDTH ** (-0.5)
    hidden = FF // chips
    loc_columns = key_value_location * (query_group + 2) * HEAD_WIDTH
    chip = lax.axis_index("chip")
    core = lax.axis_index("core")
    head = lax.axis_index("head")
    seq_index = chip * 2 + core
    dense_rows = query_key_value_weight.shape[0]

    parts = w_gate_up.reshape(loc_experts, slice_rows, 2, chips, hidden).transpose(3, 2, 1, 0, 4)
    parts = parts.reshape(chips, 2, slice_rows, loc_experts * hidden)
    piled = jnp.zeros((chips, 2, 2, slice_rows, loc_experts * hidden), bf16)
    for mask in range(chips):
        piece = lax.dynamic_index_in_dim(parts, chip ^ mask, 0, keepdims=False)
        piece = across(piece, chips, mask)
        other = sibling(piece)
        piled = lax.dynamic_update_slice(piled, piece[None, None], (chip ^ mask, core, 0, 0, 0))
        piled = lax.dynamic_update_slice(piled, other[None, None], (chip ^ mask, 1 - core, 0, 0, 0))
    piled = piled.transpose(2, 0, 1, 3, 4).reshape(2, width, loc_experts * hidden)
    expert_gate, expert_up = piled[0], piled[1]
    down_other = sibling(w_down)
    expert_down = (
        jnp.where(
            core == 0,
            jnp.concatenate([w_down, down_other], axis=1),
            jnp.concatenate([down_other, w_down], axis=1),
        )
    ).reshape(loc_experts * hidden, width)

    grad_all = lax.all_gather(
        cotangent.reshape(tokens_present, width), ("chip", "head"), axis=0, tiled=True
    )
    dense_out = lax.all_gather(output_weight, ("chip", "core", "head"), axis=0, tiled=True)

    extras = jnp.concatenate([router_weight, norm_attn[:, None], norm_ffn[:, None]], axis=1)
    extras = jnp.pad(extras, ((0, 0), (0, LANES - extras.shape[1])))
    slices = query_key_value_weight.reshape(dense_rows, head_number, loc_columns).transpose(1, 0, 2)
    slices = jnp.concatenate(
        [slices, jnp.broadcast_to(extras, (head_number,) + extras.shape)], axis=2
    )
    lined = line_exchange(slices, head_number, 1)
    dense = gather(
        lined.reshape(head_number * dense_rows, loc_columns + LANES), chips, 1, True, 2
    ).reshape(width, loc_columns + LANES)
    dense_qkv = dense[:, :loc_columns]
    dense_router = dense[:, loc_columns : loc_columns + EXPERTS]
    gain_attn = dense[:, loc_columns + EXPERTS].astype(f32)
    gain_ffn = dense[:, loc_columns + EXPERTS + 1].astype(f32)

    x_line = line_exchange(layer_input.reshape(tokens_present, width), head_number, 3, True)
    x_line = x_line.reshape(line_tokens, width).astype(f32)
    normed_line = x_line * lax.rsqrt(jnp.mean(x_line * x_line, axis=1, keepdims=True) + epsilon)
    first_line = (normed_line * gain_attn).astype(bf16)

    def to_blocks(value):
        columns = value.shape[1:]
        return (
            value.reshape((head_number, sequence_batch, token_rows) + columns)
            .swapaxes(0, 1)
            .reshape((sequence_batch, blk) + columns)
        )

    def to_lines(value):
        columns = value.shape[2:]
        return (
            value.reshape((sequence_batch, head_number, token_rows) + columns)
            .swapaxes(0, 1)
            .reshape((line_tokens,) + columns)
        )

    q_start = seq_index * blk
    q_pos = q_start + jnp.arange(blk, dtype=jnp.int32)
    cosine, sine = rope_tables(q_pos, HEAD_WIDTH)
    projected = to_blocks(jnp.dot(first_line, dense_qkv, preferred_element_type=f32)).reshape(
        sequence_batch, blk, key_value_location, query_group + 2, HEAD_WIDTH
    )
    turned = rotate(projected[:, :, :, : query_group + 1], cosine, sine)
    query_rows = turned[:, :, :, :query_group].astype(bf16)
    keys_values = (
        jnp.stack([turned[:, :, :, query_group], projected[:, :, :, query_group + 1]], axis=3)
        .astype(bf16)
        .reshape(sequence_batch * blk, key_value_location * 2 * HEAD_WIDTH)
    )
    kv_columns = key_value_location * 2 * HEAD_WIDTH
    kv_all = (
        gather(keys_values, chips, 1, True, 4)
        .reshape(2 * chips, sequence_batch, blk, kv_columns)
        .transpose(1, 0, 2, 3)
        .reshape(sequence_batch, length, kv_columns)
    )
    q_seg = lax.dynamic_slice_in_dim(segments, q_start, blk, 1)

    def key_view(piece, offset, token_count):
        portion = lax.dynamic_slice_in_dim(piece, offset, token_count, 1).reshape(
            sequence_batch, token_count, key_value_location, 2, HEAD_WIDTH
        )
        return (portion[:, :, :, 0], portion[:, :, :, 1])

    def key_mask(begin, token_count):
        k_pos = begin + jnp.arange(token_count, dtype=jnp.int32)
        k_seg = lax.dynamic_slice_in_dim(segments, begin, token_count, 1)
        same = q_seg[:, :, None] == k_seg[:, None, :]
        causal = k_pos[None, None, :] <= q_pos[None, :, None]
        return (same & causal)[:, None, None]

    def sweep(function, state):
        sub = 512

        def turn(index, inner):
            offset = index * sub
            return lax.cond(
                offset <= q_start + blk - 1,
                lambda now: function(now, kv_all, offset, sub),
                lambda now: now,
                inner,
            )

        return lax.fori_loop(0, length // sub, turn, state)

    def forward_block(state, piece, offset, token_count):
        top_now, total, accum = state
        keys, values = key_view(piece, offset, token_count)
        scores = (
            jnp.einsum("sqhgd,skhd->shgqk", query_rows, keys, preferred_element_type=f32) * scale
        )
        mask = key_mask(offset, token_count)
        scores = jnp.where(mask, scores, negative)
        top_new = jnp.maximum(top_now, jnp.max(scores, axis=-1))
        weights = jnp.where(mask, jnp.exp(scores - top_new[..., None]), 0.0)
        shrink = jnp.exp(top_now - top_new)
        total = total * shrink + jnp.sum(weights, axis=-1)
        accum = accum * shrink[..., None] + jnp.einsum(
            "shgqk,skhd->shgqd", weights.astype(bf16), values, preferred_element_type=f32
        )
        return (top_new, total, accum)

    state_zero = (
        jnp.full((sequence_batch, key_value_location, query_group, blk), negative, f32),
        jnp.zeros((sequence_batch, key_value_location, query_group, blk), f32),
        jnp.zeros((sequence_batch, key_value_location, query_group, blk, HEAD_WIDTH), f32),
    )
    top_now, total, accum = sweep(forward_block, state_zero)
    lse = top_now + jnp.log(total)
    attended = accum / total[..., None]
    group_columns = key_value_location * query_group * HEAD_WIDTH
    heads_local = to_lines(
        attended.transpose(0, 3, 1, 2, 4).reshape(sequence_batch, blk, group_columns).astype(bf16)
    )
    mixed_heads = (
        line_exchange(
            heads_local.reshape(head_number, tokens_present, group_columns), head_number, 5
        )
        .transpose(1, 0, 2)
        .reshape(tokens_present, QUERY_HEADS * HEAD_WIDTH)
    )
    tokens = layer_input.reshape(tokens_present, width).astype(f32)
    middle = tokens + jnp.dot(mixed_heads, dense_out, preferred_element_type=f32)
    inverse_two = lax.rsqrt(jnp.mean(middle * middle, axis=1, keepdims=True) + epsilon)
    normed_two = middle * inverse_two
    second_input = (normed_two * gain_ffn).astype(bf16)
    router_logits = jnp.dot(second_input, dense_router, preferred_element_type=f32)
    route_flat = routes.reshape(tokens_present, top)
    hot = route_flat[:, :, None] == jnp.arange(EXPERTS, dtype=jnp.int32)[None, None, :]
    chosen = jnp.sum(jnp.where(hot, router_logits[:, None, :], 0.0), axis=2)
    gates = jax.nn.softmax(chosen, axis=-1)
    expert_of = route_flat.reshape(pairs)
    rank = pair_rank.reshape(pairs)
    slot = jnp.sum(
        (expert_of[None, :] == expert_of[:, None]) & (rank[None, :] < rank[:, None]),
        axis=1,
        dtype=jnp.int32,
    )
    kept = (slot < CAP).reshape(tokens_present, top).astype(f32)
    weights_pair = gates * kept
    spread = jnp.sum(jnp.where(hot, weights_pair[:, :, None], 0.0), axis=1)
    spread_high = spread.astype(bf16)
    spread_low = (spread - spread_high.astype(f32)).astype(bf16)
    pad = jnp.zeros((tokens_present, LOW - EXPERTS), bf16)
    payload = jnp.concatenate([second_input, spread_high, pad, spread_low, pad], axis=1)
    columns = width + LANES
    group_tokens = chips * head_number * tokens_present
    x_all = gather(payload, chips, head_number, False, 6).reshape(group_tokens, columns)
    moe_part, back_part, d_gate_w, d_up_w, d_down_w = experts(
        x_all, grad_all, expert_gate, expert_up, expert_down, hidden
    )
    back = scatter_sum(
        back_part.reshape(chips, head_number, tokens_present, columns), chips, head_number, False, 7
    )
    moe = lax.psum_scatter(moe_part, ("chip", "head"), scatter_dimension=0, tiled=True)
    mixed_out = (middle + moe.astype(f32)).astype(bf16)
    mixed_out = mixed_out.reshape(sequence_batch, token_rows, width)

    grads = jnp.stack([d_gate_w, d_up_w]).reshape(2, chips, 2, slice_rows, loc_experts * hidden)
    keep = lax.dynamic_index_in_dim(grads, core, 2, keepdims=False)
    give = lax.dynamic_index_in_dim(grads, 1 - core, 2, keepdims=False)
    shared = (keep.astype(f32) + sibling(give).astype(f32)).astype(bf16)
    piled = jnp.zeros((chips, 2, slice_rows, loc_experts * hidden), bf16)
    for mask in range(chips):
        piece = across(lax.dynamic_index_in_dim(shared, chip ^ mask, 1, keepdims=False), chips, mask)
        piled = lax.dynamic_update_slice(piled, piece[None], (chip ^ mask, 0, 0, 0))
    up_share = (
        piled.reshape(chips, 2, slice_rows, loc_experts, hidden)
        .transpose(3, 2, 1, 0, 4)
        .astype(f32)
        .reshape(loc_experts, slice_rows, 2 * FF)
    )
    d_down_w = d_down_w.reshape(loc_experts, 2, hidden // 2, width)
    keep = lax.dynamic_index_in_dim(d_down_w, core, 1, keepdims=False)
    give = lax.dynamic_index_in_dim(d_down_w, 1 - core, 1, keepdims=False)
    down_share = keep.astype(f32) + sibling(give).astype(f32)

    grad_out = cotangent.reshape(tokens_present, width).astype(f32)
    d_kept = back[:, width : width + EXPERTS]
    grad_gate = jnp.sum(jnp.where(hot, d_kept[:, None, :], 0.0), axis=2) * kept
    grad_chosen = gates * (grad_gate - jnp.sum(gates * grad_gate, axis=1, keepdims=True))
    grad_logits = jnp.sum(jnp.where(hot, grad_chosen[:, :, None], 0.0), axis=1)
    grad_router = jnp.dot(second_input.astype(f32).T, grad_logits, precision=HIGH_PRECISION)
    grad_second = back[:, :width] + jnp.dot(
        grad_logits, dense_router.astype(f32).T, precision=HIGH_PRECISION
    )
    grad_gain_ffn = jnp.sum(grad_second * normed_two, axis=0)
    scaled_two = grad_second * gain_ffn
    grad_mid = grad_out + inverse_two * (
        scaled_two - normed_two * jnp.mean(scaled_two * normed_two, axis=1, keepdims=True)
    )
    grad_attn = grad_mid.astype(bf16)
    grad_dense_out = jnp.dot(mixed_heads.T, grad_attn, preferred_element_type=f32)
    out_share = lax.psum_scatter(
        grad_dense_out.astype(bf16), ("chip", "core", "head"), scatter_dimension=0, tiled=True
    ).astype(f32)
    grad_heads = (
        jnp.dot(grad_attn, dense_out.T, preferred_element_type=f32)
        .astype(bf16)
        .reshape(tokens_present, head_number, group_columns)
        .transpose(1, 0, 2)
    )
    grad_local = to_blocks(
        line_exchange(grad_heads, head_number, 8).reshape(line_tokens, group_columns)
    ).reshape(sequence_batch, blk, key_value_location, query_group, HEAD_WIDTH)
    delta = jnp.sum(grad_local.transpose(0, 2, 3, 1, 4).astype(f32) * attended, axis=-1)

    def backward_block(state, piece, offset, token_count):
        grad_q, grad_store = state
        keys, values = key_view(piece, offset, token_count)
        scores = (
            jnp.einsum("sqhgd,skhd->shgqk", query_rows, keys, preferred_element_type=f32) * scale
        )
        mask = key_mask(offset, token_count)
        probs = jnp.where(mask, jnp.exp(scores - lse[..., None]), 0.0)
        grad_probs = jnp.einsum("sqhgd,skhd->shgqk", grad_local, values, preferred_element_type=f32)
        grad_scores = (probs * (grad_probs - delta[..., None])).astype(bf16)
        grad_q = (
            grad_q
            + jnp.einsum("shgqk,skhd->sqhgd", grad_scores, keys, preferred_element_type=f32) * scale
        )
        grad_k = (
            jnp.einsum("shgqk,sqhgd->skhd", grad_scores, query_rows, preferred_element_type=f32)
            * scale
        )
        grad_v = jnp.einsum(
            "shgqk,sqhgd->skhd", probs.astype(bf16), grad_local, preferred_element_type=f32
        )
        block_width = jnp.stack([grad_k, grad_v], axis=3).reshape(
            sequence_batch, token_count, kv_columns
        )
        grad_store = lax.dynamic_update_slice_in_dim(
            grad_store, block_width.astype(bf16), offset, 1
        )
        return (grad_q, grad_store)

    back_zero = (
        jnp.zeros((sequence_batch, blk, key_value_location, query_group, HEAD_WIDTH), f32),
        jnp.zeros((sequence_batch, length, kv_columns), bf16),
    )
    grad_q, grad_store = sweep(backward_block, back_zero)
    grad_store = (
        grad_store.reshape(sequence_batch, 2 * chips, blk, kv_columns)
        .transpose(1, 0, 2, 3)
        .reshape(chips, 2, sequence_batch * blk, kv_columns)
    )
    grad_kv = scatter_sum(grad_store, chips, 1, True, 9).reshape(
        sequence_batch, blk, key_value_location, 2, HEAD_WIDTH
    )
    grad_proj = jnp.concatenate([grad_q.astype(bf16), grad_kv.astype(bf16)], axis=3).astype(f32)
    unturned = rotate(grad_proj[:, :, :, : query_group + 1], cosine, -sine)
    grad_qkv = to_lines(
        jnp.concatenate([unturned, grad_proj[:, :, :, query_group + 1 :]], axis=3)
        .reshape(sequence_batch, blk, loc_columns)
        .astype(bf16)
    )
    grad_first_part = jnp.dot(grad_qkv, dense_qkv.T, preferred_element_type=f32)
    grad_first = jnp.sum(
        line_exchange(
            grad_first_part.astype(bf16).reshape(head_number, tokens_present, width),
            head_number,
            10,
        ).astype(f32),
        axis=0,
    )
    grad_gain_attn = jnp.sum(grad_first_part * normed_line, axis=0)
    inverse_one = lax.rsqrt(jnp.mean(tokens * tokens, axis=1, keepdims=True) + epsilon)
    normed_one = tokens * inverse_one
    scaled_one = grad_first * gain_attn
    grad_input = grad_mid + inverse_one * (
        scaled_one - normed_one * jnp.mean(scaled_one * normed_one, axis=1, keepdims=True)
    )
    grad_dense_qkv = jnp.dot(first_line.T, grad_qkv, preferred_element_type=f32)
    sums = jnp.concatenate(
        [
            grad_dense_qkv,
            grad_router,
            grad_gain_attn[:, None],
            grad_gain_ffn[:, None],
            jnp.zeros((width, LANES - EXPERTS - 2), f32),
        ],
        axis=1,
    ).astype(bf16)
    sums = scatter_sum(
        sums.reshape(chips, 2, head_number * dense_rows, loc_columns + LANES), chips, 1, True, 11
    )
    sums = line_exchange(
        sums.reshape(head_number, dense_rows, loc_columns + LANES), head_number, 12
    )
    qkv_share = sums[:, :, :loc_columns].transpose(1, 0, 2).reshape(dense_rows, -1)
    extra = jnp.sum(sums[:, :, loc_columns:], axis=0)
    return (
        mixed_out,
        grad_input.reshape(sequence_batch, token_rows, width),
        qkv_share,
        out_share,
        extra[:, :EXPERTS],
        extra[:, EXPERTS],
        extra[:, EXPERTS + 1],
        up_share,
        down_share,
    )


def solution(mesh):
    grid = mesh.devices
    seq, heads = grid.shape
    split = Mesh(grid.reshape(seq // 2, 2, heads), ("chip", "core", "head"))
    places = ("chip", "core", "head")
    inner = ("chip", "core")
    placed = (
        P(None, places, None),
        P(),
        P(None, places, None),
        P(None, places, None),
        P(places, None),
        P(places, None),
        P(places, None),
        P(places),
        P(places),
        P("head", inner, None),
        P("head", inner, None),
        P(None, places, None),
    )
    return jax.shard_map(
        per_device,
        mesh=split,
        in_specs=placed,
        out_specs=(
            P(None, places, None),
            P(None, places, None),
            P(places, None),
            P(places, None),
            P(places, None),
            P(places),
            P(places),
            P("head", inner, None),
            P("head", inner, None),
        ),
        check_vma=False,
    )
```

```python
import functools

import jax
import jax.numpy as jnp
from jax import lax
from jax.experimental import pallas as pl
from jax.experimental.pallas import tpu as pltpu
from jax.sharding import Mesh, PartitionSpec as P

MODEL_WIDTH = 1536
QUERY_HEADS = 24
KEY_VALUE_HEADS = 8
HEAD_WIDTH = 64
EXPERTS = 40
FF = 512
CAP = 25
LANES = 128
LOW = 64

epsilon = 1e-06
negative = -1e30
theta = 10000.0
HIGH_PRECISION = lax.Precision.HIGHEST
MESH = pl.DeviceIdType.MESH
f32 = jnp.float32
bf16 = jnp.bfloat16
ANY = pl.BlockSpec(memory_space=pl.ANY)
WHOLE = pl.BlockSpec(memory_space=pltpu.VMEM)
DMA = pltpu.SemaphoreType.DMA


def rope_tables(token_positions, head_size):
    half = head_size // 2
    freq = theta ** (-jnp.arange(half, dtype=jnp.float32) / half)
    angle = token_positions.astype(jnp.float32)[:, None] * freq[None, :]
    return (jnp.cos(angle)[None, :, None, None, :], jnp.sin(angle)[None, :, None, None, :])


def rotate(value, cosine, sine):
    half = value.shape[-1] // 2
    first = value[..., :half]
    second = value[..., half:]
    return jnp.concatenate(
        [first * cosine - second * sine, second * cosine + first * sine], axis=-1
    )


def digits(count):
    number = count.bit_length() - 1
    assert 1 << number == count
    return number


def flip(index, mask):
    out = index
    bit = 0
    while (1 << bit) <= mask:
        if (mask >> bit) & 1:
            out = out + (1 - 2 * ((index // (1 << bit)) % 2)) * (1 << bit)
        bit += 1
    return out


def subsets(bits):
    out = [0]
    for bit in bits:
        out = out + [mask | (1 << bit) for mask in out]
    return out


def near(count):
    return sorted(range(1, count), key=lambda step: min(step, count - step))


def meet(peers):
    sem = pltpu.get_barrier_semaphore()
    for peer in peers:
        pl.semaphore_signal(sem, inc=1, device_id=peer, device_id_type=MESH)
    pl.semaphore_wait(sem, len(peers))


class Cube:
    def __init__(self, chips, with_core):
        self.chips = chips
        self.chip_digits = digits(chips)
        self.number = self.chip_digits + int(with_core)
        self.with_core = with_core
        up = tuple(range(self.chip_digits))
        core = (self.chip_digits,) if with_core else ()
        self.gather_orders = (up + core, up[::-1] + core)
        self.scatter_orders = (core + up, core + up[::-1])

    def place(self, mask):
        chip = flip(lax.axis_index("chip"), mask & (self.chips - 1))
        if not self.with_core:
            return (chip,)
        return (chip, flip(lax.axis_index("core"), mask >> self.chip_digits))

    def peer(self, digit):
        if digit < self.chip_digits:
            return {"chip": flip(lax.axis_index("chip"), 1 << digit)}
        return {"core": flip(lax.axis_index("core"), 1)}


def gather_kernel(cube, heads, in_ref, out_ref, local, line_send, line_recv, send, recv):
    hz = lax.axis_index("head")
    rows = in_ref.shape[0]
    half = rows // 2
    others = near(heads) if heads > 1 else []
    meet(
        [cube.peer(digit) for digit in range(cube.number)]
        + [{"head": (hz + d) % heads} for d in others]
    )

    def at(mask, d):
        index = cube.place(mask)
        return index + ((hz + heads - d) % heads,) if heads > 1 else index

    own = pltpu.make_async_copy(in_ref, out_ref.at[at(0, 0)], local)
    own.start()
    line = {}
    for d in others:
        line[d] = pltpu.make_async_remote_copy(
            src_ref=in_ref,
            dst_ref=out_ref.at[at(0, 0)],
            send_sem=line_send.at[d - 1],
            recv_sem=line_recv.at[d - 1],
            device_id={"head": (hz + d) % heads},
            device_id_type=MESH,
        )
        line[d].start()
    copies = {}

    def forward(side, mask, d):
        order = cube.gather_orders[side]
        last = max([k for k in range(cube.number) if (mask >> order[k]) & 1], default=-1)
        for k in range(last + 1, cube.number):
            later = mask | (1 << order[k])
            part = pl.ds(side * half, half)
            place = out_ref.at[at(mask, d) + (part,)]
            copy = pltpu.make_async_remote_copy(
                src_ref=in_ref.at[part] if mask == 0 and d == 0 else place,
                dst_ref=place,
                send_sem=send.at[side, later, d],
                recv_sem=recv.at[side, later, d],
                device_id=cube.peer(order[k]),
                device_id_type=MESH,
            )
            copy.start()
            copies[(side, later, d)] = copy

    for side in range(2):
        forward(side, 0, 0)
    for d in others:
        line[d].wait_recv()
        for side in range(2):
            forward(side, 0, d)
    for mask in sorted(range(1, 1 << cube.number), key=lambda m: bin(m).count("1")):
        for d in [0] + others:
            for side in range(2):
                copies[(side, mask, d)].wait_recv()
                forward(side, mask, d)
    own.wait()
    for copy in list(line.values()) + list(copies.values()):
        copy.wait_send()


def gather(value, chips, heads, with_core, number):
    rows, columns = value.shape
    cube = Cube(chips, with_core)
    lead = (chips,) + ((2,) if with_core else ()) + ((heads,) if heads > 1 else ())
    steps = max(heads - 1, 1)
    return pl.pallas_call(
        functools.partial(gather_kernel, cube, heads),
        out_shape=jax.ShapeDtypeStruct(lead + (rows, columns), value.dtype),
        in_specs=[ANY],
        out_specs=ANY,
        scratch_shapes=[
            DMA,
            DMA((steps,)),
            DMA((steps,)),
            DMA((2, 1 << cube.number, heads)),
            DMA((2, 1 << cube.number, heads)),
        ],
        compiler_params=pltpu.CompilerParams(collective_id=number, has_side_effects=True),
        name="gather",
    )(value)


def scatter_kernel(cube, heads, in_ref, out_ref, *refs):
    count = cube.number
    arrived, parts = refs[:count], refs[count : 2 * count - 1]
    line_out, line_in, line_send, line_recv, send, recv = refs[2 * count - 1 :]
    hz = lax.axis_index("head")
    half = in_ref.shape[-2] // 2
    others = near(heads) if heads > 1 else []
    order_of_lines = others[::-1] + [0]
    meet(
        [cube.peer(digit) for digit in range(count)] + [{"head": (hz + d) % heads} for d in others]
    )
    copies = {}

    def slot(side, k, mask):
        return subsets(cube.scatter_orders[side][k + 1 :]).index(mask)

    def mine(side, mask, d):
        index = cube.place(mask)
        if heads > 1:
            index = index + ((hz + d) % heads,)
        return in_ref.at[index + (pl.ds(side * half, half),)]

    def pass_on(side, k, mask, d, source):
        where = slot(side, k, mask)
        copy = pltpu.make_async_remote_copy(
            src_ref=source,
            dst_ref=arrived[k].at[side, where, d],
            send_sem=send.at[side, k, where, d],
            recv_sem=recv.at[side, k, where, d],
            device_id=cube.peer(cube.scatter_orders[side][k]),
            device_id_type=MESH,
        )
        copy.start()
        copies[(side, k, mask, d)] = copy

    def total(side, steps, mask, d):
        value = mine(side, mask, d)[...].astype(f32)
        for j in range(steps):
            copies[(side, j, mask, d)].wait_recv()
            value = value + arrived[j][side, slot(side, j, mask), d].astype(f32)
        return value

    for k in range(count):
        for d in order_of_lines:
            for side in range(2):
                order = cube.scatter_orders[side]
                for mask in subsets(order[k + 1 :])[::-1]:
                    full = mask | (1 << order[k])
                    if k == 0:
                        source = mine(side, full, d)
                    else:
                        source = parts[k - 1].at[side, slot(side, k, mask), d]
                        source[...] = total(side, k, full, d).astype(bf16)
                    pass_on(side, k, mask, d, source)
    line = {}
    for d in order_of_lines:
        for side in range(2):
            value = total(side, count, 0, d)
            if d:
                line_out[d - 1, pl.ds(side * half, half)] = value.astype(bf16)
            else:
                out_ref[pl.ds(side * half, half)] = value
        if d:
            line[d] = pltpu.make_async_remote_copy(
                src_ref=line_out.at[d - 1],
                dst_ref=line_in.at[d - 1],
                send_sem=line_send.at[d - 1],
                recv_sem=line_recv.at[d - 1],
                device_id={"head": (hz + d) % heads},
                device_id_type=MESH,
            )
            line[d].start()
    for d in others:
        line[d].wait_recv()
        out_ref[...] += line_in[d - 1].astype(f32)
    for copy in list(line.values()) + list(copies.values()):
        copy.wait_send()


def scatter_sum(value, chips, heads, with_core, number):
    rows, columns = value.shape[-2:]
    cube = Cube(chips, with_core)
    half = rows // 2
    steps = max(heads - 1, 1)
    line_rows = rows if heads > 1 else 16
    slots = [(1 << cube.number) >> (k + 1) for k in range(cube.number)]
    if 2 * value.size + 4 * heads * half * columns * (sum(slots) + sum(slots[1:])) > 40 << 20:
        names = ("chip", "core") if with_core else ("chip",)
        names = names + (("head",) if heads > 1 else ())
        flat = value.reshape(-1, columns)
        return lax.psum_scatter(flat, names, scatter_dimension=0, tiled=True).astype(f32)
    return pl.pallas_call(
        functools.partial(scatter_kernel, cube, heads),
        out_shape=jax.ShapeDtypeStruct((rows, columns), f32),
        in_specs=[WHOLE],
        out_specs=WHOLE,
        scratch_shapes=[pltpu.VMEM((2, s, heads, half, columns), bf16) for s in slots]
        + [pltpu.VMEM((2, s, heads, half, columns), bf16) for s in slots[1:]]
        + [
            pltpu.VMEM((steps, line_rows, columns), bf16),
            pltpu.VMEM((steps, line_rows, columns), bf16),
            DMA((steps,)),
            DMA((steps,)),
            DMA((2, cube.number, slots[0], heads)),
            DMA((2, cube.number, slots[0], heads)),
        ],
        compiler_params=pltpu.CompilerParams(
            collective_id=number, has_side_effects=True, vmem_limit_bytes=56 << 20
        ),
        name="scatter_sum",
    )(value)


def line_kernel(heads, same, in_ref, out_ref, local, send, recv):
    hz = lax.axis_index("head")
    others = near(heads)[::-1]
    meet([{"head": (hz + d) % heads} for d in others])

    def source(place):
        return in_ref if same else in_ref.at[place]

    own = pltpu.make_async_copy(source(hz), out_ref.at[hz], local)
    own.start()
    copies = []
    for d in others:
        place = (hz + d) % heads
        copy = pltpu.make_async_remote_copy(
            src_ref=source(place),
            dst_ref=out_ref.at[hz],
            send_sem=send.at[d - 1],
            recv_sem=recv.at[d - 1],
            device_id={"head": place},
            device_id_type=MESH,
        )
        copy.start()
        copies.append(copy)
    own.wait()
    for copy in copies:
        copy.wait()


def line_exchange(value, heads, number, same=False):
    return pl.pallas_call(
        functools.partial(line_kernel, heads, same),
        out_shape=jax.ShapeDtypeStruct((heads,) + value.shape if same else value.shape, value.dtype),
        in_specs=[ANY],
        out_specs=ANY,
        scratch_shapes=[DMA, DMA((heads - 1,)), DMA((heads - 1,))],
        compiler_params=pltpu.CompilerParams(collective_id=number, has_side_effects=True),
        name="line_exchange",
    )(value)


NT = (((1,), (1,)), ((), ()))


def experts_kernel(
    tile,
    hidden,
    x_ref,
    c_ref,
    gate_hbm,
    up_hbm,
    down_hbm,
    moe_ref,
    back_ref,
    d_gate_hbm,
    d_up_hbm,
    d_down_hbm,
    w_gate,
    w_up,
    w_down,
    d_gate_w,
    d_up_w,
    d_down_w,
    acts,
    back_gate,
    back_up,
    stage_wide,
    stage_down,
    load,
    store,
):
    step = pl.program_id(0)
    width, total = w_gate.shape

    @pl.when(step == 0)
    def _():
        loads = [
            pltpu.make_async_copy(gate_hbm, w_gate, load.at[0]),
            pltpu.make_async_copy(up_hbm, w_up, load.at[1]),
            pltpu.make_async_copy(down_hbm, w_down, load.at[2]),
        ]
        for copy in loads:
            copy.start()
        d_gate_w[...] = jnp.zeros_like(d_gate_w)
        d_up_w[...] = jnp.zeros_like(d_up_w)
        d_down_w[...] = jnp.zeros_like(d_down_w)
        for copy in loads:
            copy.wait()

    x = x_ref[:, :width]
    c = c_ref[...]
    routed = x_ref[:, width:]
    first_expert = lax.axis_index("head") * (total // hidden)
    d_gates = jnp.zeros((x.shape[0], LANES), f32)
    for begin in range(0, total, tile):
        js = pl.ds(begin, tile)
        column = begin + lax.broadcasted_iota(jnp.int32, (LANES, tile), 1)
        line = lax.broadcasted_iota(jnp.int32, (LANES, tile), 0)
        expert = first_expert + column // hidden
        here = (line == expert).astype(f32)
        both = (here + (line == expert + LOW).astype(f32)).astype(bf16)
        weight = jnp.dot(routed, both, preferred_element_type=f32)
        gate = jnp.dot(x, w_gate[:, js], preferred_element_type=f32)
        up = jnp.dot(x, w_up[:, js], preferred_element_type=f32)
        d_act = lax.dot_general(c, w_down[js, :], NT, preferred_element_type=f32)
        sigma = 1.0 / (1.0 + jnp.exp(-gate))
        silu = gate * sigma
        act = (silu * up).astype(bf16).astype(f32)
        d_gates = d_gates + lax.dot_general(
            (act * d_act).astype(bf16), here.astype(bf16), NT, preferred_element_type=f32
        )
        acts[:, js] = (act * weight).astype(bf16)
        d_act = d_act * weight
        back_up[:, js] = (d_act * silu).astype(bf16)
        back_gate[:, js] = (d_act * up * sigma * (1.0 + gate * (1.0 - sigma))).astype(bf16)
    back_ref[:, width:] = d_gates.astype(bf16)
    x_turned = x.T
    for begin in range(0, total, tile):
        js = pl.ds(begin, tile)
        d_gate_w[:, js] += jnp.dot(x_turned, back_gate[:, js], preferred_element_type=f32)
        d_up_w[:, js] += jnp.dot(x_turned, back_up[:, js], preferred_element_type=f32)
        d_down_w[js, :] += jnp.dot(acts[:, js].T, c, preferred_element_type=f32)
    for begin in range(0, width, 512):
        cs = pl.ds(begin, 512)
        moe_ref[:, cs] = jnp.dot(acts[...], w_down[:, cs], preferred_element_type=f32).astype(bf16)
        back_ref[:, cs] = (
            lax.dot_general(back_gate[...], w_gate[cs, :], NT, preferred_element_type=f32)
            + lax.dot_general(back_up[...], w_up[cs, :], NT, preferred_element_type=f32)
        ).astype(bf16)

    @pl.when(step == pl.num_programs(0) - 1)
    def _():
        rows = stage_wide.shape[1]
        jobs = [
            (source, target, stage, begin)
            for source, target, stage in (
                (d_gate_w, d_gate_hbm, stage_wide),
                (d_up_w, d_up_hbm, stage_wide),
                (d_down_w, d_down_hbm, stage_down),
            )
            for begin in range(0, source.shape[0], rows)
        ]
        flight = {}
        for index, (source, target, stage, begin) in enumerate(jobs):
            now = index % 2
            if now in flight:
                flight[now].wait()
            stage[now] = source[pl.ds(begin, rows), :].astype(bf16)
            flight[now] = pltpu.make_async_copy(
                stage.at[now], target.at[pl.ds(begin, rows), :], store.at[now]
            )
            flight[now].start()
        for copy in flight.values():
            copy.wait()


def experts(x, c, w_gate, w_up, w_down, hidden):
    tokens, columns = x.shape
    width, total = w_gate.shape
    block = min(256, tokens)
    tile = 256 if total % 256 == 0 else hidden
    return pl.pallas_call(
        functools.partial(experts_kernel, tile, hidden),
        grid=(tokens // block,),
        out_shape=(
            jax.ShapeDtypeStruct((tokens, width), bf16),
            jax.ShapeDtypeStruct((tokens, columns), bf16),
            jax.ShapeDtypeStruct((width, total), bf16),
            jax.ShapeDtypeStruct((width, total), bf16),
            jax.ShapeDtypeStruct((total, width), bf16),
        ),
        in_specs=[
            pl.BlockSpec((block, columns), lambda i: (i, 0)),
            pl.BlockSpec((block, width), lambda i: (i, 0)),
            ANY,
            ANY,
            ANY,
        ],
        out_specs=(
            pl.BlockSpec((block, width), lambda i: (i, 0)),
            pl.BlockSpec((block, columns), lambda i: (i, 0)),
            ANY,
            ANY,
            ANY,
        ),
        scratch_shapes=[
            pltpu.VMEM((width, total), bf16),
            pltpu.VMEM((width, total), bf16),
            pltpu.VMEM((total, width), bf16),
            pltpu.VMEM((width, total), f32),
            pltpu.VMEM((width, total), f32),
            pltpu.VMEM((total, width), f32),
            pltpu.VMEM((block, total), bf16),
            pltpu.VMEM((block, total), bf16),
            pltpu.VMEM((block, total), bf16),
            pltpu.VMEM((2, 64, total), bf16),
            pltpu.VMEM((2, 64, width), bf16),
            DMA((3,)),
            DMA((2,)),
        ],
        compiler_params=pltpu.CompilerParams(vmem_limit_bytes=60 << 20),
        name="experts",
    )(x, c, w_gate, w_up, w_down)


def turn_kernel(cube, heads, tile, hidden, own_ref, c_hbm, gate_hbm, up_hbm, down_hbm, out_ref, moe_hbm, d_gate_hbm, d_up_hbm, d_down_hbm, *refs):
    chips, count = cube.chips, cube.number
    tokens, turned, cots, w_gate, w_up, w_down, acts, back_gate, back_up, d_gates, moe_stage, line_in = refs[:12]
    arrived = refs[12 : 12 + count]
    load, store, own_sem, line_send, line_recv, send, recv, back_send, back_recv, end_send, end_recv = refs[12 + count :]
    hz = lax.axis_index("head")
    rows, columns = own_ref.shape
    width, total = w_gate.shape
    half = rows // 2
    line = heads * rows
    others = near(heads)
    masks = sorted(range(chips), key=lambda m: bin(m).count("1"))

    loads = [
        pltpu.make_async_copy(source, target, load.at[index])
        for index, (source, target) in enumerate(
            ((gate_hbm, w_gate), (up_hbm, w_up), (down_hbm, w_down), (c_hbm, cots))
        )
    ]
    for copy in loads:
        copy.start()
    meet([cube.peer(digit) for digit in range(count)] + [{"head": (hz + d) % heads} for d in others])

    def part(side):
        return pl.ds(side * half, half)

    def line_copy(d):
        return pltpu.make_async_remote_copy(
            src_ref=own_ref,
            dst_ref=tokens.at[cube.place(0) + (hz,)],
            send_sem=line_send.at[d - 1],
            recv_sem=line_recv.at[d - 1],
            device_id={"head": (hz + d) % heads},
            device_id_type=MESH,
        )

    def plane_copy(side, mask, k, d):
        digit = cube.gather_orders[side][k]
        later = mask | (1 << digit)
        place = tokens.at[cube.place(mask) + ((hz + heads - d) % heads, part(side))]
        return pltpu.make_async_remote_copy(
            src_ref=own_ref.at[part(side)] if mask == 0 and d == 0 else place,
            dst_ref=place,
            send_sem=send.at[side, later, d],
            recv_sem=recv.at[side, later, d],
            device_id=cube.peer(digit),
            device_id_type=MESH,
        )

    def steps_after(side, mask):
        order = cube.gather_orders[side]
        last = max([k for k in range(count) if (mask >> order[k]) & 1], default=-1)
        return range(last + 1, count)

    def arrival(side, mask, d):
        order = cube.gather_orders[side]
        k = max(k for k in range(count) if (mask >> order[k]) & 1)
        return plane_copy(side, mask & ~(1 << order[k]), k, d)

    def receive(mask):
        for d in [0] + others:
            if mask == 0 and d:
                line_copy(d).wait_recv()
            for side in range(2):
                if mask:
                    arrival(side, mask, d).wait_recv()
                for k in steps_after(side, mask):
                    plane_copy(side, mask, k, d).start()

    def sent(mask):
        for d in [0] + others:
            for side in range(2):
                for k in steps_after(side, mask):
                    plane_copy(side, mask, k, d).wait_send()

    def slot(side, k, mask):
        return subsets(cube.scatter_orders[side][k + 1 :]).index(mask)

    def back_place(side, mask, d):
        return tokens.at[cube.place(mask) + ((hz + d) % heads, part(side))]

    def back_copy(side, k, mask, d):
        order = cube.scatter_orders[side]
        where = slot(side, k, mask)
        return pltpu.make_async_remote_copy(
            src_ref=back_place(side, mask | (1 << order[k]), d),
            dst_ref=arrived[k].at[side, where, d],
            send_sem=back_send.at[side, k, where, d],
            recv_sem=back_recv.at[side, k, where, d],
            device_id=cube.peer(order[k]),
            device_id_type=MESH,
        )

    def end_copy(d):
        return pltpu.make_async_remote_copy(
            src_ref=tokens.at[cube.place(0) + ((hz + d) % heads,)],
            dst_ref=line_in.at[d - 1],
            send_sem=end_send.at[d - 1],
            recv_sem=end_recv.at[d - 1],
            device_id={"head": (hz + d) % heads},
            device_id_type=MESH,
        )

    outward = others[::-1] + [0]

    def give(mask):
        for d in outward:
            for side in range(2):
                first = 1 << cube.scatter_orders[side][0]
                if mask & first:
                    back_copy(side, 0, mask & ~first, d).start()

    own = pltpu.make_async_copy(own_ref, tokens.at[cube.place(0) + (hz,)], own_sem)
    own.start()
    for d in others:
        line_copy(d).start()
    for copy in loads:
        copy.wait()
    own.wait()

    first_expert = hz * (total // hidden)
    span = min(512, width)

    def compute(place):
        here = pl.ds(place * line, line)
        x = tokens[place, :, :, pl.ds(0, width)].reshape(line, width)
        c = cots[here, :]
        routed = tokens[place, :, :, pl.ds(width, LANES)].reshape(line, LANES)
        turned[:, here] = x.T
        d_gates[...] = jnp.zeros_like(d_gates)

        @pl.loop(0, total // tile)
        def _(j):
            js = pl.ds(pl.multiple_of(j * tile, tile), tile)
            column = j * tile + lax.broadcasted_iota(jnp.int32, (LANES, tile), 1)
            lane = lax.broadcasted_iota(jnp.int32, (LANES, tile), 0)
            expert = first_expert + column // hidden
            high = (lane == expert).astype(f32)
            both = (high + (lane == expert + LOW).astype(f32)).astype(bf16)
            weight = jnp.dot(routed, both, preferred_element_type=f32)
            gate = jnp.dot(x, w_gate[:, js], preferred_element_type=f32)
            up = jnp.dot(x, w_up[:, js], preferred_element_type=f32)
            d_act = lax.dot_general(c, w_down[js, :], NT, preferred_element_type=f32)
            sigma = 1.0 / (1.0 + jnp.exp(-gate))
            silu = gate * sigma
            act = (silu * up).astype(bf16).astype(f32)
            d_gates[...] += lax.dot_general(
                (act * d_act).astype(bf16), high.astype(bf16), NT, preferred_element_type=f32
            )
            acts[here, js] = (act * weight).astype(bf16)
            d_act = d_act * weight
            back_up[here, js] = (d_act * silu).astype(bf16)
            back_gate[here, js] = (d_act * up * sigma * (1.0 + gate * (1.0 - sigma))).astype(bf16)

    def results(place, step):
        here = pl.ds(place * line, line)

        @pl.loop(0, width // span)
        def _(j):
            cs = pl.ds(pl.multiple_of(j * span, span), span)
            value = lax.dot_general(
                back_gate[here, :], w_gate[cs, :], NT, preferred_element_type=f32
            ) + lax.dot_general(back_up[here, :], w_up[cs, :], NT, preferred_element_type=f32)
            tokens[place, :, :, cs] = value.astype(bf16).reshape(heads, rows, span)

        tokens[place, :, :, pl.ds(width, LANES)] = (
            d_gates[...].astype(bf16).reshape(heads, rows, LANES)
        )

    def moe_copy(place):
        return pltpu.make_async_copy(
            moe_stage, moe_hbm.at[pl.ds(place * line, line)], store.at[3]
        )

    def mixed(place, step):
        here = pl.ds(place * line, line)

        @pl.when(step > 0)
        def _():
            moe_copy(place).wait()

        @pl.loop(0, width // span)
        def _(j):
            cs = pl.ds(pl.multiple_of(j * span, span), span)
            moe_stage[:, cs] = jnp.dot(
                acts[here, :], w_down[:, cs], preferred_element_type=f32
            ).astype(bf16)

        moe_copy(place).start()

    @pl.loop(0, chips)
    def _(step):
        seen = -1
        for index, mask in enumerate(masks):
            level = bin(mask).count("1")
            if level > seen:
                seen = level

                @pl.when(step == index)
                def _():
                    for other in masks:
                        if bin(other).count("1") == level:
                            receive(other)

        place = cube.place(0)[0] * 0
        for index, mask in enumerate(masks):
            place = jnp.where(step == index, cube.place(mask)[0], place)
        compute(place)
        for index, mask in enumerate(masks):

            @pl.when(step == index)
            def _():
                sent(mask)

        results(place, step)
        for index, mask in enumerate(masks):
            if mask:

                @pl.when(step == index)
                def _():
                    give(mask)

        mixed(place, step)

    def sums(side, steps, mask, d):
        value = back_place(side, mask, d)[...].astype(f32)
        for j in range(steps):
            back_copy(side, j, mask, d).wait_recv()
            value = value + arrived[j][side, slot(side, j, mask), d].astype(f32)
        return value

    def weights_grad(left, right, target, hbm, index, by_rows):
        @pl.loop(0, total // tile)
        def _(j):
            js = pl.ds(pl.multiple_of(j * tile, tile), tile)
            if by_rows:
                value = jnp.dot(left[:, js].T, right[...], preferred_element_type=f32)
                target[js, :] = value.astype(bf16)
            else:
                value = jnp.dot(left[...], right[:, js], preferred_element_type=f32)
                target[:, js] = value.astype(bf16)

        pltpu.make_async_copy(target, hbm, store.at[index]).start()

    weights_grad(turned, back_gate, w_gate, d_gate_hbm, 0, False)
    for k in range(1, count):
        for d in outward:
            for side in range(2):
                order = cube.scatter_orders[side]
                for mask in subsets(order[k + 1 :])[::-1]:
                    full = mask | (1 << order[k])
                    back_place(side, full, d)[...] = sums(side, k, full, d).astype(bf16)
                    back_copy(side, k, mask, d).start()
    weights_grad(turned, back_up, w_up, d_up_hbm, 1, False)
    for d in outward:
        for side in range(2):
            value = sums(side, count, 0, d)
            if d:
                back_place(side, 0, d)[...] = value.astype(bf16)
            else:
                out_ref[part(side)] = value
        if d:
            end_copy(d).start()
    moe_copy(0).wait()
    weights_grad(acts, cots, w_down, d_down_hbm, 2, True)
    for d in others:
        end_copy(d).wait_recv()
        out_ref[...] += line_in[d - 1].astype(f32)
    for d in others:
        line_copy(d).wait_send()
        end_copy(d).wait_send()
    for side in range(2):
        for k in range(count):
            for mask in subsets(cube.scatter_orders[side][k + 1 :]):
                for d in outward:
                    back_copy(side, k, mask, d).wait_send()
    for index, (source, hbm) in enumerate(
        ((w_gate, d_gate_hbm), (w_up, d_up_hbm), (w_down, d_down_hbm))
    ):
        pltpu.make_async_copy(source, hbm, store.at[index]).wait()


def expert_turn(payload, c, w_gate, w_up, w_down, hidden, chips, heads, number):
    rows, columns = payload.shape
    width, total = w_gate.shape
    cube = Cube(chips, False)
    count = cube.number
    tokens = chips * heads * rows
    half = rows // 2
    tile = 256 if total % 256 == 0 else hidden
    slots = [chips >> (k + 1) for k in range(count)]
    return pl.pallas_call(
        functools.partial(turn_kernel, cube, heads, tile, hidden),
        out_shape=(
            jax.ShapeDtypeStruct((rows, columns), f32),
            jax.ShapeDtypeStruct((tokens, width), bf16),
            jax.ShapeDtypeStruct((width, total), bf16),
            jax.ShapeDtypeStruct((width, total), bf16),
            jax.ShapeDtypeStruct((total, width), bf16),
        ),
        in_specs=[WHOLE, ANY, ANY, ANY, ANY],
        out_specs=(WHOLE, ANY, ANY, ANY, ANY),
        scratch_shapes=[
            pltpu.VMEM((chips, heads, rows, columns), bf16),
            pltpu.VMEM((width, tokens), bf16),
            pltpu.VMEM((tokens, width), bf16),
            pltpu.VMEM((width, total), bf16),
            pltpu.VMEM((width, total), bf16),
            pltpu.VMEM((total, width), bf16),
            pltpu.VMEM((tokens, total), bf16),
            pltpu.VMEM((tokens, total), bf16),
            pltpu.VMEM((tokens, total), bf16),
            pltpu.VMEM((heads * rows, LANES), f32),
            pltpu.VMEM((heads * rows, width), bf16),
            pltpu.VMEM((heads - 1, rows, columns), bf16),
        ]
        + [pltpu.VMEM((2, s, heads, half, columns), bf16) for s in slots]
        + [
            DMA((4,)),
            DMA((4,)),
            DMA,
            DMA((heads - 1,)),
            DMA((heads - 1,)),
            DMA((2, chips, heads)),
            DMA((2, chips, heads)),
            DMA((2, count, slots[0], heads)),
            DMA((2, count, slots[0], heads)),
            DMA((heads - 1,)),
            DMA((heads - 1,)),
        ],
        compiler_params=pltpu.CompilerParams(
            collective_id=number, has_side_effects=True, vmem_limit_bytes=63 << 20
        ),
        name="expert_turn",
    )(payload, c, w_gate, w_up, w_down)


def across(value, chips, mask):
    if mask == 0:
        return value
    return lax.ppermute(value, "chip", [(i, i ^ mask) for i in range(chips)])


def sibling(value):
    return lax.ppermute(value, "core", [(0, 1), (1, 0)])


def per_device(
    layer_input,
    segments,
    routes,
    pair_rank,
    query_key_value_weight,
    output_weight,
    router_weight,
    norm_attn,
    norm_ffn,
    w_gate_up,
    w_down,
    cotangent,
):
    chips = lax.axis_size("chip")
    head_number = lax.axis_size("head")
    sequence_batch, token_rows, width = layer_input.shape
    length = segments.shape[1]
    blk = token_rows * head_number
    query_group = QUERY_HEADS // KEY_VALUE_HEADS
    key_value_location = KEY_VALUE_HEADS // head_number
    loc_experts, slice_rows = w_gate_up.shape[:2]
    top = routes.shape[2]
    tokens_present = sequence_batch * token_rows
    pairs = tokens_present * top
    line_tokens = tokens_present * head_number
    scale = HEAD_WIDTH ** (-0.5)
    hidden = FF // chips
    loc_columns = key_value_location * (query_group + 2) * HEAD_WIDTH
    chip = lax.axis_index("chip")
    core = lax.axis_index("core")
    head = lax.axis_index("head")
    seq_index = chip * 2 + core
    dense_rows = query_key_value_weight.shape[0]

    parts = w_gate_up.reshape(loc_experts, slice_rows, 2, chips, hidden).transpose(3, 2, 1, 0, 4)
    parts = parts.reshape(chips, 2, slice_rows, loc_experts * hidden)
    piled = jnp.zeros((chips, 2, 2, slice_rows, loc_experts * hidden), bf16)
    for mask in range(chips):
        piece = lax.dynamic_index_in_dim(parts, chip ^ mask, 0, keepdims=False)
        piece = across(piece, chips, mask)
        other = sibling(piece)
        piled = lax.dynamic_update_slice(piled, piece[None, None], (chip ^ mask, core, 0, 0, 0))
        piled = lax.dynamic_update_slice(piled, other[None, None], (chip ^ mask, 1 - core, 0, 0, 0))
    piled = piled.transpose(2, 0, 1, 3, 4).reshape(2, width, loc_experts * hidden)
    expert_gate, expert_up = piled[0], piled[1]
    down_other = sibling(w_down)
    expert_down = (
        jnp.where(
            core == 0,
            jnp.concatenate([w_down, down_other], axis=1),
            jnp.concatenate([down_other, w_down], axis=1),
        )
    ).reshape(loc_experts * hidden, width)

    grad_all = lax.all_gather(
        cotangent.reshape(tokens_present, width), ("chip", "head"), axis=0, tiled=True
    )
    dense_out = lax.all_gather(output_weight, ("chip", "core", "head"), axis=0, tiled=True)

    extras = jnp.concatenate([router_weight, norm_attn[:, None], norm_ffn[:, None]], axis=1)
    extras = jnp.pad(extras, ((0, 0), (0, LANES - extras.shape[1])))
    slices = query_key_value_weight.reshape(dense_rows, head_number, loc_columns).transpose(1, 0, 2)
    slices = jnp.concatenate(
        [slices, jnp.broadcast_to(extras, (head_number,) + extras.shape)], axis=2
    )
    lined = line_exchange(slices, head_number, 1)
    dense = gather(
        lined.reshape(head_number * dense_rows, loc_columns + LANES), chips, 1, True, 2
    ).reshape(width, loc_columns + LANES)
    dense_qkv = dense[:, :loc_columns]
    dense_router = dense[:, loc_columns : loc_columns + EXPERTS]
    gain_attn = dense[:, loc_columns + EXPERTS].astype(f32)
    gain_ffn = dense[:, loc_columns + EXPERTS + 1].astype(f32)

    x_line = line_exchange(layer_input.reshape(tokens_present, width), head_number, 3, True)
    x_line = x_line.reshape(line_tokens, width).astype(f32)
    normed_line = x_line * lax.rsqrt(jnp.mean(x_line * x_line, axis=1, keepdims=True) + epsilon)
    first_line = (normed_line * gain_attn).astype(bf16)

    def to_blocks(value):
        columns = value.shape[1:]
        return (
            value.reshape((head_number, sequence_batch, token_rows) + columns)
            .swapaxes(0, 1)
            .reshape((sequence_batch, blk) + columns)
        )

    def to_lines(value):
        columns = value.shape[2:]
        return (
            value.reshape((sequence_batch, head_number, token_rows) + columns)
            .swapaxes(0, 1)
            .reshape((line_tokens,) + columns)
        )

    q_start = seq_index * blk
    q_pos = q_start + jnp.arange(blk, dtype=jnp.int32)
    cosine, sine = rope_tables(q_pos, HEAD_WIDTH)
    projected = to_blocks(jnp.dot(first_line, dense_qkv, preferred_element_type=f32)).reshape(
        sequence_batch, blk, key_value_location, query_group + 2, HEAD_WIDTH
    )
    turned = rotate(projected[:, :, :, : query_group + 1], cosine, sine)
    query_rows = turned[:, :, :, :query_group].astype(bf16)
    keys_values = (
        jnp.stack([turned[:, :, :, query_group], projected[:, :, :, query_group + 1]], axis=3)
        .astype(bf16)
        .reshape(sequence_batch * blk, key_value_location * 2 * HEAD_WIDTH)
    )
    kv_columns = key_value_location * 2 * HEAD_WIDTH
    kv_all = (
        gather(keys_values, chips, 1, True, 4)
        .reshape(2 * chips, sequence_batch, blk, kv_columns)
        .transpose(1, 0, 2, 3)
        .reshape(sequence_batch, length, kv_columns)
    )
    q_seg = lax.dynamic_slice_in_dim(segments, q_start, blk, 1)

    def key_view(piece, offset, token_count):
        portion = lax.dynamic_slice_in_dim(piece, offset, token_count, 1).reshape(
            sequence_batch, token_count, key_value_location, 2, HEAD_WIDTH
        )
        return (portion[:, :, :, 0], portion[:, :, :, 1])

    def key_mask(begin, token_count):
        k_pos = begin + jnp.arange(token_count, dtype=jnp.int32)
        k_seg = lax.dynamic_slice_in_dim(segments, begin, token_count, 1)
        same = q_seg[:, :, None] == k_seg[:, None, :]
        causal = k_pos[None, None, :] <= q_pos[None, :, None]
        return (same & causal)[:, None, None]

    def sweep(function, state):
        sub = 512

        def turn(index, inner):
            offset = index * sub
            return lax.cond(
                offset <= q_start + blk - 1,
                lambda now: function(now, kv_all, offset, sub),
                lambda now: now,
                inner,
            )

        return lax.fori_loop(0, length // sub, turn, state)

    def forward_block(state, piece, offset, token_count):
        top_now, total, accum = state
        keys, values = key_view(piece, offset, token_count)
        scores = (
            jnp.einsum("sqhgd,skhd->shgqk", query_rows, keys, preferred_element_type=f32) * scale
        )
        mask = key_mask(offset, token_count)
        scores = jnp.where(mask, scores, negative)
        top_new = jnp.maximum(top_now, jnp.max(scores, axis=-1))
        weights = jnp.where(mask, jnp.exp(scores - top_new[..., None]), 0.0)
        shrink = jnp.exp(top_now - top_new)
        total = total * shrink + jnp.sum(weights, axis=-1)
        accum = accum * shrink[..., None] + jnp.einsum(
            "shgqk,skhd->shgqd", weights.astype(bf16), values, preferred_element_type=f32
        )
        return (top_new, total, accum)

    state_zero = (
        jnp.full((sequence_batch, key_value_location, query_group, blk), negative, f32),
        jnp.zeros((sequence_batch, key_value_location, query_group, blk), f32),
        jnp.zeros((sequence_batch, key_value_location, query_group, blk, HEAD_WIDTH), f32),
    )
    top_now, total, accum = sweep(forward_block, state_zero)
    lse = top_now + jnp.log(total)
    attended = accum / total[..., None]
    group_columns = key_value_location * query_group * HEAD_WIDTH
    heads_local = to_lines(
        attended.transpose(0, 3, 1, 2, 4).reshape(sequence_batch, blk, group_columns).astype(bf16)
    )
    mixed_heads = (
        line_exchange(
            heads_local.reshape(head_number, tokens_present, group_columns), head_number, 5
        )
        .transpose(1, 0, 2)
        .reshape(tokens_present, QUERY_HEADS * HEAD_WIDTH)
    )
    tokens = layer_input.reshape(tokens_present, width).astype(f32)
    middle = tokens + jnp.dot(mixed_heads, dense_out, preferred_element_type=f32)
    inverse_two = lax.rsqrt(jnp.mean(middle * middle, axis=1, keepdims=True) + epsilon)
    normed_two = middle * inverse_two
    second_input = (normed_two * gain_ffn).astype(bf16)
    router_logits = jnp.dot(second_input, dense_router, preferred_element_type=f32)
    route_flat = routes.reshape(tokens_present, top)
    hot = route_flat[:, :, None] == jnp.arange(EXPERTS, dtype=jnp.int32)[None, None, :]
    chosen = jnp.sum(jnp.where(hot, router_logits[:, None, :], 0.0), axis=2)
    gates = jax.nn.softmax(chosen, axis=-1)
    expert_of = route_flat.reshape(pairs)
    rank = pair_rank.reshape(pairs)
    slot = jnp.sum(
        (expert_of[None, :] == expert_of[:, None]) & (rank[None, :] < rank[:, None]),
        axis=1,
        dtype=jnp.int32,
    )
    kept = (slot < CAP).reshape(tokens_present, top).astype(f32)
    weights_pair = gates * kept
    spread = jnp.sum(jnp.where(hot, weights_pair[:, :, None], 0.0), axis=1)
    spread_high = spread.astype(bf16)
    spread_low = (spread - spread_high.astype(f32)).astype(bf16)
    pad = jnp.zeros((tokens_present, LOW - EXPERTS), bf16)
    payload = jnp.concatenate([second_input, spread_high, pad, spread_low, pad], axis=1)
    columns = width + LANES
    group_tokens = chips * head_number * tokens_present
    needs = 10 * group_tokens * width + 6 * width * expert_gate.shape[1]
    if needs + 6 * group_tokens * expert_gate.shape[1] <= 60 << 20:
        back, moe_part, d_gate_w, d_up_w, d_down_w = expert_turn(
            payload, grad_all, expert_gate, expert_up, expert_down, hidden, chips, head_number, 6
        )
    else:
        x_all = gather(payload, chips, head_number, False, 6).reshape(group_tokens, columns)
        moe_part, back_part, d_gate_w, d_up_w, d_down_w = experts(
            x_all, grad_all, expert_gate, expert_up, expert_down, hidden
        )
        back_part = back_part.reshape(chips, head_number, tokens_present, columns)
        back = scatter_sum(back_part, chips, head_number, False, 7)
    moe = lax.psum_scatter(moe_part, ("chip", "head"), scatter_dimension=0, tiled=True)
    mixed_out = (middle + moe.astype(f32)).astype(bf16)
    mixed_out = mixed_out.reshape(sequence_batch, token_rows, width)

    grads = jnp.stack([d_gate_w, d_up_w]).reshape(2, chips, 2, slice_rows, loc_experts * hidden)
    keep = lax.dynamic_index_in_dim(grads, core, 2, keepdims=False)
    give = lax.dynamic_index_in_dim(grads, 1 - core, 2, keepdims=False)
    shared = (keep.astype(f32) + sibling(give).astype(f32)).astype(bf16)
    piled = jnp.zeros((chips, 2, slice_rows, loc_experts * hidden), bf16)
    for mask in range(chips):
        piece = across(lax.dynamic_index_in_dim(shared, chip ^ mask, 1, keepdims=False), chips, mask)
        piled = lax.dynamic_update_slice(piled, piece[None], (chip ^ mask, 0, 0, 0))
    up_share = (
        piled.reshape(chips, 2, slice_rows, loc_experts, hidden)
        .transpose(3, 2, 1, 0, 4)
        .astype(f32)
        .reshape(loc_experts, slice_rows, 2 * FF)
    )
    d_down_w = d_down_w.reshape(loc_experts, 2, hidden // 2, width)
    keep = lax.dynamic_index_in_dim(d_down_w, core, 1, keepdims=False)
    give = lax.dynamic_index_in_dim(d_down_w, 1 - core, 1, keepdims=False)
    down_share = keep.astype(f32) + sibling(give).astype(f32)

    grad_out = cotangent.reshape(tokens_present, width).astype(f32)
    d_kept = back[:, width : width + EXPERTS]
    grad_gate = jnp.sum(jnp.where(hot, d_kept[:, None, :], 0.0), axis=2) * kept
    grad_chosen = gates * (grad_gate - jnp.sum(gates * grad_gate, axis=1, keepdims=True))
    grad_logits = jnp.sum(jnp.where(hot, grad_chosen[:, :, None], 0.0), axis=1)
    grad_router = jnp.dot(second_input.astype(f32).T, grad_logits, precision=HIGH_PRECISION)
    grad_second = back[:, :width] + jnp.dot(
        grad_logits, dense_router.astype(f32).T, precision=HIGH_PRECISION
    )
    grad_gain_ffn = jnp.sum(grad_second * normed_two, axis=0)
    scaled_two = grad_second * gain_ffn
    grad_mid = grad_out + inverse_two * (
        scaled_two - normed_two * jnp.mean(scaled_two * normed_two, axis=1, keepdims=True)
    )
    grad_attn = grad_mid.astype(bf16)
    grad_dense_out = jnp.dot(mixed_heads.T, grad_attn, preferred_element_type=f32)
    out_share = lax.psum_scatter(
        grad_dense_out.astype(bf16), ("chip", "core", "head"), scatter_dimension=0, tiled=True
    ).astype(f32)
    grad_heads = (
        jnp.dot(grad_attn, dense_out.T, preferred_element_type=f32)
        .astype(bf16)
        .reshape(tokens_present, head_number, group_columns)
        .transpose(1, 0, 2)
    )
    grad_local = to_blocks(
        line_exchange(grad_heads, head_number, 8).reshape(line_tokens, group_columns)
    ).reshape(sequence_batch, blk, key_value_location, query_group, HEAD_WIDTH)
    delta = jnp.sum(grad_local.transpose(0, 2, 3, 1, 4).astype(f32) * attended, axis=-1)

    def backward_block(state, piece, offset, token_count):
        grad_q, grad_store = state
        keys, values = key_view(piece, offset, token_count)
        scores = (
            jnp.einsum("sqhgd,skhd->shgqk", query_rows, keys, preferred_element_type=f32) * scale
        )
        mask = key_mask(offset, token_count)
        probs = jnp.where(mask, jnp.exp(scores - lse[..., None]), 0.0)
        grad_probs = jnp.einsum("sqhgd,skhd->shgqk", grad_local, values, preferred_element_type=f32)
        grad_scores = (probs * (grad_probs - delta[..., None])).astype(bf16)
        grad_q = (
            grad_q
            + jnp.einsum("shgqk,skhd->sqhgd", grad_scores, keys, preferred_element_type=f32) * scale
        )
        grad_k = (
            jnp.einsum("shgqk,sqhgd->skhd", grad_scores, query_rows, preferred_element_type=f32)
            * scale
        )
        grad_v = jnp.einsum(
            "shgqk,sqhgd->skhd", probs.astype(bf16), grad_local, preferred_element_type=f32
        )
        block_width = jnp.stack([grad_k, grad_v], axis=3).reshape(
            sequence_batch, token_count, kv_columns
        )
        grad_store = lax.dynamic_update_slice_in_dim(
            grad_store, block_width.astype(bf16), offset, 1
        )
        return (grad_q, grad_store)

    back_zero = (
        jnp.zeros((sequence_batch, blk, key_value_location, query_group, HEAD_WIDTH), f32),
        jnp.zeros((sequence_batch, length, kv_columns), bf16),
    )
    grad_q, grad_store = sweep(backward_block, back_zero)
    grad_store = (
        grad_store.reshape(sequence_batch, 2 * chips, blk, kv_columns)
        .transpose(1, 0, 2, 3)
        .reshape(chips, 2, sequence_batch * blk, kv_columns)
    )
    grad_kv = scatter_sum(grad_store, chips, 1, True, 9).reshape(
        sequence_batch, blk, key_value_location, 2, HEAD_WIDTH
    )
    grad_proj = jnp.concatenate([grad_q.astype(bf16), grad_kv.astype(bf16)], axis=3).astype(f32)
    unturned = rotate(grad_proj[:, :, :, : query_group + 1], cosine, -sine)
    grad_qkv = to_lines(
        jnp.concatenate([unturned, grad_proj[:, :, :, query_group + 1 :]], axis=3)
        .reshape(sequence_batch, blk, loc_columns)
        .astype(bf16)
    )
    grad_first_part = jnp.dot(grad_qkv, dense_qkv.T, preferred_element_type=f32)
    grad_first = jnp.sum(
        line_exchange(
            grad_first_part.astype(bf16).reshape(head_number, tokens_present, width),
            head_number,
            10,
        ).astype(f32),
        axis=0,
    )
    grad_gain_attn = jnp.sum(grad_first_part * normed_line, axis=0)
    inverse_one = lax.rsqrt(jnp.mean(tokens * tokens, axis=1, keepdims=True) + epsilon)
    normed_one = tokens * inverse_one
    scaled_one = grad_first * gain_attn
    grad_input = grad_mid + inverse_one * (
        scaled_one - normed_one * jnp.mean(scaled_one * normed_one, axis=1, keepdims=True)
    )
    grad_dense_qkv = jnp.dot(first_line.T, grad_qkv, preferred_element_type=f32)
    sums = jnp.concatenate(
        [
            grad_dense_qkv,
            grad_router,
            grad_gain_attn[:, None],
            grad_gain_ffn[:, None],
            jnp.zeros((width, LANES - EXPERTS - 2), f32),
        ],
        axis=1,
    ).astype(bf16)
    sums = scatter_sum(
        sums.reshape(chips, 2, head_number * dense_rows, loc_columns + LANES), chips, 1, True, 11
    )
    sums = line_exchange(
        sums.reshape(head_number, dense_rows, loc_columns + LANES), head_number, 12
    )
    qkv_share = sums[:, :, :loc_columns].transpose(1, 0, 2).reshape(dense_rows, -1)
    extra = jnp.sum(sums[:, :, loc_columns:], axis=0)
    return (
        mixed_out,
        grad_input.reshape(sequence_batch, token_rows, width),
        qkv_share,
        out_share,
        extra[:, :EXPERTS],
        extra[:, EXPERTS],
        extra[:, EXPERTS + 1],
        up_share,
        down_share,
    )


def solution(mesh):
    grid = mesh.devices
    seq, heads = grid.shape
    split = Mesh(grid.reshape(seq // 2, 2, heads), ("chip", "core", "head"))
    places = ("chip", "core", "head")
    inner = ("chip", "core")
    placed = (
        P(None, places, None),
        P(),
        P(None, places, None),
        P(None, places, None),
        P(places, None),
        P(places, None),
        P(places, None),
        P(places),
        P(places),
        P("head", inner, None),
        P("head", inner, None),
        P(None, places, None),
    )
    return jax.shard_map(
        per_device,
        mesh=split,
        in_specs=placed,
        out_specs=(
            P(None, places, None),
            P(None, places, None),
            P(places, None),
            P(places, None),
            P(places, None),
            P(places),
            P(places),
            P("head", inner, None),
            P("head", inner, None),
        ),
        check_vma=False,
    )
```

```python
import functools

import jax
import jax.numpy as jnp
from jax import lax
from jax.experimental import pallas as pl
from jax.experimental.pallas import tpu as pltpu
from jax.sharding import Mesh, PartitionSpec as P

MODEL_WIDTH = 1536
QUERY_HEADS = 24
KEY_VALUE_HEADS = 8
HEAD_WIDTH = 64
EXPERTS = 40
FF = 512
CAP = 25
LANES = 128
LOW = 64

epsilon = 1e-06
negative = -1e30
theta = 10000.0
HIGH_PRECISION = lax.Precision.HIGHEST
MESH = pl.DeviceIdType.MESH
f32 = jnp.float32
bf16 = jnp.bfloat16
ANY = pl.BlockSpec(memory_space=pl.ANY)
WHOLE = pl.BlockSpec(memory_space=pltpu.VMEM)
DMA = pltpu.SemaphoreType.DMA


def rope_tables(token_positions, head_size):
    half = head_size // 2
    freq = theta ** (-jnp.arange(half, dtype=jnp.float32) / half)
    angle = token_positions.astype(jnp.float32)[:, None] * freq[None, :]
    return (jnp.cos(angle)[None, :, None, None, :], jnp.sin(angle)[None, :, None, None, :])


def rotate(value, cosine, sine):
    half = value.shape[-1] // 2
    first = value[..., :half]
    second = value[..., half:]
    return jnp.concatenate(
        [first * cosine - second * sine, second * cosine + first * sine], axis=-1
    )


def digits(count):
    number = count.bit_length() - 1
    assert 1 << number == count
    return number


def flip(index, mask):
    out = index
    bit = 0
    while (1 << bit) <= mask:
        if (mask >> bit) & 1:
            out = out + (1 - 2 * ((index // (1 << bit)) % 2)) * (1 << bit)
        bit += 1
    return out


def subsets(bits):
    out = [0]
    for bit in bits:
        out = out + [mask | (1 << bit) for mask in out]
    return out


def near(count):
    return sorted(range(1, count), key=lambda step: min(step, count - step))


def meet(peers):
    sem = pltpu.get_barrier_semaphore()
    for peer in peers:
        pl.semaphore_signal(sem, inc=1, device_id=peer, device_id_type=MESH)
    pl.semaphore_wait(sem, len(peers))


class Cube:
    def __init__(self, chips, with_core):
        self.chips = chips
        self.chip_digits = digits(chips)
        self.number = self.chip_digits + int(with_core)
        self.with_core = with_core
        up = tuple(range(self.chip_digits))
        core = (self.chip_digits,) if with_core else ()
        self.gather_orders = (up + core, up[::-1] + core)
        self.scatter_orders = (core + up, core + up[::-1])

    def place(self, mask):
        chip = flip(lax.axis_index("chip"), mask & (self.chips - 1))
        if not self.with_core:
            return (chip,)
        return (chip, flip(lax.axis_index("core"), mask >> self.chip_digits))

    def peer(self, digit):
        if digit < self.chip_digits:
            return {"chip": flip(lax.axis_index("chip"), 1 << digit)}
        return {"core": flip(lax.axis_index("core"), 1)}


def gather_kernel(cube, heads, in_ref, out_ref, local, line_send, line_recv, send, recv):
    hz = lax.axis_index("head")
    rows = in_ref.shape[0]
    half = rows // 2
    others = near(heads) if heads > 1 else []
    meet(
        [cube.peer(digit) for digit in range(cube.number)]
        + [{"head": (hz + d) % heads} for d in others]
    )

    def at(mask, d):
        index = cube.place(mask)
        return index + ((hz + heads - d) % heads,) if heads > 1 else index

    own = pltpu.make_async_copy(in_ref, out_ref.at[at(0, 0)], local)
    own.start()
    line = {}
    for d in others:
        line[d] = pltpu.make_async_remote_copy(
            src_ref=in_ref,
            dst_ref=out_ref.at[at(0, 0)],
            send_sem=line_send.at[d - 1],
            recv_sem=line_recv.at[d - 1],
            device_id={"head": (hz + d) % heads},
            device_id_type=MESH,
        )
        line[d].start()
    copies = {}

    def forward(side, mask, d):
        order = cube.gather_orders[side]
        last = max([k for k in range(cube.number) if (mask >> order[k]) & 1], default=-1)
        for k in range(last + 1, cube.number):
            later = mask | (1 << order[k])
            part = pl.ds(side * half, half)
            place = out_ref.at[at(mask, d) + (part,)]
            copy = pltpu.make_async_remote_copy(
                src_ref=in_ref.at[part] if mask == 0 and d == 0 else place,
                dst_ref=place,
                send_sem=send.at[side, later, d],
                recv_sem=recv.at[side, later, d],
                device_id=cube.peer(order[k]),
                device_id_type=MESH,
            )
            copy.start()
            copies[(side, later, d)] = copy

    for side in range(2):
        forward(side, 0, 0)
    for d in others:
        line[d].wait_recv()
        for side in range(2):
            forward(side, 0, d)
    for mask in sorted(range(1, 1 << cube.number), key=lambda m: bin(m).count("1")):
        for d in [0] + others:
            for side in range(2):
                copies[(side, mask, d)].wait_recv()
                forward(side, mask, d)
    own.wait()
    for copy in list(line.values()) + list(copies.values()):
        copy.wait_send()


def gather(value, chips, heads, with_core, number):
    rows, columns = value.shape
    cube = Cube(chips, with_core)
    lead = (chips,) + ((2,) if with_core else ()) + ((heads,) if heads > 1 else ())
    steps = max(heads - 1, 1)
    return pl.pallas_call(
        functools.partial(gather_kernel, cube, heads),
        out_shape=jax.ShapeDtypeStruct(lead + (rows, columns), value.dtype),
        in_specs=[ANY],
        out_specs=ANY,
        scratch_shapes=[
            DMA,
            DMA((steps,)),
            DMA((steps,)),
            DMA((2, 1 << cube.number, heads)),
            DMA((2, 1 << cube.number, heads)),
        ],
        compiler_params=pltpu.CompilerParams(collective_id=number, has_side_effects=True),
        name="gather",
    )(value)


def scatter_kernel(cube, heads, in_ref, out_ref, *refs):
    count = cube.number
    arrived, parts = refs[:count], refs[count : 2 * count - 1]
    line_out, line_in, line_send, line_recv, send, recv = refs[2 * count - 1 :]
    hz = lax.axis_index("head")
    half = in_ref.shape[-2] // 2
    others = near(heads) if heads > 1 else []
    order_of_lines = others[::-1] + [0]
    meet(
        [cube.peer(digit) for digit in range(count)] + [{"head": (hz + d) % heads} for d in others]
    )
    copies = {}

    def slot(side, k, mask):
        return subsets(cube.scatter_orders[side][k + 1 :]).index(mask)

    def mine(side, mask, d):
        index = cube.place(mask)
        if heads > 1:
            index = index + ((hz + d) % heads,)
        return in_ref.at[index + (pl.ds(side * half, half),)]

    def pass_on(side, k, mask, d, source):
        where = slot(side, k, mask)
        copy = pltpu.make_async_remote_copy(
            src_ref=source,
            dst_ref=arrived[k].at[side, where, d],
            send_sem=send.at[side, k, where, d],
            recv_sem=recv.at[side, k, where, d],
            device_id=cube.peer(cube.scatter_orders[side][k]),
            device_id_type=MESH,
        )
        copy.start()
        copies[(side, k, mask, d)] = copy

    def total(side, steps, mask, d):
        value = mine(side, mask, d)[...].astype(f32)
        for j in range(steps):
            copies[(side, j, mask, d)].wait_recv()
            value = value + arrived[j][side, slot(side, j, mask), d].astype(f32)
        return value

    for k in range(count):
        for d in order_of_lines:
            for side in range(2):
                order = cube.scatter_orders[side]
                for mask in subsets(order[k + 1 :])[::-1]:
                    full = mask | (1 << order[k])
                    if k == 0:
                        source = mine(side, full, d)
                    else:
                        source = parts[k - 1].at[side, slot(side, k, mask), d]
                        source[...] = total(side, k, full, d).astype(bf16)
                    pass_on(side, k, mask, d, source)
    line = {}
    for d in order_of_lines:
        for side in range(2):
            value = total(side, count, 0, d)
            if d:
                line_out[d - 1, pl.ds(side * half, half)] = value.astype(bf16)
            else:
                out_ref[pl.ds(side * half, half)] = value
        if d:
            line[d] = pltpu.make_async_remote_copy(
                src_ref=line_out.at[d - 1],
                dst_ref=line_in.at[d - 1],
                send_sem=line_send.at[d - 1],
                recv_sem=line_recv.at[d - 1],
                device_id={"head": (hz + d) % heads},
                device_id_type=MESH,
            )
            line[d].start()
    for d in others:
        line[d].wait_recv()
        out_ref[...] += line_in[d - 1].astype(f32)
    for copy in list(line.values()) + list(copies.values()):
        copy.wait_send()


def scatter_sum(value, chips, heads, with_core, number):
    rows, columns = value.shape[-2:]
    cube = Cube(chips, with_core)
    half = rows // 2
    steps = max(heads - 1, 1)
    line_rows = rows if heads > 1 else 16
    slots = [(1 << cube.number) >> (k + 1) for k in range(cube.number)]
    if 2 * value.size + 4 * heads * half * columns * (sum(slots) + sum(slots[1:])) > 40 << 20:
        names = ("chip", "core") if with_core else ("chip",)
        names = names + (("head",) if heads > 1 else ())
        flat = value.reshape(-1, columns)
        return lax.psum_scatter(flat, names, scatter_dimension=0, tiled=True).astype(f32)
    return pl.pallas_call(
        functools.partial(scatter_kernel, cube, heads),
        out_shape=jax.ShapeDtypeStruct((rows, columns), f32),
        in_specs=[WHOLE],
        out_specs=WHOLE,
        scratch_shapes=[pltpu.VMEM((2, s, heads, half, columns), bf16) for s in slots]
        + [pltpu.VMEM((2, s, heads, half, columns), bf16) for s in slots[1:]]
        + [
            pltpu.VMEM((steps, line_rows, columns), bf16),
            pltpu.VMEM((steps, line_rows, columns), bf16),
            DMA((steps,)),
            DMA((steps,)),
            DMA((2, cube.number, slots[0], heads)),
            DMA((2, cube.number, slots[0], heads)),
        ],
        compiler_params=pltpu.CompilerParams(
            collective_id=number, has_side_effects=True, vmem_limit_bytes=56 << 20
        ),
        name="scatter_sum",
    )(value)


def line_kernel(heads, same, in_ref, out_ref, local, send, recv):
    hz = lax.axis_index("head")
    others = near(heads)[::-1]
    meet([{"head": (hz + d) % heads} for d in others])

    def source(place):
        return in_ref if same else in_ref.at[place]

    own = pltpu.make_async_copy(source(hz), out_ref.at[hz], local)
    own.start()
    copies = []
    for d in others:
        place = (hz + d) % heads
        copy = pltpu.make_async_remote_copy(
            src_ref=source(place),
            dst_ref=out_ref.at[hz],
            send_sem=send.at[d - 1],
            recv_sem=recv.at[d - 1],
            device_id={"head": place},
            device_id_type=MESH,
        )
        copy.start()
        copies.append(copy)
    own.wait()
    for copy in copies:
        copy.wait()


def line_exchange(value, heads, number, same=False):
    return pl.pallas_call(
        functools.partial(line_kernel, heads, same),
        out_shape=jax.ShapeDtypeStruct((heads,) + value.shape if same else value.shape, value.dtype),
        in_specs=[ANY],
        out_specs=ANY,
        scratch_shapes=[DMA, DMA((heads - 1,)), DMA((heads - 1,))],
        compiler_params=pltpu.CompilerParams(collective_id=number, has_side_effects=True),
        name="line_exchange",
    )(value)


NT = (((1,), (1,)), ((), ()))


def experts_kernel(
    tile,
    hidden,
    x_ref,
    c_ref,
    gate_hbm,
    up_hbm,
    down_hbm,
    moe_ref,
    back_ref,
    d_gate_hbm,
    d_up_hbm,
    d_down_hbm,
    w_gate,
    w_up,
    w_down,
    d_gate_w,
    d_up_w,
    d_down_w,
    acts,
    back_gate,
    back_up,
    stage_wide,
    stage_down,
    load,
    store,
):
    step = pl.program_id(0)
    width, total = w_gate.shape

    @pl.when(step == 0)
    def _():
        loads = [
            pltpu.make_async_copy(gate_hbm, w_gate, load.at[0]),
            pltpu.make_async_copy(up_hbm, w_up, load.at[1]),
            pltpu.make_async_copy(down_hbm, w_down, load.at[2]),
        ]
        for copy in loads:
            copy.start()
        d_gate_w[...] = jnp.zeros_like(d_gate_w)
        d_up_w[...] = jnp.zeros_like(d_up_w)
        d_down_w[...] = jnp.zeros_like(d_down_w)
        for copy in loads:
            copy.wait()

    x = x_ref[:, :width]
    c = c_ref[...]
    routed = x_ref[:, width:]
    first_expert = lax.axis_index("head") * (total // hidden)
    d_gates = jnp.zeros((x.shape[0], LANES), f32)
    for begin in range(0, total, tile):
        js = pl.ds(begin, tile)
        column = begin + lax.broadcasted_iota(jnp.int32, (LANES, tile), 1)
        line = lax.broadcasted_iota(jnp.int32, (LANES, tile), 0)
        expert = first_expert + column // hidden
        here = (line == expert).astype(f32)
        both = (here + (line == expert + LOW).astype(f32)).astype(bf16)
        weight = jnp.dot(routed, both, preferred_element_type=f32)
        gate = jnp.dot(x, w_gate[:, js], preferred_element_type=f32)
        up = jnp.dot(x, w_up[:, js], preferred_element_type=f32)
        d_act = lax.dot_general(c, w_down[js, :], NT, preferred_element_type=f32)
        sigma = 1.0 / (1.0 + jnp.exp(-gate))
        silu = gate * sigma
        act = (silu * up).astype(bf16).astype(f32)
        d_gates = d_gates + lax.dot_general(
            (act * d_act).astype(bf16), here.astype(bf16), NT, preferred_element_type=f32
        )
        acts[:, js] = (act * weight).astype(bf16)
        d_act = d_act * weight
        back_up[:, js] = (d_act * silu).astype(bf16)
        back_gate[:, js] = (d_act * up * sigma * (1.0 + gate * (1.0 - sigma))).astype(bf16)
    back_ref[:, width:] = d_gates.astype(bf16)
    x_turned = x.T
    for begin in range(0, total, tile):
        js = pl.ds(begin, tile)
        d_gate_w[:, js] += jnp.dot(x_turned, back_gate[:, js], preferred_element_type=f32)
        d_up_w[:, js] += jnp.dot(x_turned, back_up[:, js], preferred_element_type=f32)
        d_down_w[js, :] += jnp.dot(acts[:, js].T, c, preferred_element_type=f32)
    for begin in range(0, width, 512):
        cs = pl.ds(begin, 512)
        moe_ref[:, cs] = jnp.dot(acts[...], w_down[:, cs], preferred_element_type=f32).astype(bf16)
        back_ref[:, cs] = (
            lax.dot_general(back_gate[...], w_gate[cs, :], NT, preferred_element_type=f32)
            + lax.dot_general(back_up[...], w_up[cs, :], NT, preferred_element_type=f32)
        ).astype(bf16)

    @pl.when(step == pl.num_programs(0) - 1)
    def _():
        rows = stage_wide.shape[1]
        jobs = [
            (source, target, stage, begin)
            for source, target, stage in (
                (d_gate_w, d_gate_hbm, stage_wide),
                (d_up_w, d_up_hbm, stage_wide),
                (d_down_w, d_down_hbm, stage_down),
            )
            for begin in range(0, source.shape[0], rows)
        ]
        flight = {}
        for index, (source, target, stage, begin) in enumerate(jobs):
            now = index % 2
            if now in flight:
                flight[now].wait()
            stage[now] = source[pl.ds(begin, rows), :].astype(bf16)
            flight[now] = pltpu.make_async_copy(
                stage.at[now], target.at[pl.ds(begin, rows), :], store.at[now]
            )
            flight[now].start()
        for copy in flight.values():
            copy.wait()


def experts(x, c, w_gate, w_up, w_down, hidden):
    tokens, columns = x.shape
    width, total = w_gate.shape
    block = min(256, tokens)
    tile = 256 if total % 256 == 0 else hidden
    return pl.pallas_call(
        functools.partial(experts_kernel, tile, hidden),
        grid=(tokens // block,),
        out_shape=(
            jax.ShapeDtypeStruct((tokens, width), bf16),
            jax.ShapeDtypeStruct((tokens, columns), bf16),
            jax.ShapeDtypeStruct((width, total), bf16),
            jax.ShapeDtypeStruct((width, total), bf16),
            jax.ShapeDtypeStruct((total, width), bf16),
        ),
        in_specs=[
            pl.BlockSpec((block, columns), lambda i: (i, 0)),
            pl.BlockSpec((block, width), lambda i: (i, 0)),
            ANY,
            ANY,
            ANY,
        ],
        out_specs=(
            pl.BlockSpec((block, width), lambda i: (i, 0)),
            pl.BlockSpec((block, columns), lambda i: (i, 0)),
            ANY,
            ANY,
            ANY,
        ),
        scratch_shapes=[
            pltpu.VMEM((width, total), bf16),
            pltpu.VMEM((width, total), bf16),
            pltpu.VMEM((total, width), bf16),
            pltpu.VMEM((width, total), f32),
            pltpu.VMEM((width, total), f32),
            pltpu.VMEM((total, width), f32),
            pltpu.VMEM((block, total), bf16),
            pltpu.VMEM((block, total), bf16),
            pltpu.VMEM((block, total), bf16),
            pltpu.VMEM((2, 64, total), bf16),
            pltpu.VMEM((2, 64, width), bf16),
            DMA((3,)),
            DMA((2,)),
        ],
        compiler_params=pltpu.CompilerParams(vmem_limit_bytes=60 << 20),
        name="experts",
    )(x, c, w_gate, w_up, w_down)


def turn_kernel(cube, heads, hidden, *refs):
    chips, count = cube.chips, cube.number
    own_ref, c_hbm, up_hbm, down_hbm = refs[:4]
    out_ref, moe_hbm, keep_up_hbm, other_up_hbm, keep_down_hbm, other_down_hbm = refs[4:10]
    tokens, turned, cots, w_up, w_down, acts, backs, d_gates, moe_stage, line_in = refs[10:20]
    arrived = refs[20 : 20 + count]
    load, store, own_sem, line_send, line_recv, send, recv, back_send, back_recv = refs[
        20 + count : 29 + count
    ]
    end_send, end_recv, twin_send, twin_recv = refs[29 + count :]
    hz = lax.axis_index("head")
    rows, columns = own_ref.shape
    experts_here, width, _ = w_up.shape
    total = experts_here * hidden
    half = rows // 2
    line = heads * rows
    others = near(heads)
    masks = sorted(range(chips), key=lambda m: bin(m).count("1"))

    loads = [
        pltpu.make_async_copy(source, target, load.at[index])
        for index, (source, target) in enumerate(
            ((up_hbm, w_up), (down_hbm, w_down), (c_hbm, cots))
        )
    ]
    for copy in loads:
        copy.start()
    core = lax.axis_index("core")
    twin = {"core": 1 - core}
    meet(
        [cube.peer(digit) for digit in range(count)]
        + [{"head": (hz + d) % heads} for d in others]
        + [twin]
    )

    def part(side):
        return pl.ds(side * half, half)

    middle = jnp.minimum(hz, heads - 1 - hz)

    def source(rank):
        if rank == 0:
            return hz
        far = (rank + 1) // 2
        near_one = hz - far if rank % 2 else hz + far
        far_one = jnp.where(
            hz < heads - 1 - hz, hz + (rank - middle), hz - (rank - middle)
        )
        return jnp.where(rank <= 2 * middle, near_one, far_one)

    def line_copy(rank, step):
        head = source(rank)
        place = tokens.at[cube.place(0) + (head,)]
        return pltpu.make_async_remote_copy(
            src_ref=own_ref if rank == 0 else place,
            dst_ref=place,
            send_sem=line_send.at[heads if rank == 0 and step < 0 else head],
            recv_sem=line_recv.at[head],
            device_id={"head": (hz + step + heads) % heads},
            device_id_type=MESH,
        )

    def along(rank, act):
        head = source(rank)
        goes_up = hz + 1 < heads
        goes_down = hz > 0
        if rank:
            goes_up = goes_up & (head < hz)
            goes_down = goes_down & (head > hz)

        @pl.when(goes_up)
        def _():
            act(line_copy(rank, 1))

        @pl.when(goes_down)
        def _():
            act(line_copy(rank, -1))

    def plane_copy(side, mask, k, rank):
        digit = cube.gather_orders[side][k]
        later = mask | (1 << digit)
        head = source(rank)
        place = tokens.at[cube.place(mask) + (head, part(side))]
        return pltpu.make_async_remote_copy(
            src_ref=own_ref.at[part(side)] if mask == 0 and rank == 0 else place,
            dst_ref=place,
            send_sem=send.at[side, later, head],
            recv_sem=recv.at[side, later, head],
            device_id=cube.peer(digit),
            device_id_type=MESH,
        )

    def steps_after(side, mask):
        order = cube.gather_orders[side]
        last = max([k for k in range(count) if (mask >> order[k]) & 1], default=-1)
        return range(last + 1, count)

    def arrival(side, mask, rank):
        order = cube.gather_orders[side]
        k = max(k for k in range(count) if (mask >> order[k]) & 1)
        return plane_copy(side, mask & ~(1 << order[k]), k, rank)

    def receive(mask):
        for rank in range(heads):
            if mask == 0:
                if rank:
                    line_copy(rank, 1).wait_recv()
                along(rank, lambda copy: copy.start())
            for side in range(2):
                if mask:
                    arrival(side, mask, rank).wait_recv()
                for k in steps_after(side, mask):
                    plane_copy(side, mask, k, rank).start()

    def sent(mask):
        for rank in range(heads):
            if mask == 0:
                along(rank, lambda copy: copy.wait_send())
            for side in range(2):
                for k in steps_after(side, mask):
                    plane_copy(side, mask, k, rank).wait_send()

    def slot(side, k, mask):
        return subsets(cube.scatter_orders[side][k + 1 :]).index(mask)

    def back_place(side, mask, d):
        return tokens.at[cube.place(mask) + ((hz + d) % heads, part(side))]

    def back_copy(side, k, mask, d):
        order = cube.scatter_orders[side]
        where = slot(side, k, mask)
        return pltpu.make_async_remote_copy(
            src_ref=back_place(side, mask | (1 << order[k]), d),
            dst_ref=arrived[k].at[side, where, d],
            send_sem=back_send.at[side, k, where, d],
            recv_sem=back_recv.at[side, k, where, d],
            device_id=cube.peer(order[k]),
            device_id_type=MESH,
        )

    def end_copy(d):
        return pltpu.make_async_remote_copy(
            src_ref=tokens.at[cube.place(0) + ((hz + d) % heads,)],
            dst_ref=line_in.at[d - 1],
            send_sem=end_send.at[d - 1],
            recv_sem=end_recv.at[d - 1],
            device_id={"head": (hz + d) % heads},
            device_id_type=MESH,
        )

    outward = others[::-1] + [0]

    def give(mask, d):
        for side in range(2):
            first = 1 << cube.scatter_orders[side][0]
            if mask & first:
                back_copy(side, 0, mask & ~first, d).start()

    own = pltpu.make_async_copy(own_ref, tokens.at[cube.place(0) + (hz,)], own_sem)
    own.start()

    first_expert = hz * experts_here
    span = min(512, width)
    group = 2 if experts_here % 2 == 0 else 1
    tile = group * hidden

    def compute(place):
        here = pl.ds(place * line, line)
        x = tokens[place, :, :, pl.ds(0, width)].reshape(line, width)
        c = cots[here, :]
        routed = tokens[place, :, :, pl.ds(width, LANES)].reshape(line, LANES)
        turned[:, here] = x.T
        d_gates[...] = jnp.zeros_like(d_gates)

        @pl.loop(0, total // tile)
        def _(j):
            js = pl.ds(pl.multiple_of(j * tile, tile), tile)
            column = j * tile + lax.broadcasted_iota(jnp.int32, (LANES, tile), 1)
            lane = lax.broadcasted_iota(jnp.int32, (LANES, tile), 0)
            expert = first_expert + column // hidden
            high = (lane == expert).astype(f32)
            both = (high + (lane == expert + LOW).astype(f32)).astype(bf16)
            weight = jnp.dot(routed, both, preferred_element_type=f32)
            both_parts = [
                jnp.dot(x, w_up[j * group + i], preferred_element_type=f32) for i in range(group)
            ]
            gate = jnp.concatenate([value[:, :hidden] for value in both_parts], axis=1)
            up = jnp.concatenate([value[:, hidden:] for value in both_parts], axis=1)
            d_act = lax.dot_general(c, w_down[js, :], NT, preferred_element_type=f32)
            sigma = 1.0 / (1.0 + jnp.exp(-gate))
            silu = gate * sigma
            act = (silu * up).astype(bf16).astype(f32)
            d_gates[...] += lax.dot_general(
                (act * d_act).astype(bf16), high.astype(bf16), NT, preferred_element_type=f32
            )
            acts[here, js] = (act * weight).astype(bf16)
            d_act = d_act * weight
            d_up = (d_act * silu).astype(bf16)
            d_gate = (d_act * up * sigma * (1.0 + gate * (1.0 - sigma))).astype(bf16)
            for i in range(group):
                one = slice(i * hidden, (i + 1) * hidden)
                backs[j * group + i, here, pl.ds(0, hidden)] = d_gate[:, one]
                backs[j * group + i, here, pl.ds(hidden, hidden)] = d_up[:, one]

    def results(place, step):
        here = pl.ds(place * line, line)

        @pl.loop(0, width // span)
        def _(j):
            cs = pl.ds(pl.multiple_of(j * span, span), span)
            value = sum(
                lax.dot_general(
                    backs[e, here, :], w_up[e, cs, :], NT, preferred_element_type=f32
                )
                for e in range(experts_here)
            )
            tokens[place, :, :, cs] = value.astype(bf16).reshape(heads, rows, span)

        tokens[place, :, :, pl.ds(width, LANES)] = (
            d_gates[...].astype(bf16).reshape(heads, rows, LANES)
        )

    def moe_copy(place):
        return pltpu.make_async_copy(
            moe_stage, moe_hbm.at[pl.ds(place * line, line)], store.at[chips + 1]
        )

    def mixed(place, step):
        here = pl.ds(place * line, line)

        @pl.when(step > 0)
        def _():
            moe_copy(place).wait()

        @pl.loop(0, width // span)
        def _(j):
            cs = pl.ds(pl.multiple_of(j * span, span), span)
            moe_stage[:, cs] = jnp.dot(
                acts[here, :], w_down[:, cs], preferred_element_type=f32
            ).astype(bf16)

        moe_copy(place).start()

    @pl.loop(0, chips)
    def _(step):
        seen = -1
        for index, mask in enumerate(masks):
            level = bin(mask).count("1")
            if level > seen:
                seen = level

                @pl.when(step == index)
                def _():
                    for other in masks:
                        if bin(other).count("1") == level:
                            receive(other)

        place = cube.place(0)[0] * 0
        for index, mask in enumerate(masks):
            place = jnp.where(step == index, cube.place(mask)[0], place)

        @pl.when(step == 0)
        def _():
            own.wait()
            for copy in loads:
                copy.wait()

        compute(place)
        for index, mask in enumerate(masks):

            @pl.when(step == index)
            def _():
                sent(mask)

        results(place, step)
        for index, mask in enumerate(masks):
            if mask and mask != chips - 1:

                @pl.when(step == index)
                def _():
                    for d in outward:
                        give(mask, d)

        for index, mask in enumerate(masks[:-1]):

            @pl.when(step == index)
            def _():
                mixed(place, step)

    def sums(side, steps, mask, d):
        value = back_place(side, mask, d)[...].astype(f32)
        for j in range(steps):
            back_copy(side, j, mask, d).wait_recv()
            value = value + arrived[j][side, slot(side, j, mask), d].astype(f32)
        return value

    slices = 2 * chips
    slice_rows = width // slices

    def up_rows(ref, chip, which):
        return ref.at[:, pl.ds((chip * 2 + which) * slice_rows, slice_rows), :]

    def keep_up(chip):
        return pltpu.make_async_copy(up_rows(w_up, chip, core), keep_up_hbm.at[chip], store.at[chip])

    def give_up(chip):
        return pltpu.make_async_remote_copy(
            src_ref=up_rows(w_up, chip, 1 - core),
            dst_ref=other_up_hbm.at[chip],
            send_sem=twin_send.at[chip],
            recv_sem=twin_recv.at[chip],
            device_id=twin,
            device_id_type=MESH,
        )

    def keep_down():
        return pltpu.make_async_copy(w_down_parts(core), keep_down_hbm, store.at[chips])

    def give_down():
        return pltpu.make_async_remote_copy(
            src_ref=w_down_parts(1 - core),
            dst_ref=other_down_hbm,
            send_sem=twin_send.at[chips],
            recv_sem=twin_recv.at[chips],
            device_id=twin,
            device_id_type=MESH,
        )

    def w_down_parts(which):
        return w_down.reshape(experts_here, 2, hidden // 2, width).at[:, which]

    def up_grad(begin, end):
        @pl.loop(begin, end)
        def _(e):
            w_up[e] = jnp.dot(turned[...], backs[e], preferred_element_type=f32).astype(bf16)

        if end == experts_here:
            for chip in range(chips):
                give_up(chip).start()
                keep_up(chip).start()

    def down_grad():
        @pl.loop(0, total // tile)
        def _(j):
            js = pl.ds(pl.multiple_of(j * tile, tile), tile)
            value = jnp.dot(acts[:, js].T, cots[...], preferred_element_type=f32)
            w_down[js, :] = value.astype(bf16)

        give_down().start()
        keep_down().start()

    def last_mix():
        mixed(cube.place(chips - 1)[0], 1)

    cuts = [experts_here * i // 4 for i in range(5)]
    work = [
        last_mix,
        lambda: up_grad(cuts[0], cuts[1]),
        lambda: up_grad(cuts[1], cuts[2]),
        lambda: up_grad(cuts[2], cuts[3]),
        lambda: up_grad(cuts[3], cuts[4]),
        down_grad,
    ]
    turns = heads + count
    for turn in range(turns):
        if turn < heads:
            give(chips - 1, outward[turn])
        for piece in work[len(work) * turn // turns : len(work) * (turn + 1) // turns]:
            piece()
        for k in range(1, count):
            if 0 <= turn - k < heads:
                d = outward[turn - k]
                for side in range(2):
                    order = cube.scatter_orders[side]
                    for mask in subsets(order[k + 1 :])[::-1]:
                        full = mask | (1 << order[k])
                        back_place(side, full, d)[...] = sums(side, k, full, d).astype(bf16)
                        back_copy(side, k, mask, d).start()
        if 0 <= turn - count < heads:
            d = outward[turn - count]
            for side in range(2):
                value = sums(side, count, 0, d)
                if d:
                    back_place(side, 0, d)[...] = value.astype(bf16)
                else:
                    out_ref[part(side)] = value
            if d:
                end_copy(d).start()
    for d in others:
        end_copy(d).wait_recv()
        out_ref[...] += line_in[d - 1].astype(f32)
    for d in others:
        end_copy(d).wait_send()
    for side in range(2):
        for k in range(count):
            for mask in subsets(cube.scatter_orders[side][k + 1 :]):
                for d in outward:
                    back_copy(side, k, mask, d).wait_send()
    moe_copy(0).wait()
    for chip in range(chips):
        give_up(chip).wait()
        keep_up(chip).wait()
    give_down().wait()
    keep_down().wait()


def expert_turn(payload, c, w_up, w_down, chips, heads, number):
    rows, columns = payload.shape
    experts_here, width, double = w_up.shape
    hidden = double // 2
    total = experts_here * hidden
    cube = Cube(chips, False)
    count = cube.number
    tokens = chips * heads * rows
    half = rows // 2
    slots = [chips >> (k + 1) for k in range(count)]
    share = jax.ShapeDtypeStruct((chips, experts_here, width // (2 * chips), double), bf16)
    down_share = jax.ShapeDtypeStruct((experts_here, hidden // 2, width), bf16)
    return pl.pallas_call(
        functools.partial(turn_kernel, cube, heads, hidden),
        out_shape=(
            jax.ShapeDtypeStruct((rows, columns), f32),
            jax.ShapeDtypeStruct((tokens, width), bf16),
            share,
            share,
            down_share,
            down_share,
        ),
        in_specs=[WHOLE, ANY, ANY, ANY],
        out_specs=(WHOLE, ANY, ANY, ANY, ANY, ANY),
        scratch_shapes=[
            pltpu.VMEM((chips, heads, rows, columns), bf16),
            pltpu.VMEM((width, tokens), bf16),
            pltpu.VMEM((tokens, width), bf16),
            pltpu.VMEM((experts_here, width, double), bf16),
            pltpu.VMEM((total, width), bf16),
            pltpu.VMEM((tokens, total), bf16),
            pltpu.VMEM((experts_here, tokens, double), bf16),
            pltpu.VMEM((heads * rows, LANES), f32),
            pltpu.VMEM((heads * rows, width), bf16),
            pltpu.VMEM((heads - 1, rows, columns), bf16),
        ]
        + [pltpu.VMEM((2, s, heads, half, columns), bf16) for s in slots]
        + [
            DMA((3,)),
            DMA((chips + 2,)),
            DMA,
            DMA((heads + 1,)),
            DMA((heads,)),
            DMA((2, chips, heads)),
            DMA((2, chips, heads)),
            DMA((2, count, slots[0], heads)),
            DMA((2, count, slots[0], heads)),
            DMA((heads - 1,)),
            DMA((heads - 1,)),
            DMA((chips + 1,)),
            DMA((chips + 1,)),
        ],
        compiler_params=pltpu.CompilerParams(
            collective_id=number, has_side_effects=True, vmem_limit_bytes=63 << 20
        ),
        name="expert_turn",
    )(payload, c, w_up, w_down)


def start_kernel(cube, heads, hidden, *refs):
    x_ref, slice_ref, up_ref, down_ref, x_out, dense_out, up_out, down_out = refs[:8]
    local, x_send, x_recv, line_send, line_recv, send, recv = refs[8:15]
    up_send, up_recv, twin_send, twin_recv = refs[15:]
    chips = cube.chips
    chip, core, hz = lax.axis_index("chip"), lax.axis_index("core"), lax.axis_index("head")
    twin = {"core": 1 - core}
    others = near(heads)
    slice_rows = up_ref.shape[1]
    units = up_ref.shape[2] // 2
    part_heads = heads // 2
    meet(
        [{"chip": flip(chip, mask)} for mask in range(1, chips)]
        + [twin]
        + [{"head": (hz + d) % heads} for d in others]
    )
    middle = jnp.minimum(hz, heads - 1 - hz)

    def source(rank):
        if rank == 0:
            return hz
        far = (rank + 1) // 2
        near_one = hz - far if rank % 2 else hz + far
        far_one = jnp.where(hz < heads - 1 - hz, hz + (rank - middle), hz - (rank - middle))
        return jnp.where(rank <= 2 * middle, near_one, far_one)

    def x_copy(rank, step):
        head = source(rank)
        return pltpu.make_async_remote_copy(
            src_ref=x_ref if rank == 0 else x_out.at[head],
            dst_ref=x_out.at[head],
            send_sem=x_send.at[heads if rank == 0 and step < 0 else head],
            recv_sem=x_recv.at[head],
            device_id={"head": (hz + step + heads) % heads},
            device_id_type=MESH,
        )

    def along(rank, act):
        head = source(rank)
        goes_up = hz + 1 < heads
        goes_down = hz > 0
        if rank:
            goes_up = goes_up & (head < hz)
            goes_down = goes_down & (head > hz)

        @pl.when(goes_up)
        def _():
            act(x_copy(rank, 1))

        @pl.when(goes_down)
        def _():
            act(x_copy(rank, -1))

    def slice_copy(d):
        place = (hz + d) % heads
        return pltpu.make_async_remote_copy(
            src_ref=slice_ref.at[place],
            dst_ref=dense_out.at[chip, core, hz],
            send_sem=line_send.at[d - 1],
            recv_sem=line_recv.at[d - 1],
            device_id={"head": place},
            device_id_type=MESH,
        )

    def dense_copy(side, mask, k):
        order = cube.gather_orders[side]
        later = mask | (1 << order[k])
        place = dense_out.at[cube.place(mask) + (pl.ds(side * part_heads, part_heads),)]
        return pltpu.make_async_remote_copy(
            src_ref=place,
            dst_ref=place,
            send_sem=send.at[side, later],
            recv_sem=recv.at[side, later],
            device_id=cube.peer(order[k]),
            device_id_type=MESH,
        )

    def steps_after(side, mask):
        order = cube.gather_orders[side]
        last = max([k for k in range(cube.number) if (mask >> order[k]) & 1], default=-1)
        return range(last + 1, cube.number)

    def dense_turn(mask):
        for side in range(2):
            if mask:
                order = cube.gather_orders[side]
                k = max(k for k in range(cube.number) if (mask >> order[k]) & 1)
                dense_copy(side, mask & ~(1 << order[k]), k).wait_recv()
            for k in steps_after(side, mask):
                dense_copy(side, mask, k).start()

    def up_rows(mask):
        return pl.ds((flip(chip, mask) * 2 + core) * slice_rows, slice_rows)

    def unit_columns(part, mask):
        return pl.ds(pl.multiple_of(part * units + flip(chip, mask) * hidden, hidden), hidden)

    def up_copy(part, mask):
        return pltpu.make_async_remote_copy(
            src_ref=up_ref.at[:, :, unit_columns(part, mask)],
            dst_ref=up_out.at[:, up_rows(0), pl.ds(part * hidden, hidden)],
            send_sem=up_send.at[part, mask],
            recv_sem=up_recv.at[part, mask],
            device_id={"chip": flip(chip, mask)},
            device_id_type=MESH,
        )

    def up_twin(mask):
        place = up_out.at[:, up_rows(mask), :]
        return pltpu.make_async_remote_copy(
            src_ref=place,
            dst_ref=place,
            send_sem=twin_send.at[mask],
            recv_sem=twin_recv.at[mask],
            device_id=twin,
            device_id_type=MESH,
        )

    down_twin = pltpu.make_async_remote_copy(
        src_ref=down_ref,
        dst_ref=down_out.at[:, core],
        send_sem=twin_send.at[chips],
        recv_sem=twin_recv.at[chips],
        device_id=twin,
        device_id_type=MESH,
    )
    locals_ = [
        pltpu.make_async_copy(slice_ref.at[hz], dense_out.at[chip, core, hz], local.at[0]),
        pltpu.make_async_copy(x_ref, x_out.at[hz], local.at[1]),
        pltpu.make_async_copy(down_ref, down_out.at[:, core], local.at[2]),
    ] + [
        pltpu.make_async_copy(
            up_ref.at[:, :, unit_columns(part, 0)],
            up_out.at[:, up_rows(0), pl.ds(part * hidden, hidden)],
            local.at[3 + part],
        )
        for part in range(2)
    ]
    for d in others:
        slice_copy(d).start()
    for copy in locals_:
        copy.start()
    along(0, lambda copy: copy.start())
    down_twin.start()
    locals_[0].wait()
    for d in others:
        slice_copy(d).wait_recv()
    dense_turn(0)
    for mask in range(1, chips):
        for part in range(2):
            up_copy(part, mask).start()
    masks = sorted(range(1, 2 * chips), key=lambda m: bin(m).count("1"))
    shares = [masks[len(masks) * i // heads : len(masks) * (i + 1) // heads] for i in range(heads)]
    for mask in shares[0]:
        dense_turn(mask)
    for rank in range(1, heads):
        x_copy(rank, 1).wait_recv()
        along(rank, lambda copy: copy.start())
        for mask in shares[rank]:
            dense_turn(mask)
    for copy in locals_[3:]:
        copy.wait()
    up_twin(0).start()
    for mask in range(1, chips):
        for part in range(2):
            up_copy(part, mask).wait_recv()
        up_twin(mask).start()
    for copy in locals_[1:3]:
        copy.wait()
    down_twin.wait()
    for mask in range(chips):
        up_twin(mask).wait()
    for rank in range(heads):
        along(rank, lambda copy: copy.wait_send())
    for d in others:
        slice_copy(d).wait_send()
    for mask in [0] + masks:
        for side in range(2):
            for k in steps_after(side, mask):
                dense_copy(side, mask, k).wait_send()
    for mask in range(1, chips):
        for part in range(2):
            up_copy(part, mask).wait_send()


def start(x, slices, w_gate_up, w_down, chips, heads, hidden, number):
    cube = Cube(chips, True)
    experts_here, slice_rows, _ = w_gate_up.shape
    width = slice_rows * 2 * chips
    return pl.pallas_call(
        functools.partial(start_kernel, cube, heads, hidden),
        out_shape=(
            jax.ShapeDtypeStruct((heads,) + x.shape, bf16),
            jax.ShapeDtypeStruct((chips, 2) + slices.shape, bf16),
            jax.ShapeDtypeStruct((experts_here, width, 2 * hidden), bf16),
            jax.ShapeDtypeStruct((experts_here, 2) + w_down.shape[1:], bf16),
        ),
        in_specs=[ANY] * 4,
        out_specs=(ANY,) * 4,
        scratch_shapes=[
            DMA((5,)),
            DMA((heads + 1,)),
            DMA((heads,)),
            DMA((heads - 1,)),
            DMA((heads - 1,)),
            DMA((2, 2 * chips)),
            DMA((2, 2 * chips)),
            DMA((2, chips)),
            DMA((2, chips)),
            DMA((chips + 1,)),
            DMA((chips + 1,)),
        ],
        compiler_params=pltpu.CompilerParams(collective_id=number, has_side_effects=True),
        name="start",
    )(x, slices, w_gate_up, w_down)


def end_kernel(cube, heads, first_ref, in_ref, first_out, out_ref, *refs):
    count = cube.number
    arrived = refs[:count]
    parts = refs[count : 2 * count]
    local, first_send, first_recv, line_send, line_recv, send, recv = refs[2 * count :]
    hz = lax.axis_index("head")
    others = near(heads)[::-1]
    half = in_ref.shape[-2] // 2
    rows = in_ref.shape[-2] // heads
    meet([cube.peer(digit) for digit in range(count)] + [{"head": (hz + d) % heads} for d in others])
    own = pltpu.make_async_copy(first_ref.at[hz], first_out.at[hz], local)
    own.start()
    copies = {}

    def slot(side, k, mask):
        return subsets(cube.scatter_orders[side][k + 1 :]).index(mask)

    def mine(side, mask):
        return in_ref.at[cube.place(mask) + (pl.ds(side * half, half),)]

    def total(side, steps, mask):
        value = mine(side, mask)[...].astype(f32)
        for j in range(steps):
            copies[(side, j, mask)].wait_recv()
            value = value + arrived[j][side, slot(side, j, mask)].astype(f32)
        return value.astype(bf16)

    def first_copy(d):
        place = (hz + d) % heads
        return pltpu.make_async_remote_copy(
            src_ref=first_ref.at[place],
            dst_ref=first_out.at[hz],
            send_sem=first_send.at[d - 1],
            recv_sem=first_recv.at[d - 1],
            device_id={"head": place},
            device_id_type=MESH,
        )

    for k in range(count):
        for side in range(2):
            order = cube.scatter_orders[side]
            for mask in subsets(order[k + 1 :])[::-1]:
                full = mask | (1 << order[k])
                where = slot(side, k, mask)
                if k == 0:
                    piece = mine(side, full)
                else:
                    piece = parts[k - 1].at[side, where]
                    piece[...] = total(side, k, full)
                copies[(side, k, mask)] = pltpu.make_async_remote_copy(
                    src_ref=piece,
                    dst_ref=arrived[k].at[side, where],
                    send_sem=send.at[side, k, where],
                    recv_sem=recv.at[side, k, where],
                    device_id=cube.peer(order[k]),
                    device_id_type=MESH,
                )
                copies[(side, k, mask)].start()
        if k == 0:
            for d in others:
                first_copy(d).start()
    done = parts[count - 1]
    for side in range(2):
        done[0, pl.ds(side * half, half)] = total(side, count, 0)

    def line_copy(d):
        place = (hz + d) % heads
        return pltpu.make_async_remote_copy(
            src_ref=done.at[0, pl.ds(pl.multiple_of(place * rows, 16), rows)],
            dst_ref=out_ref.at[hz],
            send_sem=line_send.at[d - 1],
            recv_sem=line_recv.at[d - 1],
            device_id={"head": place},
            device_id_type=MESH,
        )

    for d in others:
        line_copy(d).start()
    out_ref[hz] = done[0, pl.ds(pl.multiple_of(hz * rows, 16), rows)]
    for copy in copies.values():
        copy.wait_send()
    own.wait()
    for d in others:
        line_copy(d).wait()
    for d in others:
        first_copy(d).wait()


def end(first, sums, chips, heads, number):
    rows, columns = sums.shape[-2:]
    cube = Cube(chips, True)
    count = cube.number
    half = rows // 2
    slots = [(1 << count) >> (k + 1) for k in range(count)]
    return pl.pallas_call(
        functools.partial(end_kernel, cube, heads),
        out_shape=(
            jax.ShapeDtypeStruct(first.shape, bf16),
            jax.ShapeDtypeStruct((heads, rows // heads, columns), bf16),
        ),
        in_specs=[ANY, WHOLE],
        out_specs=(ANY, WHOLE),
        scratch_shapes=[pltpu.VMEM((2, s, half, columns), bf16) for s in slots]
        + [pltpu.VMEM((2, s, half, columns), bf16) for s in slots[1:]]
        + [
            pltpu.VMEM((1, rows, columns), bf16),
            DMA,
            DMA((heads - 1,)),
            DMA((heads - 1,)),
            DMA((heads - 1,)),
            DMA((heads - 1,)),
            DMA((2, count, slots[0])),
            DMA((2, count, slots[0])),
        ],
        compiler_params=pltpu.CompilerParams(
            collective_id=number, has_side_effects=True, vmem_limit_bytes=40 << 20
        ),
        name="end",
    )(first, sums)


def place_kernel(chips, hidden, *refs):
    pieces, out_ref = refs[:chips], refs[chips]
    chip = lax.axis_index("chip")
    units = out_ref.shape[2] // 2
    for mask in range(chips):
        for part in range(2):
            begin = pl.multiple_of(part * units + flip(chip, mask) * hidden, hidden)
            out_ref[:, :, pl.ds(begin, hidden)] = pieces[mask][
                :, :, pl.ds(part * hidden, hidden)
            ].astype(f32)


def place_units(pieces, hidden):
    chips = len(pieces)
    experts_here, rows, double = pieces[0].shape
    return pl.pallas_call(
        functools.partial(place_kernel, chips, hidden),
        grid=(experts_here,),
        out_shape=jax.ShapeDtypeStruct((experts_here, rows, chips * double), f32),
        in_specs=[pl.BlockSpec((1, rows, double), lambda e: (e, 0, 0))] * chips,
        out_specs=pl.BlockSpec((1, rows, chips * double), lambda e: (e, 0, 0)),
        name="place_units",
    )(*pieces)


def across(value, chips, mask):
    if mask == 0:
        return value
    return lax.ppermute(value, "chip", [(i, i ^ mask) for i in range(chips)])


class Sums:
    def __init__(self, blocks):
        self.chips, self.heads = blocks.shape[:2]
        rows, columns = blocks.shape[2:]
        self.sides = blocks.reshape(self.chips, self.heads, 2, rows // 2, columns)
        self.cube = Cube(self.chips, False)
        self.arrived = {}
        self.shape = (rows, columns)

    def block(self, side, mask, steps):
        chip = lax.axis_index("chip")
        value = lax.dynamic_index_in_dim(self.sides[:, :, side], chip ^ mask, 0, keepdims=False)
        value = value.astype(f32)
        for j in range(steps):
            order = self.cube.scatter_orders[side]
            where = subsets(order[j + 1 :]).index(mask)
            value = value + self.arrived[(side, j)][where].astype(f32)
        return value

    def plane(self, k):
        for side in range(2):
            order = self.cube.scatter_orders[side]
            give = jnp.stack(
                [
                    self.block(side, mask | (1 << order[k]), k).astype(bf16)
                    for mask in subsets(order[k + 1 :])
                ]
            )
            self.arrived[(side, k)] = across(give, self.chips, 1 << order[k])

    def along(self):
        count = self.cube.number
        whole = jnp.concatenate([self.block(side, 0, count) for side in range(2)], axis=1)
        head = lax.axis_index("head")
        self.own = lax.dynamic_index_in_dim(whole, head, 0, keepdims=False)
        whole = whole.astype(bf16)
        self.line = []
        for d in range(1, self.heads):
            give = lax.dynamic_index_in_dim(whole, (head + d) % self.heads, 0, keepdims=False)
            pairs = [(i, (i + d) % self.heads) for i in range(self.heads)]
            self.line.append(lax.ppermute(give, "head", pairs))

    def result(self):
        return self.own + sum(value.astype(f32) for value in self.line)


def pin(sums, value):
    keys = list(sums.arrived)
    out = lax.optimization_barrier((value, [sums.arrived[key] for key in keys]))
    for key, kept in zip(keys, out[1]):
        sums.arrived[key] = kept
    return out[0]


def sibling(value):
    return lax.ppermute(value, "core", [(0, 1), (1, 0)])


def per_device(
    layer_input,
    segments,
    routes,
    pair_rank,
    query_key_value_weight,
    output_weight,
    router_weight,
    norm_attn,
    norm_ffn,
    w_gate_up,
    w_down,
    cotangent,
):
    chips = lax.axis_size("chip")
    head_number = lax.axis_size("head")
    sequence_batch, token_rows, width = layer_input.shape
    length = segments.shape[1]
    blk = token_rows * head_number
    query_group = QUERY_HEADS // KEY_VALUE_HEADS
    key_value_location = KEY_VALUE_HEADS // head_number
    loc_experts, slice_rows = w_gate_up.shape[:2]
    top = routes.shape[2]
    tokens_present = sequence_batch * token_rows
    pairs = tokens_present * top
    line_tokens = tokens_present * head_number
    scale = HEAD_WIDTH ** (-0.5)
    hidden = FF // chips
    loc_columns = key_value_location * (query_group + 2) * HEAD_WIDTH
    chip = lax.axis_index("chip")
    core = lax.axis_index("core")
    head = lax.axis_index("head")
    seq_index = chip * 2 + core
    dense_rows = query_key_value_weight.shape[0]

    extras = jnp.concatenate([router_weight, norm_attn[:, None], norm_ffn[:, None]], axis=1)
    extras = jnp.pad(extras, ((0, 0), (0, LANES - extras.shape[1])))
    slices = query_key_value_weight.reshape(dense_rows, head_number, loc_columns).transpose(1, 0, 2)
    slices = jnp.concatenate(
        [slices, jnp.broadcast_to(extras, (head_number,) + extras.shape)], axis=2
    )
    group_tokens = chips * head_number * tokens_present
    columns = width + LANES
    fused = hidden % LANES == 0 and group_tokens <= 2048
    own_tokens = layer_input.reshape(tokens_present, width)
    cots = cotangent.reshape(tokens_present, width)
    if fused:
        x_line, dense, expert_up, expert_down = start(
            own_tokens, slices, w_gate_up, w_down, chips, head_number, hidden, 1
        )
        expert_down = expert_down.reshape(loc_experts * hidden, width)
        dense = dense.reshape(width, loc_columns + LANES)
        cots, x_line = lax.optimization_barrier((cots, x_line))
    else:
        parts = w_gate_up.reshape(loc_experts, slice_rows, 2, chips, hidden).transpose(3, 2, 1, 0, 4)
        parts = parts.reshape(chips, 2, slice_rows, loc_experts * hidden)
        piled = jnp.zeros((chips, 2, 2, slice_rows, loc_experts * hidden), bf16)
        for mask in range(chips):
            piece = lax.dynamic_index_in_dim(parts, chip ^ mask, 0, keepdims=False)
            piece = across(piece, chips, mask)
            other = sibling(piece)
            piled = lax.dynamic_update_slice(piled, piece[None, None], (chip ^ mask, core, 0, 0, 0))
            piled = lax.dynamic_update_slice(piled, other[None, None], (chip ^ mask, 1 - core, 0, 0, 0))
        piled = piled.transpose(2, 0, 1, 3, 4).reshape(2, width, loc_experts * hidden)
        expert_gate, expert_up = piled[0], piled[1]
        down_other = sibling(w_down)
        expert_down = (
            jnp.where(
                core == 0,
                jnp.concatenate([w_down, down_other], axis=1),
                jnp.concatenate([down_other, w_down], axis=1),
            )
        ).reshape(loc_experts * hidden, width)

        lined = line_exchange(slices, head_number, 1)
        dense = gather(
            lined.reshape(head_number * dense_rows, loc_columns + LANES), chips, 1, True, 2
        ).reshape(width, loc_columns + LANES)
        x_line = line_exchange(layer_input.reshape(tokens_present, width), head_number, 3, True)

    grad_all = lax.all_gather(cots, ("chip", "head"), axis=0, tiled=True)
    dense_out = lax.all_gather(output_weight, ("chip", "core", "head"), axis=0, tiled=True)

    dense_qkv = dense[:, :loc_columns]
    dense_router = dense[:, loc_columns : loc_columns + EXPERTS]
    gain_attn = dense[:, loc_columns + EXPERTS].astype(f32)
    gain_ffn = dense[:, loc_columns + EXPERTS + 1].astype(f32)

    x_line = x_line.reshape(line_tokens, width).astype(f32)
    normed_line = x_line * lax.rsqrt(jnp.mean(x_line * x_line, axis=1, keepdims=True) + epsilon)
    first_line = (normed_line * gain_attn).astype(bf16)

    def to_blocks(value):
        columns = value.shape[1:]
        return (
            value.reshape((head_number, sequence_batch, token_rows) + columns)
            .swapaxes(0, 1)
            .reshape((sequence_batch, blk) + columns)
        )

    def to_lines(value):
        columns = value.shape[2:]
        return (
            value.reshape((sequence_batch, head_number, token_rows) + columns)
            .swapaxes(0, 1)
            .reshape((line_tokens,) + columns)
        )

    q_start = seq_index * blk
    q_pos = q_start + jnp.arange(blk, dtype=jnp.int32)
    cosine, sine = rope_tables(q_pos, HEAD_WIDTH)
    projected = to_blocks(jnp.dot(first_line, dense_qkv, preferred_element_type=f32)).reshape(
        sequence_batch, blk, key_value_location, query_group + 2, HEAD_WIDTH
    )
    turned = rotate(projected[:, :, :, : query_group + 1], cosine, sine)
    query_rows = turned[:, :, :, :query_group].astype(bf16)
    keys_values = (
        jnp.stack([turned[:, :, :, query_group], projected[:, :, :, query_group + 1]], axis=3)
        .astype(bf16)
        .reshape(sequence_batch * blk, key_value_location * 2 * HEAD_WIDTH)
    )
    kv_columns = key_value_location * 2 * HEAD_WIDTH
    kv_all = (
        gather(keys_values, chips, 1, True, 4)
        .reshape(2 * chips, sequence_batch, blk, kv_columns)
        .transpose(1, 0, 2, 3)
        .reshape(sequence_batch, length, kv_columns)
    )
    q_seg = lax.dynamic_slice_in_dim(segments, q_start, blk, 1)

    def key_view(piece, offset, token_count):
        portion = lax.dynamic_slice_in_dim(piece, offset, token_count, 1).reshape(
            sequence_batch, token_count, key_value_location, 2, HEAD_WIDTH
        )
        return (portion[:, :, :, 0], portion[:, :, :, 1])

    def key_mask(begin, token_count):
        k_pos = begin + jnp.arange(token_count, dtype=jnp.int32)
        k_seg = lax.dynamic_slice_in_dim(segments, begin, token_count, 1)
        same = q_seg[:, :, None] == k_seg[:, None, :]
        causal = k_pos[None, None, :] <= q_pos[None, :, None]
        return (same & causal)[:, None, None]

    def sweep(function, state):
        sub = 512

        def turn(index, inner):
            offset = index * sub
            return lax.cond(
                offset <= q_start + blk - 1,
                lambda now: function(now, kv_all, offset, sub),
                lambda now: now,
                inner,
            )

        return lax.fori_loop(0, length // sub, turn, state)

    def forward_block(state, piece, offset, token_count):
        top_now, total, accum = state
        keys, values = key_view(piece, offset, token_count)
        scores = (
            jnp.einsum("sqhgd,skhd->shgqk", query_rows, keys, preferred_element_type=f32) * scale
        )
        mask = key_mask(offset, token_count)
        scores = jnp.where(mask, scores, negative)
        top_new = jnp.maximum(top_now, jnp.max(scores, axis=-1))
        weights = jnp.where(mask, jnp.exp(scores - top_new[..., None]), 0.0)
        shrink = jnp.exp(top_now - top_new)
        total = total * shrink + jnp.sum(weights, axis=-1)
        accum = accum * shrink[..., None] + jnp.einsum(
            "shgqk,skhd->shgqd", weights.astype(bf16), values, preferred_element_type=f32
        )
        return (top_new, total, accum)

    state_zero = (
        jnp.full((sequence_batch, key_value_location, query_group, blk), negative, f32),
        jnp.zeros((sequence_batch, key_value_location, query_group, blk), f32),
        jnp.zeros((sequence_batch, key_value_location, query_group, blk, HEAD_WIDTH), f32),
    )
    top_now, total, accum = sweep(forward_block, state_zero)
    lse = top_now + jnp.log(total)
    attended = accum / total[..., None]
    group_columns = key_value_location * query_group * HEAD_WIDTH
    heads_local = to_lines(
        attended.transpose(0, 3, 1, 2, 4).reshape(sequence_batch, blk, group_columns).astype(bf16)
    )
    mixed_heads = (
        line_exchange(
            heads_local.reshape(head_number, tokens_present, group_columns), head_number, 5
        )
        .transpose(1, 0, 2)
        .reshape(tokens_present, QUERY_HEADS * HEAD_WIDTH)
    )
    tokens = layer_input.reshape(tokens_present, width).astype(f32)
    middle = tokens + jnp.dot(mixed_heads, dense_out, preferred_element_type=f32)
    inverse_two = lax.rsqrt(jnp.mean(middle * middle, axis=1, keepdims=True) + epsilon)
    normed_two = middle * inverse_two
    second_input = (normed_two * gain_ffn).astype(bf16)
    router_logits = jnp.dot(second_input, dense_router, preferred_element_type=f32)
    route_flat = routes.reshape(tokens_present, top)
    hot = route_flat[:, :, None] == jnp.arange(EXPERTS, dtype=jnp.int32)[None, None, :]
    chosen = jnp.sum(jnp.where(hot, router_logits[:, None, :], 0.0), axis=2)
    gates = jax.nn.softmax(chosen, axis=-1)
    expert_of = route_flat.reshape(pairs)
    rank = pair_rank.reshape(pairs)
    slot = jnp.sum(
        (expert_of[None, :] == expert_of[:, None]) & (rank[None, :] < rank[:, None]),
        axis=1,
        dtype=jnp.int32,
    )
    kept = (slot < CAP).reshape(tokens_present, top).astype(f32)
    weights_pair = gates * kept
    spread = jnp.sum(jnp.where(hot, weights_pair[:, :, None], 0.0), axis=1)
    spread_high = spread.astype(bf16)
    spread_low = (spread - spread_high.astype(f32)).astype(bf16)
    pad = jnp.zeros((tokens_present, LOW - EXPERTS), bf16)
    payload = jnp.concatenate([second_input, spread_high, pad, spread_low, pad], axis=1)
    if fused:
        back, moe_part, keep_up, other_up, keep_down, other_down = expert_turn(
            payload, grad_all, expert_up, expert_down, chips, head_number, 6
        )
        moe_sums = Sums(moe_part.reshape(chips, head_number, tokens_present, width))
        shared = (keep_up.astype(f32) + other_up.astype(f32)).astype(bf16)
        pieces = [
            across(lax.dynamic_index_in_dim(shared, chip ^ mask, 0, keepdims=False), chips, mask)
            for mask in range(chips)
        ]
        down_share = keep_down.astype(f32) + other_down.astype(f32)
    else:
        x_all = gather(payload, chips, head_number, False, 6).reshape(group_tokens, columns)
        moe_part, back_part, d_gate_w, d_up_w, d_down_w = experts(
            x_all, grad_all, expert_gate, expert_up, expert_down, hidden
        )
        back_part = back_part.reshape(chips, head_number, tokens_present, columns)
        back = scatter_sum(back_part, chips, head_number, False, 7)
        moe = lax.psum_scatter(moe_part, ("chip", "head"), scatter_dimension=0, tiled=True)
        grads = jnp.stack([d_gate_w, d_up_w]).reshape(2, chips, 2, slice_rows, loc_experts * hidden)
        keep = lax.dynamic_index_in_dim(grads, core, 2, keepdims=False)
        give = lax.dynamic_index_in_dim(grads, 1 - core, 2, keepdims=False)
        shared = (keep.astype(f32) + sibling(give).astype(f32)).astype(bf16)
        piled = jnp.zeros((chips, 2, slice_rows, loc_experts * hidden), bf16)
        for mask in range(chips):
            piece = across(lax.dynamic_index_in_dim(shared, chip ^ mask, 1, keepdims=False), chips, mask)
            piled = lax.dynamic_update_slice(piled, piece[None], (chip ^ mask, 0, 0, 0))
        up_share = (
            piled.reshape(chips, 2, slice_rows, loc_experts, hidden)
            .transpose(3, 2, 1, 0, 4)
            .astype(f32)
            .reshape(loc_experts, slice_rows, 2 * FF)
        )
        d_down_w = d_down_w.reshape(loc_experts, 2, hidden // 2, width)
        keep = lax.dynamic_index_in_dim(d_down_w, core, 1, keepdims=False)
        give = lax.dynamic_index_in_dim(d_down_w, 1 - core, 1, keepdims=False)
        down_share = keep.astype(f32) + sibling(give).astype(f32)

    grad_out = cotangent.reshape(tokens_present, width).astype(f32)
    d_kept = back[:, width : width + EXPERTS]
    grad_gate = jnp.sum(jnp.where(hot, d_kept[:, None, :], 0.0), axis=2) * kept
    grad_chosen = gates * (grad_gate - jnp.sum(gates * grad_gate, axis=1, keepdims=True))
    grad_logits = jnp.sum(jnp.where(hot, grad_chosen[:, :, None], 0.0), axis=1)
    grad_router = jnp.dot(second_input.astype(f32).T, grad_logits, precision=HIGH_PRECISION)
    grad_second = back[:, :width] + jnp.dot(
        grad_logits, dense_router.astype(f32).T, precision=HIGH_PRECISION
    )
    grad_gain_ffn = jnp.sum(grad_second * normed_two, axis=0)
    scaled_two = grad_second * gain_ffn
    grad_mid = grad_out + inverse_two * (
        scaled_two - normed_two * jnp.mean(scaled_two * normed_two, axis=1, keepdims=True)
    )
    grad_attn = grad_mid.astype(bf16)
    grad_dense_out = jnp.dot(mixed_heads.T, grad_attn, preferred_element_type=f32)
    out_share = lax.psum_scatter(
        grad_dense_out.astype(bf16), ("chip", "core", "head"), scatter_dimension=0, tiled=True
    ).astype(f32)
    grad_heads = (
        jnp.dot(grad_attn, dense_out.T, preferred_element_type=f32)
        .astype(bf16)
        .reshape(tokens_present, head_number, group_columns)
        .transpose(1, 0, 2)
    )
    grad_local = to_blocks(
        line_exchange(grad_heads, head_number, 8).reshape(line_tokens, group_columns)
    ).reshape(sequence_batch, blk, key_value_location, query_group, HEAD_WIDTH)
    if fused:
        moe_sums.plane(0)
        grad_local = pin(moe_sums, grad_local)
        moe_sums.plane(1)
    delta = jnp.sum(grad_local.transpose(0, 2, 3, 1, 4).astype(f32) * attended, axis=-1)

    def backward_block(state, piece, offset, token_count):
        grad_q, grad_store = state
        keys, values = key_view(piece, offset, token_count)
        scores = (
            jnp.einsum("sqhgd,skhd->shgqk", query_rows, keys, preferred_element_type=f32) * scale
        )
        mask = key_mask(offset, token_count)
        probs = jnp.where(mask, jnp.exp(scores - lse[..., None]), 0.0)
        grad_probs = jnp.einsum("sqhgd,skhd->shgqk", grad_local, values, preferred_element_type=f32)
        grad_scores = (probs * (grad_probs - delta[..., None])).astype(bf16)
        grad_q = (
            grad_q
            + jnp.einsum("shgqk,skhd->sqhgd", grad_scores, keys, preferred_element_type=f32) * scale
        )
        grad_k = (
            jnp.einsum("shgqk,sqhgd->skhd", grad_scores, query_rows, preferred_element_type=f32)
            * scale
        )
        grad_v = jnp.einsum(
            "shgqk,sqhgd->skhd", probs.astype(bf16), grad_local, preferred_element_type=f32
        )
        block_width = jnp.stack([grad_k, grad_v], axis=3).reshape(
            sequence_batch, token_count, kv_columns
        )
        grad_store = lax.dynamic_update_slice_in_dim(
            grad_store, block_width.astype(bf16), offset, 1
        )
        return (grad_q, grad_store)

    back_zero = (
        jnp.zeros((sequence_batch, blk, key_value_location, query_group, HEAD_WIDTH), f32),
        jnp.zeros((sequence_batch, length, kv_columns), bf16),
    )
    grad_q, grad_store = sweep(backward_block, back_zero)
    if fused:
        grad_store = pin(moe_sums, grad_store)
        moe_sums.along()
    grad_store = (
        grad_store.reshape(sequence_batch, 2 * chips, blk, kv_columns)
        .transpose(1, 0, 2, 3)
        .reshape(chips, 2, sequence_batch * blk, kv_columns)
    )
    grad_kv = scatter_sum(grad_store, chips, 1, True, 9).reshape(
        sequence_batch, blk, key_value_location, 2, HEAD_WIDTH
    )
    grad_proj = jnp.concatenate([grad_q.astype(bf16), grad_kv.astype(bf16)], axis=3).astype(f32)
    unturned = rotate(grad_proj[:, :, :, : query_group + 1], cosine, -sine)
    grad_qkv = to_lines(
        jnp.concatenate([unturned, grad_proj[:, :, :, query_group + 1 :]], axis=3)
        .reshape(sequence_batch, blk, loc_columns)
        .astype(bf16)
    )
    grad_first_part = jnp.dot(grad_qkv, dense_qkv.T, preferred_element_type=f32)
    grad_gain_attn = jnp.sum(grad_first_part * normed_line, axis=0)
    grad_dense_qkv = jnp.dot(first_line.T, grad_qkv, preferred_element_type=f32)
    sums = jnp.concatenate(
        [
            grad_dense_qkv,
            grad_router,
            grad_gain_attn[:, None],
            grad_gain_ffn[:, None],
            jnp.zeros((width, LANES - EXPERTS - 2), f32),
        ],
        axis=1,
    ).astype(bf16)
    if fused:
        grad_first, sums = end(
            grad_first_part.astype(bf16).reshape(head_number, tokens_present, width),
            sums.reshape(chips, 2, head_number * dense_rows, loc_columns + LANES),
            chips,
            head_number,
            13,
        )
        pieces, grad_first = lax.optimization_barrier((pieces, grad_first))
        grad_first = jnp.sum(grad_first.astype(f32), axis=0)
        sums = sums.astype(f32)
        up_share = place_units(pieces, hidden)
        moe = moe_sums.result()
    else:
        grad_first = jnp.sum(
            line_exchange(
                grad_first_part.astype(bf16).reshape(head_number, tokens_present, width),
                head_number,
                10,
            ).astype(f32),
            axis=0,
        )
        sums = scatter_sum(
            sums.reshape(chips, 2, head_number * dense_rows, loc_columns + LANES), chips, 1, True, 11
        )
        sums = line_exchange(
            sums.reshape(head_number, dense_rows, loc_columns + LANES), head_number, 12
        )
    inverse_one = lax.rsqrt(jnp.mean(tokens * tokens, axis=1, keepdims=True) + epsilon)
    normed_one = tokens * inverse_one
    scaled_one = grad_first * gain_attn
    grad_input = grad_mid + inverse_one * (
        scaled_one - normed_one * jnp.mean(scaled_one * normed_one, axis=1, keepdims=True)
    )
    mixed_out = (middle + moe.astype(f32)).astype(bf16)
    mixed_out = mixed_out.reshape(sequence_batch, token_rows, width)
    qkv_share = sums[:, :, :loc_columns].transpose(1, 0, 2).reshape(dense_rows, -1)
    extra = jnp.sum(sums[:, :, loc_columns:], axis=0)
    return (
        mixed_out,
        grad_input.reshape(sequence_batch, token_rows, width),
        qkv_share,
        out_share,
        extra[:, :EXPERTS],
        extra[:, EXPERTS],
        extra[:, EXPERTS + 1],
        up_share,
        down_share,
    )


def solution(mesh):
    grid = mesh.devices
    seq, heads = grid.shape
    split = Mesh(grid.reshape(seq // 2, 2, heads), ("chip", "core", "head"))
    places = ("chip", "core", "head")
    inner = ("chip", "core")
    placed = (
        P(None, places, None),
        P(),
        P(None, places, None),
        P(None, places, None),
        P(places, None),
        P(places, None),
        P(places, None),
        P(places),
        P(places),
        P("head", inner, None),
        P("head", inner, None),
        P(None, places, None),
    )
    return jax.shard_map(
        per_device,
        mesh=split,
        in_specs=placed,
        out_specs=(
            P(None, places, None),
            P(None, places, None),
            P(places, None),
            P(places, None),
            P(places, None),
            P(places),
            P(places),
            P("head", inner, None),
            P("head", inner, None),
        ),
        check_vma=False,
    )
```

```python
import functools

import jax
import jax.numpy as jnp
from jax import lax
from jax.experimental import pallas as pl
from jax.experimental.pallas import tpu as pltpu
from jax.sharding import Mesh, PartitionSpec as P

MODEL_WIDTH = 1536
QUERY_HEADS = 24
KEY_VALUE_HEADS = 8
HEAD_WIDTH = 64
EXPERTS = 40
FF = 512
CAP = 25
LANES = 128
LOW = 64

epsilon = 1e-06
negative = -1e30
theta = 10000.0
HIGH_PRECISION = lax.Precision.HIGHEST
MESH = pl.DeviceIdType.MESH
f32 = jnp.float32
bf16 = jnp.bfloat16
ANY = pl.BlockSpec(memory_space=pl.ANY)
WHOLE = pl.BlockSpec(memory_space=pltpu.VMEM)
DMA = pltpu.SemaphoreType.DMA


def rope_tables(token_positions, head_size):
    half = head_size // 2
    freq = theta ** (-jnp.arange(half, dtype=jnp.float32) / half)
    angle = token_positions.astype(jnp.float32)[:, None] * freq[None, :]
    return (jnp.cos(angle)[None, :, None, None, :], jnp.sin(angle)[None, :, None, None, :])


def rotate(value, cosine, sine):
    half = value.shape[-1] // 2
    first = value[..., :half]
    second = value[..., half:]
    return jnp.concatenate(
        [first * cosine - second * sine, second * cosine + first * sine], axis=-1
    )


def digits(count):
    number = count.bit_length() - 1
    assert 1 << number == count
    return number


def flip(index, mask):
    out = index
    bit = 0
    while (1 << bit) <= mask:
        if (mask >> bit) & 1:
            out = out + (1 - 2 * ((index // (1 << bit)) % 2)) * (1 << bit)
        bit += 1
    return out


def subsets(bits):
    out = [0]
    for bit in bits:
        out = out + [mask | (1 << bit) for mask in out]
    return out


def near(count):
    return sorted(range(1, count), key=lambda step: min(step, count - step))


def cut_rows(rows):
    return (rows // 2 + 15) // 16 * 16


def part_of(rows, side):
    cut = cut_rows(rows)
    return pl.ds(side * cut, rows - cut if side else cut)


def meet(peers):
    sem = pltpu.get_barrier_semaphore()
    for peer in peers:
        pl.semaphore_signal(sem, inc=1, device_id=peer, device_id_type=MESH)
    pl.semaphore_wait(sem, len(peers))


class Cube:
    def __init__(self, chips, with_core):
        self.chips = chips
        self.chip_digits = digits(chips)
        self.number = self.chip_digits + int(with_core)
        self.with_core = with_core
        up = tuple(range(self.chip_digits))
        core = (self.chip_digits,) if with_core else ()
        self.gather_orders = (up + core, up[::-1] + core)
        self.scatter_orders = (core + up, core + up[::-1])

    def place(self, mask):
        chip = flip(lax.axis_index("chip"), mask & (self.chips - 1))
        if not self.with_core:
            return (chip,)
        return (chip, flip(lax.axis_index("core"), mask >> self.chip_digits))

    def peer(self, digit):
        if digit < self.chip_digits:
            return {"chip": flip(lax.axis_index("chip"), 1 << digit)}
        return {"core": flip(lax.axis_index("core"), 1)}


def gather_kernel(cube, heads, in_ref, out_ref, local, line_send, line_recv, send, recv):
    hz = lax.axis_index("head")
    rows = in_ref.shape[0]
    half = rows // 2
    others = near(heads) if heads > 1 else []
    meet(
        [cube.peer(digit) for digit in range(cube.number)]
        + [{"head": (hz + d) % heads} for d in others]
    )

    def at(mask, d):
        index = cube.place(mask)
        return index + ((hz + heads - d) % heads,) if heads > 1 else index

    own = pltpu.make_async_copy(in_ref, out_ref.at[at(0, 0)], local)
    own.start()
    line = {}
    for d in others:
        line[d] = pltpu.make_async_remote_copy(
            src_ref=in_ref,
            dst_ref=out_ref.at[at(0, 0)],
            send_sem=line_send.at[d - 1],
            recv_sem=line_recv.at[d - 1],
            device_id={"head": (hz + d) % heads},
            device_id_type=MESH,
        )
        line[d].start()
    copies = {}

    def forward(side, mask, d):
        order = cube.gather_orders[side]
        last = max([k for k in range(cube.number) if (mask >> order[k]) & 1], default=-1)
        for k in range(last + 1, cube.number):
            later = mask | (1 << order[k])
            part = pl.ds(side * half, half)
            place = out_ref.at[at(mask, d) + (part,)]
            copy = pltpu.make_async_remote_copy(
                src_ref=in_ref.at[part] if mask == 0 and d == 0 else place,
                dst_ref=place,
                send_sem=send.at[side, later, d],
                recv_sem=recv.at[side, later, d],
                device_id=cube.peer(order[k]),
                device_id_type=MESH,
            )
            copy.start()
            copies[(side, later, d)] = copy

    for side in range(2):
        forward(side, 0, 0)
    for d in others:
        line[d].wait_recv()
        for side in range(2):
            forward(side, 0, d)
    for mask in sorted(range(1, 1 << cube.number), key=lambda m: bin(m).count("1")):
        for d in [0] + others:
            for side in range(2):
                copies[(side, mask, d)].wait_recv()
                forward(side, mask, d)
    own.wait()
    for copy in list(line.values()) + list(copies.values()):
        copy.wait_send()


def gather(value, chips, heads, with_core, number):
    rows, columns = value.shape
    cube = Cube(chips, with_core)
    lead = (chips,) + ((2,) if with_core else ()) + ((heads,) if heads > 1 else ())
    steps = max(heads - 1, 1)
    return pl.pallas_call(
        functools.partial(gather_kernel, cube, heads),
        out_shape=jax.ShapeDtypeStruct(lead + (rows, columns), value.dtype),
        in_specs=[ANY],
        out_specs=ANY,
        scratch_shapes=[
            DMA,
            DMA((steps,)),
            DMA((steps,)),
            DMA((2, 1 << cube.number, heads)),
            DMA((2, 1 << cube.number, heads)),
        ],
        compiler_params=pltpu.CompilerParams(collective_id=number, has_side_effects=True),
        name="gather",
    )(value)


def scatter_kernel(cube, heads, in_ref, out_ref, *refs):
    count = cube.number
    arrived, parts = refs[:count], refs[count : 2 * count - 1]
    line_out, line_in, line_send, line_recv, send, recv = refs[2 * count - 1 :]
    hz = lax.axis_index("head")
    half = in_ref.shape[-2] // 2
    others = near(heads) if heads > 1 else []
    order_of_lines = others[::-1] + [0]
    meet(
        [cube.peer(digit) for digit in range(count)] + [{"head": (hz + d) % heads} for d in others]
    )
    copies = {}

    def slot(side, k, mask):
        return subsets(cube.scatter_orders[side][k + 1 :]).index(mask)

    def mine(side, mask, d):
        index = cube.place(mask)
        if heads > 1:
            index = index + ((hz + d) % heads,)
        return in_ref.at[index + (pl.ds(side * half, half),)]

    def pass_on(side, k, mask, d, source):
        where = slot(side, k, mask)
        copy = pltpu.make_async_remote_copy(
            src_ref=source,
            dst_ref=arrived[k].at[side, where, d],
            send_sem=send.at[side, k, where, d],
            recv_sem=recv.at[side, k, where, d],
            device_id=cube.peer(cube.scatter_orders[side][k]),
            device_id_type=MESH,
        )
        copy.start()
        copies[(side, k, mask, d)] = copy

    def total(side, steps, mask, d):
        value = mine(side, mask, d)[...].astype(f32)
        for j in range(steps):
            copies[(side, j, mask, d)].wait_recv()
            value = value + arrived[j][side, slot(side, j, mask), d].astype(f32)
        return value

    for k in range(count):
        for d in order_of_lines:
            for side in range(2):
                order = cube.scatter_orders[side]
                for mask in subsets(order[k + 1 :])[::-1]:
                    full = mask | (1 << order[k])
                    if k == 0:
                        source = mine(side, full, d)
                    else:
                        source = parts[k - 1].at[side, slot(side, k, mask), d]
                        source[...] = total(side, k, full, d).astype(bf16)
                    pass_on(side, k, mask, d, source)
    line = {}
    for d in order_of_lines:
        for side in range(2):
            value = total(side, count, 0, d)
            if d:
                line_out[d - 1, pl.ds(side * half, half)] = value.astype(bf16)
            else:
                out_ref[pl.ds(side * half, half)] = value
        if d:
            line[d] = pltpu.make_async_remote_copy(
                src_ref=line_out.at[d - 1],
                dst_ref=line_in.at[d - 1],
                send_sem=line_send.at[d - 1],
                recv_sem=line_recv.at[d - 1],
                device_id={"head": (hz + d) % heads},
                device_id_type=MESH,
            )
            line[d].start()
    for d in others:
        line[d].wait_recv()
        out_ref[...] += line_in[d - 1].astype(f32)
    for copy in list(line.values()) + list(copies.values()):
        copy.wait_send()


def scatter_sum(value, chips, heads, with_core, number):
    rows, columns = value.shape[-2:]
    cube = Cube(chips, with_core)
    half = rows // 2
    steps = max(heads - 1, 1)
    line_rows = rows if heads > 1 else 16
    slots = [(1 << cube.number) >> (k + 1) for k in range(cube.number)]
    if 2 * value.size + 4 * heads * half * columns * (sum(slots) + sum(slots[1:])) > 40 << 20:
        names = ("chip", "core") if with_core else ("chip",)
        names = names + (("head",) if heads > 1 else ())
        flat = value.reshape(-1, columns)
        return lax.psum_scatter(flat, names, scatter_dimension=0, tiled=True).astype(f32)
    return pl.pallas_call(
        functools.partial(scatter_kernel, cube, heads),
        out_shape=jax.ShapeDtypeStruct((rows, columns), f32),
        in_specs=[WHOLE],
        out_specs=WHOLE,
        scratch_shapes=[pltpu.VMEM((2, s, heads, half, columns), bf16) for s in slots]
        + [pltpu.VMEM((2, s, heads, half, columns), bf16) for s in slots[1:]]
        + [
            pltpu.VMEM((steps, line_rows, columns), bf16),
            pltpu.VMEM((steps, line_rows, columns), bf16),
            DMA((steps,)),
            DMA((steps,)),
            DMA((2, cube.number, slots[0], heads)),
            DMA((2, cube.number, slots[0], heads)),
        ],
        compiler_params=pltpu.CompilerParams(
            collective_id=number, has_side_effects=True, vmem_limit_bytes=56 << 20
        ),
        name="scatter_sum",
    )(value)


def line_kernel(heads, same, in_ref, out_ref, local, send, recv):
    hz = lax.axis_index("head")
    others = near(heads)[::-1]
    meet([{"head": (hz + d) % heads} for d in others])

    def source(place):
        return in_ref if same else in_ref.at[place]

    own = pltpu.make_async_copy(source(hz), out_ref.at[hz], local)
    own.start()
    copies = []
    for d in others:
        place = (hz + d) % heads
        copy = pltpu.make_async_remote_copy(
            src_ref=source(place),
            dst_ref=out_ref.at[hz],
            send_sem=send.at[d - 1],
            recv_sem=recv.at[d - 1],
            device_id={"head": place},
            device_id_type=MESH,
        )
        copy.start()
        copies.append(copy)
    own.wait()
    for copy in copies:
        copy.wait()


def line_exchange(value, heads, number, same=False):
    return pl.pallas_call(
        functools.partial(line_kernel, heads, same),
        out_shape=jax.ShapeDtypeStruct((heads,) + value.shape if same else value.shape, value.dtype),
        in_specs=[ANY],
        out_specs=ANY,
        scratch_shapes=[DMA, DMA((heads - 1,)), DMA((heads - 1,))],
        compiler_params=pltpu.CompilerParams(collective_id=number, has_side_effects=True),
        name="line_exchange",
    )(value)


NT = (((1,), (1,)), ((), ()))


def experts_kernel(
    tile,
    hidden,
    x_ref,
    c_ref,
    gate_hbm,
    up_hbm,
    down_hbm,
    moe_ref,
    back_ref,
    d_gate_hbm,
    d_up_hbm,
    d_down_hbm,
    w_gate,
    w_up,
    w_down,
    d_gate_w,
    d_up_w,
    d_down_w,
    acts,
    back_gate,
    back_up,
    stage_wide,
    stage_down,
    load,
    store,
):
    step = pl.program_id(0)
    width, total = w_gate.shape

    @pl.when(step == 0)
    def _():
        loads = [
            pltpu.make_async_copy(gate_hbm, w_gate, load.at[0]),
            pltpu.make_async_copy(up_hbm, w_up, load.at[1]),
            pltpu.make_async_copy(down_hbm, w_down, load.at[2]),
        ]
        for copy in loads:
            copy.start()
        d_gate_w[...] = jnp.zeros_like(d_gate_w)
        d_up_w[...] = jnp.zeros_like(d_up_w)
        d_down_w[...] = jnp.zeros_like(d_down_w)
        for copy in loads:
            copy.wait()

    x = x_ref[:, :width]
    c = c_ref[...]
    routed = x_ref[:, width:]
    first_expert = lax.axis_index("head") * (total // hidden)
    d_gates = jnp.zeros((x.shape[0], LANES), f32)
    for begin in range(0, total, tile):
        js = pl.ds(begin, tile)
        column = begin + lax.broadcasted_iota(jnp.int32, (LANES, tile), 1)
        line = lax.broadcasted_iota(jnp.int32, (LANES, tile), 0)
        expert = first_expert + column // hidden
        here = (line == expert).astype(f32)
        both = (here + (line == expert + LOW).astype(f32)).astype(bf16)
        weight = jnp.dot(routed, both, preferred_element_type=f32)
        gate = jnp.dot(x, w_gate[:, js], preferred_element_type=f32)
        up = jnp.dot(x, w_up[:, js], preferred_element_type=f32)
        d_act = lax.dot_general(c, w_down[js, :], NT, preferred_element_type=f32)
        sigma = 1.0 / (1.0 + jnp.exp(-gate))
        silu = gate * sigma
        act = (silu * up).astype(bf16).astype(f32)
        d_gates = d_gates + lax.dot_general(
            (act * d_act).astype(bf16), here.astype(bf16), NT, preferred_element_type=f32
        )
        acts[:, js] = (act * weight).astype(bf16)
        d_act = d_act * weight
        back_up[:, js] = (d_act * silu).astype(bf16)
        back_gate[:, js] = (d_act * up * sigma * (1.0 + gate * (1.0 - sigma))).astype(bf16)
    back_ref[:, width:] = d_gates.astype(bf16)
    x_turned = x.T
    for begin in range(0, total, tile):
        js = pl.ds(begin, tile)
        d_gate_w[:, js] += jnp.dot(x_turned, back_gate[:, js], preferred_element_type=f32)
        d_up_w[:, js] += jnp.dot(x_turned, back_up[:, js], preferred_element_type=f32)
        d_down_w[js, :] += jnp.dot(acts[:, js].T, c, preferred_element_type=f32)
    for begin in range(0, width, 512):
        cs = pl.ds(begin, 512)
        moe_ref[:, cs] = jnp.dot(acts[...], w_down[:, cs], preferred_element_type=f32).astype(bf16)
        back_ref[:, cs] = (
            lax.dot_general(back_gate[...], w_gate[cs, :], NT, preferred_element_type=f32)
            + lax.dot_general(back_up[...], w_up[cs, :], NT, preferred_element_type=f32)
        ).astype(bf16)

    @pl.when(step == pl.num_programs(0) - 1)
    def _():
        rows = stage_wide.shape[1]
        jobs = [
            (source, target, stage, begin)
            for source, target, stage in (
                (d_gate_w, d_gate_hbm, stage_wide),
                (d_up_w, d_up_hbm, stage_wide),
                (d_down_w, d_down_hbm, stage_down),
            )
            for begin in range(0, source.shape[0], rows)
        ]
        flight = {}
        for index, (source, target, stage, begin) in enumerate(jobs):
            now = index % 2
            if now in flight:
                flight[now].wait()
            stage[now] = source[pl.ds(begin, rows), :].astype(bf16)
            flight[now] = pltpu.make_async_copy(
                stage.at[now], target.at[pl.ds(begin, rows), :], store.at[now]
            )
            flight[now].start()
        for copy in flight.values():
            copy.wait()


def experts(x, c, w_gate, w_up, w_down, hidden):
    tokens, columns = x.shape
    width, total = w_gate.shape
    block = min(256, tokens)
    tile = 256 if total % 256 == 0 else hidden
    return pl.pallas_call(
        functools.partial(experts_kernel, tile, hidden),
        grid=(tokens // block,),
        out_shape=(
            jax.ShapeDtypeStruct((tokens, width), bf16),
            jax.ShapeDtypeStruct((tokens, columns), bf16),
            jax.ShapeDtypeStruct((width, total), bf16),
            jax.ShapeDtypeStruct((width, total), bf16),
            jax.ShapeDtypeStruct((total, width), bf16),
        ),
        in_specs=[
            pl.BlockSpec((block, columns), lambda i: (i, 0)),
            pl.BlockSpec((block, width), lambda i: (i, 0)),
            ANY,
            ANY,
            ANY,
        ],
        out_specs=(
            pl.BlockSpec((block, width), lambda i: (i, 0)),
            pl.BlockSpec((block, columns), lambda i: (i, 0)),
            ANY,
            ANY,
            ANY,
        ),
        scratch_shapes=[
            pltpu.VMEM((width, total), bf16),
            pltpu.VMEM((width, total), bf16),
            pltpu.VMEM((total, width), bf16),
            pltpu.VMEM((width, total), f32),
            pltpu.VMEM((width, total), f32),
            pltpu.VMEM((total, width), f32),
            pltpu.VMEM((block, total), bf16),
            pltpu.VMEM((block, total), bf16),
            pltpu.VMEM((block, total), bf16),
            pltpu.VMEM((2, 64, total), bf16),
            pltpu.VMEM((2, 64, width), bf16),
            DMA((3,)),
            DMA((2,)),
        ],
        compiler_params=pltpu.CompilerParams(vmem_limit_bytes=60 << 20),
        name="experts",
    )(x, c, w_gate, w_up, w_down)


def turn_kernel(cube, heads, hidden, *refs):
    chips, count = cube.chips, cube.number
    own_ref, c_hbm, down_hbm = refs[:3]
    pieces, refs = refs[3 : 3 + chips], (None,) * 4 + refs[3 + chips :]
    out_ref, moe_hbm, keep_up_hbm, other_up_hbm, keep_down_hbm, other_down_hbm = refs[4:10]
    tokens, turned, cots, w_up, w_down, acts, backs, d_gates, moe_stage, line_in = refs[10:20]
    arrived = refs[20 : 20 + count]
    load, store, own_sem, line_send, line_recv, send, recv, back_send, back_recv = refs[
        20 + count : 29 + count
    ]
    end_send, end_recv, twin_send, twin_recv, load_send, load_recv = refs[29 + count :]
    hz = lax.axis_index("head")
    rows, columns = own_ref.shape
    experts_here, width, _ = w_up.shape
    total = experts_here * hidden
    half = rows // 2
    line = heads * rows
    others = near(heads)
    masks = sorted(range(chips), key=lambda m: bin(m).count("1"))

    core = lax.axis_index("core")
    twin = {"core": 1 - core}
    slices = 2 * chips
    slice_rows = width // slices

    def up_rows(ref, chip, which):
        return ref.at[:, pl.ds((chip * 2 + which) * slice_rows, slice_rows), :]

    def w_down_parts(which):
        return w_down.reshape(experts_here, 2, hidden // 2, width).at[:, which]

    homes = [
        (pieces[mask], up_rows(w_up, flip(lax.axis_index("chip"), mask), core))
        for mask in range(chips)
    ] + [(down_hbm, w_down_parts(core))]
    loads = [
        pltpu.make_async_copy(source, target, load.at[index])
        for index, (source, target) in enumerate([(c_hbm, cots)] + homes)
    ]
    shared = [
        pltpu.make_async_remote_copy(
            src_ref=source,
            dst_ref=target,
            send_sem=load_send.at[index],
            recv_sem=load_recv.at[index],
            device_id=twin,
            device_id_type=MESH,
        )
        for index, (source, target) in enumerate(homes)
    ]
    for copy in loads:
        copy.start()
    meet(
        [cube.peer(digit) for digit in range(count)]
        + [{"head": (hz + d) % heads} for d in others]
        + [twin]
    )

    def part(side):
        return pl.ds(side * half, half)

    middle = jnp.minimum(hz, heads - 1 - hz)

    def source(rank):
        if rank == 0:
            return hz
        far = (rank + 1) // 2
        near_one = hz - far if rank % 2 else hz + far
        far_one = jnp.where(
            hz < heads - 1 - hz, hz + (rank - middle), hz - (rank - middle)
        )
        return jnp.where(rank <= 2 * middle, near_one, far_one)

    def line_copy(rank, step):
        head = source(rank)
        place = tokens.at[cube.place(0) + (head,)]
        return pltpu.make_async_remote_copy(
            src_ref=own_ref if rank == 0 else place,
            dst_ref=place,
            send_sem=line_send.at[heads if rank == 0 and step < 0 else head],
            recv_sem=line_recv.at[head],
            device_id={"head": (hz + step + heads) % heads},
            device_id_type=MESH,
        )

    def along(rank, act):
        head = source(rank)
        goes_up = hz + 1 < heads
        goes_down = hz > 0
        if rank:
            goes_up = goes_up & (head < hz)
            goes_down = goes_down & (head > hz)

        @pl.when(goes_up)
        def _():
            act(line_copy(rank, 1))

        @pl.when(goes_down)
        def _():
            act(line_copy(rank, -1))

    def plane_copy(side, mask, k, rank):
        digit = cube.gather_orders[side][k]
        later = mask | (1 << digit)
        head = source(rank)
        place = tokens.at[cube.place(mask) + (head, part(side))]
        return pltpu.make_async_remote_copy(
            src_ref=own_ref.at[part(side)] if mask == 0 and rank == 0 else place,
            dst_ref=place,
            send_sem=send.at[side, later, head],
            recv_sem=recv.at[side, later, head],
            device_id=cube.peer(digit),
            device_id_type=MESH,
        )

    def steps_after(side, mask):
        order = cube.gather_orders[side]
        last = max([k for k in range(count) if (mask >> order[k]) & 1], default=-1)
        return range(last + 1, count)

    def arrival(side, mask, rank):
        order = cube.gather_orders[side]
        k = max(k for k in range(count) if (mask >> order[k]) & 1)
        return plane_copy(side, mask & ~(1 << order[k]), k, rank)

    def receive(mask, rank):
        if mask == 0:
            if rank:
                line_copy(rank, 1).wait_recv()
            along(rank, lambda copy: copy.start())
        for side in range(2):
            if mask:
                arrival(side, mask, rank).wait_recv()
            for k in steps_after(side, mask):
                plane_copy(side, mask, k, rank).start()

    levels = [
        [m for m in masks if bin(m).count("1") == level] for level in range(cube.number + 1)
    ]
    waits = {0: [], 1: []}
    early = max(heads - 2, 0)
    for rank in range(heads):
        waits[0].append((0, rank))
        if 0 < rank <= early and count > 0:
            waits[0] += [(m, rank - 1) for m in levels[1]]
    waits[1] = [(m, rank) for rank in range(early, heads) for m in levels[1]]
    for level in range(2, count + 1):
        waits[level] = [(m, rank) for m in levels[level] for rank in range(heads)]

    def sent(mask):
        for rank in range(heads):
            if mask == 0:
                along(rank, lambda copy: copy.wait_send())
            for side in range(2):
                for k in steps_after(side, mask):
                    plane_copy(side, mask, k, rank).wait_send()

    def slot(side, k, mask):
        return subsets(cube.scatter_orders[side][k + 1 :]).index(mask)

    def back_place(side, mask, d):
        return tokens.at[cube.place(mask) + ((hz + d) % heads, part(side))]

    def back_copy(side, k, mask, d):
        order = cube.scatter_orders[side]
        where = slot(side, k, mask)
        return pltpu.make_async_remote_copy(
            src_ref=back_place(side, mask | (1 << order[k]), d),
            dst_ref=arrived[k].at[side, where, d],
            send_sem=back_send.at[side, k, where, d],
            recv_sem=back_recv.at[side, k, where, d],
            device_id=cube.peer(order[k]),
            device_id_type=MESH,
        )

    def end_copy(d):
        return pltpu.make_async_remote_copy(
            src_ref=tokens.at[cube.place(0) + ((hz + d) % heads,)],
            dst_ref=line_in.at[d - 1],
            send_sem=end_send.at[d - 1],
            recv_sem=end_recv.at[d - 1],
            device_id={"head": (hz + d) % heads},
            device_id_type=MESH,
        )

    outward = others[::-1] + [0]

    def give(mask, d):
        for side in range(2):
            first = 1 << cube.scatter_orders[side][0]
            if mask & first:
                back_copy(side, 0, mask & ~first, d).start()

    own = pltpu.make_async_copy(own_ref, tokens.at[cube.place(0) + (hz,)], own_sem)
    own.start()
    for copy in shared:
        copy.start()

    first_expert = hz * experts_here
    span = min(512, width)
    group = 2 if experts_here % 2 == 0 else 1
    tile = group * hidden

    def compute(place):
        here = pl.ds(place * line, line)
        x = tokens[place, :, :, pl.ds(0, width)].reshape(line, width)
        c = cots[here, :]
        routed = tokens[place, :, :, pl.ds(width, LANES)].reshape(line, LANES)
        turned[:, here] = x.T
        d_gates[...] = jnp.zeros_like(d_gates)

        @pl.loop(0, total // tile)
        def _(j):
            js = pl.ds(pl.multiple_of(j * tile, tile), tile)
            column = j * tile + lax.broadcasted_iota(jnp.int32, (LANES, tile), 1)
            lane = lax.broadcasted_iota(jnp.int32, (LANES, tile), 0)
            expert = first_expert + column // hidden
            high = (lane == expert).astype(f32)
            both = (high + (lane == expert + LOW).astype(f32)).astype(bf16)
            weight = jnp.dot(routed, both, preferred_element_type=f32)
            both_parts = [
                jnp.dot(x, w_up[j * group + i], preferred_element_type=f32) for i in range(group)
            ]
            gate = jnp.concatenate([value[:, :hidden] for value in both_parts], axis=1)
            up = jnp.concatenate([value[:, hidden:] for value in both_parts], axis=1)
            d_act = lax.dot_general(c, w_down[js, :], NT, preferred_element_type=f32)
            sigma = 1.0 / (1.0 + jnp.exp(-gate))
            silu = gate * sigma
            act = (silu * up).astype(bf16).astype(f32)
            d_gates[...] += lax.dot_general(
                (act * d_act).astype(bf16), high.astype(bf16), NT, preferred_element_type=f32
            )
            acts[here, js] = (act * weight).astype(bf16)
            d_act = d_act * weight
            d_up = (d_act * silu).astype(bf16)
            d_gate = (d_act * up * sigma * (1.0 + gate * (1.0 - sigma))).astype(bf16)
            for i in range(group):
                one = slice(i * hidden, (i + 1) * hidden)
                backs[j * group + i, here, pl.ds(0, hidden)] = d_gate[:, one]
                backs[j * group + i, here, pl.ds(hidden, hidden)] = d_up[:, one]

    def results(place, step):
        here = pl.ds(place * line, line)

        @pl.loop(0, width // span)
        def _(j):
            cs = pl.ds(pl.multiple_of(j * span, span), span)
            value = sum(
                lax.dot_general(
                    backs[e, here, :], w_up[e, cs, :], NT, preferred_element_type=f32
                )
                for e in range(experts_here)
            )
            tokens[place, :, :, cs] = value.astype(bf16).reshape(heads, rows, span)

        tokens[place, :, :, pl.ds(width, LANES)] = (
            d_gates[...].astype(bf16).reshape(heads, rows, LANES)
        )

    def moe_copy(place):
        return pltpu.make_async_copy(
            moe_stage, moe_hbm.at[pl.ds(place * line, line)], store.at[chips + 1]
        )

    def mixed(place, step):
        here = pl.ds(place * line, line)

        @pl.when(step > 0)
        def _():
            moe_copy(place).wait()

        @pl.loop(0, width // span)
        def _(j):
            cs = pl.ds(pl.multiple_of(j * span, span), span)
            moe_stage[:, cs] = jnp.dot(
                acts[here, :], w_down[:, cs], preferred_element_type=f32
            ).astype(bf16)

        moe_copy(place).start()

    @pl.loop(0, chips)
    def _(step):
        seen = -1
        for index, mask in enumerate(masks):
            level = bin(mask).count("1")
            if level > seen:
                seen = level

                @pl.when(step == index)
                def _():
                    for event in waits[level]:
                        receive(*event)

        place = cube.place(0)[0] * 0
        for index, mask in enumerate(masks):
            place = jnp.where(step == index, cube.place(mask)[0], place)

        @pl.when(step == 0)
        def _():
            own.wait()
            for copy in loads + shared:
                copy.wait()

        compute(place)
        for index, mask in enumerate(masks):

            @pl.when(step == index)
            def _():
                sent(mask)

        results(place, step)
        for index, mask in enumerate(masks):
            if mask and mask != chips - 1:

                @pl.when(step == index)
                def _():
                    for d in outward:
                        give(mask, d)

    def sums(side, steps, mask, d):
        value = back_place(side, mask, d)[...].astype(f32)
        for j in range(steps):
            back_copy(side, j, mask, d).wait_recv()
            value = value + arrived[j][side, slot(side, j, mask), d].astype(f32)
        return value

    def keep_up(chip):
        return pltpu.make_async_copy(up_rows(w_up, chip, core), keep_up_hbm.at[chip], store.at[chip])

    def give_up(chip):
        return pltpu.make_async_remote_copy(
            src_ref=up_rows(w_up, chip, 1 - core),
            dst_ref=other_up_hbm.at[chip],
            send_sem=twin_send.at[chip],
            recv_sem=twin_recv.at[chip],
            device_id=twin,
            device_id_type=MESH,
        )

    def keep_down():
        return pltpu.make_async_copy(w_down_parts(core), keep_down_hbm, store.at[chips])

    def give_down():
        return pltpu.make_async_remote_copy(
            src_ref=w_down_parts(1 - core),
            dst_ref=other_down_hbm,
            send_sem=twin_send.at[chips],
            recv_sem=twin_recv.at[chips],
            device_id=twin,
            device_id_type=MESH,
        )

    def up_grad(begin, end):
        @pl.loop(begin, end)
        def _(e):
            w_up[e] = jnp.dot(turned[...], backs[e], preferred_element_type=f32).astype(bf16)

        if end == experts_here:
            for chip in range(chips):
                give_up(chip).start()
                keep_up(chip).start()

    def down_grad():
        @pl.loop(0, total // tile)
        def _(j):
            js = pl.ds(pl.multiple_of(j * tile, tile), tile)
            value = jnp.dot(acts[:, js].T, cots[...], preferred_element_type=f32)
            w_down[js, :] = value.astype(bf16)

        give_down().start()
        keep_down().start()

    def mix(begin, end):
        @pl.loop(begin, end)
        def _(index):
            mixed(index, index)

    cuts = [experts_here * i // 4 for i in range(5)]
    work = [
        lambda: mix(0, chips // 2),
        lambda: mix(chips // 2, chips),
        lambda: up_grad(cuts[0], cuts[1]),
        lambda: up_grad(cuts[1], cuts[2]),
        lambda: up_grad(cuts[2], cuts[3]),
        lambda: up_grad(cuts[3], cuts[4]),
        down_grad,
    ]
    turns = heads + count
    for turn in range(turns):
        if turn < heads:
            give(chips - 1, outward[turn])
        for piece in work[len(work) * turn // turns : len(work) * (turn + 1) // turns]:
            piece()
        for k in range(1, count):
            if 0 <= turn - k < heads:
                d = outward[turn - k]
                for side in range(2):
                    order = cube.scatter_orders[side]
                    for mask in subsets(order[k + 1 :])[::-1]:
                        full = mask | (1 << order[k])
                        back_place(side, full, d)[...] = sums(side, k, full, d).astype(bf16)
                        back_copy(side, k, mask, d).start()
        if 0 <= turn - count < heads:
            d = outward[turn - count]
            for side in range(2):
                value = sums(side, count, 0, d)
                if d:
                    back_place(side, 0, d)[...] = value.astype(bf16)
                else:
                    out_ref[part(side)] = value
            if d:
                end_copy(d).start()
    for d in others:
        end_copy(d).wait_recv()
        out_ref[...] += line_in[d - 1].astype(f32)
    for d in others:
        end_copy(d).wait_send()
    for side in range(2):
        for k in range(count):
            for mask in subsets(cube.scatter_orders[side][k + 1 :]):
                for d in outward:
                    back_copy(side, k, mask, d).wait_send()
    moe_copy(0).wait()
    for chip in range(chips):
        give_up(chip).wait()
        keep_up(chip).wait()
    give_down().wait()
    keep_down().wait()


def expert_turn(payload, c, pieces, w_down, heads, number):
    rows, columns = payload.shape
    chips, width = len(pieces), c.shape[1]
    experts_here, _, double = pieces[0].shape
    hidden = double // 2
    total = experts_here * hidden
    cube = Cube(chips, False)
    count = cube.number
    tokens = chips * heads * rows
    half = rows // 2
    slots = [chips >> (k + 1) for k in range(count)]
    share = jax.ShapeDtypeStruct((chips, experts_here, width // (2 * chips), double), bf16)
    down_share = jax.ShapeDtypeStruct((experts_here, hidden // 2, width), bf16)
    return pl.pallas_call(
        functools.partial(turn_kernel, cube, heads, hidden),
        out_shape=(
            jax.ShapeDtypeStruct((rows, columns), f32),
            jax.ShapeDtypeStruct((tokens, width), bf16),
            share,
            share,
            down_share,
            down_share,
        ),
        in_specs=[WHOLE] + [ANY] * (2 + chips),
        out_specs=(WHOLE, ANY, ANY, ANY, ANY, ANY),
        scratch_shapes=[
            pltpu.VMEM((chips, heads, rows, columns), bf16),
            pltpu.VMEM((width, tokens), bf16),
            pltpu.VMEM((tokens, width), bf16),
            pltpu.VMEM((experts_here, width, double), bf16),
            pltpu.VMEM((total, width), bf16),
            pltpu.VMEM((tokens, total), bf16),
            pltpu.VMEM((experts_here, tokens, double), bf16),
            pltpu.VMEM((heads * rows, LANES), f32),
            pltpu.VMEM((heads * rows, width), bf16),
            pltpu.VMEM((heads - 1, rows, columns), bf16),
        ]
        + [pltpu.VMEM((2, s, heads, half, columns), bf16) for s in slots]
        + [
            DMA((chips + 2,)),
            DMA((chips + 2,)),
            DMA,
            DMA((heads + 1,)),
            DMA((heads,)),
            DMA((2, chips, heads)),
            DMA((2, chips, heads)),
            DMA((2, count, slots[0], heads)),
            DMA((2, count, slots[0], heads)),
            DMA((heads - 1,)),
            DMA((heads - 1,)),
            DMA((chips + 1,)),
            DMA((chips + 1,)),
            DMA((chips + 1,)),
            DMA((chips + 1,)),
        ],
        compiler_params=pltpu.CompilerParams(
            collective_id=number, has_side_effects=True, vmem_limit_bytes=63 << 20
        ),
        name="expert_turn",
    )(payload, c, w_down, *pieces)


def start_kernel(cube, heads, *refs):
    x_ref, slice_ref, unit_ref, column_ref, row_ref, x_out, dense_out, unit_out, slot_out = refs[:9]
    local, x_send, x_recv, line_send, line_recv, send, recv, unit_send, unit_recv = refs[9:]
    chips = cube.chips
    chip, core, hz = lax.axis_index("chip"), lax.axis_index("core"), lax.axis_index("head")
    others = near(heads)
    part_heads = heads // 2
    across_all = {"chip": flip(chip, chips - 1)}
    meet(
        [cube.peer(digit) for digit in range(cube.number)]
        + [{"head": (hz + d) % heads} for d in others]
        + [across_all]
    )
    unit_copy = pltpu.make_async_remote_copy(
        src_ref=unit_ref,
        dst_ref=unit_out,
        send_sem=unit_send,
        recv_sem=unit_recv,
        device_id=across_all,
        device_id_type=MESH,
    )
    middle = jnp.minimum(hz, heads - 1 - hz)

    def source(rank):
        if rank == 0:
            return hz
        far = (rank + 1) // 2
        near_one = hz - far if rank % 2 else hz + far
        far_one = jnp.where(hz < heads - 1 - hz, hz + (rank - middle), hz - (rank - middle))
        return jnp.where(rank <= 2 * middle, near_one, far_one)

    def x_copy(rank, step):
        head = source(rank)
        return pltpu.make_async_remote_copy(
            src_ref=x_ref if rank == 0 else x_out.at[head],
            dst_ref=x_out.at[head],
            send_sem=x_send.at[heads if rank == 0 and step < 0 else head],
            recv_sem=x_recv.at[head],
            device_id={"head": (hz + step + heads) % heads},
            device_id_type=MESH,
        )

    def along(rank, act):
        head = source(rank)
        goes_up = hz + 1 < heads
        goes_down = hz > 0
        if rank:
            goes_up = goes_up & (head < hz)
            goes_down = goes_down & (head > hz)

        @pl.when(goes_up)
        def _():
            act(x_copy(rank, 1))

        @pl.when(goes_down)
        def _():
            act(x_copy(rank, -1))

    def slice_copy(d):
        place = (hz + d) % heads
        return pltpu.make_async_remote_copy(
            src_ref=slice_ref.at[place],
            dst_ref=dense_out.at[chip, core, hz],
            send_sem=line_send.at[d - 1],
            recv_sem=line_recv.at[d - 1],
            device_id={"head": place},
            device_id_type=MESH,
        )

    def dense_copy(side, mask, k):
        order = cube.gather_orders[side]
        later = mask | (1 << order[k])
        place = dense_out.at[cube.place(mask) + (pl.ds(side * part_heads, part_heads),)]
        return pltpu.make_async_remote_copy(
            src_ref=place,
            dst_ref=place,
            send_sem=send.at[side, later],
            recv_sem=recv.at[side, later],
            device_id=cube.peer(order[k]),
            device_id_type=MESH,
        )

    def steps_after(side, mask):
        order = cube.gather_orders[side]
        last = max([k for k in range(cube.number) if (mask >> order[k]) & 1], default=-1)
        return range(last + 1, cube.number)

    def dense_turn(mask):
        for side in range(2):
            if mask:
                order = cube.gather_orders[side]
                k = max(k for k in range(cube.number) if (mask >> order[k]) & 1)
                dense_copy(side, mask & ~(1 << order[k]), k).wait_recv()
            for k in steps_after(side, mask):
                dense_copy(side, mask, k).start()

    locals_ = [
        pltpu.make_async_copy(slice_ref.at[hz], dense_out.at[chip, core, hz], local.at[0]),
        pltpu.make_async_copy(x_ref, x_out.at[hz], local.at[1]),
    ]
    def count_slots():
        row = row_ref[...]
        first = row // column_ref.shape[0] * column_ref.shape[0]
        total = jnp.zeros(row.shape, jnp.int32)
        step = LANES
        for begin in range(0, column_ref.shape[0], step):
            column = column_ref[pl.ds(begin, step), :]
            earlier = ((column < row) & (column >= first)).astype(jnp.int32)
            total = total + jnp.sum(earlier, axis=0, keepdims=True)
        slot_out[...] = total

    for d in others:
        slice_copy(d).start()
    for copy in locals_:
        copy.start()
    along(0, lambda copy: copy.start())
    locals_[0].wait()
    for d in others:
        slice_copy(d).wait_recv()
    dense_turn(0)
    masks = sorted(range(1, 2 * chips), key=lambda m: bin(m).count("1"))
    shares = [masks[len(masks) * i // heads : len(masks) * (i + 1) // heads] for i in range(heads)]
    for mask in shares[0]:
        dense_turn(mask)
    for rank in range(1, heads):
        x_copy(rank, 1).wait_recv()
        along(rank, lambda copy: copy.start())
        for mask in shares[rank]:
            dense_turn(mask)
        if rank == 1:
            unit_copy.start()
            count_slots()
    unit_copy.wait()
    locals_[1].wait()
    for rank in range(heads):
        along(rank, lambda copy: copy.wait_send())
    for d in others:
        slice_copy(d).wait_send()
    for mask in [0] + masks:
        for side in range(2):
            for k in steps_after(side, mask):
                dense_copy(side, mask, k).wait_send()


def start(x, slices, unit, keys, chips, heads, number):
    cube = Cube(chips, True)
    return pl.pallas_call(
        functools.partial(start_kernel, cube, heads),
        out_shape=(
            jax.ShapeDtypeStruct((heads,) + x.shape, bf16),
            jax.ShapeDtypeStruct((chips, 2) + slices.shape, bf16),
            jax.ShapeDtypeStruct(unit.shape, bf16),
            jax.ShapeDtypeStruct((1, keys.size), jnp.int32),
        ),
        in_specs=[ANY] * 3 + [WHOLE] * 2,
        out_specs=(ANY,) * 3 + (WHOLE,),
        scratch_shapes=[
            DMA((2,)),
            DMA((heads + 1,)),
            DMA((heads,)),
            DMA((heads - 1,)),
            DMA((heads - 1,)),
            DMA((2, 2 * chips)),
            DMA((2, 2 * chips)),
            DMA,
            DMA,
        ],
        compiler_params=pltpu.CompilerParams(collective_id=number, has_side_effects=True),
        name="start",
    )(x, slices, unit, keys[:, None], keys[None, :])


def end_kernel(cube, heads, first_ref, in_ref, first_out, out_ref, *refs):
    count = cube.number
    arrived = refs[:count]
    parts = refs[count : 2 * count]
    local, first_send, first_recv, line_send, line_recv, send, recv = refs[2 * count :]
    hz = lax.axis_index("head")
    others = near(heads)[::-1]
    half = in_ref.shape[-2] // 2
    rows = in_ref.shape[-2] // heads
    meet([cube.peer(digit) for digit in range(count)] + [{"head": (hz + d) % heads} for d in others])
    own = pltpu.make_async_copy(first_ref.at[hz], first_out.at[hz], local)
    own.start()
    copies = {}

    def slot(side, k, mask):
        return subsets(cube.scatter_orders[side][k + 1 :]).index(mask)

    def mine(side, mask):
        return in_ref.at[cube.place(mask) + (pl.ds(side * half, half),)]

    def total(side, steps, mask):
        value = mine(side, mask)[...].astype(f32)
        for j in range(steps):
            copies[(side, j, mask)].wait_recv()
            value = value + arrived[j][side, slot(side, j, mask)].astype(f32)
        return value.astype(bf16)

    def first_copy(d):
        place = (hz + d) % heads
        return pltpu.make_async_remote_copy(
            src_ref=first_ref.at[place],
            dst_ref=first_out.at[hz],
            send_sem=first_send.at[d - 1],
            recv_sem=first_recv.at[d - 1],
            device_id={"head": place},
            device_id_type=MESH,
        )

    for k in range(count):
        for side in range(2):
            order = cube.scatter_orders[side]
            for mask in subsets(order[k + 1 :])[::-1]:
                full = mask | (1 << order[k])
                where = slot(side, k, mask)
                if k == 0:
                    piece = mine(side, full)
                else:
                    piece = parts[k - 1].at[side, where]
                    piece[...] = total(side, k, full)
                copies[(side, k, mask)] = pltpu.make_async_remote_copy(
                    src_ref=piece,
                    dst_ref=arrived[k].at[side, where],
                    send_sem=send.at[side, k, where],
                    recv_sem=recv.at[side, k, where],
                    device_id=cube.peer(order[k]),
                    device_id_type=MESH,
                )
                copies[(side, k, mask)].start()
        if k == 0:
            for d in others:
                first_copy(d).start()
    done = parts[count - 1]
    for side in range(2):
        done[0, pl.ds(side * half, half)] = total(side, count, 0)

    def line_copy(d):
        place = (hz + d) % heads
        return pltpu.make_async_remote_copy(
            src_ref=done.at[0, pl.ds(pl.multiple_of(place * rows, 16), rows)],
            dst_ref=out_ref.at[hz],
            send_sem=line_send.at[d - 1],
            recv_sem=line_recv.at[d - 1],
            device_id={"head": place},
            device_id_type=MESH,
        )

    for d in others:
        line_copy(d).start()
    out_ref[hz] = done[0, pl.ds(pl.multiple_of(hz * rows, 16), rows)]
    for copy in copies.values():
        copy.wait_send()
    own.wait()
    for d in others:
        line_copy(d).wait()
    for d in others:
        first_copy(d).wait()


def end(first, sums, chips, heads, number):
    rows, columns = sums.shape[-2:]
    cube = Cube(chips, True)
    count = cube.number
    half = rows // 2
    slots = [(1 << count) >> (k + 1) for k in range(count)]
    return pl.pallas_call(
        functools.partial(end_kernel, cube, heads),
        out_shape=(
            jax.ShapeDtypeStruct(first.shape, bf16),
            jax.ShapeDtypeStruct((heads, rows // heads, columns), bf16),
        ),
        in_specs=[ANY, WHOLE],
        out_specs=(ANY, WHOLE),
        scratch_shapes=[pltpu.VMEM((2, s, half, columns), bf16) for s in slots]
        + [pltpu.VMEM((2, s, half, columns), bf16) for s in slots[1:]]
        + [
            pltpu.VMEM((1, rows, columns), bf16),
            DMA,
            DMA((heads - 1,)),
            DMA((heads - 1,)),
            DMA((heads - 1,)),
            DMA((heads - 1,)),
            DMA((2, count, slots[0])),
            DMA((2, count, slots[0])),
        ],
        compiler_params=pltpu.CompilerParams(
            collective_id=number, has_side_effects=True, vmem_limit_bytes=40 << 20
        ),
        name="end",
    )(first, sums)


def place_kernel(chips, hidden, *refs):
    pieces, out_ref = refs[:chips], refs[chips]
    chip = lax.axis_index("chip")
    units = out_ref.shape[2] // 2
    for mask in range(chips):
        for part in range(2):
            begin = pl.multiple_of(part * units + flip(chip, mask) * hidden, hidden)
            out_ref[:, :, pl.ds(begin, hidden)] = pieces[mask][
                :, :, pl.ds(part * hidden, hidden)
            ].astype(f32)


def place_units(pieces, hidden):
    chips = len(pieces)
    experts_here, rows, double = pieces[0].shape
    return pl.pallas_call(
        functools.partial(place_kernel, chips, hidden),
        grid=(experts_here,),
        out_shape=jax.ShapeDtypeStruct((experts_here, rows, chips * double), f32),
        in_specs=[pl.BlockSpec((1, rows, double), lambda e: (e, 0, 0))] * chips,
        out_specs=pl.BlockSpec((1, rows, chips * double), lambda e: (e, 0, 0)),
        name="place_units",
    )(*pieces)


def across(value, chips, mask):
    if mask == 0:
        return value
    return lax.ppermute(value, "chip", [(i, i ^ mask) for i in range(chips)])


class LineGather:
    def __init__(self, cube, heads, own, out, sems):
        self.cube, self.heads, self.own, self.out = cube, heads, own, out
        self.local, self.line_send, self.line_recv, self.send, self.recv = sems
        self.hz = lax.axis_index("head")
        self.middle = jnp.minimum(self.hz, heads - 1 - self.hz)
        self.rows = own.shape[0]

    @staticmethod
    def scratch(cube, heads):
        return [
            DMA,
            DMA((heads + 1,)),
            DMA((heads,)),
            DMA((2, 1 << cube.number, heads)),
            DMA((2, 1 << cube.number, heads)),
        ]

    def source(self, rank):
        hz, heads, middle = self.hz, self.heads, self.middle
        if rank == 0:
            return hz
        far = (rank + 1) // 2
        near_one = hz - far if rank % 2 else hz + far
        far_one = jnp.where(hz < heads - 1 - hz, hz + (rank - middle), hz - (rank - middle))
        return jnp.where(rank <= 2 * middle, near_one, far_one)

    def line_copy(self, rank, step):
        head = self.source(rank)
        place = self.out.at[self.cube.place(0) + (head,)]
        return pltpu.make_async_remote_copy(
            src_ref=self.own if rank == 0 else place,
            dst_ref=place,
            send_sem=self.line_send.at[self.heads if rank == 0 and step < 0 else head],
            recv_sem=self.line_recv.at[head],
            device_id={"head": (self.hz + step + self.heads) % self.heads},
            device_id_type=MESH,
        )

    def along(self, rank, act):
        head = self.source(rank)
        goes_up = self.hz + 1 < self.heads
        goes_down = self.hz > 0
        if rank:
            goes_up = goes_up & (head < self.hz)
            goes_down = goes_down & (head > self.hz)

        @pl.when(goes_up)
        def _():
            act(self.line_copy(rank, 1))

        @pl.when(goes_down)
        def _():
            act(self.line_copy(rank, -1))

    def plane_copy(self, side, mask, k, rank):
        digit = self.cube.gather_orders[side][k]
        later = mask | (1 << digit)
        head = self.source(rank)
        part = part_of(self.rows, side)
        place = self.out.at[self.cube.place(mask) + (head, part)]
        return pltpu.make_async_remote_copy(
            src_ref=self.own.at[part] if mask == 0 and rank == 0 else place,
            dst_ref=place,
            send_sem=self.send.at[side, later, head],
            recv_sem=self.recv.at[side, later, head],
            device_id=self.cube.peer(digit),
            device_id_type=MESH,
        )

    def steps_after(self, side, mask):
        order = self.cube.gather_orders[side]
        last = max([k for k in range(self.cube.number) if (mask >> order[k]) & 1], default=-1)
        return range(last + 1, self.cube.number)

    def begin(self):
        self.own_copy = pltpu.make_async_copy(
            self.own, self.out.at[self.cube.place(0) + (self.hz,)], self.local
        )
        self.own_copy.start()

    def receive(self, mask, rank):
        if mask == 0:
            if rank:
                self.line_copy(rank, 1).wait_recv()
            self.along(rank, lambda copy: copy.start())
        for side in range(2):
            if mask:
                order = self.cube.gather_orders[side]
                k = max(k for k in range(self.cube.number) if (mask >> order[k]) & 1)
                self.plane_copy(side, mask & ~(1 << order[k]), k, rank).wait_recv()
            for k in self.steps_after(side, mask):
                self.plane_copy(side, mask, k, rank).start()

    def events(self):
        masks = sorted(range(1 << self.cube.number), key=lambda m: bin(m).count("1"))
        return [(mask, rank) for mask in masks for rank in range(self.heads)]

    def finish(self):
        self.own_copy.wait()
        for mask, rank in self.events():
            if mask == 0:
                self.along(rank, lambda copy: copy.wait_send())
            for side in range(2):
                for k in self.steps_after(side, mask):
                    self.plane_copy(side, mask, k, rank).wait_send()


class LineSums:
    def __init__(self, cube, heads, blocks, out, refs):
        self.cube, self.heads, self.blocks, self.out = cube, heads, blocks, out
        count = cube.number
        self.arrived, self.parts = refs[:count], refs[count : 2 * count - 1]
        self.line_out, self.line_in, self.send, self.recv, self.end_send, self.end_recv = refs[
            2 * count - 1 :
        ]
        self.hz = lax.axis_index("head")
        self.rows = blocks.shape[-2]
        self.outward = near(heads)[::-1] + [0]
        self.turns = heads + count

    @staticmethod
    def scratch(cube, heads, rows, columns):
        count = cube.number
        slots = [(1 << count) >> (k + 1) for k in range(count)]
        half = cut_rows(rows)
        return (
            [pltpu.VMEM((2, s, heads, half, columns), bf16) for s in slots]
            + [pltpu.VMEM((2, s, heads, half, columns), bf16) for s in slots[1:]]
            + [
                pltpu.VMEM((heads - 1, rows, columns), bf16),
                pltpu.VMEM((heads - 1, rows, columns), bf16),
                DMA((2, count, slots[0], heads)),
                DMA((2, count, slots[0], heads)),
                DMA((heads - 1,)),
                DMA((heads - 1,)),
            ]
        )

    def slot(self, side, k, mask):
        return subsets(self.cube.scatter_orders[side][k + 1 :]).index(mask)

    def mine(self, side, mask, d):
        place = self.cube.place(mask) + ((self.hz + d) % self.heads,)
        return self.blocks.at[place + (part_of(self.rows, side),)]

    def there(self, ref, side, where, d):
        return ref.at[side, where, d, pl.ds(0, part_of(self.rows, side).size)]

    def copy_of(self, side, k, mask, d):
        order = self.cube.scatter_orders[side]
        where = self.slot(side, k, mask)
        if k == 0:
            piece = self.mine(side, mask | (1 << order[0]), d)
        else:
            piece = self.there(self.parts[k - 1], side, where, d)
        return pltpu.make_async_remote_copy(
            src_ref=piece,
            dst_ref=self.there(self.arrived[k], side, where, d),
            send_sem=self.send.at[side, k, where, d],
            recv_sem=self.recv.at[side, k, where, d],
            device_id=self.cube.peer(order[k]),
            device_id_type=MESH,
        )

    def end_copy(self, d):
        return pltpu.make_async_remote_copy(
            src_ref=self.line_out.at[d - 1],
            dst_ref=self.line_in.at[d - 1],
            send_sem=self.end_send.at[d - 1],
            recv_sem=self.end_recv.at[d - 1],
            device_id={"head": (self.hz + d) % self.heads},
            device_id_type=MESH,
        )

    def sums(self, side, steps, mask, d):
        value = self.mine(side, mask, d)[...].astype(f32)
        for j in range(steps):
            self.copy_of(side, j, mask, d).wait_recv()
            value = value + self.there(self.arrived[j], side, self.slot(side, j, mask), d)[
                ...
            ].astype(f32)
        return value

    def turn(self, turn):
        count = self.cube.number
        if turn < self.heads:
            for side in range(2):
                for mask in subsets(self.cube.scatter_orders[side][1:])[::-1]:
                    self.copy_of(side, 0, mask, self.outward[turn]).start()
        for k in range(1, count):
            if 0 <= turn - k < self.heads:
                d = self.outward[turn - k]
                for side in range(2):
                    order = self.cube.scatter_orders[side]
                    for mask in subsets(order[k + 1 :])[::-1]:
                        value = self.sums(side, k, mask | (1 << order[k]), d)
                        place = self.there(self.parts[k - 1], side, self.slot(side, k, mask), d)
                        place[...] = value.astype(bf16)
                        self.copy_of(side, k, mask, d).start()
        if 0 <= turn - count < self.heads:
            d = self.outward[turn - count]
            for side in range(2):
                value = self.sums(side, count, 0, d)
                part = part_of(self.rows, side)
                if d:
                    self.line_out[d - 1, part] = value.astype(bf16)
                else:
                    self.out[part] = value
            if d:
                self.end_copy(d).start()

    def finish(self):
        others = near(self.heads)
        for d in others:
            self.end_copy(d).wait_recv()
            self.out[...] += self.line_in[d - 1].astype(f32)
        for d in others:
            self.end_copy(d).wait_send()
        for side in range(2):
            for k in range(self.cube.number):
                for mask in subsets(self.cube.scatter_orders[side][k + 1 :]):
                    for d in self.outward:
                        self.copy_of(side, k, mask, d).wait_send()


TN = (((0,), (0,)), ((), ()))


def allowed(key_segments, query_segments, block, rows, seq):
    columns = query_segments.shape[1]
    key_place = block * rows + lax.broadcasted_iota(jnp.int32, (rows, columns), 0)
    query_place = seq * rows + lax.broadcasted_iota(jnp.int32, (rows, columns), 1) % rows
    return (key_segments == query_segments) & (key_place <= query_place)


def attend_kernel(cube, heads, group, beside, *refs):
    q_ref, kv_ref, key_seg, query_seg = refs[:4]
    near_refs, refs = refs[4 : 4 + len(beside)], refs[4 + len(beside) :]
    lines_ref, kv_out, out_turned, lse_ref = refs[:4]
    far_refs, refs = refs[4 : 4 + len(beside)], refs[4 + len(beside) :]
    stage, top, total, acc, send, recv, line_send, line_recv = refs[:8]
    chip, core, hz = lax.axis_index("chip"), lax.axis_index("core"), lax.axis_index("head")
    seq = chip * 2 + core
    others = near(heads)[::-1]
    batch, rows, columns = kv_ref.shape
    kv_heads = columns // (2 * HEAD_WIDTH)
    part = rows // 2
    meet([cube.peer(digit) for digit in range(cube.number)] + [{"head": (hz + d) % heads} for d in others])
    kv_out[chip, core] = kv_ref[...]
    gathers = [
        LineGather(Cube(cube.chips, with_core), heads, *pair, refs[8 + 5 * i : 13 + 5 * i])
        for i, (with_core, pair) in enumerate(zip(beside, zip(near_refs, far_refs)))
    ]
    events = sorted(
        (
            ((index + 0.5) / len(one.events()), one, event)
            for one in gathers
            for index, event in enumerate(one.events())
        ),
        key=lambda item: item[0],
    )

    def copy_of(side, mask, k):
        order = cube.gather_orders[side]
        later = mask | (1 << order[k])
        place = cube.place(mask) + (slice(None), pl.ds(side * part, part))
        return pltpu.make_async_remote_copy(
            src_ref=kv_ref.at[:, pl.ds(side * part, part)] if mask == 0 else kv_out.at[place],
            dst_ref=kv_out.at[place],
            send_sem=send.at[side, later],
            recv_sem=recv.at[side, later],
            device_id=cube.peer(order[k]),
            device_id_type=MESH,
        )

    copies = []

    def forward(mask):
        for side in range(2):
            order = cube.gather_orders[side]
            last = max([k for k in range(cube.number) if (mask >> order[k]) & 1], default=-1)
            if mask:
                copy_of(side, mask & ~(1 << order[last]), last).wait_recv()
            for k in range(last + 1, cube.number):
                copy_of(side, mask, k).start()
                copies.append((side, mask, k))

    forward(0)
    top[...] = jnp.full_like(top, negative)
    total[...] = jnp.zeros_like(total)
    acc[...] = jnp.zeros_like(acc)

    def block_step(block):
        place = (block // 2, block % 2)
        for b in range(batch):
            mask = allowed(
                key_seg[b, pl.ds(pl.multiple_of(block * rows, rows), rows), :],
                query_seg[b],
                block,
                rows,
                seq,
            )
            for j in range(kv_heads):
                pair = b * kv_heads + j
                begin = j * 2 * HEAD_WIDTH
                keys = kv_out[place + (b, slice(None), pl.ds(begin, HEAD_WIDTH))]
                values = kv_out[place + (b, slice(None), pl.ds(begin + HEAD_WIDTH, HEAD_WIDTH))]
                scores = lax.dot_general(keys, q_ref[pair], NT, preferred_element_type=f32)
                scores = jnp.where(mask, scores, negative)
                new = jnp.maximum(top[pair], jnp.max(scores, axis=0, keepdims=True))
                weights = jnp.exp(scores - new)
                shrink = jnp.exp(top[pair] - new)
                top[pair] = new
                total[pair] = total[pair] * shrink + jnp.sum(weights, axis=0, keepdims=True)
                acc[pair] = acc[pair] * shrink + lax.dot_general(
                    values, weights.astype(bf16), TN, preferred_element_type=f32
                )

    block_step(seq)
    for one in gathers:
        one.begin()
    for _, one, event in events[: len(gathers)]:
        one.receive(*event)
    for mask in sorted(range(1, 1 << cube.number), key=lambda m: bin(m).count("1")):
        forward(mask)
    turns = 2 * cube.chips
    skip = len(gathers)
    rest = len(events) - skip
    if beside:
        for turn in range(turns):
            for _, one, event in events[
                skip + rest * turn // turns : skip + rest * (turn + 1) // turns
            ]:
                one.receive(*event)

            @pl.when(turn < seq)
            def _():
                block_step(turn)

    else:

        @pl.loop(0, seq)
        def _(block):
            block_step(block)

    spot = rows // heads
    for b in range(batch):
        for j in range(kv_heads):
            pair = b * kv_heads + j
            value = acc[pair] / total[pair]
            out_turned[pair] = value
            lse_ref[pair] = top[pair] + jnp.log(total[pair])
            value = value.T.astype(bf16)
            for g in range(group):
                for head in range(heads):
                    begin = (j * group + g) * HEAD_WIDTH
                    stage[head, pl.ds(b * spot, spot), pl.ds(begin, HEAD_WIDTH)] = value[
                        g * rows + head * spot : g * rows + (head + 1) * spot
                    ]

    def line_copy(d):
        return pltpu.make_async_remote_copy(
            src_ref=stage.at[(hz + d) % heads],
            dst_ref=lines_ref.at[hz],
            send_sem=line_send.at[d - 1],
            recv_sem=line_recv.at[d - 1],
            device_id={"head": (hz + d) % heads},
            device_id_type=MESH,
        )

    for d in others:
        line_copy(d).start()
    lines_ref[hz] = stage[hz]
    for side, mask, k in copies:
        copy_of(side, mask, k).wait_send()
    for d in others:
        line_copy(d).wait()
    for one in gathers:
        one.finish()


def attend(queries, keys_values, key_seg, query_seg, beside, chips, heads, group, number):
    batch, rows, columns = keys_values.shape
    pairs, wide, depth = queries.shape
    cube = Cube(chips, True)
    group_columns = group * columns // 2
    tokens = batch * rows // heads
    return pl.pallas_call(
        functools.partial(attend_kernel, cube, heads, group, [core for _, core in beside]),
        out_shape=(
            jax.ShapeDtypeStruct((heads, tokens, group_columns), bf16),
            jax.ShapeDtypeStruct((chips, 2, batch, rows, columns), bf16),
            jax.ShapeDtypeStruct((pairs, depth, wide), f32),
            jax.ShapeDtypeStruct((pairs, 1, wide), f32),
        )
        + tuple(
            jax.ShapeDtypeStruct((chips,) + (2,) * with_core + (heads,) + value.shape, bf16)
            for value, with_core in beside
        ),
        in_specs=[WHOLE] * 4 + [ANY] * len(beside),
        out_specs=(WHOLE,) * 4 + (ANY,) * len(beside),
        scratch_shapes=[
            pltpu.VMEM((heads, tokens, group_columns), bf16),
            pltpu.VMEM((pairs, 1, wide), f32),
            pltpu.VMEM((pairs, 1, wide), f32),
            pltpu.VMEM((pairs, depth, wide), f32),
            DMA((2, 2 * chips)),
            DMA((2, 2 * chips)),
            DMA((heads - 1,)),
            DMA((heads - 1,)),
        ]
        + [item for _, core in beside for item in LineGather.scratch(Cube(chips, core), heads)],
        compiler_params=pltpu.CompilerParams(
            collective_id=number, has_side_effects=True, vmem_limit_bytes=50 << 20
        ),
        name="attend",
    )(queries, keys_values, key_seg, query_seg, *[value for value, _ in beside])


def attend_back_kernel(cube, heads, group, beside, *refs):
    q_ref, kv_ref, key_seg, query_seg, out_turned, lse_ref, dh_ref = refs[:7]
    near_refs, refs = refs[7 : 7 + len(beside)], refs[7 + len(beside) :]
    dq_ref, dkv_ref = refs[:2]
    far_refs, refs = refs[2 : 2 + len(beside)], (None,) * 9 + refs[2 + len(beside) :]
    count = cube.number
    landed, d_out, delta, dq_turned, grads = refs[9:14]
    arrived, parts = refs[14 : 14 + count], refs[14 + count : 13 + 2 * count]
    send, recv, line_send, line_recv = refs[13 + 2 * count : 17 + 2 * count]
    turns = 2 * cube.chips
    rest = refs[17 + 2 * count :]
    sums_beside = []
    for with_core, source, target in zip(beside, near_refs, far_refs):
        own_cube = Cube(cube.chips, with_core)
        size = 2 * own_cube.number + 5
        sums_beside.append(LineSums(own_cube, heads, source, target, rest[:size]))
        rest = rest[size:]
    chip, core, hz = lax.axis_index("chip"), lax.axis_index("core"), lax.axis_index("head")
    seq = chip * 2 + core
    others = near(heads)[::-1]
    batch, rows, columns = kv_ref.shape[2:]
    kv_heads = columns // (2 * HEAD_WIDTH)
    spot = rows // heads
    half = grads.shape[2] // 2
    meet([cube.peer(digit) for digit in range(count)] + [{"head": (hz + d) % heads} for d in others])

    def line_copy(d):
        return pltpu.make_async_remote_copy(
            src_ref=dh_ref.at[(hz + d) % heads],
            dst_ref=landed.at[hz],
            send_sem=line_send.at[d - 1],
            recv_sem=line_recv.at[d - 1],
            device_id={"head": (hz + d) % heads},
            device_id_type=MESH,
        )

    for d in others:
        line_copy(d).start()
    for one in sums_beside:
        one.turn(0)
    landed[hz] = dh_ref[hz]
    grads[...] = jnp.zeros_like(grads)
    dq_turned[...] = jnp.zeros_like(dq_turned)
    for d in others:
        line_copy(d).wait()
    for b in range(batch):
        for j in range(kv_heads):
            pair = b * kv_heads + j
            for g in range(group):
                for head in range(heads):
                    begin = (j * group + g) * HEAD_WIDTH
                    d_out[pair, pl.ds(g * rows + head * spot, spot), :] = landed[
                        head, pl.ds(b * spot, spot), pl.ds(begin, HEAD_WIDTH)
                    ]
            delta[pair] = jnp.sum(
                d_out[pair].astype(f32).T * out_turned[pair], axis=0, keepdims=True
            )

    def block_step(block):
        place = (block // 2, block % 2)
        for b in range(batch):
            mask = allowed(
                key_seg[b, pl.ds(pl.multiple_of(block * rows, rows), rows), :],
                query_seg[b],
                block,
                rows,
                seq,
            )
            for j in range(kv_heads):
                pair = b * kv_heads + j
                begin = j * 2 * HEAD_WIDTH
                keys = kv_ref[place + (b, slice(None), pl.ds(begin, HEAD_WIDTH))]
                values = kv_ref[place + (b, slice(None), pl.ds(begin + HEAD_WIDTH, HEAD_WIDTH))]
                scores = lax.dot_general(keys, q_ref[pair], NT, preferred_element_type=f32)
                probs = jnp.exp(jnp.where(mask, scores, negative) - lse_ref[pair])
                d_probs = lax.dot_general(values, d_out[pair], NT, preferred_element_type=f32)
                d_scores = (probs * (d_probs - delta[pair])).astype(bf16)
                dq_turned[pair] += lax.dot_general(
                    keys, d_scores, TN, preferred_element_type=f32
                )
                d_keys = jnp.dot(d_scores, q_ref[pair], preferred_element_type=f32)
                d_values = jnp.dot(probs.astype(bf16), d_out[pair], preferred_element_type=f32)
                grads[place + (pl.ds(b * rows, rows), pl.ds(begin, 2 * HEAD_WIDTH))] = (
                    jnp.concatenate([d_keys, d_values], axis=1).astype(bf16)
                )

    done = 1
    if beside:
        for turn in range(turns):

            @pl.when(turn <= seq)
            def _():
                block_step(turn)

            if turn % 3 == 2:
                for one in sums_beside:
                    one.turn(done)
                done += 1

    else:

        @pl.loop(0, seq + 1)
        def _(block):
            block_step(block)

    def slot(side, k, mask):
        return subsets(cube.scatter_orders[side][k + 1 :]).index(mask)

    def mine(side, mask):
        return grads.at[cube.place(mask) + (pl.ds(side * half, half),)]

    copies = {}

    def sums(side, steps, mask):
        value = mine(side, mask)[...].astype(f32)
        for j in range(steps):
            copies[(side, j, mask)].wait_recv()
            value = value + arrived[j][side, slot(side, j, mask)].astype(f32)
        return value

    for k in range(count):
        for side in range(2):
            order = cube.scatter_orders[side]
            for mask in subsets(order[k + 1 :])[::-1]:
                full = mask | (1 << order[k])
                where = slot(side, k, mask)
                if k == 0:
                    piece = mine(side, full)
                else:
                    piece = parts[k - 1].at[side, where]
                    piece[...] = sums(side, k, full).astype(bf16)
                copies[(side, k, mask)] = pltpu.make_async_remote_copy(
                    src_ref=piece,
                    dst_ref=arrived[k].at[side, where],
                    send_sem=send.at[side, k, where],
                    recv_sem=recv.at[side, k, where],
                    device_id=cube.peer(order[k]),
                    device_id_type=MESH,
                )
                copies[(side, k, mask)].start()
        for one in sums_beside:
            if done < one.turns:
                one.turn(done)
        done += 1
    scale = HEAD_WIDTH ** (-0.5)
    for pair in range(batch * kv_heads):
        dq_ref[pair] = (dq_turned[pair] * scale).T.astype(bf16)
    for side in range(2):
        dkv_ref[pl.ds(side * half, half)] = sums(side, count, 0)
    for turn in range(done, max([one.turns for one in sums_beside], default=0)):
        for one in sums_beside:
            if turn < one.turns:
                one.turn(turn)
    for copy in copies.values():
        copy.wait_send()
    for one in sums_beside:
        one.finish()


def attend_back(
    queries, kv_all, key_seg, query_seg, out_turned, lse, d_heads, beside, heads, group, number
):
    chips, _, batch, rows, columns = kv_all.shape
    pairs, wide, depth = queries.shape
    cube = Cube(chips, True)
    count = cube.number
    half = batch * rows // 2
    slots = [(1 << count) >> (k + 1) for k in range(count)]
    return pl.pallas_call(
        functools.partial(attend_back_kernel, cube, heads, group, [core for _, core in beside]),
        out_shape=(
            jax.ShapeDtypeStruct((pairs, wide, depth), bf16),
            jax.ShapeDtypeStruct((batch * rows, columns), f32),
        )
        + tuple(jax.ShapeDtypeStruct(value.shape[-2:], f32) for value, _ in beside),
        in_specs=[WHOLE] * (7 + len(beside)),
        out_specs=(WHOLE,) * (2 + len(beside)),
        scratch_shapes=[
            pltpu.VMEM(d_heads.shape, bf16),
            pltpu.VMEM((pairs, wide, depth), bf16),
            pltpu.VMEM((pairs, 1, wide), f32),
            pltpu.VMEM((pairs, depth, wide), f32),
            pltpu.VMEM((chips, 2, batch * rows, columns), bf16),
        ]
        + [pltpu.VMEM((2, s, half, columns), bf16) for s in slots]
        + [pltpu.VMEM((2, s, half, columns), bf16) for s in slots[1:]]
        + [
            DMA((2, count, slots[0])),
            DMA((2, count, slots[0])),
            DMA((heads - 1,)),
            DMA((heads - 1,)),
        ]
        + [
            item
            for value, core in beside
            for item in LineSums.scratch(Cube(chips, core), *value.shape[-3:])
        ],
        compiler_params=pltpu.CompilerParams(
            collective_id=number, has_side_effects=True, vmem_limit_bytes=56 << 20
        ),
        name="attend_back",
    )(queries, kv_all, key_seg, query_seg, out_turned, lse, d_heads, *[v for v, _ in beside])


def sibling(value):
    return lax.ppermute(value, "core", [(0, 1), (1, 0)])


def per_device(
    layer_input,
    segments,
    routes,
    pair_rank,
    query_key_value_weight,
    output_weight,
    router_weight,
    norm_attn,
    norm_ffn,
    w_gate_up,
    w_down,
    cotangent,
):
    chips = lax.axis_size("chip")
    head_number = lax.axis_size("head")
    sequence_batch, token_rows, width = layer_input.shape
    length = segments.shape[1]
    blk = token_rows * head_number
    query_group = QUERY_HEADS // KEY_VALUE_HEADS
    key_value_location = KEY_VALUE_HEADS // head_number
    loc_experts, slice_rows = w_gate_up.shape[:2]
    top = routes.shape[2]
    tokens_present = sequence_batch * token_rows
    pairs = tokens_present * top
    line_tokens = tokens_present * head_number
    scale = HEAD_WIDTH ** (-0.5)
    hidden = FF // chips
    loc_columns = key_value_location * (query_group + 2) * HEAD_WIDTH
    chip = lax.axis_index("chip")
    core = lax.axis_index("core")
    head = lax.axis_index("head")
    seq_index = chip * 2 + core
    dense_rows = query_key_value_weight.shape[0]

    extras = jnp.concatenate([router_weight, norm_attn[:, None], norm_ffn[:, None]], axis=1)
    extras = jnp.pad(extras, ((0, 0), (0, LANES - extras.shape[1])))
    slices = query_key_value_weight.reshape(dense_rows, head_number, loc_columns).transpose(1, 0, 2)
    slices = jnp.concatenate(
        [slices, jnp.broadcast_to(extras, (head_number,) + extras.shape)], axis=2
    )
    group_tokens = chips * head_number * tokens_present
    columns = width + LANES
    fused = hidden % LANES == 0 and group_tokens <= 2048
    own_tokens = layer_input.reshape(tokens_present, width)
    cots = cotangent.reshape(tokens_present, width)
    if fused:

        def unit_of(weights, mask):
            begins = [part * FF + (chip ^ mask) * hidden for part in range(2)]
            cut = [lax.dynamic_slice_in_dim(weights, begin, hidden, 2) for begin in begins]
            return jnp.concatenate(cut, axis=2)

        keys = (routes * pairs + pair_rank).reshape(pairs)
        x_line, dense, last_unit, slot = start(
            own_tokens, slices, unit_of(w_gate_up, chips - 1), keys, chips, head_number, 1
        )
        x_line, w_gate_up = lax.optimization_barrier((x_line, w_gate_up))
        units = [across(unit_of(w_gate_up, mask), chips, mask) for mask in range(chips - 1)]
        units.append(last_unit)
        dense = dense.reshape(width, loc_columns + LANES)
    else:
        parts = w_gate_up.reshape(loc_experts, slice_rows, 2, chips, hidden).transpose(3, 2, 1, 0, 4)
        parts = parts.reshape(chips, 2, slice_rows, loc_experts * hidden)
        piled = jnp.zeros((chips, 2, 2, slice_rows, loc_experts * hidden), bf16)
        for mask in range(chips):
            piece = lax.dynamic_index_in_dim(parts, chip ^ mask, 0, keepdims=False)
            piece = across(piece, chips, mask)
            other = sibling(piece)
            piled = lax.dynamic_update_slice(piled, piece[None, None], (chip ^ mask, core, 0, 0, 0))
            piled = lax.dynamic_update_slice(piled, other[None, None], (chip ^ mask, 1 - core, 0, 0, 0))
        piled = piled.transpose(2, 0, 1, 3, 4).reshape(2, width, loc_experts * hidden)
        expert_gate, expert_up = piled[0], piled[1]
        down_other = sibling(w_down)
        expert_down = (
            jnp.where(
                core == 0,
                jnp.concatenate([w_down, down_other], axis=1),
                jnp.concatenate([down_other, w_down], axis=1),
            )
        ).reshape(loc_experts * hidden, width)

        lined = line_exchange(slices, head_number, 1)
        dense = gather(
            lined.reshape(head_number * dense_rows, loc_columns + LANES), chips, 1, True, 2
        ).reshape(width, loc_columns + LANES)
        x_line = line_exchange(layer_input.reshape(tokens_present, width), head_number, 3, True)

    if not fused:
        grad_all = lax.all_gather(cots, ("chip", "head"), axis=0, tiled=True)
        dense_out = lax.all_gather(output_weight, ("chip", "core", "head"), axis=0, tiled=True)

    dense_qkv = dense[:, :loc_columns]
    dense_router = dense[:, loc_columns : loc_columns + EXPERTS]
    gain_attn = dense[:, loc_columns + EXPERTS].astype(f32)
    gain_ffn = dense[:, loc_columns + EXPERTS + 1].astype(f32)

    x_line = x_line.reshape(line_tokens, width).astype(f32)
    normed_line = x_line * lax.rsqrt(jnp.mean(x_line * x_line, axis=1, keepdims=True) + epsilon)
    first_line = (normed_line * gain_attn).astype(bf16)

    def to_blocks(value):
        columns = value.shape[1:]
        return (
            value.reshape((head_number, sequence_batch, token_rows) + columns)
            .swapaxes(0, 1)
            .reshape((sequence_batch, blk) + columns)
        )

    def to_lines(value):
        columns = value.shape[2:]
        return (
            value.reshape((sequence_batch, head_number, token_rows) + columns)
            .swapaxes(0, 1)
            .reshape((line_tokens,) + columns)
        )

    q_start = seq_index * blk
    q_pos = q_start + jnp.arange(blk, dtype=jnp.int32)
    cosine, sine = rope_tables(q_pos, HEAD_WIDTH)
    projected = to_blocks(jnp.dot(first_line, dense_qkv, preferred_element_type=f32)).reshape(
        sequence_batch, blk, key_value_location, query_group + 2, HEAD_WIDTH
    )
    turned = rotate(projected[:, :, :, : query_group + 1], cosine, sine)
    query_rows = turned[:, :, :, :query_group].astype(bf16)
    keys_values = (
        jnp.stack([turned[:, :, :, query_group], projected[:, :, :, query_group + 1]], axis=3)
        .astype(bf16)
        .reshape(sequence_batch * blk, key_value_location * 2 * HEAD_WIDTH)
    )
    kv_columns = key_value_location * 2 * HEAD_WIDTH
    pairs_here = sequence_batch * key_value_location
    group_columns = key_value_location * query_group * HEAD_WIDTH
    queries = (
        (query_rows.astype(f32) * scale)
        .astype(bf16)
        .transpose(0, 2, 3, 1, 4)
        .reshape(pairs_here, query_group * blk, HEAD_WIDTH)
    )
    key_seg = segments[:, :, None]
    q_seg = lax.dynamic_slice_in_dim(segments, q_start, blk, 1)
    query_seg = jnp.tile(q_seg[:, None, :], (1, 1, query_group))
    lines, kv_all, out_turned, lse, *beside = attend(
        queries,
        keys_values.reshape(sequence_batch, blk, kv_columns),
        key_seg,
        query_seg,
        [(output_weight, True), (cots, False)] if fused else [],
        chips,
        head_number,
        query_group,
        4,
    )
    if fused:
        dense_out = beside[0].reshape(QUERY_HEADS * HEAD_WIDTH, width)
        grad_all = beside[1].reshape(group_tokens, width)
    mixed_heads = lines.transpose(1, 0, 2).reshape(tokens_present, QUERY_HEADS * HEAD_WIDTH)
    tokens = layer_input.reshape(tokens_present, width).astype(f32)
    middle = tokens + jnp.dot(mixed_heads, dense_out, preferred_element_type=f32)
    inverse_two = lax.rsqrt(jnp.mean(middle * middle, axis=1, keepdims=True) + epsilon)
    normed_two = middle * inverse_two
    second_input = (normed_two * gain_ffn).astype(bf16)
    router_logits = jnp.dot(second_input, dense_router, preferred_element_type=f32)
    route_flat = routes.reshape(tokens_present, top)
    hot = route_flat[:, :, None] == jnp.arange(EXPERTS, dtype=jnp.int32)[None, None, :]
    chosen = jnp.sum(jnp.where(hot, router_logits[:, None, :], 0.0), axis=2)
    gates = jax.nn.softmax(chosen, axis=-1)
    if not fused:
        expert_of = route_flat.reshape(pairs)
        rank = pair_rank.reshape(pairs)
        slot = jnp.sum(
            (expert_of[None, :] == expert_of[:, None]) & (rank[None, :] < rank[:, None]),
            axis=1,
            dtype=jnp.int32,
        )
    kept = (slot < CAP).reshape(tokens_present, top).astype(f32)
    weights_pair = gates * kept
    spread = jnp.sum(jnp.where(hot, weights_pair[:, :, None], 0.0), axis=1)
    spread_high = spread.astype(bf16)
    spread_low = (spread - spread_high.astype(f32)).astype(bf16)
    pad = jnp.zeros((tokens_present, LOW - EXPERTS), bf16)
    payload = jnp.concatenate([second_input, spread_high, pad, spread_low, pad], axis=1)
    if fused:
        back, moe_part, keep_up, other_up, keep_down, other_down = expert_turn(
            payload, grad_all, units, w_down, head_number, 6
        )
        down_share = keep_down.astype(f32) + other_down.astype(f32)
    else:
        x_all = gather(payload, chips, head_number, False, 6).reshape(group_tokens, columns)
        moe_part, back_part, d_gate_w, d_up_w, d_down_w = experts(
            x_all, grad_all, expert_gate, expert_up, expert_down, hidden
        )
        back_part = back_part.reshape(chips, head_number, tokens_present, columns)
        back = scatter_sum(back_part, chips, head_number, False, 7)
        moe = lax.psum_scatter(moe_part, ("chip", "head"), scatter_dimension=0, tiled=True)
        grads = jnp.stack([d_gate_w, d_up_w]).reshape(2, chips, 2, slice_rows, loc_experts * hidden)
        keep = lax.dynamic_index_in_dim(grads, core, 2, keepdims=False)
        give = lax.dynamic_index_in_dim(grads, 1 - core, 2, keepdims=False)
        shared = (keep.astype(f32) + sibling(give).astype(f32)).astype(bf16)
        piled = jnp.zeros((chips, 2, slice_rows, loc_experts * hidden), bf16)
        for mask in range(chips):
            piece = across(lax.dynamic_index_in_dim(shared, chip ^ mask, 1, keepdims=False), chips, mask)
            piled = lax.dynamic_update_slice(piled, piece[None], (chip ^ mask, 0, 0, 0))
        up_share = (
            piled.reshape(chips, 2, slice_rows, loc_experts, hidden)
            .transpose(3, 2, 1, 0, 4)
            .astype(f32)
            .reshape(loc_experts, slice_rows, 2 * FF)
        )
        d_down_w = d_down_w.reshape(loc_experts, 2, hidden // 2, width)
        keep = lax.dynamic_index_in_dim(d_down_w, core, 1, keepdims=False)
        give = lax.dynamic_index_in_dim(d_down_w, 1 - core, 1, keepdims=False)
        down_share = keep.astype(f32) + sibling(give).astype(f32)

    grad_out = cotangent.reshape(tokens_present, width).astype(f32)
    d_kept = back[:, width : width + EXPERTS]
    grad_gate = jnp.sum(jnp.where(hot, d_kept[:, None, :], 0.0), axis=2) * kept
    grad_chosen = gates * (grad_gate - jnp.sum(gates * grad_gate, axis=1, keepdims=True))
    grad_logits = jnp.sum(jnp.where(hot, grad_chosen[:, :, None], 0.0), axis=1)
    grad_router = jnp.dot(second_input.astype(f32).T, grad_logits, precision=HIGH_PRECISION)
    grad_second = back[:, :width] + jnp.dot(
        grad_logits, dense_router.astype(f32).T, precision=HIGH_PRECISION
    )
    grad_gain_ffn = jnp.sum(grad_second * normed_two, axis=0)
    scaled_two = grad_second * gain_ffn
    grad_mid = grad_out + inverse_two * (
        scaled_two - normed_two * jnp.mean(scaled_two * normed_two, axis=1, keepdims=True)
    )
    grad_attn = grad_mid.astype(bf16)
    grad_dense_out = jnp.dot(mixed_heads.T, grad_attn, preferred_element_type=f32)
    grad_dense_out = grad_dense_out.astype(bf16)
    if not fused:
        out_share = lax.psum_scatter(
            grad_dense_out, ("chip", "core", "head"), scatter_dimension=0, tiled=True
        ).astype(f32)
    grad_heads = (
        jnp.dot(grad_attn, dense_out.T, preferred_element_type=f32)
        .astype(bf16)
        .reshape(tokens_present, head_number, group_columns)
        .transpose(1, 0, 2)
    )
    grad_q, grad_kv, *beside = attend_back(
        queries,
        kv_all,
        key_seg,
        query_seg,
        out_turned,
        lse,
        grad_heads,
        [
            (moe_part.reshape(chips, head_number, tokens_present, width), False),
            (grad_dense_out.reshape(chips, 2, head_number, dense_rows, width), True),
        ]
        if fused
        else [],
        head_number,
        query_group,
        8,
    )
    if fused:
        moe, out_share = beside
        keep_up, grad_kv = lax.optimization_barrier((keep_up, grad_kv))
        shared = (keep_up.astype(f32) + other_up.astype(f32)).astype(bf16)
        pieces = [
            across(lax.dynamic_index_in_dim(shared, chip ^ mask, 0, keepdims=False), chips, mask)
            for mask in range(chips)
        ]
    grad_q = grad_q.reshape(
        sequence_batch, key_value_location, query_group, blk, HEAD_WIDTH
    ).transpose(0, 3, 1, 2, 4)
    grad_kv = grad_kv.reshape(sequence_batch, blk, key_value_location, 2, HEAD_WIDTH)
    grad_proj = jnp.concatenate([grad_q.astype(bf16), grad_kv.astype(bf16)], axis=3).astype(f32)
    unturned = rotate(grad_proj[:, :, :, : query_group + 1], cosine, -sine)
    grad_qkv = to_lines(
        jnp.concatenate([unturned, grad_proj[:, :, :, query_group + 1 :]], axis=3)
        .reshape(sequence_batch, blk, loc_columns)
        .astype(bf16)
    )
    grad_first_part = jnp.dot(grad_qkv, dense_qkv.T, preferred_element_type=f32)
    grad_gain_attn = jnp.sum(grad_first_part * normed_line, axis=0)
    grad_dense_qkv = jnp.dot(first_line.T, grad_qkv, preferred_element_type=f32)
    sums = jnp.concatenate(
        [
            grad_dense_qkv,
            grad_router,
            grad_gain_attn[:, None],
            grad_gain_ffn[:, None],
            jnp.zeros((width, LANES - EXPERTS - 2), f32),
        ],
        axis=1,
    ).astype(bf16)
    if fused:
        grad_first, sums = end(
            grad_first_part.astype(bf16).reshape(head_number, tokens_present, width),
            sums.reshape(chips, 2, head_number * dense_rows, loc_columns + LANES),
            chips,
            head_number,
            13,
        )
        pieces, grad_first = lax.optimization_barrier((pieces, grad_first))
        grad_first = jnp.sum(grad_first.astype(f32), axis=0)
        sums = sums.astype(f32)
        up_share = place_units(pieces, hidden)
    else:
        grad_first = jnp.sum(
            line_exchange(
                grad_first_part.astype(bf16).reshape(head_number, tokens_present, width),
                head_number,
                10,
            ).astype(f32),
            axis=0,
        )
        sums = scatter_sum(
            sums.reshape(chips, 2, head_number * dense_rows, loc_columns + LANES), chips, 1, True, 11
        )
        sums = line_exchange(
            sums.reshape(head_number, dense_rows, loc_columns + LANES), head_number, 12
        )
    inverse_one = lax.rsqrt(jnp.mean(tokens * tokens, axis=1, keepdims=True) + epsilon)
    normed_one = tokens * inverse_one
    scaled_one = grad_first * gain_attn
    grad_input = grad_mid + inverse_one * (
        scaled_one - normed_one * jnp.mean(scaled_one * normed_one, axis=1, keepdims=True)
    )
    mixed_out = (middle + moe.astype(f32)).astype(bf16)
    mixed_out = mixed_out.reshape(sequence_batch, token_rows, width)
    qkv_share = sums[:, :, :loc_columns].transpose(1, 0, 2).reshape(dense_rows, -1)
    extra = jnp.sum(sums[:, :, loc_columns:], axis=0)
    return (
        mixed_out,
        grad_input.reshape(sequence_batch, token_rows, width),
        qkv_share,
        out_share,
        extra[:, :EXPERTS],
        extra[:, EXPERTS],
        extra[:, EXPERTS + 1],
        up_share,
        down_share,
    )


def solution(mesh):
    grid = mesh.devices
    seq, heads = grid.shape
    split = Mesh(grid.reshape(seq // 2, 2, heads), ("chip", "core", "head"))
    places = ("chip", "core", "head")
    inner = ("chip", "core")
    placed = (
        P(None, places, None),
        P(),
        P(None, places, None),
        P(None, places, None),
        P(places, None),
        P(places, None),
        P(places, None),
        P(places),
        P(places),
        P("head", inner, None),
        P("head", inner, None),
        P(None, places, None),
    )
    return jax.shard_map(
        per_device,
        mesh=split,
        in_specs=placed,
        out_specs=(
            P(None, places, None),
            P(None, places, None),
            P(places, None),
            P(places, None),
            P(places, None),
            P(places),
            P(places),
            P("head", inner, None),
            P("head", inner, None),
        ),
        check_vma=False,
    )
```

```python
import functools

import jax
import jax.numpy as jnp
from jax import lax
from jax.experimental import pallas as pl
from jax.experimental.pallas import tpu as pltpu
from jax.sharding import Mesh, PartitionSpec as P

MODEL_WIDTH = 1536
QUERY_HEADS = 24
KEY_VALUE_HEADS = 8
HEAD_WIDTH = 64
EXPERTS = 40
FF = 512
CAP = 25
LANES = 128
LOW = 64

epsilon = 1e-06
negative = -1e30
theta = 10000.0
HIGH_PRECISION = lax.Precision.HIGHEST
MESH = pl.DeviceIdType.MESH
f32 = jnp.float32
bf16 = jnp.bfloat16
ANY = pl.BlockSpec(memory_space=pl.ANY)
WHOLE = pl.BlockSpec(memory_space=pltpu.VMEM)
DMA = pltpu.SemaphoreType.DMA


def rope_tables(token_positions, head_size):
    half = head_size // 2
    freq = theta ** (-jnp.arange(half, dtype=jnp.float32) / half)
    angle = token_positions.astype(jnp.float32)[:, None] * freq[None, :]
    return (jnp.cos(angle)[None, :, None, None, :], jnp.sin(angle)[None, :, None, None, :])


def rotate(value, cosine, sine):
    half = value.shape[-1] // 2
    first = value[..., :half]
    second = value[..., half:]
    return jnp.concatenate(
        [first * cosine - second * sine, second * cosine + first * sine], axis=-1
    )


def digits(count):
    number = count.bit_length() - 1
    assert 1 << number == count
    return number


def flip(index, mask):
    out = index
    bit = 0
    while (1 << bit) <= mask:
        if (mask >> bit) & 1:
            out = out + (1 - 2 * ((index // (1 << bit)) % 2)) * (1 << bit)
        bit += 1
    return out


def subsets(bits):
    out = [0]
    for bit in bits:
        out = out + [mask | (1 << bit) for mask in out]
    return out


def near(count):
    return sorted(range(1, count), key=lambda step: min(step, count - step))


def cut_rows(rows):
    return (rows // 2 + 15) // 16 * 16


def part_of(rows, side):
    cut = cut_rows(rows)
    return pl.ds(side * cut, rows - cut if side else cut)


def meet(peers):
    sem = pltpu.get_barrier_semaphore()
    for peer in peers:
        pl.semaphore_signal(sem, inc=1, device_id=peer, device_id_type=MESH)
    pl.semaphore_wait(sem, len(peers))


class Cube:
    def __init__(self, chips, with_core):
        self.chips = chips
        self.chip_digits = digits(chips)
        self.number = self.chip_digits + int(with_core)
        self.with_core = with_core
        up = tuple(range(self.chip_digits))
        core = (self.chip_digits,) if with_core else ()
        self.gather_orders = (up + core, up[::-1] + core)
        self.scatter_orders = (core + up, core + up[::-1])

    def place(self, mask):
        chip = flip(lax.axis_index("chip"), mask & (self.chips - 1))
        if not self.with_core:
            return (chip,)
        return (chip, flip(lax.axis_index("core"), mask >> self.chip_digits))

    def peer(self, digit):
        if digit < self.chip_digits:
            return {"chip": flip(lax.axis_index("chip"), 1 << digit)}
        return {"core": flip(lax.axis_index("core"), 1)}


def gather_kernel(cube, heads, in_ref, out_ref, local, line_send, line_recv, send, recv):
    hz = lax.axis_index("head")
    rows = in_ref.shape[0]
    half = rows // 2
    others = near(heads) if heads > 1 else []
    meet(
        [cube.peer(digit) for digit in range(cube.number)]
        + [{"head": (hz + d) % heads} for d in others]
    )

    def at(mask, d):
        index = cube.place(mask)
        return index + ((hz + heads - d) % heads,) if heads > 1 else index

    own = pltpu.make_async_copy(in_ref, out_ref.at[at(0, 0)], local)
    own.start()
    line = {}
    for d in others:
        line[d] = pltpu.make_async_remote_copy(
            src_ref=in_ref,
            dst_ref=out_ref.at[at(0, 0)],
            send_sem=line_send.at[d - 1],
            recv_sem=line_recv.at[d - 1],
            device_id={"head": (hz + d) % heads},
            device_id_type=MESH,
        )
        line[d].start()
    copies = {}

    def forward(side, mask, d):
        order = cube.gather_orders[side]
        last = max([k for k in range(cube.number) if (mask >> order[k]) & 1], default=-1)
        for k in range(last + 1, cube.number):
            later = mask | (1 << order[k])
            part = pl.ds(side * half, half)
            place = out_ref.at[at(mask, d) + (part,)]
            copy = pltpu.make_async_remote_copy(
                src_ref=in_ref.at[part] if mask == 0 and d == 0 else place,
                dst_ref=place,
                send_sem=send.at[side, later, d],
                recv_sem=recv.at[side, later, d],
                device_id=cube.peer(order[k]),
                device_id_type=MESH,
            )
            copy.start()
            copies[(side, later, d)] = copy

    for side in range(2):
        forward(side, 0, 0)
    for d in others:
        line[d].wait_recv()
        for side in range(2):
            forward(side, 0, d)
    for mask in sorted(range(1, 1 << cube.number), key=lambda m: bin(m).count("1")):
        for d in [0] + others:
            for side in range(2):
                copies[(side, mask, d)].wait_recv()
                forward(side, mask, d)
    own.wait()
    for copy in list(line.values()) + list(copies.values()):
        copy.wait_send()


def gather(value, chips, heads, with_core, number):
    rows, columns = value.shape
    cube = Cube(chips, with_core)
    lead = (chips,) + ((2,) if with_core else ()) + ((heads,) if heads > 1 else ())
    steps = max(heads - 1, 1)
    return pl.pallas_call(
        functools.partial(gather_kernel, cube, heads),
        out_shape=jax.ShapeDtypeStruct(lead + (rows, columns), value.dtype),
        in_specs=[ANY],
        out_specs=ANY,
        scratch_shapes=[
            DMA,
            DMA((steps,)),
            DMA((steps,)),
            DMA((2, 1 << cube.number, heads)),
            DMA((2, 1 << cube.number, heads)),
        ],
        compiler_params=pltpu.CompilerParams(collective_id=number, has_side_effects=True),
        name="gather",
    )(value)


def scatter_kernel(cube, heads, in_ref, out_ref, *refs):
    count = cube.number
    arrived, parts = refs[:count], refs[count : 2 * count - 1]
    line_out, line_in, line_send, line_recv, send, recv = refs[2 * count - 1 :]
    hz = lax.axis_index("head")
    half = in_ref.shape[-2] // 2
    others = near(heads) if heads > 1 else []
    order_of_lines = others[::-1] + [0]
    meet(
        [cube.peer(digit) for digit in range(count)] + [{"head": (hz + d) % heads} for d in others]
    )
    copies = {}

    def slot(side, k, mask):
        return subsets(cube.scatter_orders[side][k + 1 :]).index(mask)

    def mine(side, mask, d):
        index = cube.place(mask)
        if heads > 1:
            index = index + ((hz + d) % heads,)
        return in_ref.at[index + (pl.ds(side * half, half),)]

    def pass_on(side, k, mask, d, source):
        where = slot(side, k, mask)
        copy = pltpu.make_async_remote_copy(
            src_ref=source,
            dst_ref=arrived[k].at[side, where, d],
            send_sem=send.at[side, k, where, d],
            recv_sem=recv.at[side, k, where, d],
            device_id=cube.peer(cube.scatter_orders[side][k]),
            device_id_type=MESH,
        )
        copy.start()
        copies[(side, k, mask, d)] = copy

    def total(side, steps, mask, d):
        value = mine(side, mask, d)[...].astype(f32)
        for j in range(steps):
            copies[(side, j, mask, d)].wait_recv()
            value = value + arrived[j][side, slot(side, j, mask), d].astype(f32)
        return value

    for k in range(count):
        for d in order_of_lines:
            for side in range(2):
                order = cube.scatter_orders[side]
                for mask in subsets(order[k + 1 :])[::-1]:
                    full = mask | (1 << order[k])
                    if k == 0:
                        source = mine(side, full, d)
                    else:
                        source = parts[k - 1].at[side, slot(side, k, mask), d]
                        source[...] = total(side, k, full, d).astype(bf16)
                    pass_on(side, k, mask, d, source)
    line = {}
    for d in order_of_lines:
        for side in range(2):
            value = total(side, count, 0, d)
            if d:
                line_out[d - 1, pl.ds(side * half, half)] = value.astype(bf16)
            else:
                out_ref[pl.ds(side * half, half)] = value
        if d:
            line[d] = pltpu.make_async_remote_copy(
                src_ref=line_out.at[d - 1],
                dst_ref=line_in.at[d - 1],
                send_sem=line_send.at[d - 1],
                recv_sem=line_recv.at[d - 1],
                device_id={"head": (hz + d) % heads},
                device_id_type=MESH,
            )
            line[d].start()
    for d in others:
        line[d].wait_recv()
        out_ref[...] += line_in[d - 1].astype(f32)
    for copy in list(line.values()) + list(copies.values()):
        copy.wait_send()


def scatter_sum(value, chips, heads, with_core, number):
    rows, columns = value.shape[-2:]
    cube = Cube(chips, with_core)
    half = rows // 2
    steps = max(heads - 1, 1)
    line_rows = rows if heads > 1 else 16
    slots = [(1 << cube.number) >> (k + 1) for k in range(cube.number)]
    if 2 * value.size + 4 * heads * half * columns * (sum(slots) + sum(slots[1:])) > 40 << 20:
        names = ("chip", "core") if with_core else ("chip",)
        names = names + (("head",) if heads > 1 else ())
        flat = value.reshape(-1, columns)
        return lax.psum_scatter(flat, names, scatter_dimension=0, tiled=True).astype(f32)
    return pl.pallas_call(
        functools.partial(scatter_kernel, cube, heads),
        out_shape=jax.ShapeDtypeStruct((rows, columns), f32),
        in_specs=[WHOLE],
        out_specs=WHOLE,
        scratch_shapes=[pltpu.VMEM((2, s, heads, half, columns), bf16) for s in slots]
        + [pltpu.VMEM((2, s, heads, half, columns), bf16) for s in slots[1:]]
        + [
            pltpu.VMEM((steps, line_rows, columns), bf16),
            pltpu.VMEM((steps, line_rows, columns), bf16),
            DMA((steps,)),
            DMA((steps,)),
            DMA((2, cube.number, slots[0], heads)),
            DMA((2, cube.number, slots[0], heads)),
        ],
        compiler_params=pltpu.CompilerParams(
            collective_id=number, has_side_effects=True, vmem_limit_bytes=56 << 20
        ),
        name="scatter_sum",
    )(value)


def line_kernel(heads, same, in_ref, out_ref, local, send, recv):
    hz = lax.axis_index("head")
    others = near(heads)[::-1]
    meet([{"head": (hz + d) % heads} for d in others])

    def source(place):
        return in_ref if same else in_ref.at[place]

    own = pltpu.make_async_copy(source(hz), out_ref.at[hz], local)
    own.start()
    copies = []
    for d in others:
        place = (hz + d) % heads
        copy = pltpu.make_async_remote_copy(
            src_ref=source(place),
            dst_ref=out_ref.at[hz],
            send_sem=send.at[d - 1],
            recv_sem=recv.at[d - 1],
            device_id={"head": place},
            device_id_type=MESH,
        )
        copy.start()
        copies.append(copy)
    own.wait()
    for copy in copies:
        copy.wait()


def line_exchange(value, heads, number, same=False):
    return pl.pallas_call(
        functools.partial(line_kernel, heads, same),
        out_shape=jax.ShapeDtypeStruct((heads,) + value.shape if same else value.shape, value.dtype),
        in_specs=[ANY],
        out_specs=ANY,
        scratch_shapes=[DMA, DMA((heads - 1,)), DMA((heads - 1,))],
        compiler_params=pltpu.CompilerParams(collective_id=number, has_side_effects=True),
        name="line_exchange",
    )(value)


NT = (((1,), (1,)), ((), ()))


def experts_kernel(
    tile,
    hidden,
    x_ref,
    c_ref,
    gate_hbm,
    up_hbm,
    down_hbm,
    moe_ref,
    back_ref,
    d_gate_hbm,
    d_up_hbm,
    d_down_hbm,
    w_gate,
    w_up,
    w_down,
    d_gate_w,
    d_up_w,
    d_down_w,
    acts,
    back_gate,
    back_up,
    stage_wide,
    stage_down,
    load,
    store,
):
    step = pl.program_id(0)
    width, total = w_gate.shape

    @pl.when(step == 0)
    def _():
        loads = [
            pltpu.make_async_copy(gate_hbm, w_gate, load.at[0]),
            pltpu.make_async_copy(up_hbm, w_up, load.at[1]),
            pltpu.make_async_copy(down_hbm, w_down, load.at[2]),
        ]
        for copy in loads:
            copy.start()
        d_gate_w[...] = jnp.zeros_like(d_gate_w)
        d_up_w[...] = jnp.zeros_like(d_up_w)
        d_down_w[...] = jnp.zeros_like(d_down_w)
        for copy in loads:
            copy.wait()

    x = x_ref[:, :width]
    c = c_ref[...]
    routed = x_ref[:, width:]
    first_expert = lax.axis_index("head") * (total // hidden)
    d_gates = jnp.zeros((x.shape[0], LANES), f32)
    for begin in range(0, total, tile):
        js = pl.ds(begin, tile)
        column = begin + lax.broadcasted_iota(jnp.int32, (LANES, tile), 1)
        line = lax.broadcasted_iota(jnp.int32, (LANES, tile), 0)
        expert = first_expert + column // hidden
        here = (line == expert).astype(f32)
        both = (here + (line == expert + LOW).astype(f32)).astype(bf16)
        weight = jnp.dot(routed, both, preferred_element_type=f32)
        gate = jnp.dot(x, w_gate[:, js], preferred_element_type=f32)
        up = jnp.dot(x, w_up[:, js], preferred_element_type=f32)
        d_act = lax.dot_general(c, w_down[js, :], NT, preferred_element_type=f32)
        sigma = 1.0 / (1.0 + jnp.exp(-gate))
        silu = gate * sigma
        act = (silu * up).astype(bf16).astype(f32)
        d_gates = d_gates + lax.dot_general(
            (act * d_act).astype(bf16), here.astype(bf16), NT, preferred_element_type=f32
        )
        acts[:, js] = (act * weight).astype(bf16)
        d_act = d_act * weight
        back_up[:, js] = (d_act * silu).astype(bf16)
        back_gate[:, js] = (d_act * up * sigma * (1.0 + gate * (1.0 - sigma))).astype(bf16)
    back_ref[:, width:] = d_gates.astype(bf16)
    x_turned = x.T
    for begin in range(0, total, tile):
        js = pl.ds(begin, tile)
        d_gate_w[:, js] += jnp.dot(x_turned, back_gate[:, js], preferred_element_type=f32)
        d_up_w[:, js] += jnp.dot(x_turned, back_up[:, js], preferred_element_type=f32)
        d_down_w[js, :] += jnp.dot(acts[:, js].T, c, preferred_element_type=f32)
    for begin in range(0, width, 512):
        cs = pl.ds(begin, 512)
        moe_ref[:, cs] = jnp.dot(acts[...], w_down[:, cs], preferred_element_type=f32).astype(bf16)
        back_ref[:, cs] = (
            lax.dot_general(back_gate[...], w_gate[cs, :], NT, preferred_element_type=f32)
            + lax.dot_general(back_up[...], w_up[cs, :], NT, preferred_element_type=f32)
        ).astype(bf16)

    @pl.when(step == pl.num_programs(0) - 1)
    def _():
        rows = stage_wide.shape[1]
        jobs = [
            (source, target, stage, begin)
            for source, target, stage in (
                (d_gate_w, d_gate_hbm, stage_wide),
                (d_up_w, d_up_hbm, stage_wide),
                (d_down_w, d_down_hbm, stage_down),
            )
            for begin in range(0, source.shape[0], rows)
        ]
        flight = {}
        for index, (source, target, stage, begin) in enumerate(jobs):
            now = index % 2
            if now in flight:
                flight[now].wait()
            stage[now] = source[pl.ds(begin, rows), :].astype(bf16)
            flight[now] = pltpu.make_async_copy(
                stage.at[now], target.at[pl.ds(begin, rows), :], store.at[now]
            )
            flight[now].start()
        for copy in flight.values():
            copy.wait()


def experts(x, c, w_gate, w_up, w_down, hidden):
    tokens, columns = x.shape
    width, total = w_gate.shape
    block = min(256, tokens)
    tile = 256 if total % 256 == 0 else hidden
    return pl.pallas_call(
        functools.partial(experts_kernel, tile, hidden),
        grid=(tokens // block,),
        out_shape=(
            jax.ShapeDtypeStruct((tokens, width), bf16),
            jax.ShapeDtypeStruct((tokens, columns), bf16),
            jax.ShapeDtypeStruct((width, total), bf16),
            jax.ShapeDtypeStruct((width, total), bf16),
            jax.ShapeDtypeStruct((total, width), bf16),
        ),
        in_specs=[
            pl.BlockSpec((block, columns), lambda i: (i, 0)),
            pl.BlockSpec((block, width), lambda i: (i, 0)),
            ANY,
            ANY,
            ANY,
        ],
        out_specs=(
            pl.BlockSpec((block, width), lambda i: (i, 0)),
            pl.BlockSpec((block, columns), lambda i: (i, 0)),
            ANY,
            ANY,
            ANY,
        ),
        scratch_shapes=[
            pltpu.VMEM((width, total), bf16),
            pltpu.VMEM((width, total), bf16),
            pltpu.VMEM((total, width), bf16),
            pltpu.VMEM((width, total), f32),
            pltpu.VMEM((width, total), f32),
            pltpu.VMEM((total, width), f32),
            pltpu.VMEM((block, total), bf16),
            pltpu.VMEM((block, total), bf16),
            pltpu.VMEM((block, total), bf16),
            pltpu.VMEM((2, 64, total), bf16),
            pltpu.VMEM((2, 64, width), bf16),
            DMA((3,)),
            DMA((2,)),
        ],
        compiler_params=pltpu.CompilerParams(vmem_limit_bytes=60 << 20),
        name="experts",
    )(x, c, w_gate, w_up, w_down)


def turn_kernel(cube, heads, hidden, *refs):
    chips, count = cube.chips, cube.number
    own_ref, c_hbm, down_hbm = refs[:3]
    pieces, refs = refs[3 : 3 + chips], (None,) * 4 + refs[3 + chips :]
    out_ref, moe_hbm, keep_up_hbm, other_up_hbm, keep_down_hbm, other_down_hbm = refs[4:10]
    tokens, turned, cots, w_up, w_down, acts, backs, d_gates, moe_stage, line_in = refs[10:20]
    arrived = refs[20 : 20 + count]
    load, store, own_sem, line_send, line_recv, send, recv, back_send, back_recv = refs[
        20 + count : 29 + count
    ]
    end_send, end_recv, twin_send, twin_recv, load_send, load_recv = refs[29 + count :]
    hz = lax.axis_index("head")
    rows, columns = own_ref.shape
    experts_here, width, _ = w_up.shape
    total = experts_here * hidden
    half = rows // 2
    line = heads * rows
    others = near(heads)
    masks = sorted(range(chips), key=lambda m: bin(m).count("1"))

    core = lax.axis_index("core")
    twin = {"core": 1 - core}
    slices = 2 * chips
    slice_rows = width // slices

    def up_rows(ref, chip, which):
        return ref.at[:, pl.ds((chip * 2 + which) * slice_rows, slice_rows), :]

    def w_down_parts(which):
        return w_down.reshape(experts_here, 2, hidden // 2, width).at[:, which]

    homes = [
        (pieces[mask], up_rows(w_up, flip(lax.axis_index("chip"), mask), core))
        for mask in range(chips)
    ] + [(down_hbm, w_down_parts(core))]
    loads = [
        pltpu.make_async_copy(source, target, load.at[index])
        for index, (source, target) in enumerate([(c_hbm, cots)] + homes)
    ]
    shared = [
        pltpu.make_async_remote_copy(
            src_ref=source,
            dst_ref=target,
            send_sem=load_send.at[index],
            recv_sem=load_recv.at[index],
            device_id=twin,
            device_id_type=MESH,
        )
        for index, (source, target) in enumerate(homes)
    ]
    for copy in loads:
        copy.start()
    meet(
        [cube.peer(digit) for digit in range(count)]
        + [{"head": (hz + d) % heads} for d in others]
        + [twin]
    )

    def part(side):
        return pl.ds(side * half, half)

    middle = jnp.minimum(hz, heads - 1 - hz)

    def source(rank):
        if rank == 0:
            return hz
        far = (rank + 1) // 2
        near_one = hz - far if rank % 2 else hz + far
        far_one = jnp.where(
            hz < heads - 1 - hz, hz + (rank - middle), hz - (rank - middle)
        )
        return jnp.where(rank <= 2 * middle, near_one, far_one)

    def line_copy(rank, step):
        head = source(rank)
        place = tokens.at[cube.place(0) + (head,)]
        return pltpu.make_async_remote_copy(
            src_ref=own_ref if rank == 0 else place,
            dst_ref=place,
            send_sem=line_send.at[heads if rank == 0 and step < 0 else head],
            recv_sem=line_recv.at[head],
            device_id={"head": (hz + step + heads) % heads},
            device_id_type=MESH,
        )

    def along(rank, act):
        head = source(rank)
        goes_up = hz + 1 < heads
        goes_down = hz > 0
        if rank:
            goes_up = goes_up & (head < hz)
            goes_down = goes_down & (head > hz)

        @pl.when(goes_up)
        def _():
            act(line_copy(rank, 1))

        @pl.when(goes_down)
        def _():
            act(line_copy(rank, -1))

    def plane_copy(side, mask, k, rank):
        digit = cube.gather_orders[side][k]
        later = mask | (1 << digit)
        head = source(rank)
        place = tokens.at[cube.place(mask) + (head, part(side))]
        return pltpu.make_async_remote_copy(
            src_ref=own_ref.at[part(side)] if mask == 0 and rank == 0 else place,
            dst_ref=place,
            send_sem=send.at[side, later, head],
            recv_sem=recv.at[side, later, head],
            device_id=cube.peer(digit),
            device_id_type=MESH,
        )

    def steps_after(side, mask):
        order = cube.gather_orders[side]
        last = max([k for k in range(count) if (mask >> order[k]) & 1], default=-1)
        return range(last + 1, count)

    def arrival(side, mask, rank):
        order = cube.gather_orders[side]
        k = max(k for k in range(count) if (mask >> order[k]) & 1)
        return plane_copy(side, mask & ~(1 << order[k]), k, rank)

    def receive(mask, rank):
        if mask == 0:
            if rank:
                line_copy(rank, 1).wait_recv()
            along(rank, lambda copy: copy.start())
        for side in range(2):
            if mask:
                arrival(side, mask, rank).wait_recv()
            for k in steps_after(side, mask):
                plane_copy(side, mask, k, rank).start()

    levels = [
        [m for m in masks if bin(m).count("1") == level] for level in range(cube.number + 1)
    ]
    waits = {0: [], 1: []}
    early = max(heads - 2, 0)
    for rank in range(heads):
        waits[0].append((0, rank))
        if 0 < rank <= early and count > 0:
            waits[0] += [(m, rank - 1) for m in levels[1]]
    waits[1] = [(m, rank) for rank in range(early, heads) for m in levels[1]]
    for level in range(2, count + 1):
        waits[level] = [(m, rank) for m in levels[level] for rank in range(heads)]

    def sent(mask):
        for rank in range(heads):
            if mask == 0:
                along(rank, lambda copy: copy.wait_send())
            for side in range(2):
                for k in steps_after(side, mask):
                    plane_copy(side, mask, k, rank).wait_send()

    def slot(side, k, mask):
        return subsets(cube.scatter_orders[side][k + 1 :]).index(mask)

    def back_place(side, mask, d):
        return tokens.at[cube.place(mask) + ((hz + d) % heads, part(side))]

    def back_copy(side, k, mask, d):
        order = cube.scatter_orders[side]
        where = slot(side, k, mask)
        return pltpu.make_async_remote_copy(
            src_ref=back_place(side, mask | (1 << order[k]), d),
            dst_ref=arrived[k].at[side, where, d],
            send_sem=back_send.at[side, k, where, d],
            recv_sem=back_recv.at[side, k, where, d],
            device_id=cube.peer(order[k]),
            device_id_type=MESH,
        )

    def end_copy(d):
        return pltpu.make_async_remote_copy(
            src_ref=tokens.at[cube.place(0) + ((hz + d) % heads,)],
            dst_ref=line_in.at[d - 1],
            send_sem=end_send.at[d - 1],
            recv_sem=end_recv.at[d - 1],
            device_id={"head": (hz + d) % heads},
            device_id_type=MESH,
        )

    outward = others[::-1] + [0]

    def give(mask, d):
        for side in range(2):
            first = 1 << cube.scatter_orders[side][0]
            if mask & first:
                back_copy(side, 0, mask & ~first, d).start()

    own = pltpu.make_async_copy(own_ref, tokens.at[cube.place(0) + (hz,)], own_sem)
    own.start()
    for copy in shared:
        copy.start()

    first_expert = hz * experts_here
    span = min(512, width)
    group = 2 if experts_here % 2 == 0 else 1
    tile = group * hidden

    def compute(place):
        here = pl.ds(place * line, line)
        x = tokens[place, :, :, pl.ds(0, width)].reshape(line, width)
        c = cots[here, :]
        routed = tokens[place, :, :, pl.ds(width, LANES)].reshape(line, LANES)
        turned[:, here] = x.T
        d_gates[...] = jnp.zeros_like(d_gates)

        @pl.loop(0, total // tile)
        def _(j):
            js = pl.ds(pl.multiple_of(j * tile, tile), tile)
            column = j * tile + lax.broadcasted_iota(jnp.int32, (LANES, tile), 1)
            lane = lax.broadcasted_iota(jnp.int32, (LANES, tile), 0)
            expert = first_expert + column // hidden
            high = (lane == expert).astype(f32)
            both = (high + (lane == expert + LOW).astype(f32)).astype(bf16)
            weight = jnp.dot(routed, both, preferred_element_type=f32)
            both_parts = [
                jnp.dot(x, w_up[j * group + i], preferred_element_type=f32) for i in range(group)
            ]
            gate = jnp.concatenate([value[:, :hidden] for value in both_parts], axis=1)
            up = jnp.concatenate([value[:, hidden:] for value in both_parts], axis=1)
            d_act = lax.dot_general(c, w_down[js, :], NT, preferred_element_type=f32)
            sigma = 1.0 / (1.0 + jnp.exp(-gate))
            silu = gate * sigma
            act = (silu * up).astype(bf16).astype(f32)
            d_gates[...] += lax.dot_general(
                (act * d_act).astype(bf16), high.astype(bf16), NT, preferred_element_type=f32
            )
            acts[here, js] = (act * weight).astype(bf16)
            d_act = d_act * weight
            d_up = (d_act * silu).astype(bf16)
            d_gate = (d_act * up * sigma * (1.0 + gate * (1.0 - sigma))).astype(bf16)
            for i in range(group):
                one = slice(i * hidden, (i + 1) * hidden)
                backs[j * group + i, here, pl.ds(0, hidden)] = d_gate[:, one]
                backs[j * group + i, here, pl.ds(hidden, hidden)] = d_up[:, one]

    def results(place, step):
        here = pl.ds(place * line, line)

        @pl.loop(0, width // span)
        def _(j):
            cs = pl.ds(pl.multiple_of(j * span, span), span)
            value = sum(
                lax.dot_general(
                    backs[e, here, :], w_up[e, cs, :], NT, preferred_element_type=f32
                )
                for e in range(experts_here)
            )
            tokens[place, :, :, cs] = value.astype(bf16).reshape(heads, rows, span)

        tokens[place, :, :, pl.ds(width, LANES)] = (
            d_gates[...].astype(bf16).reshape(heads, rows, LANES)
        )

    def moe_copy(place):
        return pltpu.make_async_copy(
            moe_stage, moe_hbm.at[pl.ds(place * line, line)], store.at[chips + 1]
        )

    def mixed(place, step):
        here = pl.ds(place * line, line)

        @pl.when(step > 0)
        def _():
            moe_copy(place).wait()

        @pl.loop(0, width // span)
        def _(j):
            cs = pl.ds(pl.multiple_of(j * span, span), span)
            moe_stage[:, cs] = jnp.dot(
                acts[here, :], w_down[:, cs], preferred_element_type=f32
            ).astype(bf16)

        moe_copy(place).start()

    @pl.loop(0, chips)
    def _(step):
        seen = -1
        for index, mask in enumerate(masks):
            level = bin(mask).count("1")
            if level > seen:
                seen = level

                @pl.when(step == index)
                def _():
                    for event in waits[level]:
                        receive(*event)

        place = cube.place(0)[0] * 0
        for index, mask in enumerate(masks):
            place = jnp.where(step == index, cube.place(mask)[0], place)

        @pl.when(step == 0)
        def _():
            own.wait()
            for copy in loads + shared:
                copy.wait()

        compute(place)
        for index, mask in enumerate(masks):

            @pl.when(step == index)
            def _():
                sent(mask)

        results(place, step)
        for index, mask in enumerate(masks):
            if mask and mask != chips - 1:

                @pl.when(step == index)
                def _():
                    for d in outward:
                        give(mask, d)

    def sums(side, steps, mask, d):
        value = back_place(side, mask, d)[...].astype(f32)
        for j in range(steps):
            back_copy(side, j, mask, d).wait_recv()
            value = value + arrived[j][side, slot(side, j, mask), d].astype(f32)
        return value

    def keep_up(chip):
        return pltpu.make_async_copy(up_rows(w_up, chip, core), keep_up_hbm.at[chip], store.at[chip])

    def give_up(chip):
        return pltpu.make_async_remote_copy(
            src_ref=up_rows(w_up, chip, 1 - core),
            dst_ref=other_up_hbm.at[chip],
            send_sem=twin_send.at[chip],
            recv_sem=twin_recv.at[chip],
            device_id=twin,
            device_id_type=MESH,
        )

    def keep_down():
        return pltpu.make_async_copy(w_down_parts(core), keep_down_hbm, store.at[chips])

    def give_down():
        return pltpu.make_async_remote_copy(
            src_ref=w_down_parts(1 - core),
            dst_ref=other_down_hbm,
            send_sem=twin_send.at[chips],
            recv_sem=twin_recv.at[chips],
            device_id=twin,
            device_id_type=MESH,
        )

    def up_grad(begin, end):
        @pl.loop(begin, end)
        def _(e):
            w_up[e] = jnp.dot(turned[...], backs[e], preferred_element_type=f32).astype(bf16)

        if end == experts_here:
            for chip in range(chips):
                give_up(chip).start()
                keep_up(chip).start()

    def down_grad():
        @pl.loop(0, total // tile)
        def _(j):
            js = pl.ds(pl.multiple_of(j * tile, tile), tile)
            value = jnp.dot(acts[:, js].T, cots[...], preferred_element_type=f32)
            w_down[js, :] = value.astype(bf16)

        give_down().start()
        keep_down().start()

    def mix(begin, end):
        @pl.loop(begin, end)
        def _(index):
            mixed(index, index)

    cuts = [experts_here * i // 4 for i in range(5)]
    work = [
        lambda: mix(0, chips // 2),
        lambda: mix(chips // 2, chips),
        lambda: up_grad(cuts[0], cuts[1]),
        lambda: up_grad(cuts[1], cuts[2]),
        lambda: up_grad(cuts[2], cuts[3]),
        lambda: up_grad(cuts[3], cuts[4]),
        down_grad,
    ]
    turns = heads + count
    for turn in range(turns):
        if turn < heads:
            give(chips - 1, outward[turn])
        for piece in work[len(work) * turn // turns : len(work) * (turn + 1) // turns]:
            piece()
        for k in range(1, count):
            if 0 <= turn - k < heads:
                d = outward[turn - k]
                for side in range(2):
                    order = cube.scatter_orders[side]
                    for mask in subsets(order[k + 1 :])[::-1]:
                        full = mask | (1 << order[k])
                        back_place(side, full, d)[...] = sums(side, k, full, d).astype(bf16)
                        back_copy(side, k, mask, d).start()
        if 0 <= turn - count < heads:
            d = outward[turn - count]
            for side in range(2):
                value = sums(side, count, 0, d)
                if d:
                    back_place(side, 0, d)[...] = value.astype(bf16)
                else:
                    out_ref[part(side)] = value
            if d:
                end_copy(d).start()
    for d in others:
        end_copy(d).wait_recv()
        out_ref[...] += line_in[d - 1].astype(f32)
    for d in others:
        end_copy(d).wait_send()
    for side in range(2):
        for k in range(count):
            for mask in subsets(cube.scatter_orders[side][k + 1 :]):
                for d in outward:
                    back_copy(side, k, mask, d).wait_send()
    moe_copy(0).wait()
    for chip in range(chips):
        give_up(chip).wait()
        keep_up(chip).wait()
    give_down().wait()
    keep_down().wait()


def expert_turn(payload, c, pieces, w_down, heads, number):
    rows, columns = payload.shape
    chips, width = len(pieces), c.shape[1]
    experts_here, _, double = pieces[0].shape
    hidden = double // 2
    total = experts_here * hidden
    cube = Cube(chips, False)
    count = cube.number
    tokens = chips * heads * rows
    half = rows // 2
    slots = [chips >> (k + 1) for k in range(count)]
    share = jax.ShapeDtypeStruct((chips, experts_here, width // (2 * chips), double), bf16)
    down_share = jax.ShapeDtypeStruct((experts_here, hidden // 2, width), bf16)
    return pl.pallas_call(
        functools.partial(turn_kernel, cube, heads, hidden),
        out_shape=(
            jax.ShapeDtypeStruct((rows, columns), f32),
            jax.ShapeDtypeStruct((tokens, width), bf16),
            share,
            share,
            down_share,
            down_share,
        ),
        in_specs=[WHOLE] + [ANY] * (2 + chips),
        out_specs=(WHOLE, ANY, ANY, ANY, ANY, ANY),
        scratch_shapes=[
            pltpu.VMEM((chips, heads, rows, columns), bf16),
            pltpu.VMEM((width, tokens), bf16),
            pltpu.VMEM((tokens, width), bf16),
            pltpu.VMEM((experts_here, width, double), bf16),
            pltpu.VMEM((total, width), bf16),
            pltpu.VMEM((tokens, total), bf16),
            pltpu.VMEM((experts_here, tokens, double), bf16),
            pltpu.VMEM((heads * rows, LANES), f32),
            pltpu.VMEM((heads * rows, width), bf16),
            pltpu.VMEM((heads - 1, rows, columns), bf16),
        ]
        + [pltpu.VMEM((2, s, heads, half, columns), bf16) for s in slots]
        + [
            DMA((chips + 2,)),
            DMA((chips + 2,)),
            DMA,
            DMA((heads + 1,)),
            DMA((heads,)),
            DMA((2, chips, heads)),
            DMA((2, chips, heads)),
            DMA((2, count, slots[0], heads)),
            DMA((2, count, slots[0], heads)),
            DMA((heads - 1,)),
            DMA((heads - 1,)),
            DMA((chips + 1,)),
            DMA((chips + 1,)),
            DMA((chips + 1,)),
            DMA((chips + 1,)),
        ],
        compiler_params=pltpu.CompilerParams(
            collective_id=number, has_side_effects=True, vmem_limit_bytes=63 << 20
        ),
        name="expert_turn",
    )(payload, c, w_down, *pieces)


def start_kernel(cube, heads, *refs):
    x_ref, slice_ref, unit_ref, column_ref, row_ref, x_out, dense_out, unit_out, slot_out = refs[:9]
    local, x_send, x_recv, line_send, line_recv, send, recv, unit_send, unit_recv = refs[9:]
    chips = cube.chips
    chip, core, hz = lax.axis_index("chip"), lax.axis_index("core"), lax.axis_index("head")
    others = near(heads)
    part_heads = heads // 2
    across_all = {"chip": flip(chip, chips - 1)}
    meet(
        [cube.peer(digit) for digit in range(cube.number)]
        + [{"head": (hz + d) % heads} for d in others]
        + [across_all]
    )
    unit_copy = pltpu.make_async_remote_copy(
        src_ref=unit_ref,
        dst_ref=unit_out,
        send_sem=unit_send,
        recv_sem=unit_recv,
        device_id=across_all,
        device_id_type=MESH,
    )
    middle = jnp.minimum(hz, heads - 1 - hz)

    def source(rank):
        if rank == 0:
            return hz
        far = (rank + 1) // 2
        near_one = hz - far if rank % 2 else hz + far
        far_one = jnp.where(hz < heads - 1 - hz, hz + (rank - middle), hz - (rank - middle))
        return jnp.where(rank <= 2 * middle, near_one, far_one)

    def x_copy(rank, step):
        head = source(rank)
        return pltpu.make_async_remote_copy(
            src_ref=x_ref if rank == 0 else x_out.at[:, head],
            dst_ref=x_out.at[:, head],
            send_sem=x_send.at[heads if rank == 0 and step < 0 else head],
            recv_sem=x_recv.at[head],
            device_id={"head": (hz + step + heads) % heads},
            device_id_type=MESH,
        )

    def along(rank, act):
        head = source(rank)
        goes_up = hz + 1 < heads
        goes_down = hz > 0
        if rank:
            goes_up = goes_up & (head < hz)
            goes_down = goes_down & (head > hz)

        @pl.when(goes_up)
        def _():
            act(x_copy(rank, 1))

        @pl.when(goes_down)
        def _():
            act(x_copy(rank, -1))

    def slice_copy(d):
        place = (hz + d) % heads
        return pltpu.make_async_remote_copy(
            src_ref=slice_ref.at[place],
            dst_ref=dense_out.at[chip, core, hz],
            send_sem=line_send.at[d - 1],
            recv_sem=line_recv.at[d - 1],
            device_id={"head": place},
            device_id_type=MESH,
        )

    def dense_copy(side, mask, k):
        order = cube.gather_orders[side]
        later = mask | (1 << order[k])
        place = dense_out.at[cube.place(mask) + (pl.ds(side * part_heads, part_heads),)]
        return pltpu.make_async_remote_copy(
            src_ref=place,
            dst_ref=place,
            send_sem=send.at[side, later],
            recv_sem=recv.at[side, later],
            device_id=cube.peer(order[k]),
            device_id_type=MESH,
        )

    def steps_after(side, mask):
        order = cube.gather_orders[side]
        last = max([k for k in range(cube.number) if (mask >> order[k]) & 1], default=-1)
        return range(last + 1, cube.number)

    def dense_turn(mask):
        for side in range(2):
            if mask:
                order = cube.gather_orders[side]
                k = max(k for k in range(cube.number) if (mask >> order[k]) & 1)
                dense_copy(side, mask & ~(1 << order[k]), k).wait_recv()
            for k in steps_after(side, mask):
                dense_copy(side, mask, k).start()

    locals_ = [
        pltpu.make_async_copy(slice_ref.at[hz], dense_out.at[chip, core, hz], local.at[0]),
        pltpu.make_async_copy(x_ref, x_out.at[:, hz], local.at[1]),
    ]
    def count_slots():
        row = row_ref[...]
        first = row // column_ref.shape[0] * column_ref.shape[0]
        total = jnp.zeros(row.shape, jnp.int32)
        step = LANES
        for begin in range(0, column_ref.shape[0], step):
            column = column_ref[pl.ds(begin, step), :]
            earlier = ((column < row) & (column >= first)).astype(jnp.int32)
            total = total + jnp.sum(earlier, axis=0, keepdims=True)
        slot_out[...] = total

    for d in others:
        slice_copy(d).start()
    for copy in locals_:
        copy.start()
    along(0, lambda copy: copy.start())
    locals_[0].wait()
    for d in others:
        slice_copy(d).wait_recv()
    dense_turn(0)
    masks = sorted(range(1, 2 * chips), key=lambda m: bin(m).count("1"))
    shares = [masks[len(masks) * i // heads : len(masks) * (i + 1) // heads] for i in range(heads)]
    for mask in shares[0]:
        dense_turn(mask)
    for rank in range(1, heads):
        x_copy(rank, 1).wait_recv()
        along(rank, lambda copy: copy.start())
        for mask in shares[rank]:
            dense_turn(mask)
        if rank == 1:
            unit_copy.start()
            count_slots()
    unit_copy.wait()
    locals_[1].wait()
    for rank in range(heads):
        along(rank, lambda copy: copy.wait_send())
    for d in others:
        slice_copy(d).wait_send()
    for mask in [0] + masks:
        for side in range(2):
            for k in steps_after(side, mask):
                dense_copy(side, mask, k).wait_send()


def start(x, slices, unit, keys, chips, heads, number):
    cube = Cube(chips, True)
    return pl.pallas_call(
        functools.partial(start_kernel, cube, heads),
        out_shape=(
            jax.ShapeDtypeStruct((x.shape[0], heads) + x.shape[1:], bf16),
            jax.ShapeDtypeStruct((chips, 2) + slices.shape, bf16),
            jax.ShapeDtypeStruct(unit.shape, bf16),
            jax.ShapeDtypeStruct((1, keys.size), jnp.int32),
        ),
        in_specs=[ANY] * 3 + [WHOLE] * 2,
        out_specs=(ANY,) * 3 + (WHOLE,),
        scratch_shapes=[
            DMA((2,)),
            DMA((heads + 1,)),
            DMA((heads,)),
            DMA((heads - 1,)),
            DMA((heads - 1,)),
            DMA((2, 2 * chips)),
            DMA((2, 2 * chips)),
            DMA,
            DMA,
        ],
        compiler_params=pltpu.CompilerParams(collective_id=number, has_side_effects=True),
        name="start",
    )(x, slices, unit, keys[:, None], keys[None, :])


def end_kernel(cube, heads, first_ref, in_ref, first_out, out_ref, *refs):
    count = cube.number
    arrived = refs[:count]
    parts = refs[count : 2 * count]
    local, first_send, first_recv, line_send, line_recv, send, recv = refs[2 * count :]
    hz = lax.axis_index("head")
    others = near(heads)[::-1]
    half = in_ref.shape[-2] // 2
    rows = in_ref.shape[-2] // heads
    meet([cube.peer(digit) for digit in range(count)] + [{"head": (hz + d) % heads} for d in others])
    own = pltpu.make_async_copy(first_ref.at[:, hz], first_out.at[hz], local)
    own.start()
    copies = {}

    def slot(side, k, mask):
        return subsets(cube.scatter_orders[side][k + 1 :]).index(mask)

    def mine(side, mask):
        return in_ref.at[cube.place(mask) + (pl.ds(side * half, half),)]

    def total(side, steps, mask):
        value = mine(side, mask)[...].astype(f32)
        for j in range(steps):
            copies[(side, j, mask)].wait_recv()
            value = value + arrived[j][side, slot(side, j, mask)].astype(f32)
        return value.astype(bf16)

    def first_copy(d):
        place = (hz + d) % heads
        return pltpu.make_async_remote_copy(
            src_ref=first_ref.at[:, place],
            dst_ref=first_out.at[hz],
            send_sem=first_send.at[d - 1],
            recv_sem=first_recv.at[d - 1],
            device_id={"head": place},
            device_id_type=MESH,
        )

    for k in range(count):
        for side in range(2):
            order = cube.scatter_orders[side]
            for mask in subsets(order[k + 1 :])[::-1]:
                full = mask | (1 << order[k])
                where = slot(side, k, mask)
                if k == 0:
                    piece = mine(side, full)
                else:
                    piece = parts[k - 1].at[side, where]
                    piece[...] = total(side, k, full)
                copies[(side, k, mask)] = pltpu.make_async_remote_copy(
                    src_ref=piece,
                    dst_ref=arrived[k].at[side, where],
                    send_sem=send.at[side, k, where],
                    recv_sem=recv.at[side, k, where],
                    device_id=cube.peer(order[k]),
                    device_id_type=MESH,
                )
                copies[(side, k, mask)].start()
        if k == 0:
            for d in others:
                first_copy(d).start()
    done = parts[count - 1]
    for side in range(2):
        done[0, pl.ds(side * half, half)] = total(side, count, 0)

    def line_copy(d):
        place = (hz + d) % heads
        return pltpu.make_async_remote_copy(
            src_ref=done.at[0, pl.ds(pl.multiple_of(place * rows, 16), rows)],
            dst_ref=out_ref.at[hz],
            send_sem=line_send.at[d - 1],
            recv_sem=line_recv.at[d - 1],
            device_id={"head": place},
            device_id_type=MESH,
        )

    for d in others:
        line_copy(d).start()
    out_ref[hz] = done[0, pl.ds(pl.multiple_of(hz * rows, 16), rows)]
    for copy in copies.values():
        copy.wait_send()
    own.wait()
    for d in others:
        line_copy(d).wait()
    for d in others:
        first_copy(d).wait()


def end(first, sums, chips, heads, number):
    rows, columns = sums.shape[-2:]
    cube = Cube(chips, True)
    count = cube.number
    half = rows // 2
    slots = [(1 << count) >> (k + 1) for k in range(count)]
    return pl.pallas_call(
        functools.partial(end_kernel, cube, heads),
        out_shape=(
            jax.ShapeDtypeStruct((heads, first.shape[0]) + first.shape[2:], bf16),
            jax.ShapeDtypeStruct((heads, rows // heads, columns), bf16),
        ),
        in_specs=[ANY, WHOLE],
        out_specs=(ANY, WHOLE),
        scratch_shapes=[pltpu.VMEM((2, s, half, columns), bf16) for s in slots]
        + [pltpu.VMEM((2, s, half, columns), bf16) for s in slots[1:]]
        + [
            pltpu.VMEM((1, rows, columns), bf16),
            DMA,
            DMA((heads - 1,)),
            DMA((heads - 1,)),
            DMA((heads - 1,)),
            DMA((heads - 1,)),
            DMA((2, count, slots[0])),
            DMA((2, count, slots[0])),
        ],
        compiler_params=pltpu.CompilerParams(
            collective_id=number, has_side_effects=True, vmem_limit_bytes=40 << 20
        ),
        name="end",
    )(first, sums)


def place_kernel(chips, hidden, *refs):
    pieces, out_ref = refs[:chips], refs[chips]
    chip = lax.axis_index("chip")
    units = out_ref.shape[2] // 2
    for mask in range(chips):
        for part in range(2):
            begin = pl.multiple_of(part * units + flip(chip, mask) * hidden, hidden)
            out_ref[:, :, pl.ds(begin, hidden)] = pieces[mask][
                :, :, pl.ds(part * hidden, hidden)
            ].astype(f32)


def place_units(pieces, hidden):
    chips = len(pieces)
    experts_here, rows, double = pieces[0].shape
    group = 2 if experts_here % 2 == 0 else 1
    return pl.pallas_call(
        functools.partial(place_kernel, chips, hidden),
        grid=(experts_here // group,),
        out_shape=jax.ShapeDtypeStruct((experts_here, rows, chips * double), f32),
        in_specs=[pl.BlockSpec((group, rows, double), lambda e: (e, 0, 0))] * chips,
        out_specs=pl.BlockSpec((group, rows, chips * double), lambda e: (e, 0, 0)),
        name="place_units",
    )(*pieces)


def across(value, chips, mask):
    if mask == 0:
        return value
    return lax.ppermute(value, "chip", [(i, i ^ mask) for i in range(chips)])


class LineGather:
    def __init__(self, cube, heads, own, out, sems):
        self.cube, self.heads, self.own, self.out = cube, heads, own, out
        self.local, self.line_send, self.line_recv, self.send, self.recv = sems
        self.hz = lax.axis_index("head")
        self.middle = jnp.minimum(self.hz, heads - 1 - self.hz)
        self.rows = own.shape[0]

    @staticmethod
    def scratch(cube, heads):
        return [
            DMA,
            DMA((heads + 1,)),
            DMA((heads,)),
            DMA((2, 1 << cube.number, heads)),
            DMA((2, 1 << cube.number, heads)),
        ]

    def source(self, rank):
        hz, heads, middle = self.hz, self.heads, self.middle
        if rank == 0:
            return hz
        far = (rank + 1) // 2
        near_one = hz - far if rank % 2 else hz + far
        far_one = jnp.where(hz < heads - 1 - hz, hz + (rank - middle), hz - (rank - middle))
        return jnp.where(rank <= 2 * middle, near_one, far_one)

    def line_copy(self, rank, step):
        head = self.source(rank)
        place = self.out.at[self.cube.place(0) + (head,)]
        return pltpu.make_async_remote_copy(
            src_ref=self.own if rank == 0 else place,
            dst_ref=place,
            send_sem=self.line_send.at[self.heads if rank == 0 and step < 0 else head],
            recv_sem=self.line_recv.at[head],
            device_id={"head": (self.hz + step + self.heads) % self.heads},
            device_id_type=MESH,
        )

    def along(self, rank, act):
        head = self.source(rank)
        goes_up = self.hz + 1 < self.heads
        goes_down = self.hz > 0
        if rank:
            goes_up = goes_up & (head < self.hz)
            goes_down = goes_down & (head > self.hz)

        @pl.when(goes_up)
        def _():
            act(self.line_copy(rank, 1))

        @pl.when(goes_down)
        def _():
            act(self.line_copy(rank, -1))

    def plane_copy(self, side, mask, k, rank):
        digit = self.cube.gather_orders[side][k]
        later = mask | (1 << digit)
        head = self.source(rank)
        part = part_of(self.rows, side)
        place = self.out.at[self.cube.place(mask) + (head, part)]
        return pltpu.make_async_remote_copy(
            src_ref=self.own.at[part] if mask == 0 and rank == 0 else place,
            dst_ref=place,
            send_sem=self.send.at[side, later, head],
            recv_sem=self.recv.at[side, later, head],
            device_id=self.cube.peer(digit),
            device_id_type=MESH,
        )

    def steps_after(self, side, mask):
        order = self.cube.gather_orders[side]
        last = max([k for k in range(self.cube.number) if (mask >> order[k]) & 1], default=-1)
        return range(last + 1, self.cube.number)

    def begin(self):
        self.own_copy = pltpu.make_async_copy(
            self.own, self.out.at[self.cube.place(0) + (self.hz,)], self.local
        )
        self.own_copy.start()

    def receive(self, mask, rank):
        if mask == 0:
            if rank:
                self.line_copy(rank, 1).wait_recv()
            self.along(rank, lambda copy: copy.start())
        for side in range(2):
            if mask:
                order = self.cube.gather_orders[side]
                k = max(k for k in range(self.cube.number) if (mask >> order[k]) & 1)
                self.plane_copy(side, mask & ~(1 << order[k]), k, rank).wait_recv()
            for k in self.steps_after(side, mask):
                self.plane_copy(side, mask, k, rank).start()

    def events(self):
        masks = sorted(range(1 << self.cube.number), key=lambda m: bin(m).count("1"))
        return [(mask, rank) for mask in masks for rank in range(self.heads)]

    def finish(self):
        self.own_copy.wait()
        for mask, rank in self.events():
            if mask == 0:
                self.along(rank, lambda copy: copy.wait_send())
            for side in range(2):
                for k in self.steps_after(side, mask):
                    self.plane_copy(side, mask, k, rank).wait_send()


class DenseGather:
    def __init__(self, cube, heads, own, out, sems):
        self.cube, self.heads, self.own, self.out = cube, heads, own, out
        self.local, self.line_send, self.line_recv, self.send, self.recv = sems
        self.hz = lax.axis_index("head")

    @staticmethod
    def scratch(cube, heads):
        return [
            DMA,
            DMA((heads - 1,)),
            DMA((heads - 1,)),
            DMA((2, 1 << cube.number)),
            DMA((2, 1 << cube.number)),
        ]

    def line_copy(self, d):
        return pltpu.make_async_remote_copy(
            src_ref=self.own,
            dst_ref=self.out.at[self.cube.place(0) + (self.hz,)],
            send_sem=self.line_send.at[d - 1],
            recv_sem=self.line_recv.at[d - 1],
            device_id={"head": (self.hz + d) % self.heads},
            device_id_type=MESH,
        )

    def flat_copy(self, side, mask, k):
        digit = self.cube.gather_orders[side][k]
        later = mask | (1 << digit)
        part = self.heads // 2
        place = self.out.at[self.cube.place(mask) + (pl.ds(side * part, part),)]
        return pltpu.make_async_remote_copy(
            src_ref=place,
            dst_ref=place,
            send_sem=self.send.at[side, later],
            recv_sem=self.recv.at[side, later],
            device_id=self.cube.peer(digit),
            device_id_type=MESH,
        )

    def steps_after(self, side, mask):
        order = self.cube.gather_orders[side]
        last = max([k for k in range(self.cube.number) if (mask >> order[k]) & 1], default=-1)
        return range(last + 1, self.cube.number)

    def begin(self):
        self.own_copy = pltpu.make_async_copy(
            self.own, self.out.at[self.cube.place(0) + (self.hz,)], self.local
        )
        self.own_copy.start()
        for d in near(self.heads)[::-1]:
            self.line_copy(d).start()

    def events(self):
        return [(mask, 2) for mask in range(1 << self.cube.number)]

    def receive(self, mask, _):
        if mask == 0:
            self.own_copy.wait()
            for d in near(self.heads):
                self.line_copy(d).wait_recv()
        for side in range(2):
            if mask:
                order = self.cube.gather_orders[side]
                k = max(k for k in range(self.cube.number) if (mask >> order[k]) & 1)
                self.flat_copy(side, mask & ~(1 << order[k]), k).wait_recv()
            for k in self.steps_after(side, mask):
                self.flat_copy(side, mask, k).start()

    def finish(self):
        for d in near(self.heads):
            self.line_copy(d).wait_send()
        for mask in range(1 << self.cube.number):
            for side in range(2):
                for k in self.steps_after(side, mask):
                    self.flat_copy(side, mask, k).wait_send()


class LineSums:
    def __init__(self, cube, heads, blocks, out, refs):
        self.cube, self.heads, self.blocks, self.out = cube, heads, blocks, out
        count = cube.number
        self.arrived, self.parts = refs[:count], refs[count : 2 * count - 1]
        self.line_out, self.line_in, self.send, self.recv, self.end_send, self.end_recv = refs[
            2 * count - 1 :
        ]
        self.hz = lax.axis_index("head")
        self.rows = blocks.shape[-2]
        self.outward = near(heads)[::-1] + [0]
        self.turns = heads + count + 1

    @staticmethod
    def scratch(cube, heads, rows, columns):
        count = cube.number
        slots = [(1 << count) >> (k + 1) for k in range(count)]
        half = cut_rows(rows)
        return (
            [pltpu.VMEM((2, s, heads, half, columns), bf16) for s in slots]
            + [pltpu.VMEM((2, s, heads, half, columns), bf16) for s in slots[1:]]
            + [
                pltpu.VMEM((heads - 1, rows, columns), bf16),
                pltpu.VMEM((heads - 1, rows, columns), bf16),
                DMA((2, count, slots[0], heads)),
                DMA((2, count, slots[0], heads)),
                DMA((heads - 1,)),
                DMA((heads - 1,)),
            ]
        )

    def slot(self, side, k, mask):
        return subsets(self.cube.scatter_orders[side][k + 1 :]).index(mask)

    def mine(self, side, mask, d):
        place = self.cube.place(mask) + ((self.hz + d) % self.heads,)
        return self.blocks.at[place + (part_of(self.rows, side),)]

    def there(self, ref, side, where, d):
        return ref.at[side, where, d, pl.ds(0, part_of(self.rows, side).size)]

    def copy_of(self, side, k, mask, d):
        order = self.cube.scatter_orders[side]
        where = self.slot(side, k, mask)
        if k == 0:
            piece = self.mine(side, mask | (1 << order[0]), d)
        else:
            piece = self.there(self.parts[k - 1], side, where, d)
        return pltpu.make_async_remote_copy(
            src_ref=piece,
            dst_ref=self.there(self.arrived[k], side, where, d),
            send_sem=self.send.at[side, k, where, d],
            recv_sem=self.recv.at[side, k, where, d],
            device_id=self.cube.peer(order[k]),
            device_id_type=MESH,
        )

    def end_copy(self, d):
        return pltpu.make_async_remote_copy(
            src_ref=self.line_out.at[d - 1],
            dst_ref=self.line_in.at[d - 1],
            send_sem=self.end_send.at[d - 1],
            recv_sem=self.end_recv.at[d - 1],
            device_id={"head": (self.hz + d) % self.heads},
            device_id_type=MESH,
        )

    def sums(self, side, steps, mask, d):
        value = self.mine(side, mask, d)[...].astype(f32)
        for j in range(steps):
            self.copy_of(side, j, mask, d).wait_recv()
            value = value + self.there(self.arrived[j], side, self.slot(side, j, mask), d)[
                ...
            ].astype(f32)
        return value

    def turn(self, turn):
        count = self.cube.number
        if turn < self.heads:
            for side in range(2):
                for mask in subsets(self.cube.scatter_orders[side][1:])[::-1]:
                    self.copy_of(side, 0, mask, self.outward[turn]).start()
        for k in range(1, count):
            if 0 <= turn - k - 1 < self.heads:
                d = self.outward[turn - k - 1]
                for side in range(2):
                    order = self.cube.scatter_orders[side]
                    for mask in subsets(order[k + 1 :])[::-1]:
                        value = self.sums(side, k, mask | (1 << order[k]), d)
                        place = self.there(self.parts[k - 1], side, self.slot(side, k, mask), d)
                        place[...] = value.astype(bf16)
                        self.copy_of(side, k, mask, d).start()
        if 0 <= turn - count - 1 < self.heads:
            d = self.outward[turn - count - 1]
            for side in range(2):
                value = self.sums(side, count, 0, d)
                part = part_of(self.rows, side)
                if d:
                    self.line_out[d - 1, part] = value.astype(bf16)
                else:
                    self.out[part] = value
            if d:
                self.end_copy(d).start()

    def finish(self):
        others = near(self.heads)
        for d in others:
            self.end_copy(d).wait_recv()
            self.out[...] += self.line_in[d - 1].astype(f32)
        for d in others:
            self.end_copy(d).wait_send()
        for side in range(2):
            for k in range(self.cube.number):
                for mask in subsets(self.cube.scatter_orders[side][k + 1 :]):
                    for d in self.outward:
                        self.copy_of(side, k, mask, d).wait_send()


TN = (((0,), (0,)), ((), ()))


def allowed(key_segments, query_segments, block, rows, seq):
    columns = query_segments.shape[1]
    key_place = block * rows + lax.broadcasted_iota(jnp.int32, (rows, columns), 0)
    query_place = seq * rows + lax.broadcasted_iota(jnp.int32, (rows, columns), 1) % rows
    return (key_segments == query_segments) & (key_place <= query_place)


def attend_kernel(cube, heads, group, beside, *refs):
    q_ref, kv_ref, key_seg, query_seg = refs[:4]
    near_refs, refs = refs[4 : 4 + len(beside)], refs[4 + len(beside) :]
    lines_ref, kv_out, out_turned, lse_ref = refs[:4]
    far_refs, refs = refs[4 : 4 + len(beside)], refs[4 + len(beside) :]
    stage, top, total, acc, send, recv, line_send, line_recv = refs[:8]
    chip, core, hz = lax.axis_index("chip"), lax.axis_index("core"), lax.axis_index("head")
    seq = chip * 2 + core
    others = near(heads)[::-1]
    batch, rows, columns = kv_ref.shape
    kv_heads = columns // (2 * HEAD_WIDTH)
    part = rows // 2
    meet([cube.peer(digit) for digit in range(cube.number)] + [{"head": (hz + d) % heads} for d in others])
    kv_out[chip, core] = kv_ref[...]
    gathers = []
    rest_refs = refs[8:]
    for with_core, own_block, all_blocks in zip(beside, near_refs, far_refs):
        kind = DenseGather if with_core else LineGather
        own_cube = Cube(cube.chips, with_core)
        gathers.append(kind(own_cube, heads, own_block, all_blocks, rest_refs[:5]))
        rest_refs = rest_refs[5:]
    fronts = {}
    for one in gathers:
        for mask, rank in one.events():
            fronts.setdefault(rank + bin(mask).count("1"), []).append((one, (mask, rank)))
    last_front = max(fronts, default=0)
    now = cube.number + 1

    def pass_front(index):
        for one, event in fronts.get(index, []):
            one.receive(*event)

    def copy_of(side, mask, k):
        order = cube.gather_orders[side]
        later = mask | (1 << order[k])
        place = cube.place(mask) + (slice(None), pl.ds(side * part, part))
        return pltpu.make_async_remote_copy(
            src_ref=kv_ref.at[:, pl.ds(side * part, part)] if mask == 0 else kv_out.at[place],
            dst_ref=kv_out.at[place],
            send_sem=send.at[side, later],
            recv_sem=recv.at[side, later],
            device_id=cube.peer(order[k]),
            device_id_type=MESH,
        )

    copies = []

    def forward(mask):
        for side in range(2):
            order = cube.gather_orders[side]
            last = max([k for k in range(cube.number) if (mask >> order[k]) & 1], default=-1)
            if mask:
                copy_of(side, mask & ~(1 << order[last]), last).wait_recv()
            for k in range(last + 1, cube.number):
                copy_of(side, mask, k).start()
                copies.append((side, mask, k))

    forward(0)
    for one in gathers:
        one.begin()
    pass_front(0)
    top[...] = jnp.full_like(top, negative)
    total[...] = jnp.zeros_like(total)
    acc[...] = jnp.zeros_like(acc)

    def block_step(block):
        place = (block // 2, block % 2)
        for b in range(batch):
            mask = allowed(
                key_seg[b, pl.ds(pl.multiple_of(block * rows, rows), rows), :],
                query_seg[b],
                block,
                rows,
                seq,
            )
            for j in range(kv_heads):
                pair = b * kv_heads + j
                begin = j * 2 * HEAD_WIDTH
                keys = kv_out[place + (b, slice(None), pl.ds(begin, HEAD_WIDTH))]
                values = kv_out[place + (b, slice(None), pl.ds(begin + HEAD_WIDTH, HEAD_WIDTH))]
                scores = lax.dot_general(keys, q_ref[pair], NT, preferred_element_type=f32)
                scores = jnp.where(mask, scores, negative)
                new = jnp.maximum(top[pair], jnp.max(scores, axis=0, keepdims=True))
                weights = jnp.exp(scores - new)
                shrink = jnp.exp(top[pair] - new)
                top[pair] = new
                total[pair] = total[pair] * shrink + jnp.sum(weights, axis=0, keepdims=True)
                acc[pair] = acc[pair] * shrink + lax.dot_general(
                    values, weights.astype(bf16), TN, preferred_element_type=f32
                )

    block_step(seq)
    for level in range(1, cube.number + 1):
        for mask in range(1, 1 << cube.number):
            if bin(mask).count("1") == level:
                forward(mask)
    pass_front(1)
    now = 2
    turns = 2 * cube.chips
    if beside:
        for turn in range(turns):
            if turn == turns // 2:
                pass_front(now)
                now += 1

            @pl.when(turn < seq)
            def _():
                block_step(turn)

    else:

        @pl.loop(0, seq)
        def _(block):
            block_step(block)

    spot = rows // heads
    for b in range(batch):
        for j in range(kv_heads):
            pair = b * kv_heads + j
            value = acc[pair] / total[pair]
            out_turned[pair] = value
            lse_ref[pair] = top[pair] + jnp.log(total[pair])
            value = value.T.astype(bf16)
            for g in range(group):
                for head in range(heads):
                    begin = (j * group + g) * HEAD_WIDTH
                    stage[head, pl.ds(b * spot, spot), pl.ds(begin, HEAD_WIDTH)] = value[
                        g * rows + head * spot : g * rows + (head + 1) * spot
                    ]

    def line_copy(d):
        return pltpu.make_async_remote_copy(
            src_ref=stage.at[(hz + d) % heads],
            dst_ref=lines_ref.at[hz],
            send_sem=line_send.at[d - 1],
            recv_sem=line_recv.at[d - 1],
            device_id={"head": (hz + d) % heads},
            device_id_type=MESH,
        )

    for d in others:
        line_copy(d).start()
    lines_ref[hz] = stage[hz]
    for index in range(now, last_front + 1):
        pass_front(index)
    for side, mask, k in copies:
        copy_of(side, mask, k).wait_send()
    for d in others:
        line_copy(d).wait()
    for one in gathers:
        one.finish()


def attend(queries, keys_values, key_seg, query_seg, beside, chips, heads, group, number):
    batch, rows, columns = keys_values.shape
    pairs, wide, depth = queries.shape
    cube = Cube(chips, True)
    group_columns = group * columns // 2
    tokens = batch * rows // heads
    return pl.pallas_call(
        functools.partial(attend_kernel, cube, heads, group, [core for _, core in beside]),
        out_shape=(
            jax.ShapeDtypeStruct((heads, tokens, group_columns), bf16),
            jax.ShapeDtypeStruct((chips, 2, batch, rows, columns), bf16),
            jax.ShapeDtypeStruct((pairs, depth, wide), f32),
            jax.ShapeDtypeStruct((pairs, 1, wide), f32),
        )
        + tuple(
            jax.ShapeDtypeStruct((chips,) + (2,) * with_core + (heads,) + value.shape, bf16)
            for value, with_core in beside
        ),
        in_specs=[WHOLE] * 4 + [ANY] * len(beside),
        out_specs=(WHOLE,) * 4 + (ANY,) * len(beside),
        scratch_shapes=[
            pltpu.VMEM((heads, tokens, group_columns), bf16),
            pltpu.VMEM((pairs, 1, wide), f32),
            pltpu.VMEM((pairs, 1, wide), f32),
            pltpu.VMEM((pairs, depth, wide), f32),
            DMA((2, 2 * chips)),
            DMA((2, 2 * chips)),
            DMA((heads - 1,)),
            DMA((heads - 1,)),
        ]
        + [
            item
            for _, core in beside
            for item in (DenseGather if core else LineGather).scratch(Cube(chips, core), heads)
        ],
        compiler_params=pltpu.CompilerParams(
            collective_id=number, has_side_effects=True, vmem_limit_bytes=50 << 20
        ),
        name="attend",
    )(queries, keys_values, key_seg, query_seg, *[value for value, _ in beside])


def attend_back_kernel(cube, heads, group, beside, shares, *refs):
    q_ref, kv_ref, key_seg, query_seg, out_turned, lse_ref, dh_ref = refs[:7]
    near_refs, refs = refs[7 : 7 + len(beside)], refs[7 + len(beside) :]
    pair_refs, refs = refs[:shares], refs[shares:]
    dq_ref, dkv_ref = refs[:2]
    far_refs, refs = refs[2 : 2 + len(beside)], refs[2 + len(beside) :]
    added = refs[: cube.chips] if shares else ()
    refs = (None,) * 9 + refs[len(added) :]
    count = cube.number
    landed, d_out, delta, dq_turned, grads = refs[9:14]
    arrived, parts = refs[14 : 14 + count], refs[14 + count : 13 + 2 * count]
    send, recv, line_send, line_recv = refs[13 + 2 * count : 17 + 2 * count]
    turns = 2 * cube.chips
    rest = refs[17 + 2 * count :]
    sums_beside = []
    for with_core, source, target in zip(beside, near_refs, far_refs):
        own_cube = Cube(cube.chips, with_core)
        size = 2 * own_cube.number + 5
        sums_beside.append(LineSums(own_cube, heads, source, target, rest[:size]))
        rest = rest[size:]

    def load_pair(mask):
        place = flip(lax.axis_index("chip"), mask)
        return [
            pltpu.make_async_copy(pair_refs[i].at[place], rest[i], rest[3].at[i]) for i in range(2)
        ]

    def store_sum(mask):
        return pltpu.make_async_copy(rest[2], added[mask], rest[3].at[2])

    def add_pair(turn):
        mask = turn // 2
        if turn % 2 == 0:
            for copy in load_pair(mask):
                copy.start()
            return
        for copy in load_pair(mask):
            copy.wait()
        if mask:
            store_sum(mask - 1).wait()
        rest[2][...] = (rest[0][...].astype(f32) + rest[1][...].astype(f32)).astype(bf16)
        store_sum(mask).start()

    chip, core, hz = lax.axis_index("chip"), lax.axis_index("core"), lax.axis_index("head")
    seq = chip * 2 + core
    others = near(heads)[::-1]
    batch, rows, columns = kv_ref.shape[2:]
    kv_heads = columns // (2 * HEAD_WIDTH)
    spot = rows // heads
    half = grads.shape[2] // 2
    meet([cube.peer(digit) for digit in range(count)] + [{"head": (hz + d) % heads} for d in others])

    def line_copy(d):
        return pltpu.make_async_remote_copy(
            src_ref=dh_ref.at[(hz + d) % heads],
            dst_ref=landed.at[hz],
            send_sem=line_send.at[d - 1],
            recv_sem=line_recv.at[d - 1],
            device_id={"head": (hz + d) % heads},
            device_id_type=MESH,
        )

    for d in others:
        line_copy(d).start()
    for turn in range(2):
        for one in sums_beside:
            one.turn(turn)
    landed[hz] = dh_ref[hz]
    grads[...] = jnp.zeros_like(grads)
    dq_turned[...] = jnp.zeros_like(dq_turned)
    for d in others:
        line_copy(d).wait()
    for b in range(batch):
        for j in range(kv_heads):
            pair = b * kv_heads + j
            for g in range(group):
                for head in range(heads):
                    begin = (j * group + g) * HEAD_WIDTH
                    d_out[pair, pl.ds(g * rows + head * spot, spot), :] = landed[
                        head, pl.ds(b * spot, spot), pl.ds(begin, HEAD_WIDTH)
                    ]
            delta[pair] = jnp.sum(
                d_out[pair].astype(f32).T * out_turned[pair], axis=0, keepdims=True
            )

    def block_step(block):
        place = (block // 2, block % 2)
        for b in range(batch):
            mask = allowed(
                key_seg[b, pl.ds(pl.multiple_of(block * rows, rows), rows), :],
                query_seg[b],
                block,
                rows,
                seq,
            )
            for j in range(kv_heads):
                pair = b * kv_heads + j
                begin = j * 2 * HEAD_WIDTH
                keys = kv_ref[place + (b, slice(None), pl.ds(begin, HEAD_WIDTH))]
                values = kv_ref[place + (b, slice(None), pl.ds(begin + HEAD_WIDTH, HEAD_WIDTH))]
                scores = lax.dot_general(keys, q_ref[pair], NT, preferred_element_type=f32)
                probs = jnp.exp(jnp.where(mask, scores, negative) - lse_ref[pair])
                d_probs = lax.dot_general(values, d_out[pair], NT, preferred_element_type=f32)
                d_scores = (probs * (d_probs - delta[pair])).astype(bf16)
                dq_turned[pair] += lax.dot_general(
                    keys, d_scores, TN, preferred_element_type=f32
                )
                d_keys = jnp.dot(d_scores, q_ref[pair], preferred_element_type=f32)
                d_values = jnp.dot(probs.astype(bf16), d_out[pair], preferred_element_type=f32)
                grads[place + (pl.ds(b * rows, rows), pl.ds(begin, 2 * HEAD_WIDTH))] = (
                    jnp.concatenate([d_keys, d_values], axis=1).astype(bf16)
                )

    done = 2
    if beside:
        for turn in range(turns):

            @pl.when(turn <= seq)
            def _():
                block_step(turn)

            if shares:
                add_pair(turn)
            if turn % 3 == 2:
                for one in sums_beside:
                    one.turn(done)
                done += 1

    else:

        @pl.loop(0, seq + 1)
        def _(block):
            block_step(block)

    def slot(side, k, mask):
        return subsets(cube.scatter_orders[side][k + 1 :]).index(mask)

    def mine(side, mask):
        return grads.at[cube.place(mask) + (pl.ds(side * half, half),)]

    copies = {}

    def sums(side, steps, mask):
        value = mine(side, mask)[...].astype(f32)
        for j in range(steps):
            copies[(side, j, mask)].wait_recv()
            value = value + arrived[j][side, slot(side, j, mask)].astype(f32)
        return value

    for k in range(count):
        for side in range(2):
            order = cube.scatter_orders[side]
            for mask in subsets(order[k + 1 :])[::-1]:
                full = mask | (1 << order[k])
                where = slot(side, k, mask)
                if k == 0:
                    piece = mine(side, full)
                else:
                    piece = parts[k - 1].at[side, where]
                    piece[...] = sums(side, k, full).astype(bf16)
                copies[(side, k, mask)] = pltpu.make_async_remote_copy(
                    src_ref=piece,
                    dst_ref=arrived[k].at[side, where],
                    send_sem=send.at[side, k, where],
                    recv_sem=recv.at[side, k, where],
                    device_id=cube.peer(order[k]),
                    device_id_type=MESH,
                )
                copies[(side, k, mask)].start()
        for one in sums_beside:
            if done < one.turns:
                one.turn(done)
        done += 1
    scale = HEAD_WIDTH ** (-0.5)
    for pair in range(batch * kv_heads):
        dq_ref[pair] = (dq_turned[pair] * scale).T.astype(bf16)
    for side in range(2):
        dkv_ref[pl.ds(side * half, half)] = sums(side, count, 0)
    for turn in range(done, max([one.turns for one in sums_beside], default=0)):
        for one in sums_beside:
            if turn < one.turns:
                one.turn(turn)
    for copy in copies.values():
        copy.wait_send()
    for one in sums_beside:
        one.finish()
    if shares:
        store_sum(cube.chips - 1).wait()


def attend_back(
    queries, kv_all, key_seg, query_seg, out_turned, lse, d_heads, beside, shares, heads, group, number
):
    chips, _, batch, rows, columns = kv_all.shape
    pairs, wide, depth = queries.shape
    cube = Cube(chips, True)
    count = cube.number
    half = batch * rows // 2
    slots = [(1 << count) >> (k + 1) for k in range(count)]
    return pl.pallas_call(
        functools.partial(
            attend_back_kernel, cube, heads, group, [core for _, core in beside], len(shares)
        ),
        out_shape=(
            jax.ShapeDtypeStruct((pairs, wide, depth), bf16),
            jax.ShapeDtypeStruct((batch * rows, columns), f32),
        )
        + tuple(jax.ShapeDtypeStruct(value.shape[-2:], f32) for value, _ in beside)
        + tuple(jax.ShapeDtypeStruct(shares[0].shape[1:], bf16) for _ in range(chips) if shares),
        in_specs=[WHOLE] * (7 + len(beside)) + [ANY] * len(shares),
        out_specs=(WHOLE,) * (2 + len(beside)) + (ANY,) * (chips * bool(shares)),
        scratch_shapes=[
            pltpu.VMEM(d_heads.shape, bf16),
            pltpu.VMEM((pairs, wide, depth), bf16),
            pltpu.VMEM((pairs, 1, wide), f32),
            pltpu.VMEM((pairs, depth, wide), f32),
            pltpu.VMEM((chips, 2, batch * rows, columns), bf16),
        ]
        + [pltpu.VMEM((2, s, half, columns), bf16) for s in slots]
        + [pltpu.VMEM((2, s, half, columns), bf16) for s in slots[1:]]
        + [
            DMA((2, count, slots[0])),
            DMA((2, count, slots[0])),
            DMA((heads - 1,)),
            DMA((heads - 1,)),
        ]
        + [
            item
            for value, core in beside
            for item in LineSums.scratch(Cube(chips, core), *value.shape[-3:])
        ]
        + [pltpu.VMEM(shares[0].shape[1:], bf16) for _ in range(3) if shares]
        + [DMA((3,)) for _ in range(1) if shares],
        compiler_params=pltpu.CompilerParams(
            collective_id=number, has_side_effects=True, vmem_limit_bytes=56 << 20
        ),
        name="attend_back",
    )(
        queries, kv_all, key_seg, query_seg, out_turned, lse, d_heads, *[v for v, _ in beside], *shares
    )


def sibling(value):
    return lax.ppermute(value, "core", [(0, 1), (1, 0)])


def per_device(
    layer_input,
    segments,
    routes,
    pair_rank,
    query_key_value_weight,
    output_weight,
    router_weight,
    norm_attn,
    norm_ffn,
    w_gate_up,
    w_down,
    cotangent,
):
    chips = lax.axis_size("chip")
    head_number = lax.axis_size("head")
    sequence_batch, token_rows, width = layer_input.shape
    length = segments.shape[1]
    blk = token_rows * head_number
    query_group = QUERY_HEADS // KEY_VALUE_HEADS
    key_value_location = KEY_VALUE_HEADS // head_number
    loc_experts, slice_rows = w_gate_up.shape[:2]
    top = routes.shape[2]
    tokens_present = sequence_batch * token_rows
    pairs = tokens_present * top
    line_tokens = tokens_present * head_number
    scale = HEAD_WIDTH ** (-0.5)
    hidden = FF // chips
    loc_columns = key_value_location * (query_group + 2) * HEAD_WIDTH
    chip = lax.axis_index("chip")
    core = lax.axis_index("core")
    head = lax.axis_index("head")
    seq_index = chip * 2 + core
    dense_rows = query_key_value_weight.shape[0]

    extras = jnp.concatenate([router_weight, norm_attn[:, None], norm_ffn[:, None]], axis=1)
    extras = jnp.pad(extras, ((0, 0), (0, LANES - extras.shape[1])))
    slices = query_key_value_weight.reshape(dense_rows, head_number, loc_columns).transpose(1, 0, 2)
    slices = jnp.concatenate(
        [slices, jnp.broadcast_to(extras, (head_number,) + extras.shape)], axis=2
    )
    group_tokens = chips * head_number * tokens_present
    columns = width + LANES
    fused = hidden % LANES == 0 and group_tokens <= 2048
    own_tokens = layer_input.reshape(tokens_present, width)
    cots = cotangent.reshape(tokens_present, width)
    if fused:

        def unit_of(weights, mask):
            begins = [part * FF + (chip ^ mask) * hidden for part in range(2)]
            cut = [lax.dynamic_slice_in_dim(weights, begin, hidden, 2) for begin in begins]
            return jnp.concatenate(cut, axis=2)

        keys = (routes * pairs + pair_rank).reshape(pairs)
        x_line, dense, last_unit, slot = start(
            layer_input, slices, unit_of(w_gate_up, chips - 1), keys, chips, head_number, 1
        )
        x_line, w_gate_up = lax.optimization_barrier((x_line, w_gate_up))
        units = [across(unit_of(w_gate_up, mask), chips, mask) for mask in range(chips - 1)]
        units.append(last_unit)
        dense = dense.reshape(width, loc_columns + LANES)
    else:
        parts = w_gate_up.reshape(loc_experts, slice_rows, 2, chips, hidden).transpose(3, 2, 1, 0, 4)
        parts = parts.reshape(chips, 2, slice_rows, loc_experts * hidden)
        piled = jnp.zeros((chips, 2, 2, slice_rows, loc_experts * hidden), bf16)
        for mask in range(chips):
            piece = lax.dynamic_index_in_dim(parts, chip ^ mask, 0, keepdims=False)
            piece = across(piece, chips, mask)
            other = sibling(piece)
            piled = lax.dynamic_update_slice(piled, piece[None, None], (chip ^ mask, core, 0, 0, 0))
            piled = lax.dynamic_update_slice(piled, other[None, None], (chip ^ mask, 1 - core, 0, 0, 0))
        piled = piled.transpose(2, 0, 1, 3, 4).reshape(2, width, loc_experts * hidden)
        expert_gate, expert_up = piled[0], piled[1]
        down_other = sibling(w_down)
        expert_down = (
            jnp.where(
                core == 0,
                jnp.concatenate([w_down, down_other], axis=1),
                jnp.concatenate([down_other, w_down], axis=1),
            )
        ).reshape(loc_experts * hidden, width)

        lined = line_exchange(slices, head_number, 1)
        dense = gather(
            lined.reshape(head_number * dense_rows, loc_columns + LANES), chips, 1, True, 2
        ).reshape(width, loc_columns + LANES)
        x_line = line_exchange(layer_input.reshape(tokens_present, width), head_number, 3, True)

    if not fused:
        grad_all = lax.all_gather(cots, ("chip", "head"), axis=0, tiled=True)
        dense_out = lax.all_gather(output_weight, ("chip", "core", "head"), axis=0, tiled=True)

    dense_qkv = dense[:, :loc_columns]
    dense_router = dense[:, loc_columns : loc_columns + EXPERTS]
    gain_attn = dense[:, loc_columns + EXPERTS].astype(f32)
    gain_ffn = dense[:, loc_columns + EXPERTS + 1].astype(f32)

    x_line = x_line.reshape(line_tokens, width).astype(f32)
    normed_line = x_line * lax.rsqrt(jnp.mean(x_line * x_line, axis=1, keepdims=True) + epsilon)
    first_line = (normed_line * gain_attn).astype(bf16)

    def to_blocks(value):
        columns = value.shape[1:]
        if fused:
            return value.reshape((sequence_batch, blk) + columns)
        return (
            value.reshape((head_number, sequence_batch, token_rows) + columns)
            .swapaxes(0, 1)
            .reshape((sequence_batch, blk) + columns)
        )

    def to_lines(value):
        columns = value.shape[2:]
        if fused:
            return value.reshape((line_tokens,) + columns)
        return (
            value.reshape((sequence_batch, head_number, token_rows) + columns)
            .swapaxes(0, 1)
            .reshape((line_tokens,) + columns)
        )

    q_start = seq_index * blk
    q_pos = q_start + jnp.arange(blk, dtype=jnp.int32)
    cosine, sine = rope_tables(q_pos, HEAD_WIDTH)
    projected = to_blocks(jnp.dot(first_line, dense_qkv, preferred_element_type=f32)).reshape(
        sequence_batch, blk, key_value_location, query_group + 2, HEAD_WIDTH
    )
    turned = rotate(projected[:, :, :, : query_group + 1], cosine, sine)
    query_rows = turned[:, :, :, :query_group].astype(bf16)
    keys_values = (
        jnp.stack([turned[:, :, :, query_group], projected[:, :, :, query_group + 1]], axis=3)
        .astype(bf16)
        .reshape(sequence_batch * blk, key_value_location * 2 * HEAD_WIDTH)
    )
    kv_columns = key_value_location * 2 * HEAD_WIDTH
    pairs_here = sequence_batch * key_value_location
    group_columns = key_value_location * query_group * HEAD_WIDTH
    queries = (
        (query_rows.astype(f32) * scale)
        .astype(bf16)
        .transpose(0, 2, 3, 1, 4)
        .reshape(pairs_here, query_group * blk, HEAD_WIDTH)
    )
    key_seg = segments[:, :, None]
    q_seg = lax.dynamic_slice_in_dim(segments, q_start, blk, 1)
    query_seg = jnp.tile(q_seg[:, None, :], (1, 1, query_group))
    lines, kv_all, out_turned, lse, *beside = attend(
        queries,
        keys_values.reshape(sequence_batch, blk, kv_columns),
        key_seg,
        query_seg,
        [(cots, False), (output_weight, True)] if fused else [],
        chips,
        head_number,
        query_group,
        4,
    )
    if fused:
        grad_all = beside[0].reshape(group_tokens, width)
        dense_out = beside[1].reshape(QUERY_HEADS * HEAD_WIDTH, width)
    mixed_heads = lines.transpose(1, 0, 2).reshape(tokens_present, QUERY_HEADS * HEAD_WIDTH)
    tokens = layer_input.reshape(tokens_present, width).astype(f32)
    middle = tokens + jnp.dot(mixed_heads, dense_out, preferred_element_type=f32)
    inverse_two = lax.rsqrt(jnp.mean(middle * middle, axis=1, keepdims=True) + epsilon)
    normed_two = middle * inverse_two
    second_input = (normed_two * gain_ffn).astype(bf16)
    router_logits = jnp.dot(second_input, dense_router, preferred_element_type=f32)
    route_flat = routes.reshape(tokens_present, top)
    hot = route_flat[:, :, None] == jnp.arange(EXPERTS, dtype=jnp.int32)[None, None, :]
    chosen = jnp.sum(jnp.where(hot, router_logits[:, None, :], 0.0), axis=2)
    gates = jax.nn.softmax(chosen, axis=-1)
    if not fused:
        expert_of = route_flat.reshape(pairs)
        rank = pair_rank.reshape(pairs)
        slot = jnp.sum(
            (expert_of[None, :] == expert_of[:, None]) & (rank[None, :] < rank[:, None]),
            axis=1,
            dtype=jnp.int32,
        )
    kept = (slot < CAP).reshape(tokens_present, top).astype(f32)
    weights_pair = gates * kept
    spread = jnp.sum(jnp.where(hot, weights_pair[:, :, None], 0.0), axis=1)
    spread_high = spread.astype(bf16)
    spread_low = (spread - spread_high.astype(f32)).astype(bf16)
    pad = jnp.zeros((tokens_present, LOW - EXPERTS), bf16)
    payload = jnp.concatenate([second_input, spread_high, pad, spread_low, pad], axis=1)
    if fused:
        back, moe_part, keep_up, other_up, keep_down, other_down = expert_turn(
            payload, grad_all, units, w_down, head_number, 6
        )
        down_share = keep_down.astype(f32) + other_down.astype(f32)
    else:
        x_all = gather(payload, chips, head_number, False, 6).reshape(group_tokens, columns)
        moe_part, back_part, d_gate_w, d_up_w, d_down_w = experts(
            x_all, grad_all, expert_gate, expert_up, expert_down, hidden
        )
        back_part = back_part.reshape(chips, head_number, tokens_present, columns)
        back = scatter_sum(back_part, chips, head_number, False, 7)
        moe = lax.psum_scatter(moe_part, ("chip", "head"), scatter_dimension=0, tiled=True)
        grads = jnp.stack([d_gate_w, d_up_w]).reshape(2, chips, 2, slice_rows, loc_experts * hidden)
        keep = lax.dynamic_index_in_dim(grads, core, 2, keepdims=False)
        give = lax.dynamic_index_in_dim(grads, 1 - core, 2, keepdims=False)
        shared = (keep.astype(f32) + sibling(give).astype(f32)).astype(bf16)
        piled = jnp.zeros((chips, 2, slice_rows, loc_experts * hidden), bf16)
        for mask in range(chips):
            piece = across(lax.dynamic_index_in_dim(shared, chip ^ mask, 1, keepdims=False), chips, mask)
            piled = lax.dynamic_update_slice(piled, piece[None], (chip ^ mask, 0, 0, 0))
        up_share = (
            piled.reshape(chips, 2, slice_rows, loc_experts, hidden)
            .transpose(3, 2, 1, 0, 4)
            .astype(f32)
            .reshape(loc_experts, slice_rows, 2 * FF)
        )
        d_down_w = d_down_w.reshape(loc_experts, 2, hidden // 2, width)
        keep = lax.dynamic_index_in_dim(d_down_w, core, 1, keepdims=False)
        give = lax.dynamic_index_in_dim(d_down_w, 1 - core, 1, keepdims=False)
        down_share = keep.astype(f32) + sibling(give).astype(f32)

    grad_out = cotangent.reshape(tokens_present, width).astype(f32)
    d_kept = back[:, width : width + EXPERTS]
    grad_gate = jnp.sum(jnp.where(hot, d_kept[:, None, :], 0.0), axis=2) * kept
    grad_chosen = gates * (grad_gate - jnp.sum(gates * grad_gate, axis=1, keepdims=True))
    grad_logits = jnp.sum(jnp.where(hot, grad_chosen[:, :, None], 0.0), axis=1)
    grad_router = jnp.dot(second_input.astype(f32).T, grad_logits, precision=HIGH_PRECISION)
    grad_second = back[:, :width] + jnp.dot(
        grad_logits, dense_router.astype(f32).T, precision=HIGH_PRECISION
    )
    grad_gain_ffn = jnp.sum(grad_second * normed_two, axis=0)
    scaled_two = grad_second * gain_ffn
    grad_mid = grad_out + inverse_two * (
        scaled_two - normed_two * jnp.mean(scaled_two * normed_two, axis=1, keepdims=True)
    )
    grad_attn = grad_mid.astype(bf16)
    grad_dense_out = jnp.dot(mixed_heads.T, grad_attn, preferred_element_type=f32)
    grad_dense_out = grad_dense_out.astype(bf16)
    if not fused:
        out_share = lax.psum_scatter(
            grad_dense_out, ("chip", "core", "head"), scatter_dimension=0, tiled=True
        ).astype(f32)
    grad_heads = (
        jnp.dot(grad_attn, dense_out.T, preferred_element_type=f32)
        .astype(bf16)
        .reshape(tokens_present, head_number, group_columns)
        .transpose(1, 0, 2)
    )
    grad_q, grad_kv, *beside = attend_back(
        queries,
        kv_all,
        key_seg,
        query_seg,
        out_turned,
        lse,
        grad_heads,
        [
            (moe_part.reshape(chips, head_number, tokens_present, width), False),
            (grad_dense_out.reshape(chips, 2, head_number, dense_rows, width), True),
        ]
        if fused
        else [],
        [keep_up, other_up] if fused else [],
        head_number,
        query_group,
        8,
    )
    if fused:
        moe, out_share, *shared = beside
        pieces = [across(shared[mask], chips, mask) for mask in range(chips)]
    grad_q = grad_q.reshape(
        sequence_batch, key_value_location, query_group, blk, HEAD_WIDTH
    ).transpose(0, 3, 1, 2, 4)
    grad_kv = grad_kv.reshape(sequence_batch, blk, key_value_location, 2, HEAD_WIDTH)
    grad_proj = jnp.concatenate([grad_q.astype(bf16), grad_kv.astype(bf16)], axis=3).astype(f32)
    unturned = rotate(grad_proj[:, :, :, : query_group + 1], cosine, -sine)
    grad_qkv = to_lines(
        jnp.concatenate([unturned, grad_proj[:, :, :, query_group + 1 :]], axis=3)
        .reshape(sequence_batch, blk, loc_columns)
        .astype(bf16)
    )
    grad_first_part = jnp.dot(grad_qkv, dense_qkv.T, preferred_element_type=f32)
    grad_gain_attn = jnp.sum(grad_first_part * normed_line, axis=0)
    grad_dense_qkv = jnp.dot(first_line.T, grad_qkv, preferred_element_type=f32)
    sums = jnp.concatenate(
        [
            grad_dense_qkv,
            grad_router,
            grad_gain_attn[:, None],
            grad_gain_ffn[:, None],
            jnp.zeros((width, LANES - EXPERTS - 2), f32),
        ],
        axis=1,
    ).astype(bf16)
    if fused:
        grad_first, sums = end(
            grad_first_part.astype(bf16).reshape(sequence_batch, head_number, token_rows, width),
            sums.reshape(chips, 2, head_number * dense_rows, loc_columns + LANES),
            chips,
            head_number,
            13,
        )
        pieces, grad_first = lax.optimization_barrier((pieces, grad_first))
        grad_first = jnp.sum(grad_first.astype(f32), axis=0).reshape(tokens_present, width)
        sums = sums.astype(f32)
        up_share = place_units(pieces, hidden)
    else:
        grad_first = jnp.sum(
            line_exchange(
                grad_first_part.astype(bf16).reshape(head_number, tokens_present, width),
                head_number,
                10,
            ).astype(f32),
            axis=0,
        )
        sums = scatter_sum(
            sums.reshape(chips, 2, head_number * dense_rows, loc_columns + LANES), chips, 1, True, 11
        )
        sums = line_exchange(
            sums.reshape(head_number, dense_rows, loc_columns + LANES), head_number, 12
        )
    inverse_one = lax.rsqrt(jnp.mean(tokens * tokens, axis=1, keepdims=True) + epsilon)
    normed_one = tokens * inverse_one
    scaled_one = grad_first * gain_attn
    grad_input = grad_mid + inverse_one * (
        scaled_one - normed_one * jnp.mean(scaled_one * normed_one, axis=1, keepdims=True)
    )
    mixed_out = (middle + moe.astype(f32)).astype(bf16)
    mixed_out = mixed_out.reshape(sequence_batch, token_rows, width)
    qkv_share = sums[:, :, :loc_columns].transpose(1, 0, 2).reshape(dense_rows, -1)
    extra = jnp.sum(sums[:, :, loc_columns:], axis=0)
    return (
        mixed_out,
        grad_input.reshape(sequence_batch, token_rows, width),
        qkv_share,
        out_share,
        extra[:, :EXPERTS],
        extra[:, EXPERTS],
        extra[:, EXPERTS + 1],
        up_share,
        down_share,
    )


def solution(mesh):
    grid = mesh.devices
    seq, heads = grid.shape
    split = Mesh(grid.reshape(seq // 2, 2, heads), ("chip", "core", "head"))
    places = ("chip", "core", "head")
    inner = ("chip", "core")
    placed = (
        P(None, places, None),
        P(),
        P(None, places, None),
        P(None, places, None),
        P(places, None),
        P(places, None),
        P(places, None),
        P(places),
        P(places),
        P("head", inner, None),
        P("head", inner, None),
        P(None, places, None),
    )
    return jax.shard_map(
        per_device,
        mesh=split,
        in_specs=placed,
        out_specs=(
            P(None, places, None),
            P(None, places, None),
            P(places, None),
            P(places, None),
            P(places, None),
            P(places),
            P(places),
            P("head", inner, None),
            P("head", inner, None),
        ),
        check_vma=False,
    )
```

```python
import functools

import jax
import jax.numpy as jnp
from jax import lax
from jax.experimental import pallas as pl
from jax.experimental.pallas import tpu as pltpu
from jax.sharding import Mesh, PartitionSpec as P

MODEL_WIDTH = 1536
QUERY_HEADS = 24
KEY_VALUE_HEADS = 8
HEAD_WIDTH = 64
EXPERTS = 40
FF = 512
CAP = 25
LANES = 128
LOW = 64

epsilon = 1e-06
negative = -1e30
theta = 10000.0
HIGH_PRECISION = lax.Precision.HIGHEST
MESH = pl.DeviceIdType.MESH
f32 = jnp.float32
bf16 = jnp.bfloat16
ANY = pl.BlockSpec(memory_space=pl.ANY)
WHOLE = pl.BlockSpec(memory_space=pltpu.VMEM)
DMA = pltpu.SemaphoreType.DMA


def rope_tables(token_positions, head_size):
    half = head_size // 2
    freq = theta ** (-jnp.arange(half, dtype=jnp.float32) / half)
    angle = token_positions.astype(jnp.float32)[:, None] * freq[None, :]
    return (jnp.cos(angle)[None, :, None, None, :], jnp.sin(angle)[None, :, None, None, :])


def rotate(value, cosine, sine):
    half = value.shape[-1] // 2
    first = value[..., :half]
    second = value[..., half:]
    return jnp.concatenate(
        [first * cosine - second * sine, second * cosine + first * sine], axis=-1
    )


def digits(count):
    number = count.bit_length() - 1
    assert 1 << number == count
    return number


def flip(index, mask):
    out = index
    bit = 0
    while (1 << bit) <= mask:
        if (mask >> bit) & 1:
            out = out + (1 - 2 * ((index // (1 << bit)) % 2)) * (1 << bit)
        bit += 1
    return out


def subsets(bits):
    out = [0]
    for bit in bits:
        out = out + [mask | (1 << bit) for mask in out]
    return out


def near(count):
    return sorted(range(1, count), key=lambda step: min(step, count - step))


def cut_rows(rows):
    return (rows // 2 + 15) // 16 * 16


def part_of(rows, side):
    cut = cut_rows(rows)
    return pl.ds(side * cut, rows - cut if side else cut)


def meet(peers):
    sem = pltpu.get_barrier_semaphore()
    for peer in peers:
        pl.semaphore_signal(sem, inc=1, device_id=peer, device_id_type=MESH)
    pl.semaphore_wait(sem, len(peers))


class Cube:
    def __init__(self, chips, with_core):
        self.chips = chips
        self.chip_digits = digits(chips)
        self.number = self.chip_digits + int(with_core)
        self.with_core = with_core
        up = tuple(range(self.chip_digits))
        core = (self.chip_digits,) if with_core else ()
        self.gather_orders = (up + core, up[::-1] + core)
        self.scatter_orders = (core + up, core + up[::-1])

    def place(self, mask):
        chip = flip(lax.axis_index("chip"), mask & (self.chips - 1))
        if not self.with_core:
            return (chip,)
        return (chip, flip(lax.axis_index("core"), mask >> self.chip_digits))

    def peer(self, digit):
        if digit < self.chip_digits:
            return {"chip": flip(lax.axis_index("chip"), 1 << digit)}
        return {"core": flip(lax.axis_index("core"), 1)}


def gather_kernel(cube, heads, in_ref, out_ref, local, line_send, line_recv, send, recv):
    hz = lax.axis_index("head")
    rows = in_ref.shape[0]
    half = rows // 2
    others = near(heads) if heads > 1 else []
    meet(
        [cube.peer(digit) for digit in range(cube.number)]
        + [{"head": (hz + d) % heads} for d in others]
    )

    def at(mask, d):
        index = cube.place(mask)
        return index + ((hz + heads - d) % heads,) if heads > 1 else index

    own = pltpu.make_async_copy(in_ref, out_ref.at[at(0, 0)], local)
    own.start()
    line = {}
    for d in others:
        line[d] = pltpu.make_async_remote_copy(
            src_ref=in_ref,
            dst_ref=out_ref.at[at(0, 0)],
            send_sem=line_send.at[d - 1],
            recv_sem=line_recv.at[d - 1],
            device_id={"head": (hz + d) % heads},
            device_id_type=MESH,
        )
        line[d].start()
    copies = {}

    def forward(side, mask, d):
        order = cube.gather_orders[side]
        last = max([k for k in range(cube.number) if (mask >> order[k]) & 1], default=-1)
        for k in range(last + 1, cube.number):
            later = mask | (1 << order[k])
            part = pl.ds(side * half, half)
            place = out_ref.at[at(mask, d) + (part,)]
            copy = pltpu.make_async_remote_copy(
                src_ref=in_ref.at[part] if mask == 0 and d == 0 else place,
                dst_ref=place,
                send_sem=send.at[side, later, d],
                recv_sem=recv.at[side, later, d],
                device_id=cube.peer(order[k]),
                device_id_type=MESH,
            )
            copy.start()
            copies[(side, later, d)] = copy

    for side in range(2):
        forward(side, 0, 0)
    for d in others:
        line[d].wait_recv()
        for side in range(2):
            forward(side, 0, d)
    for mask in sorted(range(1, 1 << cube.number), key=lambda m: bin(m).count("1")):
        for d in [0] + others:
            for side in range(2):
                copies[(side, mask, d)].wait_recv()
                forward(side, mask, d)
    own.wait()
    for copy in list(line.values()) + list(copies.values()):
        copy.wait_send()


def gather(value, chips, heads, with_core, number):
    rows, columns = value.shape
    cube = Cube(chips, with_core)
    lead = (chips,) + ((2,) if with_core else ()) + ((heads,) if heads > 1 else ())
    steps = max(heads - 1, 1)
    return pl.pallas_call(
        functools.partial(gather_kernel, cube, heads),
        out_shape=jax.ShapeDtypeStruct(lead + (rows, columns), value.dtype),
        in_specs=[ANY],
        out_specs=ANY,
        scratch_shapes=[
            DMA,
            DMA((steps,)),
            DMA((steps,)),
            DMA((2, 1 << cube.number, heads)),
            DMA((2, 1 << cube.number, heads)),
        ],
        compiler_params=pltpu.CompilerParams(collective_id=number, has_side_effects=True),
        name="gather",
    )(value)


def scatter_kernel(cube, heads, in_ref, out_ref, *refs):
    count = cube.number
    arrived, parts = refs[:count], refs[count : 2 * count - 1]
    line_out, line_in, line_send, line_recv, send, recv = refs[2 * count - 1 :]
    hz = lax.axis_index("head")
    half = in_ref.shape[-2] // 2
    others = near(heads) if heads > 1 else []
    order_of_lines = others[::-1] + [0]
    meet(
        [cube.peer(digit) for digit in range(count)] + [{"head": (hz + d) % heads} for d in others]
    )
    copies = {}

    def slot(side, k, mask):
        return subsets(cube.scatter_orders[side][k + 1 :]).index(mask)

    def mine(side, mask, d):
        index = cube.place(mask)
        if heads > 1:
            index = index + ((hz + d) % heads,)
        return in_ref.at[index + (pl.ds(side * half, half),)]

    def pass_on(side, k, mask, d, source):
        where = slot(side, k, mask)
        copy = pltpu.make_async_remote_copy(
            src_ref=source,
            dst_ref=arrived[k].at[side, where, d],
            send_sem=send.at[side, k, where, d],
            recv_sem=recv.at[side, k, where, d],
            device_id=cube.peer(cube.scatter_orders[side][k]),
            device_id_type=MESH,
        )
        copy.start()
        copies[(side, k, mask, d)] = copy

    def total(side, steps, mask, d):
        value = mine(side, mask, d)[...].astype(f32)
        for j in range(steps):
            copies[(side, j, mask, d)].wait_recv()
            value = value + arrived[j][side, slot(side, j, mask), d].astype(f32)
        return value

    for k in range(count):
        for d in order_of_lines:
            for side in range(2):
                order = cube.scatter_orders[side]
                for mask in subsets(order[k + 1 :])[::-1]:
                    full = mask | (1 << order[k])
                    if k == 0:
                        source = mine(side, full, d)
                    else:
                        source = parts[k - 1].at[side, slot(side, k, mask), d]
                        source[...] = total(side, k, full, d).astype(bf16)
                    pass_on(side, k, mask, d, source)
    line = {}
    for d in order_of_lines:
        for side in range(2):
            value = total(side, count, 0, d)
            if d:
                line_out[d - 1, pl.ds(side * half, half)] = value.astype(bf16)
            else:
                out_ref[pl.ds(side * half, half)] = value
        if d:
            line[d] = pltpu.make_async_remote_copy(
                src_ref=line_out.at[d - 1],
                dst_ref=line_in.at[d - 1],
                send_sem=line_send.at[d - 1],
                recv_sem=line_recv.at[d - 1],
                device_id={"head": (hz + d) % heads},
                device_id_type=MESH,
            )
            line[d].start()
    for d in others:
        line[d].wait_recv()
        out_ref[...] += line_in[d - 1].astype(f32)
    for copy in list(line.values()) + list(copies.values()):
        copy.wait_send()


def scatter_sum(value, chips, heads, with_core, number):
    rows, columns = value.shape[-2:]
    cube = Cube(chips, with_core)
    half = rows // 2
    steps = max(heads - 1, 1)
    line_rows = rows if heads > 1 else 16
    slots = [(1 << cube.number) >> (k + 1) for k in range(cube.number)]
    if 2 * value.size + 4 * heads * half * columns * (sum(slots) + sum(slots[1:])) > 40 << 20:
        names = ("chip", "core") if with_core else ("chip",)
        names = names + (("head",) if heads > 1 else ())
        flat = value.reshape(-1, columns)
        return lax.psum_scatter(flat, names, scatter_dimension=0, tiled=True).astype(f32)
    return pl.pallas_call(
        functools.partial(scatter_kernel, cube, heads),
        out_shape=jax.ShapeDtypeStruct((rows, columns), f32),
        in_specs=[WHOLE],
        out_specs=WHOLE,
        scratch_shapes=[pltpu.VMEM((2, s, heads, half, columns), bf16) for s in slots]
        + [pltpu.VMEM((2, s, heads, half, columns), bf16) for s in slots[1:]]
        + [
            pltpu.VMEM((steps, line_rows, columns), bf16),
            pltpu.VMEM((steps, line_rows, columns), bf16),
            DMA((steps,)),
            DMA((steps,)),
            DMA((2, cube.number, slots[0], heads)),
            DMA((2, cube.number, slots[0], heads)),
        ],
        compiler_params=pltpu.CompilerParams(
            collective_id=number, has_side_effects=True, vmem_limit_bytes=56 << 20
        ),
        name="scatter_sum",
    )(value)


def line_kernel(heads, same, in_ref, out_ref, local, send, recv):
    hz = lax.axis_index("head")
    others = near(heads)[::-1]
    meet([{"head": (hz + d) % heads} for d in others])

    def source(place):
        return in_ref if same else in_ref.at[place]

    own = pltpu.make_async_copy(source(hz), out_ref.at[hz], local)
    own.start()
    copies = []
    for d in others:
        place = (hz + d) % heads
        copy = pltpu.make_async_remote_copy(
            src_ref=source(place),
            dst_ref=out_ref.at[hz],
            send_sem=send.at[d - 1],
            recv_sem=recv.at[d - 1],
            device_id={"head": place},
            device_id_type=MESH,
        )
        copy.start()
        copies.append(copy)
    own.wait()
    for copy in copies:
        copy.wait()


def line_exchange(value, heads, number, same=False):
    return pl.pallas_call(
        functools.partial(line_kernel, heads, same),
        out_shape=jax.ShapeDtypeStruct((heads,) + value.shape if same else value.shape, value.dtype),
        in_specs=[ANY],
        out_specs=ANY,
        scratch_shapes=[DMA, DMA((heads - 1,)), DMA((heads - 1,))],
        compiler_params=pltpu.CompilerParams(collective_id=number, has_side_effects=True),
        name="line_exchange",
    )(value)


NT = (((1,), (1,)), ((), ()))


def experts_kernel(
    tile,
    hidden,
    x_ref,
    c_ref,
    gate_hbm,
    up_hbm,
    down_hbm,
    moe_ref,
    back_ref,
    d_gate_hbm,
    d_up_hbm,
    d_down_hbm,
    w_gate,
    w_up,
    w_down,
    d_gate_w,
    d_up_w,
    d_down_w,
    acts,
    back_gate,
    back_up,
    stage_wide,
    stage_down,
    load,
    store,
):
    step = pl.program_id(0)
    width, total = w_gate.shape

    @pl.when(step == 0)
    def _():
        loads = [
            pltpu.make_async_copy(gate_hbm, w_gate, load.at[0]),
            pltpu.make_async_copy(up_hbm, w_up, load.at[1]),
            pltpu.make_async_copy(down_hbm, w_down, load.at[2]),
        ]
        for copy in loads:
            copy.start()
        d_gate_w[...] = jnp.zeros_like(d_gate_w)
        d_up_w[...] = jnp.zeros_like(d_up_w)
        d_down_w[...] = jnp.zeros_like(d_down_w)
        for copy in loads:
            copy.wait()

    x = x_ref[:, :width]
    c = c_ref[...]
    routed = x_ref[:, width:]
    first_expert = lax.axis_index("head") * (total // hidden)
    d_gates = jnp.zeros((x.shape[0], LANES), f32)
    for begin in range(0, total, tile):
        js = pl.ds(begin, tile)
        column = begin + lax.broadcasted_iota(jnp.int32, (LANES, tile), 1)
        line = lax.broadcasted_iota(jnp.int32, (LANES, tile), 0)
        expert = first_expert + column // hidden
        here = (line == expert).astype(f32)
        both = (here + (line == expert + LOW).astype(f32)).astype(bf16)
        weight = jnp.dot(routed, both, preferred_element_type=f32)
        gate = jnp.dot(x, w_gate[:, js], preferred_element_type=f32)
        up = jnp.dot(x, w_up[:, js], preferred_element_type=f32)
        d_act = lax.dot_general(c, w_down[js, :], NT, preferred_element_type=f32)
        sigma = 1.0 / (1.0 + jnp.exp(-gate))
        silu = gate * sigma
        act = (silu * up).astype(bf16).astype(f32)
        d_gates = d_gates + lax.dot_general(
            (act * d_act).astype(bf16), here.astype(bf16), NT, preferred_element_type=f32
        )
        acts[:, js] = (act * weight).astype(bf16)
        d_act = d_act * weight
        back_up[:, js] = (d_act * silu).astype(bf16)
        back_gate[:, js] = (d_act * up * sigma * (1.0 + gate * (1.0 - sigma))).astype(bf16)
    back_ref[:, width:] = d_gates.astype(bf16)
    x_turned = x.T
    for begin in range(0, total, tile):
        js = pl.ds(begin, tile)
        d_gate_w[:, js] += jnp.dot(x_turned, back_gate[:, js], preferred_element_type=f32)
        d_up_w[:, js] += jnp.dot(x_turned, back_up[:, js], preferred_element_type=f32)
        d_down_w[js, :] += jnp.dot(acts[:, js].T, c, preferred_element_type=f32)
    for begin in range(0, width, 512):
        cs = pl.ds(begin, 512)
        moe_ref[:, cs] = jnp.dot(acts[...], w_down[:, cs], preferred_element_type=f32).astype(bf16)
        back_ref[:, cs] = (
            lax.dot_general(back_gate[...], w_gate[cs, :], NT, preferred_element_type=f32)
            + lax.dot_general(back_up[...], w_up[cs, :], NT, preferred_element_type=f32)
        ).astype(bf16)

    @pl.when(step == pl.num_programs(0) - 1)
    def _():
        rows = stage_wide.shape[1]
        jobs = [
            (source, target, stage, begin)
            for source, target, stage in (
                (d_gate_w, d_gate_hbm, stage_wide),
                (d_up_w, d_up_hbm, stage_wide),
                (d_down_w, d_down_hbm, stage_down),
            )
            for begin in range(0, source.shape[0], rows)
        ]
        flight = {}
        for index, (source, target, stage, begin) in enumerate(jobs):
            now = index % 2
            if now in flight:
                flight[now].wait()
            stage[now] = source[pl.ds(begin, rows), :].astype(bf16)
            flight[now] = pltpu.make_async_copy(
                stage.at[now], target.at[pl.ds(begin, rows), :], store.at[now]
            )
            flight[now].start()
        for copy in flight.values():
            copy.wait()


def experts(x, c, w_gate, w_up, w_down, hidden):
    tokens, columns = x.shape
    width, total = w_gate.shape
    block = min(256, tokens)
    tile = 256 if total % 256 == 0 else hidden
    return pl.pallas_call(
        functools.partial(experts_kernel, tile, hidden),
        grid=(tokens // block,),
        out_shape=(
            jax.ShapeDtypeStruct((tokens, width), bf16),
            jax.ShapeDtypeStruct((tokens, columns), bf16),
            jax.ShapeDtypeStruct((width, total), bf16),
            jax.ShapeDtypeStruct((width, total), bf16),
            jax.ShapeDtypeStruct((total, width), bf16),
        ),
        in_specs=[
            pl.BlockSpec((block, columns), lambda i: (i, 0)),
            pl.BlockSpec((block, width), lambda i: (i, 0)),
            ANY,
            ANY,
            ANY,
        ],
        out_specs=(
            pl.BlockSpec((block, width), lambda i: (i, 0)),
            pl.BlockSpec((block, columns), lambda i: (i, 0)),
            ANY,
            ANY,
            ANY,
        ),
        scratch_shapes=[
            pltpu.VMEM((width, total), bf16),
            pltpu.VMEM((width, total), bf16),
            pltpu.VMEM((total, width), bf16),
            pltpu.VMEM((width, total), f32),
            pltpu.VMEM((width, total), f32),
            pltpu.VMEM((total, width), f32),
            pltpu.VMEM((block, total), bf16),
            pltpu.VMEM((block, total), bf16),
            pltpu.VMEM((block, total), bf16),
            pltpu.VMEM((2, 64, total), bf16),
            pltpu.VMEM((2, 64, width), bf16),
            DMA((3,)),
            DMA((2,)),
        ],
        compiler_params=pltpu.CompilerParams(vmem_limit_bytes=60 << 20),
        name="experts",
    )(x, c, w_gate, w_up, w_down)


def turn_kernel(cube, heads, hidden, *refs):
    chips, count = cube.chips, cube.number
    own_ref, c_hbm, down_hbm = refs[:3]
    pieces, refs = refs[3 : 3 + chips], (None,) * 4 + refs[3 + chips :]
    out_ref, moe_hbm, keep_up_hbm, other_up_hbm, keep_down_hbm, other_down_hbm = refs[4:10]
    tokens, turned, cots, w_up, w_down, acts, backs, d_gates, moe_stage, line_in = refs[10:20]
    arrived = refs[20 : 20 + count]
    load, store, own_sem, line_send, line_recv, send, recv, back_send, back_recv = refs[
        20 + count : 29 + count
    ]
    end_send, end_recv, twin_send, twin_recv, load_send, load_recv = refs[29 + count :]
    hz = lax.axis_index("head")
    rows, columns = own_ref.shape
    experts_here, width, _ = w_up.shape
    total = experts_here * hidden
    half = rows // 2
    line = heads * rows
    others = near(heads)
    masks = sorted(range(chips), key=lambda m: bin(m).count("1"))

    core = lax.axis_index("core")
    twin = {"core": 1 - core}
    slices = 2 * chips
    slice_rows = width // slices

    def up_rows(ref, chip, which):
        return ref.at[:, pl.ds((chip * 2 + which) * slice_rows, slice_rows), :]

    def w_down_parts(which):
        return w_down.reshape(experts_here, 2, hidden // 2, width).at[:, which]

    homes = [
        (pieces[mask], up_rows(w_up, flip(lax.axis_index("chip"), mask), core))
        for mask in range(chips)
    ] + [(down_hbm, w_down_parts(core))]
    loads = [
        pltpu.make_async_copy(source, target, load.at[index])
        for index, (source, target) in enumerate([(c_hbm, cots)] + homes)
    ]
    shared = [
        pltpu.make_async_remote_copy(
            src_ref=source,
            dst_ref=target,
            send_sem=load_send.at[index],
            recv_sem=load_recv.at[index],
            device_id=twin,
            device_id_type=MESH,
        )
        for index, (source, target) in enumerate(homes)
    ]
    for copy in loads:
        copy.start()
    meet(
        [cube.peer(digit) for digit in range(count)]
        + [{"head": (hz + d) % heads} for d in others]
        + [twin]
    )

    def part(side):
        return pl.ds(side * half, half)

    middle = jnp.minimum(hz, heads - 1 - hz)

    def source(rank):
        if rank == 0:
            return hz
        far = (rank + 1) // 2
        near_one = hz - far if rank % 2 else hz + far
        far_one = jnp.where(
            hz < heads - 1 - hz, hz + (rank - middle), hz - (rank - middle)
        )
        return jnp.where(rank <= 2 * middle, near_one, far_one)

    def line_copy(rank, step):
        head = source(rank)
        place = tokens.at[cube.place(0) + (head,)]
        return pltpu.make_async_remote_copy(
            src_ref=own_ref if rank == 0 else place,
            dst_ref=place,
            send_sem=line_send.at[heads if rank == 0 and step < 0 else head],
            recv_sem=line_recv.at[head],
            device_id={"head": (hz + step + heads) % heads},
            device_id_type=MESH,
        )

    def along(rank, act):
        head = source(rank)
        goes_up = hz + 1 < heads
        goes_down = hz > 0
        if rank:
            goes_up = goes_up & (head < hz)
            goes_down = goes_down & (head > hz)

        @pl.when(goes_up)
        def _():
            act(line_copy(rank, 1))

        @pl.when(goes_down)
        def _():
            act(line_copy(rank, -1))

    def plane_copy(side, mask, k, rank):
        digit = cube.gather_orders[side][k]
        later = mask | (1 << digit)
        head = source(rank)
        place = tokens.at[cube.place(mask) + (head, part(side))]
        return pltpu.make_async_remote_copy(
            src_ref=own_ref.at[part(side)] if mask == 0 and rank == 0 else place,
            dst_ref=place,
            send_sem=send.at[side, later, head],
            recv_sem=recv.at[side, later, head],
            device_id=cube.peer(digit),
            device_id_type=MESH,
        )

    def steps_after(side, mask):
        order = cube.gather_orders[side]
        last = max([k for k in range(count) if (mask >> order[k]) & 1], default=-1)
        return range(last + 1, count)

    def arrival(side, mask, rank):
        order = cube.gather_orders[side]
        k = max(k for k in range(count) if (mask >> order[k]) & 1)
        return plane_copy(side, mask & ~(1 << order[k]), k, rank)

    def receive(mask, rank):
        if mask == 0:
            if rank:
                line_copy(rank, 1).wait_recv()
            along(rank, lambda copy: copy.start())
        for side in range(2):
            if mask:
                arrival(side, mask, rank).wait_recv()
            for k in steps_after(side, mask):
                plane_copy(side, mask, k, rank).start()

    levels = [
        [m for m in masks if bin(m).count("1") == level] for level in range(cube.number + 1)
    ]
    waits = {0: [], 1: []}
    early = max(heads - 2, 0)
    for rank in range(heads):
        waits[0].append((0, rank))
        if 0 < rank <= early and count > 0:
            waits[0] += [(m, rank - 1) for m in levels[1]]
    waits[1] = [(m, rank) for rank in range(early, heads) for m in levels[1]]
    for level in range(2, count + 1):
        waits[level] = [(m, rank) for m in levels[level] for rank in range(heads)]

    def sent(mask):
        for rank in range(heads):
            if mask == 0:
                along(rank, lambda copy: copy.wait_send())
            for side in range(2):
                for k in steps_after(side, mask):
                    plane_copy(side, mask, k, rank).wait_send()

    def slot(side, k, mask):
        return subsets(cube.scatter_orders[side][k + 1 :]).index(mask)

    def back_place(side, mask, d):
        return tokens.at[cube.place(mask) + ((hz + d) % heads, part(side))]

    def back_copy(side, k, mask, d):
        order = cube.scatter_orders[side]
        where = slot(side, k, mask)
        return pltpu.make_async_remote_copy(
            src_ref=back_place(side, mask | (1 << order[k]), d),
            dst_ref=arrived[k].at[side, where, d],
            send_sem=back_send.at[side, k, where, d],
            recv_sem=back_recv.at[side, k, where, d],
            device_id=cube.peer(order[k]),
            device_id_type=MESH,
        )

    def end_copy(d):
        return pltpu.make_async_remote_copy(
            src_ref=tokens.at[cube.place(0) + ((hz + d) % heads,)],
            dst_ref=line_in.at[d - 1],
            send_sem=end_send.at[d - 1],
            recv_sem=end_recv.at[d - 1],
            device_id={"head": (hz + d) % heads},
            device_id_type=MESH,
        )

    outward = others[::-1] + [0]

    def give(mask, d):
        for side in range(2):
            first = 1 << cube.scatter_orders[side][0]
            if mask & first:
                back_copy(side, 0, mask & ~first, d).start()

    own = pltpu.make_async_copy(own_ref, tokens.at[cube.place(0) + (hz,)], own_sem)
    own.start()
    for copy in shared:
        copy.start()

    first_expert = hz * experts_here
    span = min(512, width)
    group = 2 if experts_here % 2 == 0 else 1
    tile = group * hidden

    def compute(place):
        here = pl.ds(place * line, line)
        x = tokens[place, :, :, pl.ds(0, width)].reshape(line, width)
        c = cots[here, :]
        routed = tokens[place, :, :, pl.ds(width, LANES)].reshape(line, LANES)
        turned[:, here] = x.T
        d_gates[...] = jnp.zeros_like(d_gates)

        @pl.loop(0, total // tile)
        def _(j):
            js = pl.ds(pl.multiple_of(j * tile, tile), tile)
            column = j * tile + lax.broadcasted_iota(jnp.int32, (LANES, tile), 1)
            lane = lax.broadcasted_iota(jnp.int32, (LANES, tile), 0)
            expert = first_expert + column // hidden
            high = (lane == expert).astype(f32)
            both = (high + (lane == expert + LOW).astype(f32)).astype(bf16)
            weight = jnp.dot(routed, both, preferred_element_type=f32)
            both_parts = [
                jnp.dot(x, w_up[j * group + i], preferred_element_type=f32) for i in range(group)
            ]
            gate = jnp.concatenate([value[:, :hidden] for value in both_parts], axis=1)
            up = jnp.concatenate([value[:, hidden:] for value in both_parts], axis=1)
            d_act = lax.dot_general(c, w_down[js, :], NT, preferred_element_type=f32)
            sigma = 1.0 / (1.0 + jnp.exp(-gate))
            silu = gate * sigma
            act = (silu * up).astype(bf16).astype(f32)
            d_gates[...] += lax.dot_general(
                (act * d_act).astype(bf16), high.astype(bf16), NT, preferred_element_type=f32
            )
            acts[here, js] = (act * weight).astype(bf16)
            d_act = d_act * weight
            d_up = (d_act * silu).astype(bf16)
            d_gate = (d_act * up * sigma * (1.0 + gate * (1.0 - sigma))).astype(bf16)
            for i in range(group):
                one = slice(i * hidden, (i + 1) * hidden)
                backs[j * group + i, here, pl.ds(0, hidden)] = d_gate[:, one]
                backs[j * group + i, here, pl.ds(hidden, hidden)] = d_up[:, one]

    def results(place, step):
        here = pl.ds(place * line, line)

        @pl.loop(0, width // span)
        def _(j):
            cs = pl.ds(pl.multiple_of(j * span, span), span)
            value = sum(
                lax.dot_general(
                    backs[e, here, :], w_up[e, cs, :], NT, preferred_element_type=f32
                )
                for e in range(experts_here)
            )
            tokens[place, :, :, cs] = value.astype(bf16).reshape(heads, rows, span)

        tokens[place, :, :, pl.ds(width, LANES)] = (
            d_gates[...].astype(bf16).reshape(heads, rows, LANES)
        )

    def moe_copy(place):
        return pltpu.make_async_copy(
            moe_stage, moe_hbm.at[pl.ds(place * line, line)], store.at[chips + 1]
        )

    def mixed(place, step):
        here = pl.ds(place * line, line)

        @pl.when(step > 0)
        def _():
            moe_copy(place).wait()

        @pl.loop(0, width // span)
        def _(j):
            cs = pl.ds(pl.multiple_of(j * span, span), span)
            moe_stage[:, cs] = jnp.dot(
                acts[here, :], w_down[:, cs], preferred_element_type=f32
            ).astype(bf16)

        moe_copy(place).start()

    @pl.loop(0, chips)
    def _(step):
        seen = -1
        for index, mask in enumerate(masks):
            level = bin(mask).count("1")
            if level > seen:
                seen = level

                @pl.when(step == index)
                def _():
                    for event in waits[level]:
                        receive(*event)

        place = cube.place(0)[0] * 0
        for index, mask in enumerate(masks):
            place = jnp.where(step == index, cube.place(mask)[0], place)

        @pl.when(step == 0)
        def _():
            own.wait()
            for copy in loads + shared:
                copy.wait()

        compute(place)
        for index, mask in enumerate(masks):

            @pl.when(step == index)
            def _():
                sent(mask)

        results(place, step)
        for index, mask in enumerate(masks):
            if mask and mask != chips - 1:

                @pl.when(step == index)
                def _():
                    for d in outward:
                        give(mask, d)

    def sums(side, steps, mask, d):
        value = back_place(side, mask, d)[...].astype(f32)
        for j in range(steps):
            back_copy(side, j, mask, d).wait_recv()
            value = value + arrived[j][side, slot(side, j, mask), d].astype(f32)
        return value

    def keep_up(chip):
        return pltpu.make_async_copy(up_rows(w_up, chip, core), keep_up_hbm.at[chip], store.at[chip])

    def give_up(chip):
        return pltpu.make_async_remote_copy(
            src_ref=up_rows(w_up, chip, 1 - core),
            dst_ref=other_up_hbm.at[chip],
            send_sem=twin_send.at[chip],
            recv_sem=twin_recv.at[chip],
            device_id=twin,
            device_id_type=MESH,
        )

    def keep_down():
        return pltpu.make_async_copy(w_down_parts(core), keep_down_hbm, store.at[chips])

    def give_down():
        return pltpu.make_async_remote_copy(
            src_ref=w_down_parts(1 - core),
            dst_ref=other_down_hbm,
            send_sem=twin_send.at[chips],
            recv_sem=twin_recv.at[chips],
            device_id=twin,
            device_id_type=MESH,
        )

    def up_grad(begin, end):
        @pl.loop(begin, end)
        def _(e):
            w_up[e] = jnp.dot(turned[...], backs[e], preferred_element_type=f32).astype(bf16)

        if end == experts_here:
            for chip in range(chips):
                give_up(chip).start()
                keep_up(chip).start()

    def down_grad():
        @pl.loop(0, total // tile)
        def _(j):
            js = pl.ds(pl.multiple_of(j * tile, tile), tile)
            value = jnp.dot(acts[:, js].T, cots[...], preferred_element_type=f32)
            w_down[js, :] = value.astype(bf16)

        give_down().start()
        keep_down().start()

    def mix(begin, end):
        @pl.loop(begin, end)
        def _(index):
            mixed(index, index)

    cuts = [experts_here * i // 4 for i in range(5)]
    work = [
        lambda: mix(0, chips // 2),
        lambda: mix(chips // 2, chips),
        lambda: up_grad(cuts[0], cuts[1]),
        lambda: up_grad(cuts[1], cuts[2]),
        lambda: up_grad(cuts[2], cuts[3]),
        lambda: up_grad(cuts[3], cuts[4]),
        down_grad,
    ]
    turns = heads + count
    for turn in range(turns):
        if turn < heads:
            give(chips - 1, outward[turn])
        for piece in work[len(work) * turn // turns : len(work) * (turn + 1) // turns]:
            piece()
        for k in range(1, count):
            if 0 <= turn - k < heads:
                d = outward[turn - k]
                for side in range(2):
                    order = cube.scatter_orders[side]
                    for mask in subsets(order[k + 1 :])[::-1]:
                        full = mask | (1 << order[k])
                        back_place(side, full, d)[...] = sums(side, k, full, d).astype(bf16)
                        back_copy(side, k, mask, d).start()
        if 0 <= turn - count < heads:
            d = outward[turn - count]
            for side in range(2):
                value = sums(side, count, 0, d)
                if d:
                    back_place(side, 0, d)[...] = value.astype(bf16)
                else:
                    out_ref[part(side)] = value
            if d:
                end_copy(d).start()
    for d in others:
        end_copy(d).wait_recv()
        out_ref[...] += line_in[d - 1].astype(f32)
    for d in others:
        end_copy(d).wait_send()
    for side in range(2):
        for k in range(count):
            for mask in subsets(cube.scatter_orders[side][k + 1 :]):
                for d in outward:
                    back_copy(side, k, mask, d).wait_send()
    moe_copy(0).wait()
    for chip in range(chips):
        give_up(chip).wait()
        keep_up(chip).wait()
    give_down().wait()
    keep_down().wait()


def expert_turn(payload, c, pieces, w_down, heads, number):
    rows, columns = payload.shape
    chips, width = len(pieces), c.shape[1]
    experts_here, _, double = pieces[0].shape
    hidden = double // 2
    total = experts_here * hidden
    cube = Cube(chips, False)
    count = cube.number
    tokens = chips * heads * rows
    half = rows // 2
    slots = [chips >> (k + 1) for k in range(count)]
    share = jax.ShapeDtypeStruct((chips, experts_here, width // (2 * chips), double), bf16)
    down_share = jax.ShapeDtypeStruct((experts_here, hidden // 2, width), bf16)
    return pl.pallas_call(
        functools.partial(turn_kernel, cube, heads, hidden),
        out_shape=(
            jax.ShapeDtypeStruct((rows, columns), f32),
            jax.ShapeDtypeStruct((tokens, width), bf16),
            share,
            share,
            down_share,
            down_share,
        ),
        in_specs=[WHOLE] + [ANY] * (2 + chips),
        out_specs=(WHOLE, ANY, ANY, ANY, ANY, ANY),
        scratch_shapes=[
            pltpu.VMEM((chips, heads, rows, columns), bf16),
            pltpu.VMEM((width, tokens), bf16),
            pltpu.VMEM((tokens, width), bf16),
            pltpu.VMEM((experts_here, width, double), bf16),
            pltpu.VMEM((total, width), bf16),
            pltpu.VMEM((tokens, total), bf16),
            pltpu.VMEM((experts_here, tokens, double), bf16),
            pltpu.VMEM((heads * rows, LANES), f32),
            pltpu.VMEM((heads * rows, width), bf16),
            pltpu.VMEM((heads - 1, rows, columns), bf16),
        ]
        + [pltpu.VMEM((2, s, heads, half, columns), bf16) for s in slots]
        + [
            DMA((chips + 2,)),
            DMA((chips + 2,)),
            DMA,
            DMA((heads + 1,)),
            DMA((heads,)),
            DMA((2, chips, heads)),
            DMA((2, chips, heads)),
            DMA((2, count, slots[0], heads)),
            DMA((2, count, slots[0], heads)),
            DMA((heads - 1,)),
            DMA((heads - 1,)),
            DMA((chips + 1,)),
            DMA((chips + 1,)),
            DMA((chips + 1,)),
            DMA((chips + 1,)),
        ],
        compiler_params=pltpu.CompilerParams(
            collective_id=number, has_side_effects=True, vmem_limit_bytes=63 << 20
        ),
        name="expert_turn",
    )(payload, c, w_down, *pieces)


def start_kernel(cube, heads, *refs):
    x_ref, slice_ref, unit_ref, column_ref, row_ref, x_out, dense_out, unit_out, slot_out = refs[:9]
    local, x_send, x_recv, line_send, line_recv, send, recv, unit_send, unit_recv = refs[9:]
    chips = cube.chips
    chip, core, hz = lax.axis_index("chip"), lax.axis_index("core"), lax.axis_index("head")
    others = near(heads)
    part_heads = heads // 2
    across_all = {"chip": flip(chip, chips - 1)}
    meet(
        [cube.peer(digit) for digit in range(cube.number)]
        + [{"head": (hz + d) % heads} for d in others]
        + [across_all]
    )
    unit_copy = pltpu.make_async_remote_copy(
        src_ref=unit_ref,
        dst_ref=unit_out,
        send_sem=unit_send,
        recv_sem=unit_recv,
        device_id=across_all,
        device_id_type=MESH,
    )
    middle = jnp.minimum(hz, heads - 1 - hz)

    def source(rank):
        if rank == 0:
            return hz
        far = (rank + 1) // 2
        near_one = hz - far if rank % 2 else hz + far
        far_one = jnp.where(hz < heads - 1 - hz, hz + (rank - middle), hz - (rank - middle))
        return jnp.where(rank <= 2 * middle, near_one, far_one)

    def x_copy(rank, step):
        head = source(rank)
        return pltpu.make_async_remote_copy(
            src_ref=x_ref if rank == 0 else x_out.at[:, head],
            dst_ref=x_out.at[:, head],
            send_sem=x_send.at[heads if rank == 0 and step < 0 else head],
            recv_sem=x_recv.at[head],
            device_id={"head": (hz + step + heads) % heads},
            device_id_type=MESH,
        )

    def along(rank, act):
        head = source(rank)
        goes_up = hz + 1 < heads
        goes_down = hz > 0
        if rank:
            goes_up = goes_up & (head < hz)
            goes_down = goes_down & (head > hz)

        @pl.when(goes_up)
        def _():
            act(x_copy(rank, 1))

        @pl.when(goes_down)
        def _():
            act(x_copy(rank, -1))

    def slice_copy(d):
        place = (hz + d) % heads
        return pltpu.make_async_remote_copy(
            src_ref=slice_ref.at[place],
            dst_ref=dense_out.at[chip, core, hz],
            send_sem=line_send.at[d - 1],
            recv_sem=line_recv.at[d - 1],
            device_id={"head": place},
            device_id_type=MESH,
        )

    def dense_copy(side, mask, k):
        order = cube.gather_orders[side]
        later = mask | (1 << order[k])
        place = dense_out.at[cube.place(mask) + (pl.ds(side * part_heads, part_heads),)]
        return pltpu.make_async_remote_copy(
            src_ref=place,
            dst_ref=place,
            send_sem=send.at[side, later],
            recv_sem=recv.at[side, later],
            device_id=cube.peer(order[k]),
            device_id_type=MESH,
        )

    def steps_after(side, mask):
        order = cube.gather_orders[side]
        last = max([k for k in range(cube.number) if (mask >> order[k]) & 1], default=-1)
        return range(last + 1, cube.number)

    def dense_turn(mask):
        for side in range(2):
            if mask:
                order = cube.gather_orders[side]
                k = max(k for k in range(cube.number) if (mask >> order[k]) & 1)
                dense_copy(side, mask & ~(1 << order[k]), k).wait_recv()
            for k in steps_after(side, mask):
                dense_copy(side, mask, k).start()

    locals_ = [
        pltpu.make_async_copy(slice_ref.at[hz], dense_out.at[chip, core, hz], local.at[0]),
        pltpu.make_async_copy(x_ref, x_out.at[:, hz], local.at[1]),
    ]
    def count_slots():
        row = row_ref[...]
        first = row // column_ref.shape[0] * column_ref.shape[0]
        total = jnp.zeros(row.shape, jnp.int32)
        step = LANES
        for begin in range(0, column_ref.shape[0], step):
            column = column_ref[pl.ds(begin, step), :]
            earlier = ((column < row) & (column >= first)).astype(jnp.int32)
            total = total + jnp.sum(earlier, axis=0, keepdims=True)
        slot_out[...] = total

    for d in others:
        slice_copy(d).start()
    for copy in locals_:
        copy.start()
    along(0, lambda copy: copy.start())
    locals_[0].wait()
    for d in others:
        slice_copy(d).wait_recv()
    dense_turn(0)
    masks = sorted(range(1, 2 * chips), key=lambda m: bin(m).count("1"))
    shares = [masks[len(masks) * i // heads : len(masks) * (i + 1) // heads] for i in range(heads)]
    for mask in shares[0]:
        dense_turn(mask)
    for rank in range(1, heads):
        x_copy(rank, 1).wait_recv()
        along(rank, lambda copy: copy.start())
        for mask in shares[rank]:
            dense_turn(mask)
        if rank == 1:
            unit_copy.start()
            count_slots()
    unit_copy.wait()
    locals_[1].wait()
    for rank in range(heads):
        along(rank, lambda copy: copy.wait_send())
    for d in others:
        slice_copy(d).wait_send()
    for mask in [0] + masks:
        for side in range(2):
            for k in steps_after(side, mask):
                dense_copy(side, mask, k).wait_send()


def start(x, slices, unit, keys, chips, heads, number):
    cube = Cube(chips, True)
    return pl.pallas_call(
        functools.partial(start_kernel, cube, heads),
        out_shape=(
            jax.ShapeDtypeStruct((x.shape[0], heads) + x.shape[1:], bf16),
            jax.ShapeDtypeStruct((chips, 2) + slices.shape, bf16),
            jax.ShapeDtypeStruct(unit.shape, bf16),
            jax.ShapeDtypeStruct((1, keys.size), jnp.int32),
        ),
        in_specs=[ANY] * 3 + [WHOLE] * 2,
        out_specs=(ANY,) * 3 + (WHOLE,),
        scratch_shapes=[
            DMA((2,)),
            DMA((heads + 1,)),
            DMA((heads,)),
            DMA((heads - 1,)),
            DMA((heads - 1,)),
            DMA((2, 2 * chips)),
            DMA((2, 2 * chips)),
            DMA,
            DMA,
        ],
        compiler_params=pltpu.CompilerParams(collective_id=number, has_side_effects=True),
        name="start",
    )(x, slices, unit, keys[:, None], keys[None, :])


def end_kernel(cube, heads, first_ref, left_ref, right_ref, extra_ref, first_out, out_ref, *refs):
    count = cube.number
    in_ref, refs = refs[0], refs[1:]
    arrived = refs[:count]
    parts = refs[count : 2 * count]
    local, first_send, first_recv, line_send, line_recv, send, recv = refs[2 * count :]
    hz = lax.axis_index("head")
    others = near(heads)[::-1]
    half = in_ref.shape[-2] // 2
    rows = in_ref.shape[-2] // heads
    meet([cube.peer(digit) for digit in range(count)] + [{"head": (hz + d) % heads} for d in others])
    own = pltpu.make_async_copy(first_ref.at[:, hz], first_out.at[hz], local)
    own.start()
    copies = {}

    def slot(side, k, mask):
        return subsets(cube.scatter_orders[side][k + 1 :]).index(mask)

    def mine(side, mask):
        return in_ref.at[cube.place(mask) + (pl.ds(side * half, half),)]

    def total(side, steps, mask):
        value = mine(side, mask)[...].astype(f32)
        for j in range(steps):
            copies[(side, j, mask)].wait_recv()
            value = value + arrived[j][side, slot(side, j, mask)].astype(f32)
        return value.astype(bf16)

    def first_copy(d):
        place = (hz + d) % heads
        return pltpu.make_async_remote_copy(
            src_ref=first_ref.at[:, place],
            dst_ref=first_out.at[hz],
            send_sem=first_send.at[d - 1],
            recv_sem=first_recv.at[d - 1],
            device_id={"head": place},
            device_id_type=MESH,
        )

    for d in others:
        first_copy(d).start()
    strip = extra_ref.shape[0] // cube.chips
    product = right_ref.shape[1]
    for chip in range(cube.chips):
        rows_here = pl.ds(chip * strip, strip)
        value = lax.dot_general(
            left_ref[:, rows_here], right_ref[...], TN, preferred_element_type=f32
        )
        in_ref[chip, :, :, pl.ds(0, product)] = value.astype(bf16).reshape(2, strip // 2, product)
        in_ref[chip, :, :, pl.ds(product, LANES)] = extra_ref[rows_here, :].reshape(
            2, strip // 2, LANES
        )
    for k in range(count):
        for side in range(2):
            order = cube.scatter_orders[side]
            for mask in subsets(order[k + 1 :])[::-1]:
                full = mask | (1 << order[k])
                where = slot(side, k, mask)
                if k == 0:
                    piece = mine(side, full)
                else:
                    piece = parts[k - 1].at[side, where]
                    piece[...] = total(side, k, full)
                copies[(side, k, mask)] = pltpu.make_async_remote_copy(
                    src_ref=piece,
                    dst_ref=arrived[k].at[side, where],
                    send_sem=send.at[side, k, where],
                    recv_sem=recv.at[side, k, where],
                    device_id=cube.peer(order[k]),
                    device_id_type=MESH,
                )
                copies[(side, k, mask)].start()
    done = parts[count - 1]
    for side in range(2):
        done[0, pl.ds(side * half, half)] = total(side, count, 0)

    def line_copy(d):
        place = (hz + d) % heads
        return pltpu.make_async_remote_copy(
            src_ref=done.at[0, pl.ds(pl.multiple_of(place * rows, 16), rows)],
            dst_ref=out_ref.at[hz],
            send_sem=line_send.at[d - 1],
            recv_sem=line_recv.at[d - 1],
            device_id={"head": place},
            device_id_type=MESH,
        )

    for d in others:
        line_copy(d).start()
    out_ref[hz] = done[0, pl.ds(pl.multiple_of(hz * rows, 16), rows)]
    for copy in copies.values():
        copy.wait_send()
    own.wait()
    for d in others:
        line_copy(d).wait()
    for d in others:
        first_copy(d).wait()


def end(first, left, right, extra, chips, heads, number):
    rows, columns = extra.shape[0] // (2 * chips), right.shape[1] + LANES
    cube = Cube(chips, True)
    count = cube.number
    half = rows // 2
    slots = [(1 << count) >> (k + 1) for k in range(count)]
    return pl.pallas_call(
        functools.partial(end_kernel, cube, heads),
        out_shape=(
            jax.ShapeDtypeStruct((heads, first.shape[0]) + first.shape[2:], bf16),
            jax.ShapeDtypeStruct((heads, rows // heads, columns), bf16),
        ),
        in_specs=[ANY] + [WHOLE] * 3,
        out_specs=(ANY, WHOLE),
        scratch_shapes=[pltpu.VMEM((chips, 2, rows, columns), bf16)]
        + [pltpu.VMEM((2, s, half, columns), bf16) for s in slots]
        + [pltpu.VMEM((2, s, half, columns), bf16) for s in slots[1:]]
        + [
            pltpu.VMEM((1, rows, columns), bf16),
            DMA,
            DMA((heads - 1,)),
            DMA((heads - 1,)),
            DMA((heads - 1,)),
            DMA((heads - 1,)),
            DMA((2, count, slots[0])),
            DMA((2, count, slots[0])),
        ],
        compiler_params=pltpu.CompilerParams(
            collective_id=number, has_side_effects=True, vmem_limit_bytes=40 << 20
        ),
        cost_estimate=pl.CostEstimate(
            flops=50_000_000_000, bytes_accessed=150_000_000, transcendentals=0
        ),
        name="end",
    )(first, left, right, extra)


def place_kernel(chips, hidden, *refs):
    pieces, out_ref = refs[:chips], refs[chips]
    chip = lax.axis_index("chip")
    units = out_ref.shape[2] // 2
    for mask in range(chips):
        for part in range(2):
            begin = pl.multiple_of(part * units + flip(chip, mask) * hidden, hidden)
            out_ref[:, :, pl.ds(begin, hidden)] = pieces[mask][
                :, :, pl.ds(part * hidden, hidden)
            ].astype(f32)


def place_units(pieces, hidden):
    chips = len(pieces)
    experts_here, rows, double = pieces[0].shape
    group = 2 if experts_here % 2 == 0 else 1
    return pl.pallas_call(
        functools.partial(place_kernel, chips, hidden),
        grid=(experts_here // group,),
        out_shape=jax.ShapeDtypeStruct((experts_here, rows, chips * double), f32),
        in_specs=[pl.BlockSpec((group, rows, double), lambda e: (e, 0, 0))] * chips,
        out_specs=pl.BlockSpec((group, rows, chips * double), lambda e: (e, 0, 0)),
        name="place_units",
    )(*pieces)


def across(value, chips, mask):
    if mask == 0:
        return value
    return lax.ppermute(value, "chip", [(i, i ^ mask) for i in range(chips)])


class LineGather:
    def __init__(self, cube, heads, own, out, sems):
        self.cube, self.heads, self.own, self.out = cube, heads, own, out
        self.local, self.line_send, self.line_recv, self.send, self.recv = sems
        self.hz = lax.axis_index("head")
        self.middle = jnp.minimum(self.hz, heads - 1 - self.hz)
        self.rows = own.shape[0]

    @staticmethod
    def scratch(cube, heads):
        return [
            DMA,
            DMA((heads + 1,)),
            DMA((heads,)),
            DMA((2, 1 << cube.number, heads)),
            DMA((2, 1 << cube.number, heads)),
        ]

    def source(self, rank):
        hz, heads, middle = self.hz, self.heads, self.middle
        if rank == 0:
            return hz
        far = (rank + 1) // 2
        near_one = hz - far if rank % 2 else hz + far
        far_one = jnp.where(hz < heads - 1 - hz, hz + (rank - middle), hz - (rank - middle))
        return jnp.where(rank <= 2 * middle, near_one, far_one)

    def line_copy(self, rank, step):
        head = self.source(rank)
        place = self.out.at[self.cube.place(0) + (head,)]
        return pltpu.make_async_remote_copy(
            src_ref=self.own if rank == 0 else place,
            dst_ref=place,
            send_sem=self.line_send.at[self.heads if rank == 0 and step < 0 else head],
            recv_sem=self.line_recv.at[head],
            device_id={"head": (self.hz + step + self.heads) % self.heads},
            device_id_type=MESH,
        )

    def along(self, rank, act):
        head = self.source(rank)
        goes_up = self.hz + 1 < self.heads
        goes_down = self.hz > 0
        if rank:
            goes_up = goes_up & (head < self.hz)
            goes_down = goes_down & (head > self.hz)

        @pl.when(goes_up)
        def _():
            act(self.line_copy(rank, 1))

        @pl.when(goes_down)
        def _():
            act(self.line_copy(rank, -1))

    def plane_copy(self, side, mask, k, rank):
        digit = self.cube.gather_orders[side][k]
        later = mask | (1 << digit)
        head = self.source(rank)
        part = part_of(self.rows, side)
        place = self.out.at[self.cube.place(mask) + (head, part)]
        return pltpu.make_async_remote_copy(
            src_ref=self.own.at[part] if mask == 0 and rank == 0 else place,
            dst_ref=place,
            send_sem=self.send.at[side, later, head],
            recv_sem=self.recv.at[side, later, head],
            device_id=self.cube.peer(digit),
            device_id_type=MESH,
        )

    def steps_after(self, side, mask):
        order = self.cube.gather_orders[side]
        last = max([k for k in range(self.cube.number) if (mask >> order[k]) & 1], default=-1)
        return range(last + 1, self.cube.number)

    def begin(self):
        self.own_copy = pltpu.make_async_copy(
            self.own, self.out.at[self.cube.place(0) + (self.hz,)], self.local
        )
        self.own_copy.start()

    def receive(self, mask, rank):
        if mask == 0:
            if rank:
                self.line_copy(rank, 1).wait_recv()
            self.along(rank, lambda copy: copy.start())
        for side in range(2):
            if mask:
                order = self.cube.gather_orders[side]
                k = max(k for k in range(self.cube.number) if (mask >> order[k]) & 1)
                self.plane_copy(side, mask & ~(1 << order[k]), k, rank).wait_recv()
            for k in self.steps_after(side, mask):
                self.plane_copy(side, mask, k, rank).start()

    def events(self):
        masks = sorted(range(1 << self.cube.number), key=lambda m: bin(m).count("1"))
        return [(mask, rank) for mask in masks for rank in range(self.heads)]

    def finish(self):
        self.own_copy.wait()
        for mask, rank in self.events():
            if mask == 0:
                self.along(rank, lambda copy: copy.wait_send())
            for side in range(2):
                for k in self.steps_after(side, mask):
                    self.plane_copy(side, mask, k, rank).wait_send()


class DenseGather:
    def __init__(self, cube, heads, own, out, sems):
        self.cube, self.heads, self.own, self.out = cube, heads, own, out
        self.local, self.line_send, self.line_recv, self.send, self.recv = sems
        self.hz = lax.axis_index("head")

    @staticmethod
    def scratch(cube, heads):
        return [
            DMA,
            DMA((heads - 1,)),
            DMA((heads - 1,)),
            DMA((2, 1 << cube.number)),
            DMA((2, 1 << cube.number)),
        ]

    def line_copy(self, d):
        return pltpu.make_async_remote_copy(
            src_ref=self.own,
            dst_ref=self.out.at[self.cube.place(0) + (self.hz,)],
            send_sem=self.line_send.at[d - 1],
            recv_sem=self.line_recv.at[d - 1],
            device_id={"head": (self.hz + d) % self.heads},
            device_id_type=MESH,
        )

    def flat_copy(self, side, mask, k):
        digit = self.cube.gather_orders[side][k]
        later = mask | (1 << digit)
        part = self.heads // 2
        place = self.out.at[self.cube.place(mask) + (pl.ds(side * part, part),)]
        return pltpu.make_async_remote_copy(
            src_ref=place,
            dst_ref=place,
            send_sem=self.send.at[side, later],
            recv_sem=self.recv.at[side, later],
            device_id=self.cube.peer(digit),
            device_id_type=MESH,
        )

    def steps_after(self, side, mask):
        order = self.cube.gather_orders[side]
        last = max([k for k in range(self.cube.number) if (mask >> order[k]) & 1], default=-1)
        return range(last + 1, self.cube.number)

    def begin(self):
        self.own_copy = pltpu.make_async_copy(
            self.own, self.out.at[self.cube.place(0) + (self.hz,)], self.local
        )
        self.own_copy.start()
        for d in near(self.heads)[::-1]:
            self.line_copy(d).start()

    def events(self):
        return [(mask, 2) for mask in range(1 << self.cube.number)]

    def receive(self, mask, _):
        if mask == 0:
            self.own_copy.wait()
            for d in near(self.heads):
                self.line_copy(d).wait_recv()
        for side in range(2):
            if mask:
                order = self.cube.gather_orders[side]
                k = max(k for k in range(self.cube.number) if (mask >> order[k]) & 1)
                self.flat_copy(side, mask & ~(1 << order[k]), k).wait_recv()
            for k in self.steps_after(side, mask):
                self.flat_copy(side, mask, k).start()

    def finish(self):
        for d in near(self.heads):
            self.line_copy(d).wait_send()
        for mask in range(1 << self.cube.number):
            for side in range(2):
                for k in self.steps_after(side, mask):
                    self.flat_copy(side, mask, k).wait_send()


class LineSums:
    def __init__(self, cube, heads, blocks, out, refs):
        self.cube, self.heads, self.blocks, self.out = cube, heads, blocks, out
        count = cube.number
        self.arrived, self.parts = refs[:count], refs[count : 2 * count - 1]
        self.line_out, self.line_in, self.send, self.recv, self.end_send, self.end_recv = refs[
            2 * count - 1 :
        ]
        self.hz = lax.axis_index("head")
        self.rows = blocks.shape[-2]
        self.outward = near(heads)[::-1] + [0]
        self.turns = heads + count + 1

    @staticmethod
    def scratch(cube, heads, rows, columns):
        count = cube.number
        slots = [(1 << count) >> (k + 1) for k in range(count)]
        half = cut_rows(rows)
        return (
            [pltpu.VMEM((2, s, heads, half, columns), bf16) for s in slots]
            + [pltpu.VMEM((2, s, heads, half, columns), bf16) for s in slots[1:]]
            + [
                pltpu.VMEM((heads - 1, rows, columns), bf16),
                pltpu.VMEM((heads - 1, rows, columns), bf16),
                DMA((2, count, slots[0], heads)),
                DMA((2, count, slots[0], heads)),
                DMA((heads - 1,)),
                DMA((heads - 1,)),
            ]
        )

    def slot(self, side, k, mask):
        return subsets(self.cube.scatter_orders[side][k + 1 :]).index(mask)

    def mine(self, side, mask, d):
        place = self.cube.place(mask) + ((self.hz + d) % self.heads,)
        return self.blocks.at[place + (part_of(self.rows, side),)]

    def there(self, ref, side, where, d):
        return ref.at[side, where, d, pl.ds(0, part_of(self.rows, side).size)]

    def copy_of(self, side, k, mask, d):
        order = self.cube.scatter_orders[side]
        where = self.slot(side, k, mask)
        if k == 0:
            piece = self.mine(side, mask | (1 << order[0]), d)
        else:
            piece = self.there(self.parts[k - 1], side, where, d)
        return pltpu.make_async_remote_copy(
            src_ref=piece,
            dst_ref=self.there(self.arrived[k], side, where, d),
            send_sem=self.send.at[side, k, where, d],
            recv_sem=self.recv.at[side, k, where, d],
            device_id=self.cube.peer(order[k]),
            device_id_type=MESH,
        )

    def end_copy(self, d):
        return pltpu.make_async_remote_copy(
            src_ref=self.line_out.at[d - 1],
            dst_ref=self.line_in.at[d - 1],
            send_sem=self.end_send.at[d - 1],
            recv_sem=self.end_recv.at[d - 1],
            device_id={"head": (self.hz + d) % self.heads},
            device_id_type=MESH,
        )

    def sums(self, side, steps, mask, d):
        value = self.mine(side, mask, d)[...].astype(f32)
        for j in range(steps):
            self.copy_of(side, j, mask, d).wait_recv()
            value = value + self.there(self.arrived[j], side, self.slot(side, j, mask), d)[
                ...
            ].astype(f32)
        return value

    def turn(self, turn):
        count = self.cube.number
        if turn < self.heads:
            for side in range(2):
                for mask in subsets(self.cube.scatter_orders[side][1:])[::-1]:
                    self.copy_of(side, 0, mask, self.outward[turn]).start()
        for k in range(1, count):
            if 0 <= turn - k - 1 < self.heads:
                d = self.outward[turn - k - 1]
                for side in range(2):
                    order = self.cube.scatter_orders[side]
                    for mask in subsets(order[k + 1 :])[::-1]:
                        value = self.sums(side, k, mask | (1 << order[k]), d)
                        place = self.there(self.parts[k - 1], side, self.slot(side, k, mask), d)
                        place[...] = value.astype(bf16)
                        self.copy_of(side, k, mask, d).start()
        if 0 <= turn - count - 1 < self.heads:
            d = self.outward[turn - count - 1]
            for side in range(2):
                value = self.sums(side, count, 0, d)
                part = part_of(self.rows, side)
                if d:
                    self.line_out[d - 1, part] = value.astype(bf16)
                else:
                    self.out[part] = value
            if d:
                self.end_copy(d).start()

    def finish(self):
        others = near(self.heads)
        for d in others:
            self.end_copy(d).wait_recv()
            self.out[...] += self.line_in[d - 1].astype(f32)
        for d in others:
            self.end_copy(d).wait_send()
        for side in range(2):
            for k in range(self.cube.number):
                for mask in subsets(self.cube.scatter_orders[side][k + 1 :]):
                    for d in self.outward:
                        self.copy_of(side, k, mask, d).wait_send()


TN = (((0,), (0,)), ((), ()))


def allowed(key_segments, query_segments, block, rows, seq):
    columns = query_segments.shape[1]
    key_place = block * rows + lax.broadcasted_iota(jnp.int32, (rows, columns), 0)
    query_place = seq * rows + lax.broadcasted_iota(jnp.int32, (rows, columns), 1) % rows
    return (key_segments == query_segments) & (key_place <= query_place)


def attend_kernel(cube, heads, group, beside, *refs):
    q_ref, kv_ref, key_seg, query_seg = refs[:4]
    near_refs, refs = refs[4 : 4 + len(beside)], refs[4 + len(beside) :]
    lines_ref, kv_out, out_turned, lse_ref = refs[:4]
    far_refs, refs = refs[4 : 4 + len(beside)], refs[4 + len(beside) :]
    stage, top, total, acc, send, recv, line_send, line_recv = refs[:8]
    chip, core, hz = lax.axis_index("chip"), lax.axis_index("core"), lax.axis_index("head")
    seq = chip * 2 + core
    others = near(heads)[::-1]
    batch, rows, columns = kv_ref.shape
    kv_heads = columns // (2 * HEAD_WIDTH)
    part = rows // 2
    meet([cube.peer(digit) for digit in range(cube.number)] + [{"head": (hz + d) % heads} for d in others])
    kv_out[chip, core] = kv_ref[...]
    gathers = []
    rest_refs = refs[8:]
    for with_core, own_block, all_blocks in zip(beside, near_refs, far_refs):
        kind = DenseGather if with_core else LineGather
        own_cube = Cube(cube.chips, with_core)
        gathers.append(kind(own_cube, heads, own_block, all_blocks, rest_refs[:5]))
        rest_refs = rest_refs[5:]
    fronts = {}
    for one in gathers:
        for mask, rank in one.events():
            fronts.setdefault(rank + bin(mask).count("1"), []).append((one, (mask, rank)))
    last_front = max(fronts, default=0)
    now = cube.number + 1

    def pass_front(index):
        for one, event in fronts.get(index, []):
            one.receive(*event)

    def copy_of(side, mask, k):
        order = cube.gather_orders[side]
        later = mask | (1 << order[k])
        place = cube.place(mask) + (slice(None), pl.ds(side * part, part))
        return pltpu.make_async_remote_copy(
            src_ref=kv_ref.at[:, pl.ds(side * part, part)] if mask == 0 else kv_out.at[place],
            dst_ref=kv_out.at[place],
            send_sem=send.at[side, later],
            recv_sem=recv.at[side, later],
            device_id=cube.peer(order[k]),
            device_id_type=MESH,
        )

    copies = []

    def forward(mask):
        for side in range(2):
            order = cube.gather_orders[side]
            last = max([k for k in range(cube.number) if (mask >> order[k]) & 1], default=-1)
            if mask:
                copy_of(side, mask & ~(1 << order[last]), last).wait_recv()
            for k in range(last + 1, cube.number):
                copy_of(side, mask, k).start()
                copies.append((side, mask, k))

    forward(0)
    for one in gathers:
        one.begin()
    pass_front(0)
    top[...] = jnp.full_like(top, negative)
    total[...] = jnp.zeros_like(total)
    acc[...] = jnp.zeros_like(acc)

    def block_step(block):
        place = (block // 2, block % 2)
        for b in range(batch):
            mask = allowed(
                key_seg[b, pl.ds(pl.multiple_of(block * rows, rows), rows), :],
                query_seg[b],
                block,
                rows,
                seq,
            )
            for j in range(kv_heads):
                pair = b * kv_heads + j
                begin = j * 2 * HEAD_WIDTH
                keys = kv_out[place + (b, slice(None), pl.ds(begin, HEAD_WIDTH))]
                values = kv_out[place + (b, slice(None), pl.ds(begin + HEAD_WIDTH, HEAD_WIDTH))]
                scores = lax.dot_general(keys, q_ref[pair], NT, preferred_element_type=f32)
                scores = jnp.where(mask, scores, negative)
                new = jnp.maximum(top[pair], jnp.max(scores, axis=0, keepdims=True))
                weights = jnp.exp(scores - new)
                shrink = jnp.exp(top[pair] - new)
                top[pair] = new
                total[pair] = total[pair] * shrink + jnp.sum(weights, axis=0, keepdims=True)
                acc[pair] = acc[pair] * shrink + lax.dot_general(
                    values, weights.astype(bf16), TN, preferred_element_type=f32
                )

    block_step(seq)
    for level in range(1, cube.number + 1):
        for mask in range(1, 1 << cube.number):
            if bin(mask).count("1") == level:
                forward(mask)
    pass_front(1)
    now = 2
    turns = 2 * cube.chips
    if beside:
        for turn in range(turns):
            if turn == turns // 2:
                pass_front(now)
                now += 1

            @pl.when(turn < seq)
            def _():
                block_step(turn)

    else:

        @pl.loop(0, seq)
        def _(block):
            block_step(block)

    spot = rows // heads
    for b in range(batch):
        for j in range(kv_heads):
            pair = b * kv_heads + j
            value = acc[pair] / total[pair]
            out_turned[pair] = value
            lse_ref[pair] = top[pair] + jnp.log(total[pair])
            value = value.T.astype(bf16)
            for g in range(group):
                for head in range(heads):
                    begin = (j * group + g) * HEAD_WIDTH
                    stage[head, pl.ds(b * spot, spot), pl.ds(begin, HEAD_WIDTH)] = value[
                        g * rows + head * spot : g * rows + (head + 1) * spot
                    ]

    def line_copy(d):
        return pltpu.make_async_remote_copy(
            src_ref=stage.at[(hz + d) % heads],
            dst_ref=lines_ref.at[hz],
            send_sem=line_send.at[d - 1],
            recv_sem=line_recv.at[d - 1],
            device_id={"head": (hz + d) % heads},
            device_id_type=MESH,
        )

    for d in others:
        line_copy(d).start()
    lines_ref[hz] = stage[hz]
    for index in range(now, last_front + 1):
        pass_front(index)
    for side, mask, k in copies:
        copy_of(side, mask, k).wait_send()
    for d in others:
        line_copy(d).wait()
    for one in gathers:
        one.finish()


def attend(queries, keys_values, key_seg, query_seg, beside, chips, heads, group, number):
    batch, rows, columns = keys_values.shape
    pairs, wide, depth = queries.shape
    cube = Cube(chips, True)
    group_columns = group * columns // 2
    tokens = batch * rows // heads
    return pl.pallas_call(
        functools.partial(attend_kernel, cube, heads, group, [core for _, core in beside]),
        out_shape=(
            jax.ShapeDtypeStruct((heads, tokens, group_columns), bf16),
            jax.ShapeDtypeStruct((chips, 2, batch, rows, columns), bf16),
            jax.ShapeDtypeStruct((pairs, depth, wide), f32),
            jax.ShapeDtypeStruct((pairs, 1, wide), f32),
        )
        + tuple(
            jax.ShapeDtypeStruct((chips,) + (2,) * with_core + (heads,) + value.shape, bf16)
            for value, with_core in beside
        ),
        in_specs=[WHOLE] * 4 + [ANY] * len(beside),
        out_specs=(WHOLE,) * 4 + (ANY,) * len(beside),
        scratch_shapes=[
            pltpu.VMEM((heads, tokens, group_columns), bf16),
            pltpu.VMEM((pairs, 1, wide), f32),
            pltpu.VMEM((pairs, 1, wide), f32),
            pltpu.VMEM((pairs, depth, wide), f32),
            DMA((2, 2 * chips)),
            DMA((2, 2 * chips)),
            DMA((heads - 1,)),
            DMA((heads - 1,)),
        ]
        + [
            item
            for _, core in beside
            for item in (DenseGather if core else LineGather).scratch(Cube(chips, core), heads)
        ],
        compiler_params=pltpu.CompilerParams(
            collective_id=number, has_side_effects=True, vmem_limit_bytes=50 << 20
        ),
        name="attend",
    )(queries, keys_values, key_seg, query_seg, *[value for value, _ in beside])


def attend_back_kernel(cube, heads, group, beside, shares, *refs):
    q_ref, kv_ref, key_seg, query_seg, out_turned, lse_ref, dh_ref = refs[:7]
    near_refs, refs = refs[7 : 7 + len(beside)], refs[7 + len(beside) :]
    pair_refs, refs = refs[:shares], refs[shares:]
    dq_ref, dkv_ref = refs[:2]
    far_refs, refs = refs[2 : 2 + len(beside)], refs[2 + len(beside) :]
    added = refs[: cube.chips] if shares else ()
    refs = (None,) * 9 + refs[len(added) :]
    count = cube.number
    landed, d_out, delta, dq_turned, grads = refs[9:14]
    arrived, parts = refs[14 : 14 + count], refs[14 + count : 13 + 2 * count]
    send, recv, line_send, line_recv = refs[13 + 2 * count : 17 + 2 * count]
    turns = 2 * cube.chips
    rest = refs[17 + 2 * count :]
    sums_beside = []
    for with_core, source, target in zip(beside, near_refs, far_refs):
        own_cube = Cube(cube.chips, with_core)
        size = 2 * own_cube.number + 5
        sums_beside.append(LineSums(own_cube, heads, source, target, rest[:size]))
        rest = rest[size:]

    def load_pair(mask):
        place = flip(lax.axis_index("chip"), mask)
        return [
            pltpu.make_async_copy(pair_refs[i].at[place], rest[i], rest[3].at[i]) for i in range(2)
        ]

    def store_sum(mask):
        return pltpu.make_async_copy(rest[2], added[mask], rest[3].at[2])

    def add_pair(turn):
        mask = turn // 2
        if turn % 2 == 0:
            for copy in load_pair(mask):
                copy.start()
            return
        for copy in load_pair(mask):
            copy.wait()
        if mask:
            store_sum(mask - 1).wait()
        rest[2][...] = (rest[0][...].astype(f32) + rest[1][...].astype(f32)).astype(bf16)
        store_sum(mask).start()

    chip, core, hz = lax.axis_index("chip"), lax.axis_index("core"), lax.axis_index("head")
    seq = chip * 2 + core
    others = near(heads)[::-1]
    batch, rows, columns = kv_ref.shape[2:]
    kv_heads = columns // (2 * HEAD_WIDTH)
    spot = rows // heads
    half = grads.shape[2] // 2
    meet([cube.peer(digit) for digit in range(count)] + [{"head": (hz + d) % heads} for d in others])

    def line_copy(d):
        return pltpu.make_async_remote_copy(
            src_ref=dh_ref.at[(hz + d) % heads],
            dst_ref=landed.at[hz],
            send_sem=line_send.at[d - 1],
            recv_sem=line_recv.at[d - 1],
            device_id={"head": (hz + d) % heads},
            device_id_type=MESH,
        )

    for d in others:
        line_copy(d).start()
    for turn in range(2):
        for one in sums_beside:
            one.turn(turn)
    landed[hz] = dh_ref[hz]
    grads[...] = jnp.zeros_like(grads)
    dq_turned[...] = jnp.zeros_like(dq_turned)
    for d in others:
        line_copy(d).wait()
    for b in range(batch):
        for j in range(kv_heads):
            pair = b * kv_heads + j
            for g in range(group):
                for head in range(heads):
                    begin = (j * group + g) * HEAD_WIDTH
                    d_out[pair, pl.ds(g * rows + head * spot, spot), :] = landed[
                        head, pl.ds(b * spot, spot), pl.ds(begin, HEAD_WIDTH)
                    ]
            delta[pair] = jnp.sum(
                d_out[pair].astype(f32).T * out_turned[pair], axis=0, keepdims=True
            )

    def block_step(block):
        place = (block // 2, block % 2)
        for b in range(batch):
            mask = allowed(
                key_seg[b, pl.ds(pl.multiple_of(block * rows, rows), rows), :],
                query_seg[b],
                block,
                rows,
                seq,
            )
            for j in range(kv_heads):
                pair = b * kv_heads + j
                begin = j * 2 * HEAD_WIDTH
                keys = kv_ref[place + (b, slice(None), pl.ds(begin, HEAD_WIDTH))]
                values = kv_ref[place + (b, slice(None), pl.ds(begin + HEAD_WIDTH, HEAD_WIDTH))]
                scores = lax.dot_general(keys, q_ref[pair], NT, preferred_element_type=f32)
                probs = jnp.exp(jnp.where(mask, scores, negative) - lse_ref[pair])
                d_probs = lax.dot_general(values, d_out[pair], NT, preferred_element_type=f32)
                d_scores = (probs * (d_probs - delta[pair])).astype(bf16)
                dq_turned[pair] += lax.dot_general(
                    keys, d_scores, TN, preferred_element_type=f32
                )
                d_keys = jnp.dot(d_scores, q_ref[pair], preferred_element_type=f32)
                d_values = jnp.dot(probs.astype(bf16), d_out[pair], preferred_element_type=f32)
                grads[place + (pl.ds(b * rows, rows), pl.ds(begin, 2 * HEAD_WIDTH))] = (
                    jnp.concatenate([d_keys, d_values], axis=1).astype(bf16)
                )

    done = 2
    if beside:
        for turn in range(turns):

            @pl.when(turn <= seq)
            def _():
                block_step(turn)

            if shares:
                add_pair(turn)
            if turn % 3 == 2:
                for one in sums_beside:
                    one.turn(done)
                done += 1

    else:

        @pl.loop(0, seq + 1)
        def _(block):
            block_step(block)

    def slot(side, k, mask):
        return subsets(cube.scatter_orders[side][k + 1 :]).index(mask)

    def mine(side, mask):
        return grads.at[cube.place(mask) + (pl.ds(side * half, half),)]

    copies = {}

    def sums(side, steps, mask):
        value = mine(side, mask)[...].astype(f32)
        for j in range(steps):
            copies[(side, j, mask)].wait_recv()
            value = value + arrived[j][side, slot(side, j, mask)].astype(f32)
        return value

    for k in range(count):
        for side in range(2):
            order = cube.scatter_orders[side]
            for mask in subsets(order[k + 1 :])[::-1]:
                full = mask | (1 << order[k])
                where = slot(side, k, mask)
                if k == 0:
                    piece = mine(side, full)
                else:
                    piece = parts[k - 1].at[side, where]
                    piece[...] = sums(side, k, full).astype(bf16)
                copies[(side, k, mask)] = pltpu.make_async_remote_copy(
                    src_ref=piece,
                    dst_ref=arrived[k].at[side, where],
                    send_sem=send.at[side, k, where],
                    recv_sem=recv.at[side, k, where],
                    device_id=cube.peer(order[k]),
                    device_id_type=MESH,
                )
                copies[(side, k, mask)].start()
        for one in sums_beside:
            if done < one.turns:
                one.turn(done)
        done += 1
    scale = HEAD_WIDTH ** (-0.5)
    for pair in range(batch * kv_heads):
        dq_ref[pair] = (dq_turned[pair] * scale).T.astype(bf16)
    for side in range(2):
        dkv_ref[pl.ds(side * half, half)] = sums(side, count, 0)
    for turn in range(done, max([one.turns for one in sums_beside], default=0)):
        for one in sums_beside:
            if turn < one.turns:
                one.turn(turn)
    for copy in copies.values():
        copy.wait_send()
    for one in sums_beside:
        one.finish()
    if shares:
        store_sum(cube.chips - 1).wait()


def attend_back(
    queries, kv_all, key_seg, query_seg, out_turned, lse, d_heads, beside, shares, heads, group, number
):
    chips, _, batch, rows, columns = kv_all.shape
    pairs, wide, depth = queries.shape
    cube = Cube(chips, True)
    count = cube.number
    half = batch * rows // 2
    slots = [(1 << count) >> (k + 1) for k in range(count)]
    return pl.pallas_call(
        functools.partial(
            attend_back_kernel, cube, heads, group, [core for _, core in beside], len(shares)
        ),
        out_shape=(
            jax.ShapeDtypeStruct((pairs, wide, depth), bf16),
            jax.ShapeDtypeStruct((batch * rows, columns), f32),
        )
        + tuple(jax.ShapeDtypeStruct(value.shape[-2:], f32) for value, _ in beside)
        + tuple(jax.ShapeDtypeStruct(shares[0].shape[1:], bf16) for _ in range(chips) if shares),
        in_specs=[WHOLE] * (7 + len(beside)) + [ANY] * len(shares),
        out_specs=(WHOLE,) * (2 + len(beside)) + (ANY,) * (chips * bool(shares)),
        scratch_shapes=[
            pltpu.VMEM(d_heads.shape, bf16),
            pltpu.VMEM((pairs, wide, depth), bf16),
            pltpu.VMEM((pairs, 1, wide), f32),
            pltpu.VMEM((pairs, depth, wide), f32),
            pltpu.VMEM((chips, 2, batch * rows, columns), bf16),
        ]
        + [pltpu.VMEM((2, s, half, columns), bf16) for s in slots]
        + [pltpu.VMEM((2, s, half, columns), bf16) for s in slots[1:]]
        + [
            DMA((2, count, slots[0])),
            DMA((2, count, slots[0])),
            DMA((heads - 1,)),
            DMA((heads - 1,)),
        ]
        + [
            item
            for value, core in beside
            for item in LineSums.scratch(Cube(chips, core), *value.shape[-3:])
        ]
        + [pltpu.VMEM(shares[0].shape[1:], bf16) for _ in range(3) if shares]
        + [DMA((3,)) for _ in range(1) if shares],
        compiler_params=pltpu.CompilerParams(
            collective_id=number, has_side_effects=True, vmem_limit_bytes=56 << 20
        ),
        name="attend_back",
    )(
        queries, kv_all, key_seg, query_seg, out_turned, lse, d_heads, *[v for v, _ in beside], *shares
    )


def sibling(value):
    return lax.ppermute(value, "core", [(0, 1), (1, 0)])


def per_device(
    layer_input,
    segments,
    routes,
    pair_rank,
    query_key_value_weight,
    output_weight,
    router_weight,
    norm_attn,
    norm_ffn,
    w_gate_up,
    w_down,
    cotangent,
):
    chips = lax.axis_size("chip")
    head_number = lax.axis_size("head")
    sequence_batch, token_rows, width = layer_input.shape
    length = segments.shape[1]
    blk = token_rows * head_number
    query_group = QUERY_HEADS // KEY_VALUE_HEADS
    key_value_location = KEY_VALUE_HEADS // head_number
    loc_experts, slice_rows = w_gate_up.shape[:2]
    top = routes.shape[2]
    tokens_present = sequence_batch * token_rows
    pairs = tokens_present * top
    line_tokens = tokens_present * head_number
    scale = HEAD_WIDTH ** (-0.5)
    hidden = FF // chips
    loc_columns = key_value_location * (query_group + 2) * HEAD_WIDTH
    chip = lax.axis_index("chip")
    core = lax.axis_index("core")
    head = lax.axis_index("head")
    seq_index = chip * 2 + core
    dense_rows = query_key_value_weight.shape[0]

    extras = jnp.concatenate([router_weight, norm_attn[:, None], norm_ffn[:, None]], axis=1)
    extras = jnp.pad(extras, ((0, 0), (0, LANES - extras.shape[1])))
    slices = query_key_value_weight.reshape(dense_rows, head_number, loc_columns).transpose(1, 0, 2)
    slices = jnp.concatenate(
        [slices, jnp.broadcast_to(extras, (head_number,) + extras.shape)], axis=2
    )
    group_tokens = chips * head_number * tokens_present
    columns = width + LANES
    fused = hidden % LANES == 0 and group_tokens <= 2048
    own_tokens = layer_input.reshape(tokens_present, width)
    cots = cotangent.reshape(tokens_present, width)
    if fused:

        def unit_of(weights, mask):
            begins = [part * FF + (chip ^ mask) * hidden for part in range(2)]
            cut = [lax.dynamic_slice_in_dim(weights, begin, hidden, 2) for begin in begins]
            return jnp.concatenate(cut, axis=2)

        keys = (routes * pairs + pair_rank).reshape(pairs)
        x_line, dense, last_unit, slot = start(
            layer_input, slices, unit_of(w_gate_up, chips - 1), keys, chips, head_number, 1
        )
        x_line, w_gate_up = lax.optimization_barrier((x_line, w_gate_up))
        units = [across(unit_of(w_gate_up, mask), chips, mask) for mask in range(chips - 1)]
        units.append(last_unit)
        dense = dense.reshape(width, loc_columns + LANES)
    else:
        parts = w_gate_up.reshape(loc_experts, slice_rows, 2, chips, hidden).transpose(3, 2, 1, 0, 4)
        parts = parts.reshape(chips, 2, slice_rows, loc_experts * hidden)
        piled = jnp.zeros((chips, 2, 2, slice_rows, loc_experts * hidden), bf16)
        for mask in range(chips):
            piece = lax.dynamic_index_in_dim(parts, chip ^ mask, 0, keepdims=False)
            piece = across(piece, chips, mask)
            other = sibling(piece)
            piled = lax.dynamic_update_slice(piled, piece[None, None], (chip ^ mask, core, 0, 0, 0))
            piled = lax.dynamic_update_slice(piled, other[None, None], (chip ^ mask, 1 - core, 0, 0, 0))
        piled = piled.transpose(2, 0, 1, 3, 4).reshape(2, width, loc_experts * hidden)
        expert_gate, expert_up = piled[0], piled[1]
        down_other = sibling(w_down)
        expert_down = (
            jnp.where(
                core == 0,
                jnp.concatenate([w_down, down_other], axis=1),
                jnp.concatenate([down_other, w_down], axis=1),
            )
        ).reshape(loc_experts * hidden, width)

        lined = line_exchange(slices, head_number, 1)
        dense = gather(
            lined.reshape(head_number * dense_rows, loc_columns + LANES), chips, 1, True, 2
        ).reshape(width, loc_columns + LANES)
        x_line = line_exchange(layer_input.reshape(tokens_present, width), head_number, 3, True)

    if not fused:
        grad_all = lax.all_gather(cots, ("chip", "head"), axis=0, tiled=True)
        dense_out = lax.all_gather(output_weight, ("chip", "core", "head"), axis=0, tiled=True)

    dense_qkv = dense[:, :loc_columns]
    dense_router = dense[:, loc_columns : loc_columns + EXPERTS]
    gain_attn = dense[:, loc_columns + EXPERTS].astype(f32)
    gain_ffn = dense[:, loc_columns + EXPERTS + 1].astype(f32)

    x_line = x_line.reshape(line_tokens, width).astype(f32)
    normed_line = x_line * lax.rsqrt(jnp.mean(x_line * x_line, axis=1, keepdims=True) + epsilon)
    first_line = (normed_line * gain_attn).astype(bf16)

    def to_blocks(value):
        columns = value.shape[1:]
        if fused:
            return value.reshape((sequence_batch, blk) + columns)
        return (
            value.reshape((head_number, sequence_batch, token_rows) + columns)
            .swapaxes(0, 1)
            .reshape((sequence_batch, blk) + columns)
        )

    def to_lines(value):
        columns = value.shape[2:]
        if fused:
            return value.reshape((line_tokens,) + columns)
        return (
            value.reshape((sequence_batch, head_number, token_rows) + columns)
            .swapaxes(0, 1)
            .reshape((line_tokens,) + columns)
        )

    q_start = seq_index * blk
    q_pos = q_start + jnp.arange(blk, dtype=jnp.int32)
    cosine, sine = rope_tables(q_pos, HEAD_WIDTH)
    projected = to_blocks(jnp.dot(first_line, dense_qkv, preferred_element_type=f32)).reshape(
        sequence_batch, blk, key_value_location, query_group + 2, HEAD_WIDTH
    )
    turned = rotate(projected[:, :, :, : query_group + 1], cosine, sine)
    query_rows = turned[:, :, :, :query_group].astype(bf16)
    keys_values = (
        jnp.stack([turned[:, :, :, query_group], projected[:, :, :, query_group + 1]], axis=3)
        .astype(bf16)
        .reshape(sequence_batch * blk, key_value_location * 2 * HEAD_WIDTH)
    )
    kv_columns = key_value_location * 2 * HEAD_WIDTH
    pairs_here = sequence_batch * key_value_location
    group_columns = key_value_location * query_group * HEAD_WIDTH
    queries = (
        (query_rows.astype(f32) * scale)
        .astype(bf16)
        .transpose(0, 2, 3, 1, 4)
        .reshape(pairs_here, query_group * blk, HEAD_WIDTH)
    )
    key_seg = segments[:, :, None]
    q_seg = lax.dynamic_slice_in_dim(segments, q_start, blk, 1)
    query_seg = jnp.tile(q_seg[:, None, :], (1, 1, query_group))
    lines, kv_all, out_turned, lse, *beside = attend(
        queries,
        keys_values.reshape(sequence_batch, blk, kv_columns),
        key_seg,
        query_seg,
        [(cots, False), (output_weight, True)] if fused else [],
        chips,
        head_number,
        query_group,
        4,
    )
    if fused:
        grad_all = beside[0].reshape(group_tokens, width)
        dense_out = beside[1].reshape(QUERY_HEADS * HEAD_WIDTH, width)
    mixed_heads = lines.transpose(1, 0, 2).reshape(tokens_present, QUERY_HEADS * HEAD_WIDTH)
    tokens = layer_input.reshape(tokens_present, width).astype(f32)
    middle = tokens + jnp.dot(mixed_heads, dense_out, preferred_element_type=f32)
    inverse_two = lax.rsqrt(jnp.mean(middle * middle, axis=1, keepdims=True) + epsilon)
    normed_two = middle * inverse_two
    second_input = (normed_two * gain_ffn).astype(bf16)
    router_logits = jnp.dot(second_input, dense_router, preferred_element_type=f32)
    route_flat = routes.reshape(tokens_present, top)
    hot = route_flat[:, :, None] == jnp.arange(EXPERTS, dtype=jnp.int32)[None, None, :]
    chosen = jnp.sum(jnp.where(hot, router_logits[:, None, :], 0.0), axis=2)
    gates = jax.nn.softmax(chosen, axis=-1)
    if not fused:
        expert_of = route_flat.reshape(pairs)
        rank = pair_rank.reshape(pairs)
        slot = jnp.sum(
            (expert_of[None, :] == expert_of[:, None]) & (rank[None, :] < rank[:, None]),
            axis=1,
            dtype=jnp.int32,
        )
    kept = (slot < CAP).reshape(tokens_present, top).astype(f32)
    weights_pair = gates * kept
    spread = jnp.sum(jnp.where(hot, weights_pair[:, :, None], 0.0), axis=1)
    spread_high = spread.astype(bf16)
    spread_low = (spread - spread_high.astype(f32)).astype(bf16)
    pad = jnp.zeros((tokens_present, LOW - EXPERTS), bf16)
    payload = jnp.concatenate([second_input, spread_high, pad, spread_low, pad], axis=1)
    if fused:
        back, moe_part, keep_up, other_up, keep_down, other_down = expert_turn(
            payload, grad_all, units, w_down, head_number, 6
        )
        down_share = keep_down.astype(f32) + other_down.astype(f32)
    else:
        x_all = gather(payload, chips, head_number, False, 6).reshape(group_tokens, columns)
        moe_part, back_part, d_gate_w, d_up_w, d_down_w = experts(
            x_all, grad_all, expert_gate, expert_up, expert_down, hidden
        )
        back_part = back_part.reshape(chips, head_number, tokens_present, columns)
        back = scatter_sum(back_part, chips, head_number, False, 7)
        moe = lax.psum_scatter(moe_part, ("chip", "head"), scatter_dimension=0, tiled=True)
        grads = jnp.stack([d_gate_w, d_up_w]).reshape(2, chips, 2, slice_rows, loc_experts * hidden)
        keep = lax.dynamic_index_in_dim(grads, core, 2, keepdims=False)
        give = lax.dynamic_index_in_dim(grads, 1 - core, 2, keepdims=False)
        shared = (keep.astype(f32) + sibling(give).astype(f32)).astype(bf16)
        piled = jnp.zeros((chips, 2, slice_rows, loc_experts * hidden), bf16)
        for mask in range(chips):
            piece = across(lax.dynamic_index_in_dim(shared, chip ^ mask, 1, keepdims=False), chips, mask)
            piled = lax.dynamic_update_slice(piled, piece[None], (chip ^ mask, 0, 0, 0))
        up_share = (
            piled.reshape(chips, 2, slice_rows, loc_experts, hidden)
            .transpose(3, 2, 1, 0, 4)
            .astype(f32)
            .reshape(loc_experts, slice_rows, 2 * FF)
        )
        d_down_w = d_down_w.reshape(loc_experts, 2, hidden // 2, width)
        keep = lax.dynamic_index_in_dim(d_down_w, core, 1, keepdims=False)
        give = lax.dynamic_index_in_dim(d_down_w, 1 - core, 1, keepdims=False)
        down_share = keep.astype(f32) + sibling(give).astype(f32)

    grad_out = cotangent.reshape(tokens_present, width).astype(f32)
    d_kept = back[:, width : width + EXPERTS]
    grad_gate = jnp.sum(jnp.where(hot, d_kept[:, None, :], 0.0), axis=2) * kept
    grad_chosen = gates * (grad_gate - jnp.sum(gates * grad_gate, axis=1, keepdims=True))
    grad_logits = jnp.sum(jnp.where(hot, grad_chosen[:, :, None], 0.0), axis=1)
    grad_router = jnp.dot(second_input.astype(f32).T, grad_logits, precision=HIGH_PRECISION)
    grad_second = back[:, :width] + jnp.dot(
        grad_logits, dense_router.astype(f32).T, precision=HIGH_PRECISION
    )
    grad_gain_ffn = jnp.sum(grad_second * normed_two, axis=0)
    scaled_two = grad_second * gain_ffn
    grad_mid = grad_out + inverse_two * (
        scaled_two - normed_two * jnp.mean(scaled_two * normed_two, axis=1, keepdims=True)
    )
    grad_attn = grad_mid.astype(bf16)
    grad_dense_out = jnp.dot(mixed_heads.T, grad_attn, preferred_element_type=f32)
    grad_dense_out = grad_dense_out.astype(bf16)
    if not fused:
        out_share = lax.psum_scatter(
            grad_dense_out, ("chip", "core", "head"), scatter_dimension=0, tiled=True
        ).astype(f32)
    grad_heads = (
        jnp.dot(grad_attn, dense_out.T, preferred_element_type=f32)
        .astype(bf16)
        .reshape(tokens_present, head_number, group_columns)
        .transpose(1, 0, 2)
    )
    grad_q, grad_kv, *beside = attend_back(
        queries,
        kv_all,
        key_seg,
        query_seg,
        out_turned,
        lse,
        grad_heads,
        [
            (moe_part.reshape(chips, head_number, tokens_present, width), False),
            (grad_dense_out.reshape(chips, 2, head_number, dense_rows, width), True),
        ]
        if fused
        else [],
        [keep_up, other_up] if fused else [],
        head_number,
        query_group,
        8,
    )
    if fused:
        moe, out_share, *shared = beside
        pieces = [across(shared[mask], chips, mask) for mask in range(chips)]
    grad_q = grad_q.reshape(
        sequence_batch, key_value_location, query_group, blk, HEAD_WIDTH
    ).transpose(0, 3, 1, 2, 4)
    grad_kv = grad_kv.reshape(sequence_batch, blk, key_value_location, 2, HEAD_WIDTH)
    grad_proj = jnp.concatenate([grad_q.astype(bf16), grad_kv.astype(bf16)], axis=3).astype(f32)
    unturned = rotate(grad_proj[:, :, :, : query_group + 1], cosine, -sine)
    grad_qkv = to_lines(
        jnp.concatenate([unturned, grad_proj[:, :, :, query_group + 1 :]], axis=3)
        .reshape(sequence_batch, blk, loc_columns)
        .astype(bf16)
    )
    grad_first_part = jnp.dot(grad_qkv, dense_qkv.T, preferred_element_type=f32)
    grad_gain_attn = jnp.sum(grad_first_part * normed_line, axis=0)
    extras = jnp.concatenate(
        [
            grad_router,
            grad_gain_attn[:, None],
            grad_gain_ffn[:, None],
            jnp.zeros((width, LANES - EXPERTS - 2), f32),
        ],
        axis=1,
    ).astype(bf16)
    if fused:
        grad_first, sums = end(
            grad_first_part.astype(bf16).reshape(sequence_batch, head_number, token_rows, width),
            first_line,
            grad_qkv,
            extras,
            chips,
            head_number,
            13,
        )
        pieces, grad_first, sums = lax.optimization_barrier((pieces, grad_first, sums))
        up_share = place_units(pieces, hidden)
        up_share, grad_first, sums, moe, down_share = lax.optimization_barrier(
            (up_share, grad_first, sums, moe, down_share)
        )
        grad_first = jnp.sum(grad_first.astype(f32), axis=0).reshape(tokens_present, width)
        sums = sums.astype(f32)
    else:
        grad_first = jnp.sum(
            line_exchange(
                grad_first_part.astype(bf16).reshape(head_number, tokens_present, width),
                head_number,
                10,
            ).astype(f32),
            axis=0,
        )
        grad_dense_qkv = jnp.dot(first_line.T, grad_qkv, preferred_element_type=f32)
        sums = jnp.concatenate([grad_dense_qkv.astype(bf16), extras], axis=1)
        sums = scatter_sum(
            sums.reshape(chips, 2, head_number * dense_rows, loc_columns + LANES), chips, 1, True, 11
        )
        sums = line_exchange(
            sums.reshape(head_number, dense_rows, loc_columns + LANES), head_number, 12
        )
    inverse_one = lax.rsqrt(jnp.mean(tokens * tokens, axis=1, keepdims=True) + epsilon)
    normed_one = tokens * inverse_one
    scaled_one = grad_first * gain_attn
    grad_input = grad_mid + inverse_one * (
        scaled_one - normed_one * jnp.mean(scaled_one * normed_one, axis=1, keepdims=True)
    )
    mixed_out = (middle + moe.astype(f32)).astype(bf16)
    mixed_out = mixed_out.reshape(sequence_batch, token_rows, width)
    qkv_share = sums[:, :, :loc_columns].transpose(1, 0, 2).reshape(dense_rows, -1)
    extra = jnp.sum(sums[:, :, loc_columns:], axis=0)
    return (
        mixed_out,
        grad_input.reshape(sequence_batch, token_rows, width),
        qkv_share,
        out_share,
        extra[:, :EXPERTS],
        extra[:, EXPERTS],
        extra[:, EXPERTS + 1],
        up_share,
        down_share,
    )


def solution(mesh):
    grid = mesh.devices
    seq, heads = grid.shape
    split = Mesh(grid.reshape(seq // 2, 2, heads), ("chip", "core", "head"))
    places = ("chip", "core", "head")
    inner = ("chip", "core")
    placed = (
        P(None, places, None),
        P(),
        P(None, places, None),
        P(None, places, None),
        P(places, None),
        P(places, None),
        P(places, None),
        P(places),
        P(places),
        P("head", inner, None),
        P("head", inner, None),
        P(None, places, None),
    )
    return jax.shard_map(
        per_device,
        mesh=split,
        in_specs=placed,
        out_specs=(
            P(None, places, None),
            P(None, places, None),
            P(places, None),
            P(places, None),
            P(places, None),
            P(places),
            P(places),
            P("head", inner, None),
            P("head", inner, None),
        ),
        check_vma=False,
    )
```

```python
import functools

import jax
import jax.numpy as jnp
from jax import lax
from jax.experimental import pallas as pl
from jax.experimental.pallas import tpu as pltpu
from jax.sharding import Mesh, PartitionSpec as P

MODEL_WIDTH = 1536
QUERY_HEADS = 24
KEY_VALUE_HEADS = 8
HEAD_WIDTH = 64
EXPERTS = 40
FF = 512
CAP = 25
LANES = 128
LOW = 64

epsilon = 1e-06
negative = -1e30
theta = 10000.0
HIGH_PRECISION = lax.Precision.HIGHEST
MESH = pl.DeviceIdType.MESH
f32 = jnp.float32
bf16 = jnp.bfloat16
ANY = pl.BlockSpec(memory_space=pl.ANY)
WHOLE = pl.BlockSpec(memory_space=pltpu.VMEM)
DMA = pltpu.SemaphoreType.DMA


def rope_tables(token_positions, head_size):
    half = head_size // 2
    freq = theta ** (-jnp.arange(half, dtype=jnp.float32) / half)
    angle = token_positions.astype(jnp.float32)[:, None] * freq[None, :]
    return (jnp.cos(angle)[None, :, None, None, :], jnp.sin(angle)[None, :, None, None, :])


def rotate(value, cosine, sine):
    half = value.shape[-1] // 2
    first = value[..., :half]
    second = value[..., half:]
    return jnp.concatenate(
        [first * cosine - second * sine, second * cosine + first * sine], axis=-1
    )


def digits(count):
    number = count.bit_length() - 1
    assert 1 << number == count
    return number


def flip(index, mask):
    out = index
    bit = 0
    while (1 << bit) <= mask:
        if (mask >> bit) & 1:
            out = out + (1 - 2 * ((index // (1 << bit)) % 2)) * (1 << bit)
        bit += 1
    return out


def subsets(bits):
    out = [0]
    for bit in bits:
        out = out + [mask | (1 << bit) for mask in out]
    return out


def near(count):
    return sorted(range(1, count), key=lambda step: min(step, count - step))


def cut_rows(rows):
    return (rows // 2 + 15) // 16 * 16


def part_of(rows, side):
    cut = cut_rows(rows)
    return pl.ds(side * cut, rows - cut if side else cut)


def meet(peers):
    sem = pltpu.get_barrier_semaphore()
    for peer in peers:
        pl.semaphore_signal(sem, inc=1, device_id=peer, device_id_type=MESH)
    pl.semaphore_wait(sem, len(peers))


class Cube:
    def __init__(self, chips, with_core):
        self.chips = chips
        self.chip_digits = digits(chips)
        self.number = self.chip_digits + int(with_core)
        self.with_core = with_core
        up = tuple(range(self.chip_digits))
        core = (self.chip_digits,) if with_core else ()
        self.gather_orders = (up + core, up[::-1] + core)
        self.scatter_orders = (core + up, core + up[::-1])

    def place(self, mask):
        chip = flip(lax.axis_index("chip"), mask & (self.chips - 1))
        if not self.with_core:
            return (chip,)
        return (chip, flip(lax.axis_index("core"), mask >> self.chip_digits))

    def peer(self, digit):
        if digit < self.chip_digits:
            return {"chip": flip(lax.axis_index("chip"), 1 << digit)}
        return {"core": flip(lax.axis_index("core"), 1)}


def gather_kernel(cube, heads, in_ref, out_ref, local, line_send, line_recv, send, recv):
    hz = lax.axis_index("head")
    rows = in_ref.shape[0]
    half = rows // 2
    others = near(heads) if heads > 1 else []
    meet(
        [cube.peer(digit) for digit in range(cube.number)]
        + [{"head": (hz + d) % heads} for d in others]
    )

    def at(mask, d):
        index = cube.place(mask)
        return index + ((hz + heads - d) % heads,) if heads > 1 else index

    own = pltpu.make_async_copy(in_ref, out_ref.at[at(0, 0)], local)
    own.start()
    line = {}
    for d in others:
        line[d] = pltpu.make_async_remote_copy(
            src_ref=in_ref,
            dst_ref=out_ref.at[at(0, 0)],
            send_sem=line_send.at[d - 1],
            recv_sem=line_recv.at[d - 1],
            device_id={"head": (hz + d) % heads},
            device_id_type=MESH,
        )
        line[d].start()
    copies = {}

    def forward(side, mask, d):
        order = cube.gather_orders[side]
        last = max([k for k in range(cube.number) if (mask >> order[k]) & 1], default=-1)
        for k in range(last + 1, cube.number):
            later = mask | (1 << order[k])
            part = pl.ds(side * half, half)
            place = out_ref.at[at(mask, d) + (part,)]
            copy = pltpu.make_async_remote_copy(
                src_ref=in_ref.at[part] if mask == 0 and d == 0 else place,
                dst_ref=place,
                send_sem=send.at[side, later, d],
                recv_sem=recv.at[side, later, d],
                device_id=cube.peer(order[k]),
                device_id_type=MESH,
            )
            copy.start()
            copies[(side, later, d)] = copy

    for side in range(2):
        forward(side, 0, 0)
    for d in others:
        line[d].wait_recv()
        for side in range(2):
            forward(side, 0, d)
    for mask in sorted(range(1, 1 << cube.number), key=lambda m: bin(m).count("1")):
        for d in [0] + others:
            for side in range(2):
                copies[(side, mask, d)].wait_recv()
                forward(side, mask, d)
    own.wait()
    for copy in list(line.values()) + list(copies.values()):
        copy.wait_send()


def gather(value, chips, heads, with_core, number):
    rows, columns = value.shape
    cube = Cube(chips, with_core)
    lead = (chips,) + ((2,) if with_core else ()) + ((heads,) if heads > 1 else ())
    steps = max(heads - 1, 1)
    return pl.pallas_call(
        functools.partial(gather_kernel, cube, heads),
        out_shape=jax.ShapeDtypeStruct(lead + (rows, columns), value.dtype),
        in_specs=[ANY],
        out_specs=ANY,
        scratch_shapes=[
            DMA,
            DMA((steps,)),
            DMA((steps,)),
            DMA((2, 1 << cube.number, heads)),
            DMA((2, 1 << cube.number, heads)),
        ],
        compiler_params=pltpu.CompilerParams(collective_id=number, has_side_effects=True),
        name="gather",
    )(value)


def scatter_kernel(cube, heads, in_ref, out_ref, *refs):
    count = cube.number
    arrived, parts = refs[:count], refs[count : 2 * count - 1]
    line_out, line_in, line_send, line_recv, send, recv = refs[2 * count - 1 :]
    hz = lax.axis_index("head")
    half = in_ref.shape[-2] // 2
    others = near(heads) if heads > 1 else []
    order_of_lines = others[::-1] + [0]
    meet(
        [cube.peer(digit) for digit in range(count)] + [{"head": (hz + d) % heads} for d in others]
    )
    copies = {}

    def slot(side, k, mask):
        return subsets(cube.scatter_orders[side][k + 1 :]).index(mask)

    def mine(side, mask, d):
        index = cube.place(mask)
        if heads > 1:
            index = index + ((hz + d) % heads,)
        return in_ref.at[index + (pl.ds(side * half, half),)]

    def pass_on(side, k, mask, d, source):
        where = slot(side, k, mask)
        copy = pltpu.make_async_remote_copy(
            src_ref=source,
            dst_ref=arrived[k].at[side, where, d],
            send_sem=send.at[side, k, where, d],
            recv_sem=recv.at[side, k, where, d],
            device_id=cube.peer(cube.scatter_orders[side][k]),
            device_id_type=MESH,
        )
        copy.start()
        copies[(side, k, mask, d)] = copy

    def total(side, steps, mask, d):
        value = mine(side, mask, d)[...].astype(f32)
        for j in range(steps):
            copies[(side, j, mask, d)].wait_recv()
            value = value + arrived[j][side, slot(side, j, mask), d].astype(f32)
        return value

    for k in range(count):
        for d in order_of_lines:
            for side in range(2):
                order = cube.scatter_orders[side]
                for mask in subsets(order[k + 1 :])[::-1]:
                    full = mask | (1 << order[k])
                    if k == 0:
                        source = mine(side, full, d)
                    else:
                        source = parts[k - 1].at[side, slot(side, k, mask), d]
                        source[...] = total(side, k, full, d).astype(bf16)
                    pass_on(side, k, mask, d, source)
    line = {}
    for d in order_of_lines:
        for side in range(2):
            value = total(side, count, 0, d)
            if d:
                line_out[d - 1, pl.ds(side * half, half)] = value.astype(bf16)
            else:
                out_ref[pl.ds(side * half, half)] = value
        if d:
            line[d] = pltpu.make_async_remote_copy(
                src_ref=line_out.at[d - 1],
                dst_ref=line_in.at[d - 1],
                send_sem=line_send.at[d - 1],
                recv_sem=line_recv.at[d - 1],
                device_id={"head": (hz + d) % heads},
                device_id_type=MESH,
            )
            line[d].start()
    for d in others:
        line[d].wait_recv()
        out_ref[...] += line_in[d - 1].astype(f32)
    for copy in list(line.values()) + list(copies.values()):
        copy.wait_send()


def scatter_sum(value, chips, heads, with_core, number):
    rows, columns = value.shape[-2:]
    cube = Cube(chips, with_core)
    half = rows // 2
    steps = max(heads - 1, 1)
    line_rows = rows if heads > 1 else 16
    slots = [(1 << cube.number) >> (k + 1) for k in range(cube.number)]
    if 2 * value.size + 4 * heads * half * columns * (sum(slots) + sum(slots[1:])) > 40 << 20:
        names = ("chip", "core") if with_core else ("chip",)
        names = names + (("head",) if heads > 1 else ())
        flat = value.reshape(-1, columns)
        return lax.psum_scatter(flat, names, scatter_dimension=0, tiled=True).astype(f32)
    return pl.pallas_call(
        functools.partial(scatter_kernel, cube, heads),
        out_shape=jax.ShapeDtypeStruct((rows, columns), f32),
        in_specs=[WHOLE],
        out_specs=WHOLE,
        scratch_shapes=[pltpu.VMEM((2, s, heads, half, columns), bf16) for s in slots]
        + [pltpu.VMEM((2, s, heads, half, columns), bf16) for s in slots[1:]]
        + [
            pltpu.VMEM((steps, line_rows, columns), bf16),
            pltpu.VMEM((steps, line_rows, columns), bf16),
            DMA((steps,)),
            DMA((steps,)),
            DMA((2, cube.number, slots[0], heads)),
            DMA((2, cube.number, slots[0], heads)),
        ],
        compiler_params=pltpu.CompilerParams(
            collective_id=number, has_side_effects=True, vmem_limit_bytes=56 << 20
        ),
        name="scatter_sum",
    )(value)


def line_kernel(heads, same, in_ref, out_ref, local, send, recv):
    hz = lax.axis_index("head")
    others = near(heads)[::-1]
    meet([{"head": (hz + d) % heads} for d in others])

    def source(place):
        return in_ref if same else in_ref.at[place]

    own = pltpu.make_async_copy(source(hz), out_ref.at[hz], local)
    own.start()
    copies = []
    for d in others:
        place = (hz + d) % heads
        copy = pltpu.make_async_remote_copy(
            src_ref=source(place),
            dst_ref=out_ref.at[hz],
            send_sem=send.at[d - 1],
            recv_sem=recv.at[d - 1],
            device_id={"head": place},
            device_id_type=MESH,
        )
        copy.start()
        copies.append(copy)
    own.wait()
    for copy in copies:
        copy.wait()


def line_exchange(value, heads, number, same=False):
    return pl.pallas_call(
        functools.partial(line_kernel, heads, same),
        out_shape=jax.ShapeDtypeStruct((heads,) + value.shape if same else value.shape, value.dtype),
        in_specs=[ANY],
        out_specs=ANY,
        scratch_shapes=[DMA, DMA((heads - 1,)), DMA((heads - 1,))],
        compiler_params=pltpu.CompilerParams(collective_id=number, has_side_effects=True),
        name="line_exchange",
    )(value)


NT = (((1,), (1,)), ((), ()))


def experts_kernel(
    tile,
    hidden,
    x_ref,
    c_ref,
    gate_hbm,
    up_hbm,
    down_hbm,
    moe_ref,
    back_ref,
    d_gate_hbm,
    d_up_hbm,
    d_down_hbm,
    w_gate,
    w_up,
    w_down,
    d_gate_w,
    d_up_w,
    d_down_w,
    acts,
    back_gate,
    back_up,
    stage_wide,
    stage_down,
    load,
    store,
):
    step = pl.program_id(0)
    width, total = w_gate.shape

    @pl.when(step == 0)
    def _():
        loads = [
            pltpu.make_async_copy(gate_hbm, w_gate, load.at[0]),
            pltpu.make_async_copy(up_hbm, w_up, load.at[1]),
            pltpu.make_async_copy(down_hbm, w_down, load.at[2]),
        ]
        for copy in loads:
            copy.start()
        d_gate_w[...] = jnp.zeros_like(d_gate_w)
        d_up_w[...] = jnp.zeros_like(d_up_w)
        d_down_w[...] = jnp.zeros_like(d_down_w)
        for copy in loads:
            copy.wait()

    x = x_ref[:, :width]
    c = c_ref[...]
    routed = x_ref[:, width:]
    first_expert = lax.axis_index("head") * (total // hidden)
    d_gates = jnp.zeros((x.shape[0], LANES), f32)
    for begin in range(0, total, tile):
        js = pl.ds(begin, tile)
        column = begin + lax.broadcasted_iota(jnp.int32, (LANES, tile), 1)
        line = lax.broadcasted_iota(jnp.int32, (LANES, tile), 0)
        expert = first_expert + column // hidden
        here = (line == expert).astype(f32)
        both = (here + (line == expert + LOW).astype(f32)).astype(bf16)
        weight = jnp.dot(routed, both, preferred_element_type=f32)
        gate = jnp.dot(x, w_gate[:, js], preferred_element_type=f32)
        up = jnp.dot(x, w_up[:, js], preferred_element_type=f32)
        d_act = lax.dot_general(c, w_down[js, :], NT, preferred_element_type=f32)
        sigma = 1.0 / (1.0 + jnp.exp(-gate))
        silu = gate * sigma
        act = (silu * up).astype(bf16).astype(f32)
        d_gates = d_gates + lax.dot_general(
            (act * d_act).astype(bf16), here.astype(bf16), NT, preferred_element_type=f32
        )
        acts[:, js] = (act * weight).astype(bf16)
        d_act = d_act * weight
        back_up[:, js] = (d_act * silu).astype(bf16)
        back_gate[:, js] = (d_act * up * sigma * (1.0 + gate * (1.0 - sigma))).astype(bf16)
    back_ref[:, width:] = d_gates.astype(bf16)
    x_turned = x.T
    for begin in range(0, total, tile):
        js = pl.ds(begin, tile)
        d_gate_w[:, js] += jnp.dot(x_turned, back_gate[:, js], preferred_element_type=f32)
        d_up_w[:, js] += jnp.dot(x_turned, back_up[:, js], preferred_element_type=f32)
        d_down_w[js, :] += jnp.dot(acts[:, js].T, c, preferred_element_type=f32)
    for begin in range(0, width, 512):
        cs = pl.ds(begin, 512)
        moe_ref[:, cs] = jnp.dot(acts[...], w_down[:, cs], preferred_element_type=f32).astype(bf16)
        back_ref[:, cs] = (
            lax.dot_general(back_gate[...], w_gate[cs, :], NT, preferred_element_type=f32)
            + lax.dot_general(back_up[...], w_up[cs, :], NT, preferred_element_type=f32)
        ).astype(bf16)

    @pl.when(step == pl.num_programs(0) - 1)
    def _():
        rows = stage_wide.shape[1]
        jobs = [
            (source, target, stage, begin)
            for source, target, stage in (
                (d_gate_w, d_gate_hbm, stage_wide),
                (d_up_w, d_up_hbm, stage_wide),
                (d_down_w, d_down_hbm, stage_down),
            )
            for begin in range(0, source.shape[0], rows)
        ]
        flight = {}
        for index, (source, target, stage, begin) in enumerate(jobs):
            now = index % 2
            if now in flight:
                flight[now].wait()
            stage[now] = source[pl.ds(begin, rows), :].astype(bf16)
            flight[now] = pltpu.make_async_copy(
                stage.at[now], target.at[pl.ds(begin, rows), :], store.at[now]
            )
            flight[now].start()
        for copy in flight.values():
            copy.wait()


def experts(x, c, w_gate, w_up, w_down, hidden):
    tokens, columns = x.shape
    width, total = w_gate.shape
    block = min(256, tokens)
    tile = 256 if total % 256 == 0 else hidden
    return pl.pallas_call(
        functools.partial(experts_kernel, tile, hidden),
        grid=(tokens // block,),
        out_shape=(
            jax.ShapeDtypeStruct((tokens, width), bf16),
            jax.ShapeDtypeStruct((tokens, columns), bf16),
            jax.ShapeDtypeStruct((width, total), bf16),
            jax.ShapeDtypeStruct((width, total), bf16),
            jax.ShapeDtypeStruct((total, width), bf16),
        ),
        in_specs=[
            pl.BlockSpec((block, columns), lambda i: (i, 0)),
            pl.BlockSpec((block, width), lambda i: (i, 0)),
            ANY,
            ANY,
            ANY,
        ],
        out_specs=(
            pl.BlockSpec((block, width), lambda i: (i, 0)),
            pl.BlockSpec((block, columns), lambda i: (i, 0)),
            ANY,
            ANY,
            ANY,
        ),
        scratch_shapes=[
            pltpu.VMEM((width, total), bf16),
            pltpu.VMEM((width, total), bf16),
            pltpu.VMEM((total, width), bf16),
            pltpu.VMEM((width, total), f32),
            pltpu.VMEM((width, total), f32),
            pltpu.VMEM((total, width), f32),
            pltpu.VMEM((block, total), bf16),
            pltpu.VMEM((block, total), bf16),
            pltpu.VMEM((block, total), bf16),
            pltpu.VMEM((2, 64, total), bf16),
            pltpu.VMEM((2, 64, width), bf16),
            DMA((3,)),
            DMA((2,)),
        ],
        compiler_params=pltpu.CompilerParams(vmem_limit_bytes=60 << 20),
        name="experts",
    )(x, c, w_gate, w_up, w_down)


def turn_kernel(cube, heads, hidden, *refs):
    chips, count = cube.chips, cube.number
    own_ref, c_hbm, down_hbm = refs[:3]
    pieces, refs = refs[3 : 3 + chips], (None,) * 4 + refs[3 + chips :]
    out_ref, moe_hbm, keep_up_hbm, other_up_hbm, keep_down_hbm, other_down_hbm = refs[4:10]
    tokens, turned, cots, w_up, w_down, acts, backs, d_gates, moe_stage, line_in = refs[10:20]
    arrived = refs[20 : 20 + count]
    load, store, own_sem, line_send, line_recv, send, recv, back_send, back_recv = refs[
        20 + count : 29 + count
    ]
    end_send, end_recv, twin_send, twin_recv, load_send, load_recv = refs[29 + count :]
    hz = lax.axis_index("head")
    rows, columns = own_ref.shape
    experts_here, width, _ = w_up.shape
    total = experts_here * hidden
    half = rows // 2
    line = heads * rows
    others = near(heads)
    masks = sorted(range(chips), key=lambda m: bin(m).count("1"))

    core = lax.axis_index("core")
    twin = {"core": 1 - core}
    slices = 2 * chips
    slice_rows = width // slices

    def up_rows(ref, chip, which):
        return ref.at[:, pl.ds((chip * 2 + which) * slice_rows, slice_rows), :]

    def w_down_parts(which):
        return w_down.reshape(experts_here, 2, hidden // 2, width).at[:, which]

    homes = [
        (pieces[mask], up_rows(w_up, flip(lax.axis_index("chip"), mask), core))
        for mask in range(chips)
    ] + [(down_hbm, w_down_parts(core))]
    loads = [
        pltpu.make_async_copy(source, target, load.at[index])
        for index, (source, target) in enumerate([(c_hbm, cots)] + homes)
    ]
    shared = [
        pltpu.make_async_remote_copy(
            src_ref=source,
            dst_ref=target,
            send_sem=load_send.at[index],
            recv_sem=load_recv.at[index],
            device_id=twin,
            device_id_type=MESH,
        )
        for index, (source, target) in enumerate(homes)
    ]
    for copy in loads:
        copy.start()
    meet(
        [cube.peer(digit) for digit in range(count)]
        + [{"head": (hz + d) % heads} for d in others]
        + [twin]
    )

    def part(side):
        return pl.ds(side * half, half)

    middle = jnp.minimum(hz, heads - 1 - hz)

    def source(rank):
        if rank == 0:
            return hz
        far = (rank + 1) // 2
        near_one = hz - far if rank % 2 else hz + far
        far_one = jnp.where(
            hz < heads - 1 - hz, hz + (rank - middle), hz - (rank - middle)
        )
        return jnp.where(rank <= 2 * middle, near_one, far_one)

    def line_copy(rank, step):
        head = source(rank)
        place = tokens.at[cube.place(0) + (head,)]
        return pltpu.make_async_remote_copy(
            src_ref=own_ref if rank == 0 else place,
            dst_ref=place,
            send_sem=line_send.at[heads if rank == 0 and step < 0 else head],
            recv_sem=line_recv.at[head],
            device_id={"head": (hz + step + heads) % heads},
            device_id_type=MESH,
        )

    def along(rank, act):
        head = source(rank)
        goes_up = hz + 1 < heads
        goes_down = hz > 0
        if rank:
            goes_up = goes_up & (head < hz)
            goes_down = goes_down & (head > hz)

        @pl.when(goes_up)
        def _():
            act(line_copy(rank, 1))

        @pl.when(goes_down)
        def _():
            act(line_copy(rank, -1))

    def plane_copy(side, mask, k, rank):
        digit = cube.gather_orders[side][k]
        later = mask | (1 << digit)
        head = source(rank)
        place = tokens.at[cube.place(mask) + (head, part(side))]
        return pltpu.make_async_remote_copy(
            src_ref=own_ref.at[part(side)] if mask == 0 and rank == 0 else place,
            dst_ref=place,
            send_sem=send.at[side, later, head],
            recv_sem=recv.at[side, later, head],
            device_id=cube.peer(digit),
            device_id_type=MESH,
        )

    def steps_after(side, mask):
        order = cube.gather_orders[side]
        last = max([k for k in range(count) if (mask >> order[k]) & 1], default=-1)
        return range(last + 1, count)

    def arrival(side, mask, rank):
        order = cube.gather_orders[side]
        k = max(k for k in range(count) if (mask >> order[k]) & 1)
        return plane_copy(side, mask & ~(1 << order[k]), k, rank)

    def receive(mask, rank):
        if mask == 0:
            if rank:
                line_copy(rank, 1).wait_recv()
            along(rank, lambda copy: copy.start())
        for side in range(2):
            if mask:
                arrival(side, mask, rank).wait_recv()
            for k in steps_after(side, mask):
                plane_copy(side, mask, k, rank).start()

    levels = [
        [m for m in masks if bin(m).count("1") == level] for level in range(cube.number + 1)
    ]
    waits = {0: [], 1: []}
    early = max(heads - 2, 0)
    for rank in range(heads):
        waits[0].append((0, rank))
        if 0 < rank <= early and count > 0:
            waits[0] += [(m, rank - 1) for m in levels[1]]
    waits[1] = [(m, rank) for rank in range(early, heads) for m in levels[1]]
    for level in range(2, count + 1):
        waits[level] = [(m, rank) for m in levels[level] for rank in range(heads)]

    def sent(mask):
        for rank in range(heads):
            if mask == 0:
                along(rank, lambda copy: copy.wait_send())
            for side in range(2):
                for k in steps_after(side, mask):
                    plane_copy(side, mask, k, rank).wait_send()

    def slot(side, k, mask):
        return subsets(cube.scatter_orders[side][k + 1 :]).index(mask)

    def back_place(side, mask, d):
        return tokens.at[cube.place(mask) + ((hz + d) % heads, part(side))]

    def back_copy(side, k, mask, d):
        order = cube.scatter_orders[side]
        where = slot(side, k, mask)
        return pltpu.make_async_remote_copy(
            src_ref=back_place(side, mask | (1 << order[k]), d),
            dst_ref=arrived[k].at[side, where, d],
            send_sem=back_send.at[side, k, where, d],
            recv_sem=back_recv.at[side, k, where, d],
            device_id=cube.peer(order[k]),
            device_id_type=MESH,
        )

    def end_copy(d):
        return pltpu.make_async_remote_copy(
            src_ref=tokens.at[cube.place(0) + ((hz + d) % heads,)],
            dst_ref=line_in.at[d - 1],
            send_sem=end_send.at[d - 1],
            recv_sem=end_recv.at[d - 1],
            device_id={"head": (hz + d) % heads},
            device_id_type=MESH,
        )

    outward = others[::-1] + [0]

    def give(mask, d):
        for side in range(2):
            first = 1 << cube.scatter_orders[side][0]
            if mask & first:
                back_copy(side, 0, mask & ~first, d).start()

    own = pltpu.make_async_copy(own_ref, tokens.at[cube.place(0) + (hz,)], own_sem)
    own.start()
    for copy in shared:
        copy.start()

    first_expert = hz * experts_here
    span = min(512, width)
    group = 2 if experts_here % 2 == 0 else 1
    tile = group * hidden

    def compute(place):
        here = pl.ds(place * line, line)
        x = tokens[place, :, :, pl.ds(0, width)].reshape(line, width)
        c = cots[here, :]
        routed = tokens[place, :, :, pl.ds(width, LANES)].reshape(line, LANES)
        turned[:, here] = x.T
        d_gates[...] = jnp.zeros_like(d_gates)

        @pl.loop(0, total // tile)
        def _(j):
            js = pl.ds(pl.multiple_of(j * tile, tile), tile)
            column = j * tile + lax.broadcasted_iota(jnp.int32, (LANES, tile), 1)
            lane = lax.broadcasted_iota(jnp.int32, (LANES, tile), 0)
            expert = first_expert + column // hidden
            high = (lane == expert).astype(f32)
            both = (high + (lane == expert + LOW).astype(f32)).astype(bf16)
            weight = jnp.dot(routed, both, preferred_element_type=f32)
            both_parts = [
                jnp.dot(x, w_up[j * group + i], preferred_element_type=f32) for i in range(group)
            ]
            gate = jnp.concatenate([value[:, :hidden] for value in both_parts], axis=1)
            up = jnp.concatenate([value[:, hidden:] for value in both_parts], axis=1)
            d_act = lax.dot_general(c, w_down[js, :], NT, preferred_element_type=f32)
            sigma = 1.0 / (1.0 + jnp.exp(-gate))
            silu = gate * sigma
            act = (silu * up).astype(bf16).astype(f32)
            d_gates[...] += lax.dot_general(
                (act * d_act).astype(bf16), high.astype(bf16), NT, preferred_element_type=f32
            )
            acts[here, js] = (act * weight).astype(bf16)
            d_act = d_act * weight
            d_up = (d_act * silu).astype(bf16)
            d_gate = (d_act * up * sigma * (1.0 + gate * (1.0 - sigma))).astype(bf16)
            for i in range(group):
                one = slice(i * hidden, (i + 1) * hidden)
                backs[j * group + i, here, pl.ds(0, hidden)] = d_gate[:, one]
                backs[j * group + i, here, pl.ds(hidden, hidden)] = d_up[:, one]

    def results(place, step):
        here = pl.ds(place * line, line)

        @pl.loop(0, width // span)
        def _(j):
            cs = pl.ds(pl.multiple_of(j * span, span), span)
            value = sum(
                lax.dot_general(
                    backs[e, here, :], w_up[e, cs, :], NT, preferred_element_type=f32
                )
                for e in range(experts_here)
            )
            tokens[place, :, :, cs] = value.astype(bf16).reshape(heads, rows, span)

        tokens[place, :, :, pl.ds(width, LANES)] = (
            d_gates[...].astype(bf16).reshape(heads, rows, LANES)
        )

    def moe_copy(place):
        return pltpu.make_async_copy(
            moe_stage, moe_hbm.at[pl.ds(place * line, line)], store.at[chips + 1]
        )

    def mixed(place, step):
        here = pl.ds(place * line, line)

        @pl.when(step > 0)
        def _():
            moe_copy(place).wait()

        @pl.loop(0, width // span)
        def _(j):
            cs = pl.ds(pl.multiple_of(j * span, span), span)
            moe_stage[:, cs] = jnp.dot(
                acts[here, :], w_down[:, cs], preferred_element_type=f32
            ).astype(bf16)

        moe_copy(place).start()

    @pl.loop(0, chips)
    def _(step):
        seen = -1
        for index, mask in enumerate(masks):
            level = bin(mask).count("1")
            if level > seen:
                seen = level

                @pl.when(step == index)
                def _():
                    for event in waits[level]:
                        receive(*event)

        place = cube.place(0)[0] * 0
        for index, mask in enumerate(masks):
            place = jnp.where(step == index, cube.place(mask)[0], place)

        @pl.when(step == 0)
        def _():
            own.wait()
            for copy in loads + shared:
                copy.wait()

        compute(place)
        for index, mask in enumerate(masks):

            @pl.when(step == index)
            def _():
                sent(mask)

        results(place, step)
        for index, mask in enumerate(masks):
            if mask and mask != chips - 1:

                @pl.when(step == index)
                def _():
                    for d in outward:
                        give(mask, d)

    def sums(side, steps, mask, d):
        value = back_place(side, mask, d)[...].astype(f32)
        for j in range(steps):
            back_copy(side, j, mask, d).wait_recv()
            value = value + arrived[j][side, slot(side, j, mask), d].astype(f32)
        return value

    def keep_up(chip):
        return pltpu.make_async_copy(up_rows(w_up, chip, core), keep_up_hbm.at[chip], store.at[chip])

    def give_up(chip):
        return pltpu.make_async_remote_copy(
            src_ref=up_rows(w_up, chip, 1 - core),
            dst_ref=other_up_hbm.at[chip],
            send_sem=twin_send.at[chip],
            recv_sem=twin_recv.at[chip],
            device_id=twin,
            device_id_type=MESH,
        )

    def keep_down():
        return pltpu.make_async_copy(w_down_parts(core), keep_down_hbm, store.at[chips])

    def give_down():
        return pltpu.make_async_remote_copy(
            src_ref=w_down_parts(1 - core),
            dst_ref=other_down_hbm,
            send_sem=twin_send.at[chips],
            recv_sem=twin_recv.at[chips],
            device_id=twin,
            device_id_type=MESH,
        )

    def up_grad(begin, end):
        @pl.loop(begin, end)
        def _(e):
            w_up[e] = jnp.dot(turned[...], backs[e], preferred_element_type=f32).astype(bf16)

        if end == experts_here:
            for chip in range(chips):
                give_up(chip).start()
                keep_up(chip).start()

    def down_grad():
        @pl.loop(0, total // tile)
        def _(j):
            js = pl.ds(pl.multiple_of(j * tile, tile), tile)
            value = jnp.dot(acts[:, js].T, cots[...], preferred_element_type=f32)
            w_down[js, :] = value.astype(bf16)

        give_down().start()
        keep_down().start()

    def mix(begin, end):
        @pl.loop(begin, end)
        def _(index):
            mixed(index, index)

    cuts = [experts_here * i // 4 for i in range(5)]
    work = [
        lambda: mix(0, chips // 2),
        lambda: mix(chips // 2, chips),
        lambda: up_grad(cuts[0], cuts[1]),
        lambda: up_grad(cuts[1], cuts[2]),
        lambda: up_grad(cuts[2], cuts[3]),
        lambda: up_grad(cuts[3], cuts[4]),
        down_grad,
    ]
    turns = heads + count
    for turn in range(turns):
        if turn < heads:
            give(chips - 1, outward[turn])
        for piece in work[len(work) * turn // turns : len(work) * (turn + 1) // turns]:
            piece()
        for k in range(1, count):
            if 0 <= turn - k < heads:
                d = outward[turn - k]
                for side in range(2):
                    order = cube.scatter_orders[side]
                    for mask in subsets(order[k + 1 :])[::-1]:
                        full = mask | (1 << order[k])
                        back_place(side, full, d)[...] = sums(side, k, full, d).astype(bf16)
                        back_copy(side, k, mask, d).start()
        if 0 <= turn - count < heads:
            d = outward[turn - count]
            for side in range(2):
                value = sums(side, count, 0, d)
                if d:
                    back_place(side, 0, d)[...] = value.astype(bf16)
                else:
                    out_ref[part(side)] = value
            if d:
                end_copy(d).start()
    for d in others:
        end_copy(d).wait_recv()
        out_ref[...] += line_in[d - 1].astype(f32)
    for d in others:
        end_copy(d).wait_send()
    for side in range(2):
        for k in range(count):
            for mask in subsets(cube.scatter_orders[side][k + 1 :]):
                for d in outward:
                    back_copy(side, k, mask, d).wait_send()
    moe_copy(0).wait()
    for chip in range(chips):
        give_up(chip).wait()
        keep_up(chip).wait()
    give_down().wait()
    keep_down().wait()


def expert_turn(payload, c, pieces, w_down, heads, number):
    rows, columns = payload.shape
    chips, width = len(pieces), c.shape[1]
    experts_here, _, double = pieces[0].shape
    hidden = double // 2
    total = experts_here * hidden
    cube = Cube(chips, False)
    count = cube.number
    tokens = chips * heads * rows
    half = rows // 2
    slots = [chips >> (k + 1) for k in range(count)]
    share = jax.ShapeDtypeStruct((chips, experts_here, width // (2 * chips), double), bf16)
    down_share = jax.ShapeDtypeStruct((experts_here, hidden // 2, width), bf16)
    return pl.pallas_call(
        functools.partial(turn_kernel, cube, heads, hidden),
        out_shape=(
            jax.ShapeDtypeStruct((rows, columns), f32),
            jax.ShapeDtypeStruct((tokens, width), bf16),
            share,
            share,
            down_share,
            down_share,
        ),
        in_specs=[WHOLE] + [ANY] * (2 + chips),
        out_specs=(WHOLE, ANY, ANY, ANY, ANY, ANY),
        scratch_shapes=[
            pltpu.VMEM((chips, heads, rows, columns), bf16),
            pltpu.VMEM((width, tokens), bf16),
            pltpu.VMEM((tokens, width), bf16),
            pltpu.VMEM((experts_here, width, double), bf16),
            pltpu.VMEM((total, width), bf16),
            pltpu.VMEM((tokens, total), bf16),
            pltpu.VMEM((experts_here, tokens, double), bf16),
            pltpu.VMEM((heads * rows, LANES), f32),
            pltpu.VMEM((heads * rows, width), bf16),
            pltpu.VMEM((heads - 1, rows, columns), bf16),
        ]
        + [pltpu.VMEM((2, s, heads, half, columns), bf16) for s in slots]
        + [
            DMA((chips + 2,)),
            DMA((chips + 2,)),
            DMA,
            DMA((heads + 1,)),
            DMA((heads,)),
            DMA((2, chips, heads)),
            DMA((2, chips, heads)),
            DMA((2, count, slots[0], heads)),
            DMA((2, count, slots[0], heads)),
            DMA((heads - 1,)),
            DMA((heads - 1,)),
            DMA((chips + 1,)),
            DMA((chips + 1,)),
            DMA((chips + 1,)),
            DMA((chips + 1,)),
        ],
        compiler_params=pltpu.CompilerParams(
            collective_id=number, has_side_effects=True, vmem_limit_bytes=63 << 20
        ),
        name="expert_turn",
    )(payload, c, w_down, *pieces)


def start_kernel(cube, heads, *refs):
    x_ref, slice_ref, unit_ref, column_ref, row_ref, x_out, dense_out, unit_out, slot_out = refs[:9]
    local, x_send, x_recv, line_send, line_recv, send, recv, unit_send, unit_recv = refs[9:]
    chips = cube.chips
    chip, core, hz = lax.axis_index("chip"), lax.axis_index("core"), lax.axis_index("head")
    others = near(heads)
    part_heads = heads // 2
    across_all = {"chip": flip(chip, chips - 1)}
    meet(
        [cube.peer(digit) for digit in range(cube.number)]
        + [{"head": (hz + d) % heads} for d in others]
        + [across_all]
    )
    unit_copy = pltpu.make_async_remote_copy(
        src_ref=unit_ref,
        dst_ref=unit_out,
        send_sem=unit_send,
        recv_sem=unit_recv,
        device_id=across_all,
        device_id_type=MESH,
    )
    middle = jnp.minimum(hz, heads - 1 - hz)

    def source(rank):
        if rank == 0:
            return hz
        far = (rank + 1) // 2
        near_one = hz - far if rank % 2 else hz + far
        far_one = jnp.where(hz < heads - 1 - hz, hz + (rank - middle), hz - (rank - middle))
        return jnp.where(rank <= 2 * middle, near_one, far_one)

    def x_copy(rank, step):
        head = source(rank)
        return pltpu.make_async_remote_copy(
            src_ref=x_ref if rank == 0 else x_out.at[:, head],
            dst_ref=x_out.at[:, head],
            send_sem=x_send.at[heads if rank == 0 and step < 0 else head],
            recv_sem=x_recv.at[head],
            device_id={"head": (hz + step + heads) % heads},
            device_id_type=MESH,
        )

    def along(rank, act):
        head = source(rank)
        goes_up = hz + 1 < heads
        goes_down = hz > 0
        if rank:
            goes_up = goes_up & (head < hz)
            goes_down = goes_down & (head > hz)

        @pl.when(goes_up)
        def _():
            act(x_copy(rank, 1))

        @pl.when(goes_down)
        def _():
            act(x_copy(rank, -1))

    def slice_copy(d):
        place = (hz + d) % heads
        return pltpu.make_async_remote_copy(
            src_ref=slice_ref.at[place],
            dst_ref=dense_out.at[chip, core, hz],
            send_sem=line_send.at[d - 1],
            recv_sem=line_recv.at[d - 1],
            device_id={"head": place},
            device_id_type=MESH,
        )

    def dense_copy(side, mask, k):
        order = cube.gather_orders[side]
        later = mask | (1 << order[k])
        place = dense_out.at[cube.place(mask) + (pl.ds(side * part_heads, part_heads),)]
        return pltpu.make_async_remote_copy(
            src_ref=place,
            dst_ref=place,
            send_sem=send.at[side, later],
            recv_sem=recv.at[side, later],
            device_id=cube.peer(order[k]),
            device_id_type=MESH,
        )

    def steps_after(side, mask):
        order = cube.gather_orders[side]
        last = max([k for k in range(cube.number) if (mask >> order[k]) & 1], default=-1)
        return range(last + 1, cube.number)

    def dense_turn(mask):
        for side in range(2):
            if mask:
                order = cube.gather_orders[side]
                k = max(k for k in range(cube.number) if (mask >> order[k]) & 1)
                dense_copy(side, mask & ~(1 << order[k]), k).wait_recv()
            for k in steps_after(side, mask):
                dense_copy(side, mask, k).start()

    locals_ = [
        pltpu.make_async_copy(slice_ref.at[hz], dense_out.at[chip, core, hz], local.at[0]),
        pltpu.make_async_copy(x_ref, x_out.at[:, hz], local.at[1]),
    ]
    def count_slots():
        row = row_ref[...]
        first = row // column_ref.shape[0] * column_ref.shape[0]
        total = jnp.zeros(row.shape, jnp.int32)
        step = LANES
        for begin in range(0, column_ref.shape[0], step):
            column = column_ref[pl.ds(begin, step), :]
            earlier = ((column < row) & (column >= first)).astype(jnp.int32)
            total = total + jnp.sum(earlier, axis=0, keepdims=True)
        slot_out[...] = total

    for d in others:
        slice_copy(d).start()
    for copy in locals_:
        copy.start()
    along(0, lambda copy: copy.start())
    locals_[0].wait()
    for d in others:
        slice_copy(d).wait_recv()
    dense_turn(0)
    masks = sorted(range(1, 2 * chips), key=lambda m: bin(m).count("1"))
    shares = [masks[len(masks) * i // heads : len(masks) * (i + 1) // heads] for i in range(heads)]
    for mask in shares[0]:
        dense_turn(mask)
    for rank in range(1, heads):
        x_copy(rank, 1).wait_recv()
        along(rank, lambda copy: copy.start())
        for mask in shares[rank]:
            dense_turn(mask)
        if rank == 1:
            unit_copy.start()
            count_slots()
    unit_copy.wait()
    locals_[1].wait()
    for rank in range(heads):
        along(rank, lambda copy: copy.wait_send())
    for d in others:
        slice_copy(d).wait_send()
    for mask in [0] + masks:
        for side in range(2):
            for k in steps_after(side, mask):
                dense_copy(side, mask, k).wait_send()


def start(x, slices, unit, keys, chips, heads, number):
    cube = Cube(chips, True)
    return pl.pallas_call(
        functools.partial(start_kernel, cube, heads),
        out_shape=(
            jax.ShapeDtypeStruct((x.shape[0], heads) + x.shape[1:], bf16),
            jax.ShapeDtypeStruct((chips, 2) + slices.shape, bf16),
            jax.ShapeDtypeStruct(unit.shape, bf16),
            jax.ShapeDtypeStruct((1, keys.size), jnp.int32),
        ),
        in_specs=[ANY] * 3 + [WHOLE] * 2,
        out_specs=(ANY,) * 3 + (WHOLE,),
        scratch_shapes=[
            DMA((2,)),
            DMA((heads + 1,)),
            DMA((heads,)),
            DMA((heads - 1,)),
            DMA((heads - 1,)),
            DMA((2, 2 * chips)),
            DMA((2, 2 * chips)),
            DMA,
            DMA,
        ],
        compiler_params=pltpu.CompilerParams(collective_id=number, has_side_effects=True),
        name="start",
    )(x, slices, unit, keys[:, None], keys[None, :])


def end_kernel(cube, heads, first_ref, left_ref, right_ref, extra_ref, first_out, out_ref, *refs):
    count = cube.number
    in_ref, refs = refs[0], refs[1:]
    arrived = refs[:count]
    parts = refs[count : 2 * count]
    local, first_send, first_recv, line_send, line_recv, send, recv = refs[2 * count :]
    hz = lax.axis_index("head")
    others = near(heads)[::-1]
    half = in_ref.shape[-2] // 2
    rows = in_ref.shape[-2] // heads
    meet([cube.peer(digit) for digit in range(count)] + [{"head": (hz + d) % heads} for d in others])
    own = pltpu.make_async_copy(first_ref.at[:, hz], first_out.at[hz], local)
    own.start()
    copies = {}

    def slot(side, k, mask):
        return subsets(cube.scatter_orders[side][k + 1 :]).index(mask)

    def mine(side, mask):
        return in_ref.at[cube.place(mask) + (pl.ds(side * half, half),)]

    def total(side, steps, mask):
        value = mine(side, mask)[...].astype(f32)
        for j in range(steps):
            copies[(side, j, mask)].wait_recv()
            value = value + arrived[j][side, slot(side, j, mask)].astype(f32)
        return value.astype(bf16)

    def first_copy(d):
        place = (hz + d) % heads
        return pltpu.make_async_remote_copy(
            src_ref=first_ref.at[:, place],
            dst_ref=first_out.at[hz],
            send_sem=first_send.at[d - 1],
            recv_sem=first_recv.at[d - 1],
            device_id={"head": place},
            device_id_type=MESH,
        )

    for d in others:
        first_copy(d).start()
    strip = extra_ref.shape[0] // cube.chips
    product = right_ref.shape[1]
    for chip in range(cube.chips):
        rows_here = pl.ds(chip * strip, strip)
        value = lax.dot_general(
            left_ref[:, rows_here], right_ref[...], TN, preferred_element_type=f32
        )
        in_ref[chip, :, :, pl.ds(0, product)] = value.astype(bf16).reshape(2, strip // 2, product)
        in_ref[chip, :, :, pl.ds(product, LANES)] = extra_ref[rows_here, :].reshape(
            2, strip // 2, LANES
        )
    for k in range(count):
        for side in range(2):
            order = cube.scatter_orders[side]
            for mask in subsets(order[k + 1 :])[::-1]:
                full = mask | (1 << order[k])
                where = slot(side, k, mask)
                if k == 0:
                    piece = mine(side, full)
                else:
                    piece = parts[k - 1].at[side, where]
                    piece[...] = total(side, k, full)
                copies[(side, k, mask)] = pltpu.make_async_remote_copy(
                    src_ref=piece,
                    dst_ref=arrived[k].at[side, where],
                    send_sem=send.at[side, k, where],
                    recv_sem=recv.at[side, k, where],
                    device_id=cube.peer(order[k]),
                    device_id_type=MESH,
                )
                copies[(side, k, mask)].start()
    done = parts[count - 1]
    for side in range(2):
        done[0, pl.ds(side * half, half)] = total(side, count, 0)

    def line_copy(d):
        place = (hz + d) % heads
        return pltpu.make_async_remote_copy(
            src_ref=done.at[0, pl.ds(pl.multiple_of(place * rows, 16), rows)],
            dst_ref=out_ref.at[hz],
            send_sem=line_send.at[d - 1],
            recv_sem=line_recv.at[d - 1],
            device_id={"head": place},
            device_id_type=MESH,
        )

    for d in others:
        line_copy(d).start()
    out_ref[hz] = done[0, pl.ds(pl.multiple_of(hz * rows, 16), rows)]
    for copy in copies.values():
        copy.wait_send()
    own.wait()
    for d in others:
        line_copy(d).wait()
    for d in others:
        first_copy(d).wait()


def end(first, left, right, extra, chips, heads, number):
    rows, columns = extra.shape[0] // (2 * chips), right.shape[1] + LANES
    cube = Cube(chips, True)
    count = cube.number
    half = rows // 2
    slots = [(1 << count) >> (k + 1) for k in range(count)]
    return pl.pallas_call(
        functools.partial(end_kernel, cube, heads),
        out_shape=(
            jax.ShapeDtypeStruct((heads, first.shape[0]) + first.shape[2:], bf16),
            jax.ShapeDtypeStruct((heads, rows // heads, columns), bf16),
        ),
        in_specs=[ANY] + [WHOLE] * 3,
        out_specs=(ANY, WHOLE),
        scratch_shapes=[pltpu.VMEM((chips, 2, rows, columns), bf16)]
        + [pltpu.VMEM((2, s, half, columns), bf16) for s in slots]
        + [pltpu.VMEM((2, s, half, columns), bf16) for s in slots[1:]]
        + [
            pltpu.VMEM((1, rows, columns), bf16),
            DMA,
            DMA((heads - 1,)),
            DMA((heads - 1,)),
            DMA((heads - 1,)),
            DMA((heads - 1,)),
            DMA((2, count, slots[0])),
            DMA((2, count, slots[0])),
        ],
        compiler_params=pltpu.CompilerParams(
            collective_id=number, has_side_effects=True, vmem_limit_bytes=40 << 20
        ),
        cost_estimate=pl.CostEstimate(
            flops=2000000000, bytes_accessed=1_000_000, transcendentals=0
        ),
        name="end",
    )(first, left, right, extra)


def place_kernel(chips, hidden, *refs):
    pieces, out_ref = refs[:chips], refs[chips]
    chip = lax.axis_index("chip")
    units = out_ref.shape[2] // 2
    for mask in range(chips):
        for part in range(2):
            begin = pl.multiple_of(part * units + flip(chip, mask) * hidden, hidden)
            out_ref[:, :, pl.ds(begin, hidden)] = pieces[mask][
                :, :, pl.ds(part * hidden, hidden)
            ].astype(f32)


def place_units(pieces, hidden):
    chips = len(pieces)
    experts_here, rows, double = pieces[0].shape
    group = 2 if experts_here % 2 == 0 else 1
    return pl.pallas_call(
        functools.partial(place_kernel, chips, hidden),
        grid=(experts_here // group,),
        out_shape=jax.ShapeDtypeStruct((experts_here, rows, chips * double), f32),
        in_specs=[pl.BlockSpec((group, rows, double), lambda e: (e, 0, 0))] * chips,
        out_specs=pl.BlockSpec((group, rows, chips * double), lambda e: (e, 0, 0)),
        name="place_units",
    )(*pieces)


def across(value, chips, mask):
    if mask == 0:
        return value
    return lax.ppermute(value, "chip", [(i, i ^ mask) for i in range(chips)])


class LineGather:
    def __init__(self, cube, heads, own, out, sems):
        self.cube, self.heads, self.own, self.out = cube, heads, own, out
        self.local, self.line_send, self.line_recv, self.send, self.recv = sems
        self.hz = lax.axis_index("head")
        self.middle = jnp.minimum(self.hz, heads - 1 - self.hz)
        self.rows = own.shape[0]

    @staticmethod
    def scratch(cube, heads):
        return [
            DMA,
            DMA((heads + 1,)),
            DMA((heads,)),
            DMA((2, 1 << cube.number, heads)),
            DMA((2, 1 << cube.number, heads)),
        ]

    def source(self, rank):
        hz, heads, middle = self.hz, self.heads, self.middle
        if rank == 0:
            return hz
        far = (rank + 1) // 2
        near_one = hz - far if rank % 2 else hz + far
        far_one = jnp.where(hz < heads - 1 - hz, hz + (rank - middle), hz - (rank - middle))
        return jnp.where(rank <= 2 * middle, near_one, far_one)

    def line_copy(self, rank, step):
        head = self.source(rank)
        place = self.out.at[self.cube.place(0) + (head,)]
        return pltpu.make_async_remote_copy(
            src_ref=self.own if rank == 0 else place,
            dst_ref=place,
            send_sem=self.line_send.at[self.heads if rank == 0 and step < 0 else head],
            recv_sem=self.line_recv.at[head],
            device_id={"head": (self.hz + step + self.heads) % self.heads},
            device_id_type=MESH,
        )

    def along(self, rank, act):
        head = self.source(rank)
        goes_up = self.hz + 1 < self.heads
        goes_down = self.hz > 0
        if rank:
            goes_up = goes_up & (head < self.hz)
            goes_down = goes_down & (head > self.hz)

        @pl.when(goes_up)
        def _():
            act(self.line_copy(rank, 1))

        @pl.when(goes_down)
        def _():
            act(self.line_copy(rank, -1))

    def plane_copy(self, side, mask, k, rank):
        digit = self.cube.gather_orders[side][k]
        later = mask | (1 << digit)
        head = self.source(rank)
        part = part_of(self.rows, side)
        place = self.out.at[self.cube.place(mask) + (head, part)]
        return pltpu.make_async_remote_copy(
            src_ref=self.own.at[part] if mask == 0 and rank == 0 else place,
            dst_ref=place,
            send_sem=self.send.at[side, later, head],
            recv_sem=self.recv.at[side, later, head],
            device_id=self.cube.peer(digit),
            device_id_type=MESH,
        )

    def steps_after(self, side, mask):
        order = self.cube.gather_orders[side]
        last = max([k for k in range(self.cube.number) if (mask >> order[k]) & 1], default=-1)
        return range(last + 1, self.cube.number)

    def begin(self):
        self.own_copy = pltpu.make_async_copy(
            self.own, self.out.at[self.cube.place(0) + (self.hz,)], self.local
        )
        self.own_copy.start()

    def receive(self, mask, rank):
        if mask == 0:
            if rank:
                self.line_copy(rank, 1).wait_recv()
            self.along(rank, lambda copy: copy.start())
        for side in range(2):
            if mask:
                order = self.cube.gather_orders[side]
                k = max(k for k in range(self.cube.number) if (mask >> order[k]) & 1)
                self.plane_copy(side, mask & ~(1 << order[k]), k, rank).wait_recv()
            for k in self.steps_after(side, mask):
                self.plane_copy(side, mask, k, rank).start()

    def events(self):
        masks = sorted(range(1 << self.cube.number), key=lambda m: bin(m).count("1"))
        return [(mask, rank) for mask in masks for rank in range(self.heads)]

    def finish(self):
        self.own_copy.wait()
        for mask, rank in self.events():
            if mask == 0:
                self.along(rank, lambda copy: copy.wait_send())
            for side in range(2):
                for k in self.steps_after(side, mask):
                    self.plane_copy(side, mask, k, rank).wait_send()


class DenseGather:
    def __init__(self, cube, heads, own, out, sems):
        self.cube, self.heads, self.own, self.out = cube, heads, own, out
        self.local, self.line_send, self.line_recv, self.send, self.recv = sems
        self.hz = lax.axis_index("head")

    @staticmethod
    def scratch(cube, heads):
        return [
            DMA,
            DMA((heads - 1,)),
            DMA((heads - 1,)),
            DMA((2, 1 << cube.number)),
            DMA((2, 1 << cube.number)),
        ]

    def line_copy(self, d):
        return pltpu.make_async_remote_copy(
            src_ref=self.own,
            dst_ref=self.out.at[self.cube.place(0) + (self.hz,)],
            send_sem=self.line_send.at[d - 1],
            recv_sem=self.line_recv.at[d - 1],
            device_id={"head": (self.hz + d) % self.heads},
            device_id_type=MESH,
        )

    def flat_copy(self, side, mask, k):
        digit = self.cube.gather_orders[side][k]
        later = mask | (1 << digit)
        part = self.heads // 2
        place = self.out.at[self.cube.place(mask) + (pl.ds(side * part, part),)]
        return pltpu.make_async_remote_copy(
            src_ref=place,
            dst_ref=place,
            send_sem=self.send.at[side, later],
            recv_sem=self.recv.at[side, later],
            device_id=self.cube.peer(digit),
            device_id_type=MESH,
        )

    def steps_after(self, side, mask):
        order = self.cube.gather_orders[side]
        last = max([k for k in range(self.cube.number) if (mask >> order[k]) & 1], default=-1)
        return range(last + 1, self.cube.number)

    def begin(self):
        self.own_copy = pltpu.make_async_copy(
            self.own, self.out.at[self.cube.place(0) + (self.hz,)], self.local
        )
        self.own_copy.start()
        for d in near(self.heads)[::-1]:
            self.line_copy(d).start()

    def events(self):
        return [(mask, 2) for mask in range(1 << self.cube.number)]

    def receive(self, mask, _):
        if mask == 0:
            self.own_copy.wait()
            for d in near(self.heads):
                self.line_copy(d).wait_recv()
        for side in range(2):
            if mask:
                order = self.cube.gather_orders[side]
                k = max(k for k in range(self.cube.number) if (mask >> order[k]) & 1)
                self.flat_copy(side, mask & ~(1 << order[k]), k).wait_recv()
            for k in self.steps_after(side, mask):
                self.flat_copy(side, mask, k).start()

    def finish(self):
        for d in near(self.heads):
            self.line_copy(d).wait_send()
        for mask in range(1 << self.cube.number):
            for side in range(2):
                for k in self.steps_after(side, mask):
                    self.flat_copy(side, mask, k).wait_send()


class LineSums:
    def __init__(self, cube, heads, blocks, out, refs):
        self.cube, self.heads, self.blocks, self.out = cube, heads, blocks, out
        count = cube.number
        self.arrived, self.parts = refs[:count], refs[count : 2 * count - 1]
        self.line_out, self.line_in, self.send, self.recv, self.end_send, self.end_recv = refs[
            2 * count - 1 :
        ]
        self.hz = lax.axis_index("head")
        self.rows = blocks.shape[-2]
        self.outward = near(heads)[::-1] + [0]
        self.turns = heads + count + 1

    @staticmethod
    def scratch(cube, heads, rows, columns):
        count = cube.number
        slots = [(1 << count) >> (k + 1) for k in range(count)]
        half = cut_rows(rows)
        return (
            [pltpu.VMEM((2, s, heads, half, columns), bf16) for s in slots]
            + [pltpu.VMEM((2, s, heads, half, columns), bf16) for s in slots[1:]]
            + [
                pltpu.VMEM((heads - 1, rows, columns), bf16),
                pltpu.VMEM((heads - 1, rows, columns), bf16),
                DMA((2, count, slots[0], heads)),
                DMA((2, count, slots[0], heads)),
                DMA((heads - 1,)),
                DMA((heads - 1,)),
            ]
        )

    def slot(self, side, k, mask):
        return subsets(self.cube.scatter_orders[side][k + 1 :]).index(mask)

    def mine(self, side, mask, d):
        place = self.cube.place(mask) + ((self.hz + d) % self.heads,)
        return self.blocks.at[place + (part_of(self.rows, side),)]

    def there(self, ref, side, where, d):
        return ref.at[side, where, d, pl.ds(0, part_of(self.rows, side).size)]

    def copy_of(self, side, k, mask, d):
        order = self.cube.scatter_orders[side]
        where = self.slot(side, k, mask)
        if k == 0:
            piece = self.mine(side, mask | (1 << order[0]), d)
        else:
            piece = self.there(self.parts[k - 1], side, where, d)
        return pltpu.make_async_remote_copy(
            src_ref=piece,
            dst_ref=self.there(self.arrived[k], side, where, d),
            send_sem=self.send.at[side, k, where, d],
            recv_sem=self.recv.at[side, k, where, d],
            device_id=self.cube.peer(order[k]),
            device_id_type=MESH,
        )

    def end_copy(self, d):
        return pltpu.make_async_remote_copy(
            src_ref=self.line_out.at[d - 1],
            dst_ref=self.line_in.at[d - 1],
            send_sem=self.end_send.at[d - 1],
            recv_sem=self.end_recv.at[d - 1],
            device_id={"head": (self.hz + d) % self.heads},
            device_id_type=MESH,
        )

    def sums(self, side, steps, mask, d):
        value = self.mine(side, mask, d)[...].astype(f32)
        for j in range(steps):
            self.copy_of(side, j, mask, d).wait_recv()
            value = value + self.there(self.arrived[j], side, self.slot(side, j, mask), d)[
                ...
            ].astype(f32)
        return value

    def turn(self, turn):
        count = self.cube.number
        if turn < self.heads:
            for side in range(2):
                for mask in subsets(self.cube.scatter_orders[side][1:])[::-1]:
                    self.copy_of(side, 0, mask, self.outward[turn]).start()
        for k in range(1, count):
            if 0 <= turn - k - 1 < self.heads:
                d = self.outward[turn - k - 1]
                for side in range(2):
                    order = self.cube.scatter_orders[side]
                    for mask in subsets(order[k + 1 :])[::-1]:
                        value = self.sums(side, k, mask | (1 << order[k]), d)
                        place = self.there(self.parts[k - 1], side, self.slot(side, k, mask), d)
                        place[...] = value.astype(bf16)
                        self.copy_of(side, k, mask, d).start()
        if 0 <= turn - count - 1 < self.heads:
            d = self.outward[turn - count - 1]
            for side in range(2):
                value = self.sums(side, count, 0, d)
                part = part_of(self.rows, side)
                if d:
                    self.line_out[d - 1, part] = value.astype(bf16)
                else:
                    self.out[part] = value
            if d:
                self.end_copy(d).start()

    def finish(self):
        others = near(self.heads)
        for d in others:
            self.end_copy(d).wait_recv()
            self.out[...] += self.line_in[d - 1].astype(f32)
        for d in others:
            self.end_copy(d).wait_send()
        for side in range(2):
            for k in range(self.cube.number):
                for mask in subsets(self.cube.scatter_orders[side][k + 1 :]):
                    for d in self.outward:
                        self.copy_of(side, k, mask, d).wait_send()


TN = (((0,), (0,)), ((), ()))


def allowed(key_segments, query_segments, block, rows, seq):
    columns = query_segments.shape[1]
    key_place = block * rows + lax.broadcasted_iota(jnp.int32, (rows, columns), 0)
    query_place = seq * rows + lax.broadcasted_iota(jnp.int32, (rows, columns), 1) % rows
    return (key_segments == query_segments) & (key_place <= query_place)


def attend_kernel(cube, heads, group, beside, *refs):
    q_ref, kv_ref, key_seg, query_seg = refs[:4]
    near_refs, refs = refs[4 : 4 + len(beside)], refs[4 + len(beside) :]
    lines_ref, kv_out, out_turned, lse_ref = refs[:4]
    far_refs, refs = refs[4 : 4 + len(beside)], refs[4 + len(beside) :]
    stage, top, total, acc, send, recv, line_send, line_recv = refs[:8]
    chip, core, hz = lax.axis_index("chip"), lax.axis_index("core"), lax.axis_index("head")
    seq = chip * 2 + core
    others = near(heads)[::-1]
    batch, rows, columns = kv_ref.shape
    kv_heads = columns // (2 * HEAD_WIDTH)
    part = rows // 2
    meet([cube.peer(digit) for digit in range(cube.number)] + [{"head": (hz + d) % heads} for d in others])
    kv_out[chip, core] = kv_ref[...]
    gathers = []
    rest_refs = refs[8:]
    for with_core, own_block, all_blocks in zip(beside, near_refs, far_refs):
        kind = DenseGather if with_core else LineGather
        own_cube = Cube(cube.chips, with_core)
        gathers.append(kind(own_cube, heads, own_block, all_blocks, rest_refs[:5]))
        rest_refs = rest_refs[5:]
    fronts = {}
    for one in gathers:
        for mask, rank in one.events():
            fronts.setdefault(rank + bin(mask).count("1"), []).append((one, (mask, rank)))
    last_front = max(fronts, default=0)
    now = cube.number + 1

    def pass_front(index):
        for one, event in fronts.get(index, []):
            one.receive(*event)

    def copy_of(side, mask, k):
        order = cube.gather_orders[side]
        later = mask | (1 << order[k])
        place = cube.place(mask) + (slice(None), pl.ds(side * part, part))
        return pltpu.make_async_remote_copy(
            src_ref=kv_ref.at[:, pl.ds(side * part, part)] if mask == 0 else kv_out.at[place],
            dst_ref=kv_out.at[place],
            send_sem=send.at[side, later],
            recv_sem=recv.at[side, later],
            device_id=cube.peer(order[k]),
            device_id_type=MESH,
        )

    copies = []

    def forward(mask):
        for side in range(2):
            order = cube.gather_orders[side]
            last = max([k for k in range(cube.number) if (mask >> order[k]) & 1], default=-1)
            if mask:
                copy_of(side, mask & ~(1 << order[last]), last).wait_recv()
            for k in range(last + 1, cube.number):
                copy_of(side, mask, k).start()
                copies.append((side, mask, k))

    forward(0)
    for one in gathers:
        one.begin()
    pass_front(0)
    top[...] = jnp.full_like(top, negative)
    total[...] = jnp.zeros_like(total)
    acc[...] = jnp.zeros_like(acc)

    def block_step(block):
        place = (block // 2, block % 2)
        for b in range(batch):
            mask = allowed(
                key_seg[b, pl.ds(pl.multiple_of(block * rows, rows), rows), :],
                query_seg[b],
                block,
                rows,
                seq,
            )
            for j in range(kv_heads):
                pair = b * kv_heads + j
                begin = j * 2 * HEAD_WIDTH
                keys = kv_out[place + (b, slice(None), pl.ds(begin, HEAD_WIDTH))]
                values = kv_out[place + (b, slice(None), pl.ds(begin + HEAD_WIDTH, HEAD_WIDTH))]
                scores = lax.dot_general(keys, q_ref[pair], NT, preferred_element_type=f32)
                scores = jnp.where(mask, scores, negative)
                new = jnp.maximum(top[pair], jnp.max(scores, axis=0, keepdims=True))
                weights = jnp.exp(scores - new)
                shrink = jnp.exp(top[pair] - new)
                top[pair] = new
                total[pair] = total[pair] * shrink + jnp.sum(weights, axis=0, keepdims=True)
                acc[pair] = acc[pair] * shrink + lax.dot_general(
                    values, weights.astype(bf16), TN, preferred_element_type=f32
                )

    block_step(seq)
    for level in range(1, cube.number + 1):
        for mask in range(1, 1 << cube.number):
            if bin(mask).count("1") == level:
                forward(mask)
    pass_front(1)
    now = 2
    turns = 2 * cube.chips
    if beside:
        for turn in range(turns):
            if turn == turns // 2:
                pass_front(now)
                now += 1

            @pl.when(turn < seq)
            def _():
                block_step(turn)

    else:

        @pl.loop(0, seq)
        def _(block):
            block_step(block)

    spot = rows // heads
    for b in range(batch):
        for j in range(kv_heads):
            pair = b * kv_heads + j
            value = acc[pair] / total[pair]
            out_turned[pair] = value
            lse_ref[pair] = top[pair] + jnp.log(total[pair])
            value = value.T.astype(bf16)
            for g in range(group):
                for head in range(heads):
                    begin = (j * group + g) * HEAD_WIDTH
                    stage[head, pl.ds(b * spot, spot), pl.ds(begin, HEAD_WIDTH)] = value[
                        g * rows + head * spot : g * rows + (head + 1) * spot
                    ]

    def line_copy(d):
        return pltpu.make_async_remote_copy(
            src_ref=stage.at[(hz + d) % heads],
            dst_ref=lines_ref.at[hz],
            send_sem=line_send.at[d - 1],
            recv_sem=line_recv.at[d - 1],
            device_id={"head": (hz + d) % heads},
            device_id_type=MESH,
        )

    for d in others:
        line_copy(d).start()
    lines_ref[hz] = stage[hz]
    for index in range(now, last_front + 1):
        pass_front(index)
    for side, mask, k in copies:
        copy_of(side, mask, k).wait_send()
    for d in others:
        line_copy(d).wait()
    for one in gathers:
        one.finish()


def attend(queries, keys_values, key_seg, query_seg, beside, chips, heads, group, number):
    batch, rows, columns = keys_values.shape
    pairs, wide, depth = queries.shape
    cube = Cube(chips, True)
    group_columns = group * columns // 2
    tokens = batch * rows // heads
    return pl.pallas_call(
        functools.partial(attend_kernel, cube, heads, group, [core for _, core in beside]),
        out_shape=(
            jax.ShapeDtypeStruct((heads, tokens, group_columns), bf16),
            jax.ShapeDtypeStruct((chips, 2, batch, rows, columns), bf16),
            jax.ShapeDtypeStruct((pairs, depth, wide), f32),
            jax.ShapeDtypeStruct((pairs, 1, wide), f32),
        )
        + tuple(
            jax.ShapeDtypeStruct((chips,) + (2,) * with_core + (heads,) + value.shape, bf16)
            for value, with_core in beside
        ),
        in_specs=[WHOLE] * 4 + [ANY] * len(beside),
        out_specs=(WHOLE,) * 4 + (ANY,) * len(beside),
        scratch_shapes=[
            pltpu.VMEM((heads, tokens, group_columns), bf16),
            pltpu.VMEM((pairs, 1, wide), f32),
            pltpu.VMEM((pairs, 1, wide), f32),
            pltpu.VMEM((pairs, depth, wide), f32),
            DMA((2, 2 * chips)),
            DMA((2, 2 * chips)),
            DMA((heads - 1,)),
            DMA((heads - 1,)),
        ]
        + [
            item
            for _, core in beside
            for item in (DenseGather if core else LineGather).scratch(Cube(chips, core), heads)
        ],
        compiler_params=pltpu.CompilerParams(
            collective_id=number, has_side_effects=True, vmem_limit_bytes=50 << 20
        ),
        name="attend",
    )(queries, keys_values, key_seg, query_seg, *[value for value, _ in beside])


def attend_back_kernel(cube, heads, group, beside, shares, *refs):
    q_ref, kv_ref, key_seg, query_seg, out_turned, lse_ref, dh_ref = refs[:7]
    near_refs, refs = refs[7 : 7 + len(beside)], refs[7 + len(beside) :]
    pair_refs, refs = refs[:shares], refs[shares:]
    dq_ref, dkv_ref = refs[:2]
    far_refs, refs = refs[2 : 2 + len(beside)], refs[2 + len(beside) :]
    added = refs[: cube.chips] if shares else ()
    refs = (None,) * 9 + refs[len(added) :]
    count = cube.number
    landed, d_out, delta, dq_turned, grads = refs[9:14]
    arrived, parts = refs[14 : 14 + count], refs[14 + count : 13 + 2 * count]
    send, recv, line_send, line_recv = refs[13 + 2 * count : 17 + 2 * count]
    turns = 2 * cube.chips
    rest = refs[17 + 2 * count :]
    sums_beside = []
    for with_core, source, target in zip(beside, near_refs, far_refs):
        own_cube = Cube(cube.chips, with_core)
        size = 2 * own_cube.number + 5
        sums_beside.append(LineSums(own_cube, heads, source, target, rest[:size]))
        rest = rest[size:]

    def load_pair(mask):
        place = flip(lax.axis_index("chip"), mask)
        return [
            pltpu.make_async_copy(pair_refs[i].at[place], rest[i], rest[3].at[i]) for i in range(2)
        ]

    def store_sum(mask):
        return pltpu.make_async_copy(rest[2], added[mask], rest[3].at[2])

    def add_pair(turn):
        mask = turn // 2
        if turn % 2 == 0:
            for copy in load_pair(mask):
                copy.start()
            return
        for copy in load_pair(mask):
            copy.wait()
        if mask:
            store_sum(mask - 1).wait()
        rest[2][...] = (rest[0][...].astype(f32) + rest[1][...].astype(f32)).astype(bf16)
        store_sum(mask).start()

    chip, core, hz = lax.axis_index("chip"), lax.axis_index("core"), lax.axis_index("head")
    seq = chip * 2 + core
    others = near(heads)[::-1]
    batch, rows, columns = kv_ref.shape[2:]
    kv_heads = columns // (2 * HEAD_WIDTH)
    spot = rows // heads
    half = grads.shape[2] // 2
    meet([cube.peer(digit) for digit in range(count)] + [{"head": (hz + d) % heads} for d in others])

    def line_copy(d):
        return pltpu.make_async_remote_copy(
            src_ref=dh_ref.at[(hz + d) % heads],
            dst_ref=landed.at[hz],
            send_sem=line_send.at[d - 1],
            recv_sem=line_recv.at[d - 1],
            device_id={"head": (hz + d) % heads},
            device_id_type=MESH,
        )

    for d in others:
        line_copy(d).start()
    for turn in range(2):
        for one in sums_beside:
            one.turn(turn)
    landed[hz] = dh_ref[hz]
    grads[...] = jnp.zeros_like(grads)
    dq_turned[...] = jnp.zeros_like(dq_turned)
    for d in others:
        line_copy(d).wait()
    for b in range(batch):
        for j in range(kv_heads):
            pair = b * kv_heads + j
            for g in range(group):
                for head in range(heads):
                    begin = (j * group + g) * HEAD_WIDTH
                    d_out[pair, pl.ds(g * rows + head * spot, spot), :] = landed[
                        head, pl.ds(b * spot, spot), pl.ds(begin, HEAD_WIDTH)
                    ]
            delta[pair] = jnp.sum(
                d_out[pair].astype(f32).T * out_turned[pair], axis=0, keepdims=True
            )

    def block_step(block):
        place = (block // 2, block % 2)
        for b in range(batch):
            mask = allowed(
                key_seg[b, pl.ds(pl.multiple_of(block * rows, rows), rows), :],
                query_seg[b],
                block,
                rows,
                seq,
            )
            for j in range(kv_heads):
                pair = b * kv_heads + j
                begin = j * 2 * HEAD_WIDTH
                keys = kv_ref[place + (b, slice(None), pl.ds(begin, HEAD_WIDTH))]
                values = kv_ref[place + (b, slice(None), pl.ds(begin + HEAD_WIDTH, HEAD_WIDTH))]
                scores = lax.dot_general(keys, q_ref[pair], NT, preferred_element_type=f32)
                probs = jnp.exp(jnp.where(mask, scores, negative) - lse_ref[pair])
                d_probs = lax.dot_general(values, d_out[pair], NT, preferred_element_type=f32)
                d_scores = (probs * (d_probs - delta[pair])).astype(bf16)
                dq_turned[pair] += lax.dot_general(
                    keys, d_scores, TN, preferred_element_type=f32
                )
                d_keys = jnp.dot(d_scores, q_ref[pair], preferred_element_type=f32)
                d_values = jnp.dot(probs.astype(bf16), d_out[pair], preferred_element_type=f32)
                grads[place + (pl.ds(b * rows, rows), pl.ds(begin, 2 * HEAD_WIDTH))] = (
                    jnp.concatenate([d_keys, d_values], axis=1).astype(bf16)
                )

    done = 2
    if beside:
        for turn in range(turns):

            @pl.when(turn <= seq)
            def _():
                block_step(turn)

            if shares:
                add_pair(turn)
            if turn % 3 == 2:
                for one in sums_beside:
                    one.turn(done)
                done += 1

    else:

        @pl.loop(0, seq + 1)
        def _(block):
            block_step(block)

    def slot(side, k, mask):
        return subsets(cube.scatter_orders[side][k + 1 :]).index(mask)

    def mine(side, mask):
        return grads.at[cube.place(mask) + (pl.ds(side * half, half),)]

    copies = {}

    def sums(side, steps, mask):
        value = mine(side, mask)[...].astype(f32)
        for j in range(steps):
            copies[(side, j, mask)].wait_recv()
            value = value + arrived[j][side, slot(side, j, mask)].astype(f32)
        return value

    for k in range(count):
        for side in range(2):
            order = cube.scatter_orders[side]
            for mask in subsets(order[k + 1 :])[::-1]:
                full = mask | (1 << order[k])
                where = slot(side, k, mask)
                if k == 0:
                    piece = mine(side, full)
                else:
                    piece = parts[k - 1].at[side, where]
                    piece[...] = sums(side, k, full).astype(bf16)
                copies[(side, k, mask)] = pltpu.make_async_remote_copy(
                    src_ref=piece,
                    dst_ref=arrived[k].at[side, where],
                    send_sem=send.at[side, k, where],
                    recv_sem=recv.at[side, k, where],
                    device_id=cube.peer(order[k]),
                    device_id_type=MESH,
                )
                copies[(side, k, mask)].start()
        for one in sums_beside:
            if done < one.turns:
                one.turn(done)
        done += 1
    scale = HEAD_WIDTH ** (-0.5)
    for pair in range(batch * kv_heads):
        dq_ref[pair] = (dq_turned[pair] * scale).T.astype(bf16)
    for side in range(2):
        dkv_ref[pl.ds(side * half, half)] = sums(side, count, 0)
    for turn in range(done, max([one.turns for one in sums_beside], default=0)):
        for one in sums_beside:
            if turn < one.turns:
                one.turn(turn)
    for copy in copies.values():
        copy.wait_send()
    for one in sums_beside:
        one.finish()
    if shares:
        store_sum(cube.chips - 1).wait()


def attend_back(
    queries, kv_all, key_seg, query_seg, out_turned, lse, d_heads, beside, shares, heads, group, number
):
    chips, _, batch, rows, columns = kv_all.shape
    pairs, wide, depth = queries.shape
    cube = Cube(chips, True)
    count = cube.number
    half = batch * rows // 2
    slots = [(1 << count) >> (k + 1) for k in range(count)]
    return pl.pallas_call(
        functools.partial(
            attend_back_kernel, cube, heads, group, [core for _, core in beside], len(shares)
        ),
        out_shape=(
            jax.ShapeDtypeStruct((pairs, wide, depth), bf16),
            jax.ShapeDtypeStruct((batch * rows, columns), f32),
        )
        + tuple(jax.ShapeDtypeStruct(value.shape[-2:], f32) for value, _ in beside)
        + tuple(jax.ShapeDtypeStruct(shares[0].shape[1:], bf16) for _ in range(chips) if shares),
        in_specs=[WHOLE] * (7 + len(beside)) + [ANY] * len(shares),
        out_specs=(WHOLE,) * (2 + len(beside)) + (ANY,) * (chips * bool(shares)),
        scratch_shapes=[
            pltpu.VMEM(d_heads.shape, bf16),
            pltpu.VMEM((pairs, wide, depth), bf16),
            pltpu.VMEM((pairs, 1, wide), f32),
            pltpu.VMEM((pairs, depth, wide), f32),
            pltpu.VMEM((chips, 2, batch * rows, columns), bf16),
        ]
        + [pltpu.VMEM((2, s, half, columns), bf16) for s in slots]
        + [pltpu.VMEM((2, s, half, columns), bf16) for s in slots[1:]]
        + [
            DMA((2, count, slots[0])),
            DMA((2, count, slots[0])),
            DMA((heads - 1,)),
            DMA((heads - 1,)),
        ]
        + [
            item
            for value, core in beside
            for item in LineSums.scratch(Cube(chips, core), *value.shape[-3:])
        ]
        + [pltpu.VMEM(shares[0].shape[1:], bf16) for _ in range(3) if shares]
        + [DMA((3,)) for _ in range(1) if shares],
        compiler_params=pltpu.CompilerParams(
            collective_id=number, has_side_effects=True, vmem_limit_bytes=56 << 20
        ),
        name="attend_back",
    )(
        queries, kv_all, key_seg, query_seg, out_turned, lse, d_heads, *[v for v, _ in beside], *shares
    )


def sibling(value):
    return lax.ppermute(value, "core", [(0, 1), (1, 0)])


def per_device(
    layer_input,
    segments,
    routes,
    pair_rank,
    query_key_value_weight,
    output_weight,
    router_weight,
    norm_attn,
    norm_ffn,
    w_gate_up,
    w_down,
    cotangent,
):
    chips = lax.axis_size("chip")
    head_number = lax.axis_size("head")
    sequence_batch, token_rows, width = layer_input.shape
    length = segments.shape[1]
    blk = token_rows * head_number
    query_group = QUERY_HEADS // KEY_VALUE_HEADS
    key_value_location = KEY_VALUE_HEADS // head_number
    loc_experts, slice_rows = w_gate_up.shape[:2]
    top = routes.shape[2]
    tokens_present = sequence_batch * token_rows
    pairs = tokens_present * top
    line_tokens = tokens_present * head_number
    scale = HEAD_WIDTH ** (-0.5)
    hidden = FF // chips
    loc_columns = key_value_location * (query_group + 2) * HEAD_WIDTH
    chip = lax.axis_index("chip")
    core = lax.axis_index("core")
    head = lax.axis_index("head")
    seq_index = chip * 2 + core
    dense_rows = query_key_value_weight.shape[0]

    extras = jnp.concatenate([router_weight, norm_attn[:, None], norm_ffn[:, None]], axis=1)
    extras = jnp.pad(extras, ((0, 0), (0, LANES - extras.shape[1])))
    slices = query_key_value_weight.reshape(dense_rows, head_number, loc_columns).transpose(1, 0, 2)
    slices = jnp.concatenate(
        [slices, jnp.broadcast_to(extras, (head_number,) + extras.shape)], axis=2
    )
    group_tokens = chips * head_number * tokens_present
    columns = width + LANES
    fused = hidden % LANES == 0 and group_tokens <= 2048
    own_tokens = layer_input.reshape(tokens_present, width)
    cots = cotangent.reshape(tokens_present, width)
    if fused:

        def unit_of(weights, mask):
            begins = [part * FF + (chip ^ mask) * hidden for part in range(2)]
            cut = [lax.dynamic_slice_in_dim(weights, begin, hidden, 2) for begin in begins]
            return jnp.concatenate(cut, axis=2)

        keys = (routes * pairs + pair_rank).reshape(pairs)
        x_line, dense, last_unit, slot = start(
            layer_input, slices, unit_of(w_gate_up, chips - 1), keys, chips, head_number, 1
        )
        x_line, w_gate_up = lax.optimization_barrier((x_line, w_gate_up))
        units = [across(unit_of(w_gate_up, mask), chips, mask) for mask in range(chips - 1)]
        units.append(last_unit)
        dense = dense.reshape(width, loc_columns + LANES)
    else:
        parts = w_gate_up.reshape(loc_experts, slice_rows, 2, chips, hidden).transpose(3, 2, 1, 0, 4)
        parts = parts.reshape(chips, 2, slice_rows, loc_experts * hidden)
        piled = jnp.zeros((chips, 2, 2, slice_rows, loc_experts * hidden), bf16)
        for mask in range(chips):
            piece = lax.dynamic_index_in_dim(parts, chip ^ mask, 0, keepdims=False)
            piece = across(piece, chips, mask)
            other = sibling(piece)
            piled = lax.dynamic_update_slice(piled, piece[None, None], (chip ^ mask, core, 0, 0, 0))
            piled = lax.dynamic_update_slice(piled, other[None, None], (chip ^ mask, 1 - core, 0, 0, 0))
        piled = piled.transpose(2, 0, 1, 3, 4).reshape(2, width, loc_experts * hidden)
        expert_gate, expert_up = piled[0], piled[1]
        down_other = sibling(w_down)
        expert_down = (
            jnp.where(
                core == 0,
                jnp.concatenate([w_down, down_other], axis=1),
                jnp.concatenate([down_other, w_down], axis=1),
            )
        ).reshape(loc_experts * hidden, width)

        lined = line_exchange(slices, head_number, 1)
        dense = gather(
            lined.reshape(head_number * dense_rows, loc_columns + LANES), chips, 1, True, 2
        ).reshape(width, loc_columns + LANES)
        x_line = line_exchange(layer_input.reshape(tokens_present, width), head_number, 3, True)

    if not fused:
        grad_all = lax.all_gather(cots, ("chip", "head"), axis=0, tiled=True)
        dense_out = lax.all_gather(output_weight, ("chip", "core", "head"), axis=0, tiled=True)

    dense_qkv = dense[:, :loc_columns]
    dense_router = dense[:, loc_columns : loc_columns + EXPERTS]
    gain_attn = dense[:, loc_columns + EXPERTS].astype(f32)
    gain_ffn = dense[:, loc_columns + EXPERTS + 1].astype(f32)

    x_line = x_line.reshape(line_tokens, width).astype(f32)
    normed_line = x_line * lax.rsqrt(jnp.mean(x_line * x_line, axis=1, keepdims=True) + epsilon)
    first_line = (normed_line * gain_attn).astype(bf16)

    def to_blocks(value):
        columns = value.shape[1:]
        if fused:
            return value.reshape((sequence_batch, blk) + columns)
        return (
            value.reshape((head_number, sequence_batch, token_rows) + columns)
            .swapaxes(0, 1)
            .reshape((sequence_batch, blk) + columns)
        )

    def to_lines(value):
        columns = value.shape[2:]
        if fused:
            return value.reshape((line_tokens,) + columns)
        return (
            value.reshape((sequence_batch, head_number, token_rows) + columns)
            .swapaxes(0, 1)
            .reshape((line_tokens,) + columns)
        )

    q_start = seq_index * blk
    q_pos = q_start + jnp.arange(blk, dtype=jnp.int32)
    cosine, sine = rope_tables(q_pos, HEAD_WIDTH)
    projected = to_blocks(jnp.dot(first_line, dense_qkv, preferred_element_type=f32)).reshape(
        sequence_batch, blk, key_value_location, query_group + 2, HEAD_WIDTH
    )
    turned = rotate(projected[:, :, :, : query_group + 1], cosine, sine)
    query_rows = turned[:, :, :, :query_group].astype(bf16)
    keys_values = (
        jnp.stack([turned[:, :, :, query_group], projected[:, :, :, query_group + 1]], axis=3)
        .astype(bf16)
        .reshape(sequence_batch * blk, key_value_location * 2 * HEAD_WIDTH)
    )
    kv_columns = key_value_location * 2 * HEAD_WIDTH
    pairs_here = sequence_batch * key_value_location
    group_columns = key_value_location * query_group * HEAD_WIDTH
    queries = (
        (query_rows.astype(f32) * scale)
        .astype(bf16)
        .transpose(0, 2, 3, 1, 4)
        .reshape(pairs_here, query_group * blk, HEAD_WIDTH)
    )
    key_seg = segments[:, :, None]
    q_seg = lax.dynamic_slice_in_dim(segments, q_start, blk, 1)
    query_seg = jnp.tile(q_seg[:, None, :], (1, 1, query_group))
    lines, kv_all, out_turned, lse, *beside = attend(
        queries,
        keys_values.reshape(sequence_batch, blk, kv_columns),
        key_seg,
        query_seg,
        [(cots, False), (output_weight, True)] if fused else [],
        chips,
        head_number,
        query_group,
        4,
    )
    if fused:
        grad_all = beside[0].reshape(group_tokens, width)
        dense_out = beside[1].reshape(QUERY_HEADS * HEAD_WIDTH, width)
    mixed_heads = lines.transpose(1, 0, 2).reshape(tokens_present, QUERY_HEADS * HEAD_WIDTH)
    tokens = layer_input.reshape(tokens_present, width).astype(f32)
    middle = tokens + jnp.dot(mixed_heads, dense_out, preferred_element_type=f32)
    inverse_two = lax.rsqrt(jnp.mean(middle * middle, axis=1, keepdims=True) + epsilon)
    normed_two = middle * inverse_two
    second_input = (normed_two * gain_ffn).astype(bf16)
    router_logits = jnp.dot(second_input, dense_router, preferred_element_type=f32)
    route_flat = routes.reshape(tokens_present, top)
    hot = route_flat[:, :, None] == jnp.arange(EXPERTS, dtype=jnp.int32)[None, None, :]
    chosen = jnp.sum(jnp.where(hot, router_logits[:, None, :], 0.0), axis=2)
    gates = jax.nn.softmax(chosen, axis=-1)
    if not fused:
        expert_of = route_flat.reshape(pairs)
        rank = pair_rank.reshape(pairs)
        slot = jnp.sum(
            (expert_of[None, :] == expert_of[:, None]) & (rank[None, :] < rank[:, None]),
            axis=1,
            dtype=jnp.int32,
        )
    kept = (slot < CAP).reshape(tokens_present, top).astype(f32)
    weights_pair = gates * kept
    spread = jnp.sum(jnp.where(hot, weights_pair[:, :, None], 0.0), axis=1)
    spread_high = spread.astype(bf16)
    spread_low = (spread - spread_high.astype(f32)).astype(bf16)
    pad = jnp.zeros((tokens_present, LOW - EXPERTS), bf16)
    payload = jnp.concatenate([second_input, spread_high, pad, spread_low, pad], axis=1)
    if fused:
        back, moe_part, keep_up, other_up, keep_down, other_down = expert_turn(
            payload, grad_all, units, w_down, head_number, 6
        )
        down_share = keep_down.astype(f32) + other_down.astype(f32)
    else:
        x_all = gather(payload, chips, head_number, False, 6).reshape(group_tokens, columns)
        moe_part, back_part, d_gate_w, d_up_w, d_down_w = experts(
            x_all, grad_all, expert_gate, expert_up, expert_down, hidden
        )
        back_part = back_part.reshape(chips, head_number, tokens_present, columns)
        back = scatter_sum(back_part, chips, head_number, False, 7)
        moe = lax.psum_scatter(moe_part, ("chip", "head"), scatter_dimension=0, tiled=True)
        grads = jnp.stack([d_gate_w, d_up_w]).reshape(2, chips, 2, slice_rows, loc_experts * hidden)
        keep = lax.dynamic_index_in_dim(grads, core, 2, keepdims=False)
        give = lax.dynamic_index_in_dim(grads, 1 - core, 2, keepdims=False)
        shared = (keep.astype(f32) + sibling(give).astype(f32)).astype(bf16)
        piled = jnp.zeros((chips, 2, slice_rows, loc_experts * hidden), bf16)
        for mask in range(chips):
            piece = across(lax.dynamic_index_in_dim(shared, chip ^ mask, 1, keepdims=False), chips, mask)
            piled = lax.dynamic_update_slice(piled, piece[None], (chip ^ mask, 0, 0, 0))
        up_share = (
            piled.reshape(chips, 2, slice_rows, loc_experts, hidden)
            .transpose(3, 2, 1, 0, 4)
            .astype(f32)
            .reshape(loc_experts, slice_rows, 2 * FF)
        )
        d_down_w = d_down_w.reshape(loc_experts, 2, hidden // 2, width)
        keep = lax.dynamic_index_in_dim(d_down_w, core, 1, keepdims=False)
        give = lax.dynamic_index_in_dim(d_down_w, 1 - core, 1, keepdims=False)
        down_share = keep.astype(f32) + sibling(give).astype(f32)

    grad_out = cotangent.reshape(tokens_present, width).astype(f32)
    d_kept = back[:, width : width + EXPERTS]
    grad_gate = jnp.sum(jnp.where(hot, d_kept[:, None, :], 0.0), axis=2) * kept
    grad_chosen = gates * (grad_gate - jnp.sum(gates * grad_gate, axis=1, keepdims=True))
    grad_logits = jnp.sum(jnp.where(hot, grad_chosen[:, :, None], 0.0), axis=1)
    grad_router = jnp.dot(second_input.astype(f32).T, grad_logits, precision=HIGH_PRECISION)
    grad_second = back[:, :width] + jnp.dot(
        grad_logits, dense_router.astype(f32).T, precision=HIGH_PRECISION
    )
    grad_gain_ffn = jnp.sum(grad_second * normed_two, axis=0)
    scaled_two = grad_second * gain_ffn
    grad_mid = grad_out + inverse_two * (
        scaled_two - normed_two * jnp.mean(scaled_two * normed_two, axis=1, keepdims=True)
    )
    grad_attn = grad_mid.astype(bf16)
    grad_dense_out = jnp.dot(mixed_heads.T, grad_attn, preferred_element_type=f32)
    grad_dense_out = grad_dense_out.astype(bf16)
    if not fused:
        out_share = lax.psum_scatter(
            grad_dense_out, ("chip", "core", "head"), scatter_dimension=0, tiled=True
        ).astype(f32)
    grad_heads = (
        jnp.dot(grad_attn, dense_out.T, preferred_element_type=f32)
        .astype(bf16)
        .reshape(tokens_present, head_number, group_columns)
        .transpose(1, 0, 2)
    )
    grad_q, grad_kv, *beside = attend_back(
        queries,
        kv_all,
        key_seg,
        query_seg,
        out_turned,
        lse,
        grad_heads,
        [
            (moe_part.reshape(chips, head_number, tokens_present, width), False),
            (grad_dense_out.reshape(chips, 2, head_number, dense_rows, width), True),
        ]
        if fused
        else [],
        [keep_up, other_up] if fused else [],
        head_number,
        query_group,
        8,
    )
    if fused:
        moe, out_share, *shared = beside
        pieces = [across(shared[mask], chips, mask) for mask in range(chips)]
    grad_q = grad_q.reshape(
        sequence_batch, key_value_location, query_group, blk, HEAD_WIDTH
    ).transpose(0, 3, 1, 2, 4)
    grad_kv = grad_kv.reshape(sequence_batch, blk, key_value_location, 2, HEAD_WIDTH)
    grad_proj = jnp.concatenate([grad_q.astype(bf16), grad_kv.astype(bf16)], axis=3).astype(f32)
    unturned = rotate(grad_proj[:, :, :, : query_group + 1], cosine, -sine)
    grad_qkv = to_lines(
        jnp.concatenate([unturned, grad_proj[:, :, :, query_group + 1 :]], axis=3)
        .reshape(sequence_batch, blk, loc_columns)
        .astype(bf16)
    )
    grad_first_part = jnp.dot(grad_qkv, dense_qkv.T, preferred_element_type=f32)
    grad_gain_attn = jnp.sum(grad_first_part * normed_line, axis=0)
    extras = jnp.concatenate(
        [
            grad_router,
            grad_gain_attn[:, None],
            grad_gain_ffn[:, None],
            jnp.zeros((width, LANES - EXPERTS - 2), f32),
        ],
        axis=1,
    ).astype(bf16)
    if fused:
        x_again, gain_again, grad_qkv = lax.optimization_barrier((x_line, gain_attn, grad_qkv))
        scale_again = lax.rsqrt(jnp.mean(x_again * x_again, axis=1, keepdims=True) + epsilon)
        first_line = (x_again * scale_again * gain_again).astype(bf16)
        grad_first, sums = end(
            grad_first_part.astype(bf16).reshape(sequence_batch, head_number, token_rows, width),
            first_line,
            grad_qkv,
            extras,
            chips,
            head_number,
            13,
        )
        pieces, grad_first, sums = lax.optimization_barrier((pieces, grad_first, sums))
        up_share = place_units(pieces, hidden)
        up_share, grad_first, sums, moe, down_share = lax.optimization_barrier(
            (up_share, grad_first, sums, moe, down_share)
        )
        grad_first = jnp.sum(grad_first.astype(f32), axis=0).reshape(tokens_present, width)
        sums = sums.astype(f32)
    else:
        grad_first = jnp.sum(
            line_exchange(
                grad_first_part.astype(bf16).reshape(head_number, tokens_present, width),
                head_number,
                10,
            ).astype(f32),
            axis=0,
        )
        grad_dense_qkv = jnp.dot(first_line.T, grad_qkv, preferred_element_type=f32)
        sums = jnp.concatenate([grad_dense_qkv.astype(bf16), extras], axis=1)
        sums = scatter_sum(
            sums.reshape(chips, 2, head_number * dense_rows, loc_columns + LANES), chips, 1, True, 11
        )
        sums = line_exchange(
            sums.reshape(head_number, dense_rows, loc_columns + LANES), head_number, 12
        )
    inverse_one = lax.rsqrt(jnp.mean(tokens * tokens, axis=1, keepdims=True) + epsilon)
    normed_one = tokens * inverse_one
    scaled_one = grad_first * gain_attn
    grad_input = grad_mid + inverse_one * (
        scaled_one - normed_one * jnp.mean(scaled_one * normed_one, axis=1, keepdims=True)
    )
    mixed_out = (middle + moe.astype(f32)).astype(bf16)
    mixed_out = mixed_out.reshape(sequence_batch, token_rows, width)
    qkv_share = sums[:, :, :loc_columns].transpose(1, 0, 2).reshape(dense_rows, -1)
    extra = jnp.sum(sums[:, :, loc_columns:], axis=0)
    return (
        mixed_out,
        grad_input.reshape(sequence_batch, token_rows, width),
        qkv_share,
        out_share,
        extra[:, :EXPERTS],
        extra[:, EXPERTS],
        extra[:, EXPERTS + 1],
        up_share,
        down_share,
    )


def solution(mesh):
    grid = mesh.devices
    seq, heads = grid.shape
    split = Mesh(grid.reshape(seq // 2, 2, heads), ("chip", "core", "head"))
    places = ("chip", "core", "head")
    inner = ("chip", "core")
    placed = (
        P(None, places, None),
        P(),
        P(None, places, None),
        P(None, places, None),
        P(places, None),
        P(places, None),
        P(places, None),
        P(places),
        P(places),
        P("head", inner, None),
        P("head", inner, None),
        P(None, places, None),
    )
    return jax.shard_map(
        per_device,
        mesh=split,
        in_specs=placed,
        out_specs=(
            P(None, places, None),
            P(None, places, None),
            P(places, None),
            P(places, None),
            P(places, None),
            P(places),
            P(places),
            P("head", inner, None),
            P("head", inner, None),
        ),
        check_vma=False,
    )
```

```python
import functools

import jax
import jax.numpy as jnp
from jax import lax
from jax.experimental import pallas as pl
from jax.experimental.pallas import tpu as pltpu
from jax.sharding import Mesh, PartitionSpec as P

MODEL_WIDTH = 1536
QUERY_HEADS = 24
KEY_VALUE_HEADS = 8
HEAD_WIDTH = 64
EXPERTS = 40
FF = 512
CAP = 25
LANES = 128
LOW = 64

epsilon = 1e-06
negative = -1e30
theta = 10000.0
HIGH_PRECISION = lax.Precision.HIGHEST
MESH = pl.DeviceIdType.MESH
f32 = jnp.float32
bf16 = jnp.bfloat16
ANY = pl.BlockSpec(memory_space=pl.ANY)
WHOLE = pl.BlockSpec(memory_space=pltpu.VMEM)
DMA = pltpu.SemaphoreType.DMA


def rope_tables(token_positions, head_size):
    half = head_size // 2
    freq = theta ** (-jnp.arange(half, dtype=jnp.float32) / half)
    angle = token_positions.astype(jnp.float32)[:, None] * freq[None, :]
    return (jnp.cos(angle)[None, :, None, None, :], jnp.sin(angle)[None, :, None, None, :])


def rotate(value, cosine, sine):
    half = value.shape[-1] // 2
    first = value[..., :half]
    second = value[..., half:]
    return jnp.concatenate(
        [first * cosine - second * sine, second * cosine + first * sine], axis=-1
    )


def digits(count):
    number = count.bit_length() - 1
    assert 1 << number == count
    return number


def flip(index, mask):
    out = index
    bit = 0
    while (1 << bit) <= mask:
        if (mask >> bit) & 1:
            out = out + (1 - 2 * ((index // (1 << bit)) % 2)) * (1 << bit)
        bit += 1
    return out


def subsets(bits):
    out = [0]
    for bit in bits:
        out = out + [mask | (1 << bit) for mask in out]
    return out


def near(count):
    return sorted(range(1, count), key=lambda step: min(step, count - step))


def cut_rows(rows):
    return (rows // 2 + 15) // 16 * 16


def part_of(rows, side):
    cut = cut_rows(rows)
    return pl.ds(side * cut, rows - cut if side else cut)


def meet(peers):
    sem = pltpu.get_barrier_semaphore()
    for peer in peers:
        pl.semaphore_signal(sem, inc=1, device_id=peer, device_id_type=MESH)
    pl.semaphore_wait(sem, len(peers))


class Cube:
    def __init__(self, chips, with_core):
        self.chips = chips
        self.chip_digits = digits(chips)
        self.number = self.chip_digits + int(with_core)
        self.with_core = with_core
        up = tuple(range(self.chip_digits))
        core = (self.chip_digits,) if with_core else ()
        self.gather_orders = (up + core, up[::-1] + core)
        self.scatter_orders = (core + up, core + up[::-1])

    def place(self, mask):
        chip = flip(lax.axis_index("chip"), mask & (self.chips - 1))
        if not self.with_core:
            return (chip,)
        return (chip, flip(lax.axis_index("core"), mask >> self.chip_digits))

    def peer(self, digit):
        if digit < self.chip_digits:
            return {"chip": flip(lax.axis_index("chip"), 1 << digit)}
        return {"core": flip(lax.axis_index("core"), 1)}


def gather_kernel(cube, heads, in_ref, out_ref, local, line_send, line_recv, send, recv):
    hz = lax.axis_index("head")
    rows = in_ref.shape[0]
    half = rows // 2
    others = near(heads) if heads > 1 else []
    meet(
        [cube.peer(digit) for digit in range(cube.number)]
        + [{"head": (hz + d) % heads} for d in others]
    )

    def at(mask, d):
        index = cube.place(mask)
        return index + ((hz + heads - d) % heads,) if heads > 1 else index

    own = pltpu.make_async_copy(in_ref, out_ref.at[at(0, 0)], local)
    own.start()
    line = {}
    for d in others:
        line[d] = pltpu.make_async_remote_copy(
            src_ref=in_ref,
            dst_ref=out_ref.at[at(0, 0)],
            send_sem=line_send.at[d - 1],
            recv_sem=line_recv.at[d - 1],
            device_id={"head": (hz + d) % heads},
            device_id_type=MESH,
        )
        line[d].start()
    copies = {}

    def forward(side, mask, d):
        order = cube.gather_orders[side]
        last = max([k for k in range(cube.number) if (mask >> order[k]) & 1], default=-1)
        for k in range(last + 1, cube.number):
            later = mask | (1 << order[k])
            part = pl.ds(side * half, half)
            place = out_ref.at[at(mask, d) + (part,)]
            copy = pltpu.make_async_remote_copy(
                src_ref=in_ref.at[part] if mask == 0 and d == 0 else place,
                dst_ref=place,
                send_sem=send.at[side, later, d],
                recv_sem=recv.at[side, later, d],
                device_id=cube.peer(order[k]),
                device_id_type=MESH,
            )
            copy.start()
            copies[(side, later, d)] = copy

    for side in range(2):
        forward(side, 0, 0)
    for d in others:
        line[d].wait_recv()
        for side in range(2):
            forward(side, 0, d)
    for mask in sorted(range(1, 1 << cube.number), key=lambda m: bin(m).count("1")):
        for d in [0] + others:
            for side in range(2):
                copies[(side, mask, d)].wait_recv()
                forward(side, mask, d)
    own.wait()
    for copy in list(line.values()) + list(copies.values()):
        copy.wait_send()


def gather(value, chips, heads, with_core, number):
    rows, columns = value.shape
    cube = Cube(chips, with_core)
    lead = (chips,) + ((2,) if with_core else ()) + ((heads,) if heads > 1 else ())
    steps = max(heads - 1, 1)
    return pl.pallas_call(
        functools.partial(gather_kernel, cube, heads),
        out_shape=jax.ShapeDtypeStruct(lead + (rows, columns), value.dtype),
        in_specs=[ANY],
        out_specs=ANY,
        scratch_shapes=[
            DMA,
            DMA((steps,)),
            DMA((steps,)),
            DMA((2, 1 << cube.number, heads)),
            DMA((2, 1 << cube.number, heads)),
        ],
        compiler_params=pltpu.CompilerParams(collective_id=number, has_side_effects=True),
        name="gather",
    )(value)


def scatter_kernel(cube, heads, in_ref, out_ref, *refs):
    count = cube.number
    arrived, parts = refs[:count], refs[count : 2 * count - 1]
    line_out, line_in, line_send, line_recv, send, recv = refs[2 * count - 1 :]
    hz = lax.axis_index("head")
    half = in_ref.shape[-2] // 2
    others = near(heads) if heads > 1 else []
    order_of_lines = others[::-1] + [0]
    meet(
        [cube.peer(digit) for digit in range(count)] + [{"head": (hz + d) % heads} for d in others]
    )
    copies = {}

    def slot(side, k, mask):
        return subsets(cube.scatter_orders[side][k + 1 :]).index(mask)

    def mine(side, mask, d):
        index = cube.place(mask)
        if heads > 1:
            index = index + ((hz + d) % heads,)
        return in_ref.at[index + (pl.ds(side * half, half),)]

    def pass_on(side, k, mask, d, source):
        where = slot(side, k, mask)
        copy = pltpu.make_async_remote_copy(
            src_ref=source,
            dst_ref=arrived[k].at[side, where, d],
            send_sem=send.at[side, k, where, d],
            recv_sem=recv.at[side, k, where, d],
            device_id=cube.peer(cube.scatter_orders[side][k]),
            device_id_type=MESH,
        )
        copy.start()
        copies[(side, k, mask, d)] = copy

    def total(side, steps, mask, d):
        value = mine(side, mask, d)[...].astype(f32)
        for j in range(steps):
            copies[(side, j, mask, d)].wait_recv()
            value = value + arrived[j][side, slot(side, j, mask), d].astype(f32)
        return value

    for k in range(count):
        for d in order_of_lines:
            for side in range(2):
                order = cube.scatter_orders[side]
                for mask in subsets(order[k + 1 :])[::-1]:
                    full = mask | (1 << order[k])
                    if k == 0:
                        source = mine(side, full, d)
                    else:
                        source = parts[k - 1].at[side, slot(side, k, mask), d]
                        source[...] = total(side, k, full, d).astype(bf16)
                    pass_on(side, k, mask, d, source)
    line = {}
    for d in order_of_lines:
        for side in range(2):
            value = total(side, count, 0, d)
            if d:
                line_out[d - 1, pl.ds(side * half, half)] = value.astype(bf16)
            else:
                out_ref[pl.ds(side * half, half)] = value
        if d:
            line[d] = pltpu.make_async_remote_copy(
                src_ref=line_out.at[d - 1],
                dst_ref=line_in.at[d - 1],
                send_sem=line_send.at[d - 1],
                recv_sem=line_recv.at[d - 1],
                device_id={"head": (hz + d) % heads},
                device_id_type=MESH,
            )
            line[d].start()
    for d in others:
        line[d].wait_recv()
        out_ref[...] += line_in[d - 1].astype(f32)
    for copy in list(line.values()) + list(copies.values()):
        copy.wait_send()


def scatter_sum(value, chips, heads, with_core, number):
    rows, columns = value.shape[-2:]
    cube = Cube(chips, with_core)
    half = rows // 2
    steps = max(heads - 1, 1)
    line_rows = rows if heads > 1 else 16
    slots = [(1 << cube.number) >> (k + 1) for k in range(cube.number)]
    if 2 * value.size + 4 * heads * half * columns * (sum(slots) + sum(slots[1:])) > 40 << 20:
        names = ("chip", "core") if with_core else ("chip",)
        names = names + (("head",) if heads > 1 else ())
        flat = value.reshape(-1, columns)
        return lax.psum_scatter(flat, names, scatter_dimension=0, tiled=True).astype(f32)
    return pl.pallas_call(
        functools.partial(scatter_kernel, cube, heads),
        out_shape=jax.ShapeDtypeStruct((rows, columns), f32),
        in_specs=[WHOLE],
        out_specs=WHOLE,
        scratch_shapes=[pltpu.VMEM((2, s, heads, half, columns), bf16) for s in slots]
        + [pltpu.VMEM((2, s, heads, half, columns), bf16) for s in slots[1:]]
        + [
            pltpu.VMEM((steps, line_rows, columns), bf16),
            pltpu.VMEM((steps, line_rows, columns), bf16),
            DMA((steps,)),
            DMA((steps,)),
            DMA((2, cube.number, slots[0], heads)),
            DMA((2, cube.number, slots[0], heads)),
        ],
        compiler_params=pltpu.CompilerParams(
            collective_id=number, has_side_effects=True, vmem_limit_bytes=56 << 20
        ),
        name="scatter_sum",
    )(value)


def line_kernel(heads, same, in_ref, out_ref, local, send, recv):
    hz = lax.axis_index("head")
    others = near(heads)[::-1]
    meet([{"head": (hz + d) % heads} for d in others])

    def source(place):
        return in_ref if same else in_ref.at[place]

    own = pltpu.make_async_copy(source(hz), out_ref.at[hz], local)
    own.start()
    copies = []
    for d in others:
        place = (hz + d) % heads
        copy = pltpu.make_async_remote_copy(
            src_ref=source(place),
            dst_ref=out_ref.at[hz],
            send_sem=send.at[d - 1],
            recv_sem=recv.at[d - 1],
            device_id={"head": place},
            device_id_type=MESH,
        )
        copy.start()
        copies.append(copy)
    own.wait()
    for copy in copies:
        copy.wait()


def line_exchange(value, heads, number, same=False):
    return pl.pallas_call(
        functools.partial(line_kernel, heads, same),
        out_shape=jax.ShapeDtypeStruct((heads,) + value.shape if same else value.shape, value.dtype),
        in_specs=[ANY],
        out_specs=ANY,
        scratch_shapes=[DMA, DMA((heads - 1,)), DMA((heads - 1,))],
        compiler_params=pltpu.CompilerParams(collective_id=number, has_side_effects=True),
        name="line_exchange",
    )(value)


NT = (((1,), (1,)), ((), ()))


def experts_kernel(
    tile,
    hidden,
    x_ref,
    c_ref,
    gate_hbm,
    up_hbm,
    down_hbm,
    moe_ref,
    back_ref,
    d_gate_hbm,
    d_up_hbm,
    d_down_hbm,
    w_gate,
    w_up,
    w_down,
    d_gate_w,
    d_up_w,
    d_down_w,
    acts,
    back_gate,
    back_up,
    stage_wide,
    stage_down,
    load,
    store,
):
    step = pl.program_id(0)
    width, total = w_gate.shape

    @pl.when(step == 0)
    def _():
        loads = [
            pltpu.make_async_copy(gate_hbm, w_gate, load.at[0]),
            pltpu.make_async_copy(up_hbm, w_up, load.at[1]),
            pltpu.make_async_copy(down_hbm, w_down, load.at[2]),
        ]
        for copy in loads:
            copy.start()
        d_gate_w[...] = jnp.zeros_like(d_gate_w)
        d_up_w[...] = jnp.zeros_like(d_up_w)
        d_down_w[...] = jnp.zeros_like(d_down_w)
        for copy in loads:
            copy.wait()

    x = x_ref[:, :width]
    c = c_ref[...]
    routed = x_ref[:, width:]
    first_expert = lax.axis_index("head") * (total // hidden)
    d_gates = jnp.zeros((x.shape[0], LANES), f32)
    for begin in range(0, total, tile):
        js = pl.ds(begin, tile)
        column = begin + lax.broadcasted_iota(jnp.int32, (LANES, tile), 1)
        line = lax.broadcasted_iota(jnp.int32, (LANES, tile), 0)
        expert = first_expert + column // hidden
        here = (line == expert).astype(f32)
        both = (here + (line == expert + LOW).astype(f32)).astype(bf16)
        weight = jnp.dot(routed, both, preferred_element_type=f32)
        gate = jnp.dot(x, w_gate[:, js], preferred_element_type=f32)
        up = jnp.dot(x, w_up[:, js], preferred_element_type=f32)
        d_act = lax.dot_general(c, w_down[js, :], NT, preferred_element_type=f32)
        sigma = 1.0 / (1.0 + jnp.exp(-gate))
        silu = gate * sigma
        act = (silu * up).astype(bf16).astype(f32)
        d_gates = d_gates + lax.dot_general(
            (act * d_act).astype(bf16), here.astype(bf16), NT, preferred_element_type=f32
        )
        acts[:, js] = (act * weight).astype(bf16)
        d_act = d_act * weight
        back_up[:, js] = (d_act * silu).astype(bf16)
        back_gate[:, js] = (d_act * up * sigma * (1.0 + gate * (1.0 - sigma))).astype(bf16)
    back_ref[:, width:] = d_gates.astype(bf16)
    x_turned = x.T
    for begin in range(0, total, tile):
        js = pl.ds(begin, tile)
        d_gate_w[:, js] += jnp.dot(x_turned, back_gate[:, js], preferred_element_type=f32)
        d_up_w[:, js] += jnp.dot(x_turned, back_up[:, js], preferred_element_type=f32)
        d_down_w[js, :] += jnp.dot(acts[:, js].T, c, preferred_element_type=f32)
    for begin in range(0, width, 512):
        cs = pl.ds(begin, 512)
        moe_ref[:, cs] = jnp.dot(acts[...], w_down[:, cs], preferred_element_type=f32).astype(bf16)
        back_ref[:, cs] = (
            lax.dot_general(back_gate[...], w_gate[cs, :], NT, preferred_element_type=f32)
            + lax.dot_general(back_up[...], w_up[cs, :], NT, preferred_element_type=f32)
        ).astype(bf16)

    @pl.when(step == pl.num_programs(0) - 1)
    def _():
        rows = stage_wide.shape[1]
        jobs = [
            (source, target, stage, begin)
            for source, target, stage in (
                (d_gate_w, d_gate_hbm, stage_wide),
                (d_up_w, d_up_hbm, stage_wide),
                (d_down_w, d_down_hbm, stage_down),
            )
            for begin in range(0, source.shape[0], rows)
        ]
        flight = {}
        for index, (source, target, stage, begin) in enumerate(jobs):
            now = index % 2
            if now in flight:
                flight[now].wait()
            stage[now] = source[pl.ds(begin, rows), :].astype(bf16)
            flight[now] = pltpu.make_async_copy(
                stage.at[now], target.at[pl.ds(begin, rows), :], store.at[now]
            )
            flight[now].start()
        for copy in flight.values():
            copy.wait()


def experts(x, c, w_gate, w_up, w_down, hidden):
    tokens, columns = x.shape
    width, total = w_gate.shape
    block = min(256, tokens)
    tile = 256 if total % 256 == 0 else hidden
    return pl.pallas_call(
        functools.partial(experts_kernel, tile, hidden),
        grid=(tokens // block,),
        out_shape=(
            jax.ShapeDtypeStruct((tokens, width), bf16),
            jax.ShapeDtypeStruct((tokens, columns), bf16),
            jax.ShapeDtypeStruct((width, total), bf16),
            jax.ShapeDtypeStruct((width, total), bf16),
            jax.ShapeDtypeStruct((total, width), bf16),
        ),
        in_specs=[
            pl.BlockSpec((block, columns), lambda i: (i, 0)),
            pl.BlockSpec((block, width), lambda i: (i, 0)),
            ANY,
            ANY,
            ANY,
        ],
        out_specs=(
            pl.BlockSpec((block, width), lambda i: (i, 0)),
            pl.BlockSpec((block, columns), lambda i: (i, 0)),
            ANY,
            ANY,
            ANY,
        ),
        scratch_shapes=[
            pltpu.VMEM((width, total), bf16),
            pltpu.VMEM((width, total), bf16),
            pltpu.VMEM((total, width), bf16),
            pltpu.VMEM((width, total), f32),
            pltpu.VMEM((width, total), f32),
            pltpu.VMEM((total, width), f32),
            pltpu.VMEM((block, total), bf16),
            pltpu.VMEM((block, total), bf16),
            pltpu.VMEM((block, total), bf16),
            pltpu.VMEM((2, 64, total), bf16),
            pltpu.VMEM((2, 64, width), bf16),
            DMA((3,)),
            DMA((2,)),
        ],
        compiler_params=pltpu.CompilerParams(vmem_limit_bytes=60 << 20),
        name="experts",
    )(x, c, w_gate, w_up, w_down)


def turn_kernel(cube, heads, hidden, *refs):
    chips, count = cube.chips, cube.number
    own_ref, c_hbm, down_hbm = refs[:3]
    pieces, refs = refs[3 : 3 + chips], (None,) * 4 + refs[3 + chips :]
    out_ref, moe_hbm, keep_up_hbm, other_up_hbm, keep_down_hbm, other_down_hbm = refs[4:10]
    tokens, turned, cots, w_up, w_down, acts, backs, d_gates, moe_stage, line_in = refs[10:20]
    arrived = refs[20 : 20 + count]
    load, store, own_sem, line_send, line_recv, send, recv, back_send, back_recv = refs[
        20 + count : 29 + count
    ]
    end_send, end_recv, twin_send, twin_recv, load_send, load_recv = refs[29 + count :]
    hz = lax.axis_index("head")
    rows, columns = own_ref.shape
    experts_here, width, _ = w_up.shape
    total = experts_here * hidden
    half = rows // 2
    line = heads * rows
    others = near(heads)
    masks = sorted(range(chips), key=lambda m: bin(m).count("1"))

    core = lax.axis_index("core")
    twin = {"core": 1 - core}
    slices = 2 * chips
    slice_rows = width // slices

    def up_rows(ref, chip, which):
        return ref.at[:, pl.ds((chip * 2 + which) * slice_rows, slice_rows), :]

    def w_down_parts(which):
        return w_down.reshape(experts_here, 2, hidden // 2, width).at[:, which]

    homes = [
        (pieces[mask], up_rows(w_up, flip(lax.axis_index("chip"), mask), core))
        for mask in range(chips)
    ] + [(down_hbm, w_down_parts(core))]
    loads = [
        pltpu.make_async_copy(source, target, load.at[index])
        for index, (source, target) in enumerate([(c_hbm, cots)] + homes)
    ]
    shared = [
        pltpu.make_async_remote_copy(
            src_ref=source,
            dst_ref=target,
            send_sem=load_send.at[index],
            recv_sem=load_recv.at[index],
            device_id=twin,
            device_id_type=MESH,
        )
        for index, (source, target) in enumerate(homes)
    ]
    for copy in loads:
        copy.start()
    meet(
        [cube.peer(digit) for digit in range(count)]
        + [{"head": (hz + d) % heads} for d in others]
        + [twin]
    )

    def part(side):
        return pl.ds(side * half, half)

    middle = jnp.minimum(hz, heads - 1 - hz)

    def source(rank):
        if rank == 0:
            return hz
        far = (rank + 1) // 2
        near_one = hz - far if rank % 2 else hz + far
        far_one = jnp.where(
            hz < heads - 1 - hz, hz + (rank - middle), hz - (rank - middle)
        )
        return jnp.where(rank <= 2 * middle, near_one, far_one)

    def line_copy(rank, step):
        head = source(rank)
        place = tokens.at[cube.place(0) + (head,)]
        return pltpu.make_async_remote_copy(
            src_ref=own_ref if rank == 0 else place,
            dst_ref=place,
            send_sem=line_send.at[heads if rank == 0 and step < 0 else head],
            recv_sem=line_recv.at[head],
            device_id={"head": (hz + step + heads) % heads},
            device_id_type=MESH,
        )

    def along(rank, act):
        head = source(rank)
        goes_up = hz + 1 < heads
        goes_down = hz > 0
        if rank:
            goes_up = goes_up & (head < hz)
            goes_down = goes_down & (head > hz)

        @pl.when(goes_up)
        def _():
            act(line_copy(rank, 1))

        @pl.when(goes_down)
        def _():
            act(line_copy(rank, -1))

    def plane_copy(side, mask, k, rank):
        digit = cube.gather_orders[side][k]
        later = mask | (1 << digit)
        head = source(rank)
        place = tokens.at[cube.place(mask) + (head, part(side))]
        return pltpu.make_async_remote_copy(
            src_ref=own_ref.at[part(side)] if mask == 0 and rank == 0 else place,
            dst_ref=place,
            send_sem=send.at[side, later, head],
            recv_sem=recv.at[side, later, head],
            device_id=cube.peer(digit),
            device_id_type=MESH,
        )

    def steps_after(side, mask):
        order = cube.gather_orders[side]
        last = max([k for k in range(count) if (mask >> order[k]) & 1], default=-1)
        return range(last + 1, count)

    def arrival(side, mask, rank):
        order = cube.gather_orders[side]
        k = max(k for k in range(count) if (mask >> order[k]) & 1)
        return plane_copy(side, mask & ~(1 << order[k]), k, rank)

    def receive(mask, rank):
        if mask == 0:
            if rank:
                line_copy(rank, 1).wait_recv()
            along(rank, lambda copy: copy.start())
        for side in range(2):
            if mask:
                arrival(side, mask, rank).wait_recv()
            for k in steps_after(side, mask):
                plane_copy(side, mask, k, rank).start()

    levels = [
        [m for m in masks if bin(m).count("1") == level] for level in range(cube.number + 1)
    ]
    waits = {0: [], 1: []}
    early = max(heads - 2, 0)
    for rank in range(heads):
        waits[0].append((0, rank))
        if 0 < rank <= early and count > 0:
            waits[0] += [(m, rank - 1) for m in levels[1]]
    waits[1] = [(m, rank) for rank in range(early, heads) for m in levels[1]]
    for level in range(2, count + 1):
        waits[level] = [(m, rank) for m in levels[level] for rank in range(heads)]

    def sent(mask):
        for rank in range(heads):
            if mask == 0:
                along(rank, lambda copy: copy.wait_send())
            for side in range(2):
                for k in steps_after(side, mask):
                    plane_copy(side, mask, k, rank).wait_send()

    def slot(side, k, mask):
        return subsets(cube.scatter_orders[side][k + 1 :]).index(mask)

    def back_place(side, mask, d):
        return tokens.at[cube.place(mask) + ((hz + d) % heads, part(side))]

    def back_copy(side, k, mask, d):
        order = cube.scatter_orders[side]
        where = slot(side, k, mask)
        return pltpu.make_async_remote_copy(
            src_ref=back_place(side, mask | (1 << order[k]), d),
            dst_ref=arrived[k].at[side, where, d],
            send_sem=back_send.at[side, k, where, d],
            recv_sem=back_recv.at[side, k, where, d],
            device_id=cube.peer(order[k]),
            device_id_type=MESH,
        )

    def end_copy(d):
        return pltpu.make_async_remote_copy(
            src_ref=tokens.at[cube.place(0) + ((hz + d) % heads,)],
            dst_ref=line_in.at[d - 1],
            send_sem=end_send.at[d - 1],
            recv_sem=end_recv.at[d - 1],
            device_id={"head": (hz + d) % heads},
            device_id_type=MESH,
        )

    outward = others[::-1] + [0]

    def give(mask, d):
        for side in range(2):
            first = 1 << cube.scatter_orders[side][0]
            if mask & first:
                back_copy(side, 0, mask & ~first, d).start()

    own = pltpu.make_async_copy(own_ref, tokens.at[cube.place(0) + (hz,)], own_sem)
    own.start()
    for copy in shared:
        copy.start()

    first_expert = hz * experts_here
    span = min(512, width)
    group = 2 if experts_here % 2 == 0 else 1
    tile = group * hidden

    def compute(place):
        here = pl.ds(place * line, line)
        x = tokens[place, :, :, pl.ds(0, width)].reshape(line, width)
        c = cots[here, :]
        routed = tokens[place, :, :, pl.ds(width, LANES)].reshape(line, LANES)
        turned[:, here] = x.T
        d_gates[...] = jnp.zeros_like(d_gates)

        @pl.loop(0, total // tile)
        def _(j):
            js = pl.ds(pl.multiple_of(j * tile, tile), tile)
            column = j * tile + lax.broadcasted_iota(jnp.int32, (LANES, tile), 1)
            lane = lax.broadcasted_iota(jnp.int32, (LANES, tile), 0)
            expert = first_expert + column // hidden
            high = (lane == expert).astype(f32)
            both = (high + (lane == expert + LOW).astype(f32)).astype(bf16)
            weight = jnp.dot(routed, both, preferred_element_type=f32)
            both_parts = [
                jnp.dot(x, w_up[j * group + i], preferred_element_type=f32) for i in range(group)
            ]
            gate = jnp.concatenate([value[:, :hidden] for value in both_parts], axis=1)
            up = jnp.concatenate([value[:, hidden:] for value in both_parts], axis=1)
            d_act = lax.dot_general(c, w_down[js, :], NT, preferred_element_type=f32)
            sigma = 1.0 / (1.0 + jnp.exp(-gate))
            silu = gate * sigma
            act = (silu * up).astype(bf16).astype(f32)
            d_gates[...] += lax.dot_general(
                (act * d_act).astype(bf16), high.astype(bf16), NT, preferred_element_type=f32
            )
            acts[here, js] = (act * weight).astype(bf16)
            d_act = d_act * weight
            d_up = (d_act * silu).astype(bf16)
            d_gate = (d_act * up * sigma * (1.0 + gate * (1.0 - sigma))).astype(bf16)
            for i in range(group):
                one = slice(i * hidden, (i + 1) * hidden)
                backs[j * group + i, here, pl.ds(0, hidden)] = d_gate[:, one]
                backs[j * group + i, here, pl.ds(hidden, hidden)] = d_up[:, one]

    def results(place, step):
        here = pl.ds(place * line, line)

        @pl.loop(0, width // span)
        def _(j):
            cs = pl.ds(pl.multiple_of(j * span, span), span)
            value = sum(
                lax.dot_general(
                    backs[e, here, :], w_up[e, cs, :], NT, preferred_element_type=f32
                )
                for e in range(experts_here)
            )
            tokens[place, :, :, cs] = value.astype(bf16).reshape(heads, rows, span)

        tokens[place, :, :, pl.ds(width, LANES)] = (
            d_gates[...].astype(bf16).reshape(heads, rows, LANES)
        )

    def moe_copy(place):
        return pltpu.make_async_copy(
            moe_stage, moe_hbm.at[pl.ds(place * line, line)], store.at[chips + 1]
        )

    def mixed(place, step):
        here = pl.ds(place * line, line)

        @pl.when(step > 0)
        def _():
            moe_copy(place).wait()

        @pl.loop(0, width // span)
        def _(j):
            cs = pl.ds(pl.multiple_of(j * span, span), span)
            moe_stage[:, cs] = jnp.dot(
                acts[here, :], w_down[:, cs], preferred_element_type=f32
            ).astype(bf16)

        moe_copy(place).start()

    @pl.loop(0, chips)
    def _(step):
        seen = -1
        for index, mask in enumerate(masks):
            level = bin(mask).count("1")
            if level > seen:
                seen = level

                @pl.when(step == index)
                def _():
                    for event in waits[level]:
                        receive(*event)

        place = cube.place(0)[0] * 0
        for index, mask in enumerate(masks):
            place = jnp.where(step == index, cube.place(mask)[0], place)

        @pl.when(step == 0)
        def _():
            own.wait()
            for copy in loads + shared:
                copy.wait()

        compute(place)
        for index, mask in enumerate(masks):

            @pl.when(step == index)
            def _():
                sent(mask)

        results(place, step)
        for index, mask in enumerate(masks):
            if mask and mask != chips - 1:

                @pl.when(step == index)
                def _():
                    for d in outward:
                        give(mask, d)

    def sums(side, steps, mask, d):
        value = back_place(side, mask, d)[...].astype(f32)
        for j in range(steps):
            back_copy(side, j, mask, d).wait_recv()
            value = value + arrived[j][side, slot(side, j, mask), d].astype(f32)
        return value

    def keep_up(chip):
        return pltpu.make_async_copy(up_rows(w_up, chip, core), keep_up_hbm.at[chip], store.at[chip])

    def give_up(chip):
        return pltpu.make_async_remote_copy(
            src_ref=up_rows(w_up, chip, 1 - core),
            dst_ref=other_up_hbm.at[chip],
            send_sem=twin_send.at[chip],
            recv_sem=twin_recv.at[chip],
            device_id=twin,
            device_id_type=MESH,
        )

    def keep_down():
        return pltpu.make_async_copy(w_down_parts(core), keep_down_hbm, store.at[chips])

    def give_down():
        return pltpu.make_async_remote_copy(
            src_ref=w_down_parts(1 - core),
            dst_ref=other_down_hbm,
            send_sem=twin_send.at[chips],
            recv_sem=twin_recv.at[chips],
            device_id=twin,
            device_id_type=MESH,
        )

    def up_grad(begin, end):
        @pl.loop(begin, end)
        def _(e):
            w_up[e] = jnp.dot(turned[...], backs[e], preferred_element_type=f32).astype(bf16)

        if end == experts_here:
            for chip in range(chips):
                give_up(chip).start()
                keep_up(chip).start()

    def down_grad():
        @pl.loop(0, total // tile)
        def _(j):
            js = pl.ds(pl.multiple_of(j * tile, tile), tile)
            value = jnp.dot(acts[:, js].T, cots[...], preferred_element_type=f32)
            w_down[js, :] = value.astype(bf16)

        give_down().start()
        keep_down().start()

    def mix(begin, end):
        @pl.loop(begin, end)
        def _(index):
            mixed(index, index)

    cuts = [experts_here * i // 4 for i in range(5)]
    work = [
        lambda: mix(0, chips // 2),
        lambda: mix(chips // 2, chips),
        lambda: up_grad(cuts[0], cuts[1]),
        lambda: up_grad(cuts[1], cuts[2]),
        lambda: up_grad(cuts[2], cuts[3]),
        lambda: up_grad(cuts[3], cuts[4]),
        down_grad,
    ]
    turns = heads + count
    for turn in range(turns):
        if turn < heads:
            give(chips - 1, outward[turn])
        for piece in work[len(work) * turn // turns : len(work) * (turn + 1) // turns]:
            piece()
        for k in range(1, count):
            if 0 <= turn - k < heads:
                d = outward[turn - k]
                for side in range(2):
                    order = cube.scatter_orders[side]
                    for mask in subsets(order[k + 1 :])[::-1]:
                        full = mask | (1 << order[k])
                        back_place(side, full, d)[...] = sums(side, k, full, d).astype(bf16)
                        back_copy(side, k, mask, d).start()
        if 0 <= turn - count < heads:
            d = outward[turn - count]
            for side in range(2):
                value = sums(side, count, 0, d)
                if d:
                    back_place(side, 0, d)[...] = value.astype(bf16)
                else:
                    out_ref[part(side)] = value
            if d:
                end_copy(d).start()
    for d in others:
        end_copy(d).wait_recv()
        out_ref[...] += line_in[d - 1].astype(f32)
    for d in others:
        end_copy(d).wait_send()
    for side in range(2):
        for k in range(count):
            for mask in subsets(cube.scatter_orders[side][k + 1 :]):
                for d in outward:
                    back_copy(side, k, mask, d).wait_send()
    moe_copy(0).wait()
    for chip in range(chips):
        give_up(chip).wait()
        keep_up(chip).wait()
    give_down().wait()
    keep_down().wait()


def expert_turn(payload, c, pieces, w_down, heads, number):
    rows, columns = payload.shape
    chips, width = len(pieces), c.shape[1]
    experts_here, _, double = pieces[0].shape
    hidden = double // 2
    total = experts_here * hidden
    cube = Cube(chips, False)
    count = cube.number
    tokens = chips * heads * rows
    half = rows // 2
    slots = [chips >> (k + 1) for k in range(count)]
    share = jax.ShapeDtypeStruct((chips, experts_here, width // (2 * chips), double), bf16)
    down_share = jax.ShapeDtypeStruct((experts_here, hidden // 2, width), bf16)
    return pl.pallas_call(
        functools.partial(turn_kernel, cube, heads, hidden),
        out_shape=(
            jax.ShapeDtypeStruct((rows, columns), f32),
            jax.ShapeDtypeStruct((tokens, width), bf16),
            share,
            share,
            down_share,
            down_share,
        ),
        in_specs=[WHOLE] + [ANY] * (2 + chips),
        out_specs=(WHOLE, ANY, ANY, ANY, ANY, ANY),
        scratch_shapes=[
            pltpu.VMEM((chips, heads, rows, columns), bf16),
            pltpu.VMEM((width, tokens), bf16),
            pltpu.VMEM((tokens, width), bf16),
            pltpu.VMEM((experts_here, width, double), bf16),
            pltpu.VMEM((total, width), bf16),
            pltpu.VMEM((tokens, total), bf16),
            pltpu.VMEM((experts_here, tokens, double), bf16),
            pltpu.VMEM((heads * rows, LANES), f32),
            pltpu.VMEM((heads * rows, width), bf16),
            pltpu.VMEM((heads - 1, rows, columns), bf16),
        ]
        + [pltpu.VMEM((2, s, heads, half, columns), bf16) for s in slots]
        + [
            DMA((chips + 2,)),
            DMA((chips + 2,)),
            DMA,
            DMA((heads + 1,)),
            DMA((heads,)),
            DMA((2, chips, heads)),
            DMA((2, chips, heads)),
            DMA((2, count, slots[0], heads)),
            DMA((2, count, slots[0], heads)),
            DMA((heads - 1,)),
            DMA((heads - 1,)),
            DMA((chips + 1,)),
            DMA((chips + 1,)),
            DMA((chips + 1,)),
            DMA((chips + 1,)),
        ],
        compiler_params=pltpu.CompilerParams(
            collective_id=number, has_side_effects=True, vmem_limit_bytes=63 << 20
        ),
        name="expert_turn",
    )(payload, c, w_down, *pieces)


def start_kernel(cube, heads, *refs):
    x_ref, slice_ref, unit_ref, column_ref, row_ref, x_out, dense_out, unit_out, slot_out = refs[:9]
    local, x_send, x_recv, line_send, line_recv, send, recv, unit_send, unit_recv = refs[9:]
    chips = cube.chips
    chip, core, hz = lax.axis_index("chip"), lax.axis_index("core"), lax.axis_index("head")
    others = near(heads)
    part_heads = heads // 2
    across_all = {"chip": flip(chip, chips - 1)}
    meet(
        [cube.peer(digit) for digit in range(cube.number)]
        + [{"head": (hz + d) % heads} for d in others]
        + [across_all]
    )
    unit_copy = pltpu.make_async_remote_copy(
        src_ref=unit_ref,
        dst_ref=unit_out,
        send_sem=unit_send,
        recv_sem=unit_recv,
        device_id=across_all,
        device_id_type=MESH,
    )
    middle = jnp.minimum(hz, heads - 1 - hz)

    def source(rank):
        if rank == 0:
            return hz
        far = (rank + 1) // 2
        near_one = hz - far if rank % 2 else hz + far
        far_one = jnp.where(hz < heads - 1 - hz, hz + (rank - middle), hz - (rank - middle))
        return jnp.where(rank <= 2 * middle, near_one, far_one)

    def x_copy(rank, step):
        head = source(rank)
        return pltpu.make_async_remote_copy(
            src_ref=x_ref if rank == 0 else x_out.at[:, head],
            dst_ref=x_out.at[:, head],
            send_sem=x_send.at[heads if rank == 0 and step < 0 else head],
            recv_sem=x_recv.at[head],
            device_id={"head": (hz + step + heads) % heads},
            device_id_type=MESH,
        )

    def along(rank, act):
        head = source(rank)
        goes_up = hz + 1 < heads
        goes_down = hz > 0
        if rank:
            goes_up = goes_up & (head < hz)
            goes_down = goes_down & (head > hz)

        @pl.when(goes_up)
        def _():
            act(x_copy(rank, 1))

        @pl.when(goes_down)
        def _():
            act(x_copy(rank, -1))

    def slice_copy(d):
        place = (hz + d) % heads
        return pltpu.make_async_remote_copy(
            src_ref=slice_ref.at[place],
            dst_ref=dense_out.at[chip, core, hz],
            send_sem=line_send.at[d - 1],
            recv_sem=line_recv.at[d - 1],
            device_id={"head": place},
            device_id_type=MESH,
        )

    def dense_copy(side, mask, k):
        order = cube.gather_orders[side]
        later = mask | (1 << order[k])
        place = dense_out.at[cube.place(mask) + (pl.ds(side * part_heads, part_heads),)]
        return pltpu.make_async_remote_copy(
            src_ref=place,
            dst_ref=place,
            send_sem=send.at[side, later],
            recv_sem=recv.at[side, later],
            device_id=cube.peer(order[k]),
            device_id_type=MESH,
        )

    def steps_after(side, mask):
        order = cube.gather_orders[side]
        last = max([k for k in range(cube.number) if (mask >> order[k]) & 1], default=-1)
        return range(last + 1, cube.number)

    def dense_turn(mask):
        for side in range(2):
            if mask:
                order = cube.gather_orders[side]
                k = max(k for k in range(cube.number) if (mask >> order[k]) & 1)
                dense_copy(side, mask & ~(1 << order[k]), k).wait_recv()
            for k in steps_after(side, mask):
                dense_copy(side, mask, k).start()

    locals_ = [
        pltpu.make_async_copy(slice_ref.at[hz], dense_out.at[chip, core, hz], local.at[0]),
        pltpu.make_async_copy(x_ref, x_out.at[:, hz], local.at[1]),
    ]
    def count_slots():
        row = row_ref[...]
        first = row // column_ref.shape[0] * column_ref.shape[0]
        total = jnp.zeros(row.shape, jnp.int32)
        step = LANES
        for begin in range(0, column_ref.shape[0], step):
            column = column_ref[pl.ds(begin, step), :]
            earlier = ((column < row) & (column >= first)).astype(jnp.int32)
            total = total + jnp.sum(earlier, axis=0, keepdims=True)
        slot_out[...] = total

    for d in others:
        slice_copy(d).start()
    for copy in locals_:
        copy.start()
    along(0, lambda copy: copy.start())
    locals_[0].wait()
    for d in others:
        slice_copy(d).wait_recv()
    dense_turn(0)
    masks = sorted(range(1, 2 * chips), key=lambda m: bin(m).count("1"))
    shares = [masks[len(masks) * i // heads : len(masks) * (i + 1) // heads] for i in range(heads)]
    for mask in shares[0]:
        dense_turn(mask)
    for rank in range(1, heads):
        x_copy(rank, 1).wait_recv()
        along(rank, lambda copy: copy.start())
        for mask in shares[rank]:
            dense_turn(mask)
        if rank == 1:
            unit_copy.start()
            count_slots()
    unit_copy.wait()
    locals_[1].wait()
    for rank in range(heads):
        along(rank, lambda copy: copy.wait_send())
    for d in others:
        slice_copy(d).wait_send()
    for mask in [0] + masks:
        for side in range(2):
            for k in steps_after(side, mask):
                dense_copy(side, mask, k).wait_send()


def start(x, slices, unit, keys, chips, heads, number):
    cube = Cube(chips, True)
    return pl.pallas_call(
        functools.partial(start_kernel, cube, heads),
        out_shape=(
            jax.ShapeDtypeStruct((x.shape[0], heads) + x.shape[1:], bf16),
            jax.ShapeDtypeStruct((chips, 2) + slices.shape, bf16),
            jax.ShapeDtypeStruct(unit.shape, bf16),
            jax.ShapeDtypeStruct((1, keys.size), jnp.int32),
        ),
        in_specs=[ANY] * 3 + [WHOLE] * 2,
        out_specs=(ANY,) * 3 + (WHOLE,),
        scratch_shapes=[
            DMA((2,)),
            DMA((heads + 1,)),
            DMA((heads,)),
            DMA((heads - 1,)),
            DMA((heads - 1,)),
            DMA((2, 2 * chips)),
            DMA((2, 2 * chips)),
            DMA,
            DMA,
        ],
        compiler_params=pltpu.CompilerParams(collective_id=number, has_side_effects=True),
        name="start",
    )(x, slices, unit, keys[:, None], keys[None, :])


def end_kernel(cube, heads, first_ref, left_ref, right_ref, extra_ref, first_out, out_ref, *refs):
    count = cube.number
    in_ref, refs = refs[0], refs[1:]
    arrived = refs[:count]
    parts = refs[count : 2 * count]
    local, first_send, first_recv, line_send, line_recv, send, recv = refs[2 * count :]
    hz = lax.axis_index("head")
    others = near(heads)[::-1]
    half = in_ref.shape[-2] // 2
    rows = in_ref.shape[-2] // heads
    meet([cube.peer(digit) for digit in range(count)] + [{"head": (hz + d) % heads} for d in others])
    own = pltpu.make_async_copy(first_ref.at[:, hz], first_out.at[hz], local)
    own.start()
    copies = {}

    def slot(side, k, mask):
        return subsets(cube.scatter_orders[side][k + 1 :]).index(mask)

    def mine(side, mask):
        return in_ref.at[cube.place(mask) + (pl.ds(side * half, half),)]

    def total(side, steps, mask):
        value = mine(side, mask)[...].astype(f32)
        for j in range(steps):
            copies[(side, j, mask)].wait_recv()
            value = value + arrived[j][side, slot(side, j, mask)].astype(f32)
        return value.astype(bf16)

    def first_copy(d):
        place = (hz + d) % heads
        return pltpu.make_async_remote_copy(
            src_ref=first_ref.at[:, place],
            dst_ref=first_out.at[hz],
            send_sem=first_send.at[d - 1],
            recv_sem=first_recv.at[d - 1],
            device_id={"head": place},
            device_id_type=MESH,
        )

    for d in others:
        first_copy(d).start()
    strip = extra_ref.shape[0] // cube.chips
    product = right_ref.shape[1]
    for chip in range(cube.chips):
        rows_here = pl.ds(chip * strip, strip)
        value = lax.dot_general(
            left_ref[:, rows_here], right_ref[...], TN, preferred_element_type=f32
        )
        in_ref[chip, :, :, pl.ds(0, product)] = value.astype(bf16).reshape(2, strip // 2, product)
        in_ref[chip, :, :, pl.ds(product, LANES)] = extra_ref[rows_here, :].reshape(
            2, strip // 2, LANES
        )
    for k in range(count):
        for side in range(2):
            order = cube.scatter_orders[side]
            for mask in subsets(order[k + 1 :])[::-1]:
                full = mask | (1 << order[k])
                where = slot(side, k, mask)
                if k == 0:
                    piece = mine(side, full)
                else:
                    piece = parts[k - 1].at[side, where]
                    piece[...] = total(side, k, full)
                copies[(side, k, mask)] = pltpu.make_async_remote_copy(
                    src_ref=piece,
                    dst_ref=arrived[k].at[side, where],
                    send_sem=send.at[side, k, where],
                    recv_sem=recv.at[side, k, where],
                    device_id=cube.peer(order[k]),
                    device_id_type=MESH,
                )
                copies[(side, k, mask)].start()
    done = parts[count - 1]
    for side in range(2):
        done[0, pl.ds(side * half, half)] = total(side, count, 0)

    def line_copy(d):
        place = (hz + d) % heads
        return pltpu.make_async_remote_copy(
            src_ref=done.at[0, pl.ds(pl.multiple_of(place * rows, 16), rows)],
            dst_ref=out_ref.at[hz],
            send_sem=line_send.at[d - 1],
            recv_sem=line_recv.at[d - 1],
            device_id={"head": place},
            device_id_type=MESH,
        )

    for d in others:
        line_copy(d).start()
    out_ref[hz] = done[0, pl.ds(pl.multiple_of(hz * rows, 16), rows)]
    for copy in copies.values():
        copy.wait_send()
    own.wait()
    for d in others:
        line_copy(d).wait()
    for d in others:
        first_copy(d).wait()


def end(first, left, right, extra, chips, heads, number):
    rows, columns = extra.shape[0] // (2 * chips), right.shape[1] + LANES
    cube = Cube(chips, True)
    count = cube.number
    half = rows // 2
    slots = [(1 << count) >> (k + 1) for k in range(count)]
    return pl.pallas_call(
        functools.partial(end_kernel, cube, heads),
        out_shape=(
            jax.ShapeDtypeStruct((heads, first.shape[0]) + first.shape[2:], bf16),
            jax.ShapeDtypeStruct((heads, rows // heads, columns), bf16),
        ),
        in_specs=[ANY] + [WHOLE] * 3,
        out_specs=(ANY, WHOLE),
        scratch_shapes=[pltpu.VMEM((chips, 2, rows, columns), bf16)]
        + [pltpu.VMEM((2, s, half, columns), bf16) for s in slots]
        + [pltpu.VMEM((2, s, half, columns), bf16) for s in slots[1:]]
        + [
            pltpu.VMEM((1, rows, columns), bf16),
            DMA,
            DMA((heads - 1,)),
            DMA((heads - 1,)),
            DMA((heads - 1,)),
            DMA((heads - 1,)),
            DMA((2, count, slots[0])),
            DMA((2, count, slots[0])),
        ],
        compiler_params=pltpu.CompilerParams(
            collective_id=number, has_side_effects=True, vmem_limit_bytes=40 << 20
        ),
        cost_estimate=pl.CostEstimate(
            flops=2000000000, bytes_accessed=1_000_000, transcendentals=0
        ),
        name="end",
    )(first, left, right, extra)


def place_kernel(chips, hidden, *refs):
    pieces, out_ref = refs[:chips], refs[chips]
    chip = lax.axis_index("chip")
    units = out_ref.shape[2] // 2
    for mask in range(chips):
        for part in range(2):
            begin = pl.multiple_of(part * units + flip(chip, mask) * hidden, hidden)
            out_ref[:, :, pl.ds(begin, hidden)] = pieces[mask][
                :, :, pl.ds(part * hidden, hidden)
            ].astype(f32)


def place_units(pieces, hidden):
    chips = len(pieces)
    experts_here, rows, double = pieces[0].shape
    group = 2 if experts_here % 2 == 0 else 1
    return pl.pallas_call(
        functools.partial(place_kernel, chips, hidden),
        grid=(experts_here // group,),
        out_shape=jax.ShapeDtypeStruct((experts_here, rows, chips * double), f32),
        in_specs=[pl.BlockSpec((group, rows, double), lambda e: (e, 0, 0))] * chips,
        out_specs=pl.BlockSpec((group, rows, chips * double), lambda e: (e, 0, 0)),
        name="place_units",
    )(*pieces)


def across(value, chips, mask):
    if mask == 0:
        return value
    return lax.ppermute(value, "chip", [(i, i ^ mask) for i in range(chips)])


class LineGather:
    def __init__(self, cube, heads, own, out, sems):
        self.cube, self.heads, self.own, self.out = cube, heads, own, out
        self.local, self.line_send, self.line_recv, self.send, self.recv = sems
        self.hz = lax.axis_index("head")
        self.middle = jnp.minimum(self.hz, heads - 1 - self.hz)
        self.rows = own.shape[0]

    @staticmethod
    def scratch(cube, heads):
        return [
            DMA,
            DMA((heads + 1,)),
            DMA((heads,)),
            DMA((2, 1 << cube.number, heads)),
            DMA((2, 1 << cube.number, heads)),
        ]

    def source(self, rank):
        hz, heads, middle = self.hz, self.heads, self.middle
        if rank == 0:
            return hz
        far = (rank + 1) // 2
        near_one = hz - far if rank % 2 else hz + far
        far_one = jnp.where(hz < heads - 1 - hz, hz + (rank - middle), hz - (rank - middle))
        return jnp.where(rank <= 2 * middle, near_one, far_one)

    def line_copy(self, rank, step):
        head = self.source(rank)
        place = self.out.at[self.cube.place(0) + (head,)]
        return pltpu.make_async_remote_copy(
            src_ref=self.own if rank == 0 else place,
            dst_ref=place,
            send_sem=self.line_send.at[self.heads if rank == 0 and step < 0 else head],
            recv_sem=self.line_recv.at[head],
            device_id={"head": (self.hz + step + self.heads) % self.heads},
            device_id_type=MESH,
        )

    def along(self, rank, act):
        head = self.source(rank)
        goes_up = self.hz + 1 < self.heads
        goes_down = self.hz > 0
        if rank:
            goes_up = goes_up & (head < self.hz)
            goes_down = goes_down & (head > self.hz)

        @pl.when(goes_up)
        def _():
            act(self.line_copy(rank, 1))

        @pl.when(goes_down)
        def _():
            act(self.line_copy(rank, -1))

    def plane_copy(self, side, mask, k, rank):
        digit = self.cube.gather_orders[side][k]
        later = mask | (1 << digit)
        head = self.source(rank)
        part = part_of(self.rows, side)
        place = self.out.at[self.cube.place(mask) + (head, part)]
        return pltpu.make_async_remote_copy(
            src_ref=self.own.at[part] if mask == 0 and rank == 0 else place,
            dst_ref=place,
            send_sem=self.send.at[side, later, head],
            recv_sem=self.recv.at[side, later, head],
            device_id=self.cube.peer(digit),
            device_id_type=MESH,
        )

    def steps_after(self, side, mask):
        order = self.cube.gather_orders[side]
        last = max([k for k in range(self.cube.number) if (mask >> order[k]) & 1], default=-1)
        return range(last + 1, self.cube.number)

    def begin(self):
        self.own_copy = pltpu.make_async_copy(
            self.own, self.out.at[self.cube.place(0) + (self.hz,)], self.local
        )
        self.own_copy.start()

    def receive(self, mask, rank):
        if mask == 0:
            if rank:
                self.line_copy(rank, 1).wait_recv()
            self.along(rank, lambda copy: copy.start())
        for side in range(2):
            if mask:
                order = self.cube.gather_orders[side]
                k = max(k for k in range(self.cube.number) if (mask >> order[k]) & 1)
                self.plane_copy(side, mask & ~(1 << order[k]), k, rank).wait_recv()
            for k in self.steps_after(side, mask):
                self.plane_copy(side, mask, k, rank).start()

    def events(self):
        masks = sorted(range(1 << self.cube.number), key=lambda m: bin(m).count("1"))
        return [(mask, rank) for mask in masks for rank in range(self.heads)]

    def finish(self):
        self.own_copy.wait()
        for mask, rank in self.events():
            if mask == 0:
                self.along(rank, lambda copy: copy.wait_send())
            for side in range(2):
                for k in self.steps_after(side, mask):
                    self.plane_copy(side, mask, k, rank).wait_send()


class DenseGather:
    def __init__(self, cube, heads, own, out, sems):
        self.cube, self.heads, self.own, self.out = cube, heads, own, out
        self.local, self.line_send, self.line_recv, self.send, self.recv = sems
        self.hz = lax.axis_index("head")

    @staticmethod
    def scratch(cube, heads):
        return [
            DMA,
            DMA((heads - 1,)),
            DMA((heads - 1,)),
            DMA((2, 1 << cube.number)),
            DMA((2, 1 << cube.number)),
        ]

    def line_copy(self, d):
        return pltpu.make_async_remote_copy(
            src_ref=self.own,
            dst_ref=self.out.at[self.cube.place(0) + (self.hz,)],
            send_sem=self.line_send.at[d - 1],
            recv_sem=self.line_recv.at[d - 1],
            device_id={"head": (self.hz + d) % self.heads},
            device_id_type=MESH,
        )

    def flat_copy(self, side, mask, k):
        digit = self.cube.gather_orders[side][k]
        later = mask | (1 << digit)
        part = self.heads // 2
        place = self.out.at[self.cube.place(mask) + (pl.ds(side * part, part),)]
        return pltpu.make_async_remote_copy(
            src_ref=place,
            dst_ref=place,
            send_sem=self.send.at[side, later],
            recv_sem=self.recv.at[side, later],
            device_id=self.cube.peer(digit),
            device_id_type=MESH,
        )

    def steps_after(self, side, mask):
        order = self.cube.gather_orders[side]
        last = max([k for k in range(self.cube.number) if (mask >> order[k]) & 1], default=-1)
        return range(last + 1, self.cube.number)

    def begin(self):
        self.own_copy = pltpu.make_async_copy(
            self.own, self.out.at[self.cube.place(0) + (self.hz,)], self.local
        )
        self.own_copy.start()
        for d in near(self.heads)[::-1]:
            self.line_copy(d).start()

    def events(self):
        return [(mask, 2) for mask in range(1 << self.cube.number)]

    def receive(self, mask, _):
        if mask == 0:
            self.own_copy.wait()
            for d in near(self.heads):
                self.line_copy(d).wait_recv()
        for side in range(2):
            if mask:
                order = self.cube.gather_orders[side]
                k = max(k for k in range(self.cube.number) if (mask >> order[k]) & 1)
                self.flat_copy(side, mask & ~(1 << order[k]), k).wait_recv()
            for k in self.steps_after(side, mask):
                self.flat_copy(side, mask, k).start()

    def finish(self):
        for d in near(self.heads):
            self.line_copy(d).wait_send()
        for mask in range(1 << self.cube.number):
            for side in range(2):
                for k in self.steps_after(side, mask):
                    self.flat_copy(side, mask, k).wait_send()


class LineSums:
    def __init__(self, cube, heads, blocks, out, refs):
        self.cube, self.heads, self.blocks, self.out = cube, heads, blocks, out
        count = cube.number
        self.arrived, self.parts = refs[:count], refs[count : 2 * count - 1]
        self.line_out, self.line_in, self.send, self.recv, self.end_send, self.end_recv = refs[
            2 * count - 1 :
        ]
        self.hz = lax.axis_index("head")
        self.rows = blocks.shape[-2]
        self.outward = near(heads)[::-1] + [0]
        self.turns = heads + count + 1

    @staticmethod
    def scratch(cube, heads, rows, columns):
        count = cube.number
        slots = [(1 << count) >> (k + 1) for k in range(count)]
        half = cut_rows(rows)
        return (
            [pltpu.VMEM((2, s, heads, half, columns), bf16) for s in slots]
            + [pltpu.VMEM((2, s, heads, half, columns), bf16) for s in slots[1:]]
            + [
                pltpu.VMEM((heads - 1, rows, columns), bf16),
                pltpu.VMEM((heads - 1, rows, columns), bf16),
                DMA((2, count, slots[0], heads)),
                DMA((2, count, slots[0], heads)),
                DMA((heads - 1,)),
                DMA((heads - 1,)),
            ]
        )

    def slot(self, side, k, mask):
        return subsets(self.cube.scatter_orders[side][k + 1 :]).index(mask)

    def mine(self, side, mask, d):
        place = self.cube.place(mask) + ((self.hz + d) % self.heads,)
        return self.blocks.at[place + (part_of(self.rows, side),)]

    def there(self, ref, side, where, d):
        return ref.at[side, where, d, pl.ds(0, part_of(self.rows, side).size)]

    def copy_of(self, side, k, mask, d):
        order = self.cube.scatter_orders[side]
        where = self.slot(side, k, mask)
        if k == 0:
            piece = self.mine(side, mask | (1 << order[0]), d)
        else:
            piece = self.there(self.parts[k - 1], side, where, d)
        return pltpu.make_async_remote_copy(
            src_ref=piece,
            dst_ref=self.there(self.arrived[k], side, where, d),
            send_sem=self.send.at[side, k, where, d],
            recv_sem=self.recv.at[side, k, where, d],
            device_id=self.cube.peer(order[k]),
            device_id_type=MESH,
        )

    def end_copy(self, d):
        return pltpu.make_async_remote_copy(
            src_ref=self.line_out.at[d - 1],
            dst_ref=self.line_in.at[d - 1],
            send_sem=self.end_send.at[d - 1],
            recv_sem=self.end_recv.at[d - 1],
            device_id={"head": (self.hz + d) % self.heads},
            device_id_type=MESH,
        )

    def sums(self, side, steps, mask, d):
        value = self.mine(side, mask, d)[...].astype(f32)
        for j in range(steps):
            self.copy_of(side, j, mask, d).wait_recv()
            value = value + self.there(self.arrived[j], side, self.slot(side, j, mask), d)[
                ...
            ].astype(f32)
        return value

    def turn(self, turn):
        count = self.cube.number
        if turn < self.heads:
            for side in range(2):
                for mask in subsets(self.cube.scatter_orders[side][1:])[::-1]:
                    self.copy_of(side, 0, mask, self.outward[turn]).start()
        for k in range(1, count):
            if 0 <= turn - k - 1 < self.heads:
                d = self.outward[turn - k - 1]
                for side in range(2):
                    order = self.cube.scatter_orders[side]
                    for mask in subsets(order[k + 1 :])[::-1]:
                        value = self.sums(side, k, mask | (1 << order[k]), d)
                        place = self.there(self.parts[k - 1], side, self.slot(side, k, mask), d)
                        place[...] = value.astype(bf16)
                        self.copy_of(side, k, mask, d).start()
        if 0 <= turn - count - 1 < self.heads:
            d = self.outward[turn - count - 1]
            for side in range(2):
                value = self.sums(side, count, 0, d)
                part = part_of(self.rows, side)
                if d:
                    self.line_out[d - 1, part] = value.astype(bf16)
                else:
                    self.out[part] = value
            if d:
                self.end_copy(d).start()

    def finish(self):
        others = near(self.heads)
        for d in others:
            self.end_copy(d).wait_recv()
            self.out[...] += self.line_in[d - 1].astype(f32)
        for d in others:
            self.end_copy(d).wait_send()
        for side in range(2):
            for k in range(self.cube.number):
                for mask in subsets(self.cube.scatter_orders[side][k + 1 :]):
                    for d in self.outward:
                        self.copy_of(side, k, mask, d).wait_send()


TN = (((0,), (0,)), ((), ()))


def column_of(row):
    return jnp.broadcast_to(row, (8, row.shape[1])).T[:, :1]


def allowed(key_segments, query_segments, block, rows, seq):
    columns = query_segments.shape[1]
    key_place = block * rows + lax.broadcasted_iota(jnp.int32, (rows, columns), 0)
    query_place = seq * rows + lax.broadcasted_iota(jnp.int32, (rows, columns), 1) % rows
    return (key_segments == query_segments) & (key_place <= query_place)


def attend_kernel(cube, heads, group, beside, *refs):
    q_ref, kv_ref, key_seg, query_seg = refs[:4]
    near_refs, refs = refs[4 : 4 + len(beside)], refs[4 + len(beside) :]
    lines_ref, kv_out, out_turned, lse_ref = refs[:4]
    far_refs, refs = refs[4 : 4 + len(beside)], refs[4 + len(beside) :]
    stage, top, total, acc, send, recv, line_send, line_recv = refs[:8]
    chip, core, hz = lax.axis_index("chip"), lax.axis_index("core"), lax.axis_index("head")
    seq = chip * 2 + core
    others = near(heads)[::-1]
    batch, rows, columns = kv_ref.shape
    kv_heads = columns // (2 * HEAD_WIDTH)
    part = rows // 2
    meet([cube.peer(digit) for digit in range(cube.number)] + [{"head": (hz + d) % heads} for d in others])
    kv_out[chip, core] = kv_ref[...]
    gathers = []
    rest_refs = refs[8:]
    for with_core, own_block, all_blocks in zip(beside, near_refs, far_refs):
        kind = DenseGather if with_core else LineGather
        own_cube = Cube(cube.chips, with_core)
        gathers.append(kind(own_cube, heads, own_block, all_blocks, rest_refs[:5]))
        rest_refs = rest_refs[5:]
    fronts = {}
    for one in gathers:
        for mask, rank in one.events():
            fronts.setdefault(rank + bin(mask).count("1"), []).append((one, (mask, rank)))
    last_front = max(fronts, default=0)
    now = cube.number + 1

    def pass_front(index):
        for one, event in fronts.get(index, []):
            one.receive(*event)

    def copy_of(side, mask, k):
        order = cube.gather_orders[side]
        later = mask | (1 << order[k])
        place = cube.place(mask) + (slice(None), pl.ds(side * part, part))
        return pltpu.make_async_remote_copy(
            src_ref=kv_ref.at[:, pl.ds(side * part, part)] if mask == 0 else kv_out.at[place],
            dst_ref=kv_out.at[place],
            send_sem=send.at[side, later],
            recv_sem=recv.at[side, later],
            device_id=cube.peer(order[k]),
            device_id_type=MESH,
        )

    copies = []

    def forward(mask):
        for side in range(2):
            order = cube.gather_orders[side]
            last = max([k for k in range(cube.number) if (mask >> order[k]) & 1], default=-1)
            if mask:
                copy_of(side, mask & ~(1 << order[last]), last).wait_recv()
            for k in range(last + 1, cube.number):
                copy_of(side, mask, k).start()
                copies.append((side, mask, k))

    forward(0)
    for one in gathers:
        one.begin()
    pass_front(0)
    top[...] = jnp.full_like(top, negative)
    total[...] = jnp.zeros_like(total)
    acc[...] = jnp.zeros_like(acc)

    def block_step(block):
        place = (block // 2, block % 2)
        for b in range(batch):
            mask = allowed(
                column_of(key_seg[b, :, pl.ds(pl.multiple_of(block * rows, rows), rows)]),
                query_seg[b],
                block,
                rows,
                seq,
            )
            for j in range(kv_heads):
                pair = b * kv_heads + j
                begin = j * 2 * HEAD_WIDTH
                keys = kv_out[place + (b, slice(None), pl.ds(begin, HEAD_WIDTH))]
                values = kv_out[place + (b, slice(None), pl.ds(begin + HEAD_WIDTH, HEAD_WIDTH))]
                scores = lax.dot_general(keys, q_ref[pair], NT, preferred_element_type=f32)
                scores = jnp.where(mask, scores, negative)
                new = jnp.maximum(top[pair], jnp.max(scores, axis=0, keepdims=True))
                weights = jnp.exp(scores - new)
                shrink = jnp.exp(top[pair] - new)
                top[pair] = new
                total[pair] = total[pair] * shrink + jnp.sum(weights, axis=0, keepdims=True)
                acc[pair] = acc[pair] * shrink + lax.dot_general(
                    values, weights.astype(bf16), TN, preferred_element_type=f32
                )

    block_step(seq)
    for level in range(1, cube.number + 1):
        for mask in range(1, 1 << cube.number):
            if bin(mask).count("1") == level:
                forward(mask)
    pass_front(1)
    now = 2
    turns = 2 * cube.chips
    if beside:
        for turn in range(turns):
            if turn == turns // 2:
                pass_front(now)
                now += 1

            @pl.when(turn < seq)
            def _():
                block_step(turn)

    else:

        @pl.loop(0, seq)
        def _(block):
            block_step(block)

    spot = rows // heads
    for b in range(batch):
        for j in range(kv_heads):
            pair = b * kv_heads + j
            value = acc[pair] / total[pair]
            out_turned[pair] = value
            lse_ref[pair] = top[pair] + jnp.log(total[pair])
            value = value.T.astype(bf16)
            for g in range(group):
                for head in range(heads):
                    begin = (j * group + g) * HEAD_WIDTH
                    stage[head, pl.ds(b * spot, spot), pl.ds(begin, HEAD_WIDTH)] = value[
                        g * rows + head * spot : g * rows + (head + 1) * spot
                    ]

    def line_copy(d):
        return pltpu.make_async_remote_copy(
            src_ref=stage.at[(hz + d) % heads],
            dst_ref=lines_ref.at[hz],
            send_sem=line_send.at[d - 1],
            recv_sem=line_recv.at[d - 1],
            device_id={"head": (hz + d) % heads},
            device_id_type=MESH,
        )

    for d in others:
        line_copy(d).start()
    lines_ref[hz] = stage[hz]
    for index in range(now, last_front + 1):
        pass_front(index)
    for side, mask, k in copies:
        copy_of(side, mask, k).wait_send()
    for d in others:
        line_copy(d).wait()
    for one in gathers:
        one.finish()


def attend(queries, keys_values, key_seg, query_seg, beside, chips, heads, group, number):
    batch, rows, columns = keys_values.shape
    pairs, wide, depth = queries.shape
    cube = Cube(chips, True)
    group_columns = group * columns // 2
    tokens = batch * rows // heads
    return pl.pallas_call(
        functools.partial(attend_kernel, cube, heads, group, [core for _, core in beside]),
        out_shape=(
            jax.ShapeDtypeStruct((heads, tokens, group_columns), bf16),
            jax.ShapeDtypeStruct((chips, 2, batch, rows, columns), bf16),
            jax.ShapeDtypeStruct((pairs, depth, wide), f32),
            jax.ShapeDtypeStruct((pairs, 1, wide), f32),
        )
        + tuple(
            jax.ShapeDtypeStruct((chips,) + (2,) * with_core + (heads,) + value.shape, bf16)
            for value, with_core in beside
        ),
        in_specs=[WHOLE] * 4 + [ANY] * len(beside),
        out_specs=(WHOLE,) * 4 + (ANY,) * len(beside),
        scratch_shapes=[
            pltpu.VMEM((heads, tokens, group_columns), bf16),
            pltpu.VMEM((pairs, 1, wide), f32),
            pltpu.VMEM((pairs, 1, wide), f32),
            pltpu.VMEM((pairs, depth, wide), f32),
            DMA((2, 2 * chips)),
            DMA((2, 2 * chips)),
            DMA((heads - 1,)),
            DMA((heads - 1,)),
        ]
        + [
            item
            for _, core in beside
            for item in (DenseGather if core else LineGather).scratch(Cube(chips, core), heads)
        ],
        compiler_params=pltpu.CompilerParams(
            collective_id=number, has_side_effects=True, vmem_limit_bytes=50 << 20
        ),
        name="attend",
    )(queries, keys_values, key_seg, query_seg, *[value for value, _ in beside])


def attend_back_kernel(cube, heads, group, beside, shares, *refs):
    q_ref, kv_ref, key_seg, query_seg, out_turned, lse_ref, dh_ref = refs[:7]
    near_refs, refs = refs[7 : 7 + len(beside)], refs[7 + len(beside) :]
    pair_refs, refs = refs[:shares], refs[shares:]
    dq_ref, dkv_ref = refs[:2]
    far_refs, refs = refs[2 : 2 + len(beside)], refs[2 + len(beside) :]
    added = refs[: cube.chips] if shares else ()
    refs = (None,) * 9 + refs[len(added) :]
    count = cube.number
    landed, d_out, delta, dq_turned, grads = refs[9:14]
    arrived, parts = refs[14 : 14 + count], refs[14 + count : 13 + 2 * count]
    send, recv, line_send, line_recv = refs[13 + 2 * count : 17 + 2 * count]
    turns = 2 * cube.chips
    rest = refs[17 + 2 * count :]
    sums_beside = []
    for with_core, source, target in zip(beside, near_refs, far_refs):
        own_cube = Cube(cube.chips, with_core)
        size = 2 * own_cube.number + 5
        sums_beside.append(LineSums(own_cube, heads, source, target, rest[:size]))
        rest = rest[size:]

    def load_pair(mask):
        place = flip(lax.axis_index("chip"), mask)
        return [
            pltpu.make_async_copy(pair_refs[i].at[place], rest[i], rest[3].at[i]) for i in range(2)
        ]

    def store_sum(mask):
        return pltpu.make_async_copy(rest[2], added[mask], rest[3].at[2])

    def add_pair(turn):
        mask = turn // 2
        if turn % 2 == 0:
            for copy in load_pair(mask):
                copy.start()
            return
        for copy in load_pair(mask):
            copy.wait()
        if mask:
            store_sum(mask - 1).wait()
        rest[2][...] = (rest[0][...].astype(f32) + rest[1][...].astype(f32)).astype(bf16)
        store_sum(mask).start()

    chip, core, hz = lax.axis_index("chip"), lax.axis_index("core"), lax.axis_index("head")
    seq = chip * 2 + core
    others = near(heads)[::-1]
    batch, rows, columns = kv_ref.shape[2:]
    kv_heads = columns // (2 * HEAD_WIDTH)
    spot = rows // heads
    half = grads.shape[2] // 2
    meet([cube.peer(digit) for digit in range(count)] + [{"head": (hz + d) % heads} for d in others])

    def line_copy(d):
        return pltpu.make_async_remote_copy(
            src_ref=dh_ref.at[(hz + d) % heads],
            dst_ref=landed.at[hz],
            send_sem=line_send.at[d - 1],
            recv_sem=line_recv.at[d - 1],
            device_id={"head": (hz + d) % heads},
            device_id_type=MESH,
        )

    for d in others:
        line_copy(d).start()
    for turn in range(2):
        for one in sums_beside:
            one.turn(turn)
    landed[hz] = dh_ref[hz]
    grads[...] = jnp.zeros_like(grads)
    dq_turned[...] = jnp.zeros_like(dq_turned)
    for d in others:
        line_copy(d).wait()
    for b in range(batch):
        for j in range(kv_heads):
            pair = b * kv_heads + j
            for g in range(group):
                for head in range(heads):
                    begin = (j * group + g) * HEAD_WIDTH
                    d_out[pair, pl.ds(g * rows + head * spot, spot), :] = landed[
                        head, pl.ds(b * spot, spot), pl.ds(begin, HEAD_WIDTH)
                    ]
            delta[pair] = jnp.sum(
                d_out[pair].astype(f32).T * out_turned[pair], axis=0, keepdims=True
            )

    def block_step(block):
        place = (block // 2, block % 2)
        for b in range(batch):
            mask = allowed(
                column_of(key_seg[b, :, pl.ds(pl.multiple_of(block * rows, rows), rows)]),
                query_seg[b],
                block,
                rows,
                seq,
            )
            for j in range(kv_heads):
                pair = b * kv_heads + j
                begin = j * 2 * HEAD_WIDTH
                keys = kv_ref[place + (b, slice(None), pl.ds(begin, HEAD_WIDTH))]
                values = kv_ref[place + (b, slice(None), pl.ds(begin + HEAD_WIDTH, HEAD_WIDTH))]
                scores = lax.dot_general(keys, q_ref[pair], NT, preferred_element_type=f32)
                probs = jnp.exp(jnp.where(mask, scores, negative) - lse_ref[pair])
                d_probs = lax.dot_general(values, d_out[pair], NT, preferred_element_type=f32)
                d_scores = (probs * (d_probs - delta[pair])).astype(bf16)
                dq_turned[pair] += lax.dot_general(
                    keys, d_scores, TN, preferred_element_type=f32
                )
                d_keys = jnp.dot(d_scores, q_ref[pair], preferred_element_type=f32)
                d_values = jnp.dot(probs.astype(bf16), d_out[pair], preferred_element_type=f32)
                grads[place + (pl.ds(b * rows, rows), pl.ds(begin, 2 * HEAD_WIDTH))] = (
                    jnp.concatenate([d_keys, d_values], axis=1).astype(bf16)
                )

    done = 2
    if beside:
        for turn in range(turns):

            @pl.when(turn <= seq)
            def _():
                block_step(turn)

            if shares:
                add_pair(turn)
            if turn % 3 == 2:
                for one in sums_beside:
                    one.turn(done)
                done += 1

    else:

        @pl.loop(0, seq + 1)
        def _(block):
            block_step(block)

    def slot(side, k, mask):
        return subsets(cube.scatter_orders[side][k + 1 :]).index(mask)

    def mine(side, mask):
        return grads.at[cube.place(mask) + (pl.ds(side * half, half),)]

    copies = {}

    def sums(side, steps, mask):
        value = mine(side, mask)[...].astype(f32)
        for j in range(steps):
            copies[(side, j, mask)].wait_recv()
            value = value + arrived[j][side, slot(side, j, mask)].astype(f32)
        return value

    for k in range(count):
        for side in range(2):
            order = cube.scatter_orders[side]
            for mask in subsets(order[k + 1 :])[::-1]:
                full = mask | (1 << order[k])
                where = slot(side, k, mask)
                if k == 0:
                    piece = mine(side, full)
                else:
                    piece = parts[k - 1].at[side, where]
                    piece[...] = sums(side, k, full).astype(bf16)
                copies[(side, k, mask)] = pltpu.make_async_remote_copy(
                    src_ref=piece,
                    dst_ref=arrived[k].at[side, where],
                    send_sem=send.at[side, k, where],
                    recv_sem=recv.at[side, k, where],
                    device_id=cube.peer(order[k]),
                    device_id_type=MESH,
                )
                copies[(side, k, mask)].start()
        for one in sums_beside:
            if done < one.turns:
                one.turn(done)
        done += 1
    scale = HEAD_WIDTH ** (-0.5)
    for pair in range(batch * kv_heads):
        dq_ref[pair] = (dq_turned[pair] * scale).T.astype(bf16)
    for side in range(2):
        dkv_ref[pl.ds(side * half, half)] = sums(side, count, 0)
    for turn in range(done, max([one.turns for one in sums_beside], default=0)):
        for one in sums_beside:
            if turn < one.turns:
                one.turn(turn)
    for copy in copies.values():
        copy.wait_send()
    for one in sums_beside:
        one.finish()
    if shares:
        store_sum(cube.chips - 1).wait()


def attend_back(
    queries, kv_all, key_seg, query_seg, out_turned, lse, d_heads, beside, shares, heads, group, number
):
    chips, _, batch, rows, columns = kv_all.shape
    pairs, wide, depth = queries.shape
    cube = Cube(chips, True)
    count = cube.number
    half = batch * rows // 2
    slots = [(1 << count) >> (k + 1) for k in range(count)]
    return pl.pallas_call(
        functools.partial(
            attend_back_kernel, cube, heads, group, [core for _, core in beside], len(shares)
        ),
        out_shape=(
            jax.ShapeDtypeStruct((pairs, wide, depth), bf16),
            jax.ShapeDtypeStruct((batch * rows, columns), f32),
        )
        + tuple(jax.ShapeDtypeStruct(value.shape[-2:], f32) for value, _ in beside)
        + tuple(jax.ShapeDtypeStruct(shares[0].shape[1:], bf16) for _ in range(chips) if shares),
        in_specs=[WHOLE] * (7 + len(beside)) + [ANY] * len(shares),
        out_specs=(WHOLE,) * (2 + len(beside)) + (ANY,) * (chips * bool(shares)),
        scratch_shapes=[
            pltpu.VMEM(d_heads.shape, bf16),
            pltpu.VMEM((pairs, wide, depth), bf16),
            pltpu.VMEM((pairs, 1, wide), f32),
            pltpu.VMEM((pairs, depth, wide), f32),
            pltpu.VMEM((chips, 2, batch * rows, columns), bf16),
        ]
        + [pltpu.VMEM((2, s, half, columns), bf16) for s in slots]
        + [pltpu.VMEM((2, s, half, columns), bf16) for s in slots[1:]]
        + [
            DMA((2, count, slots[0])),
            DMA((2, count, slots[0])),
            DMA((heads - 1,)),
            DMA((heads - 1,)),
        ]
        + [
            item
            for value, core in beside
            for item in LineSums.scratch(Cube(chips, core), *value.shape[-3:])
        ]
        + [pltpu.VMEM(shares[0].shape[1:], bf16) for _ in range(3) if shares]
        + [DMA((3,)) for _ in range(1) if shares],
        compiler_params=pltpu.CompilerParams(
            collective_id=number, has_side_effects=True, vmem_limit_bytes=56 << 20
        ),
        name="attend_back",
    )(
        queries, kv_all, key_seg, query_seg, out_turned, lse, d_heads, *[v for v, _ in beside], *shares
    )


def sibling(value):
    return lax.ppermute(value, "core", [(0, 1), (1, 0)])


def per_device(
    layer_input,
    segments,
    routes,
    pair_rank,
    query_key_value_weight,
    output_weight,
    router_weight,
    norm_attn,
    norm_ffn,
    w_gate_up,
    w_down,
    cotangent,
):
    chips = lax.axis_size("chip")
    head_number = lax.axis_size("head")
    sequence_batch, token_rows, width = layer_input.shape
    length = segments.shape[1]
    blk = token_rows * head_number
    query_group = QUERY_HEADS // KEY_VALUE_HEADS
    key_value_location = KEY_VALUE_HEADS // head_number
    loc_experts, slice_rows = w_gate_up.shape[:2]
    top = routes.shape[2]
    tokens_present = sequence_batch * token_rows
    pairs = tokens_present * top
    line_tokens = tokens_present * head_number
    scale = HEAD_WIDTH ** (-0.5)
    hidden = FF // chips
    loc_columns = key_value_location * (query_group + 2) * HEAD_WIDTH
    chip = lax.axis_index("chip")
    core = lax.axis_index("core")
    head = lax.axis_index("head")
    seq_index = chip * 2 + core
    dense_rows = query_key_value_weight.shape[0]

    extras = jnp.concatenate([router_weight, norm_attn[:, None], norm_ffn[:, None]], axis=1)
    extras = jnp.pad(extras, ((0, 0), (0, LANES - extras.shape[1])))
    slices = query_key_value_weight.reshape(dense_rows, head_number, loc_columns).transpose(1, 0, 2)
    slices = jnp.concatenate(
        [slices, jnp.broadcast_to(extras, (head_number,) + extras.shape)], axis=2
    )
    group_tokens = chips * head_number * tokens_present
    columns = width + LANES
    fused = hidden % LANES == 0 and group_tokens <= 2048
    own_tokens = layer_input.reshape(tokens_present, width)
    cots = cotangent.reshape(tokens_present, width)
    if fused:

        def unit_of(weights, mask):
            begins = [part * FF + (chip ^ mask) * hidden for part in range(2)]
            cut = [lax.dynamic_slice_in_dim(weights, begin, hidden, 2) for begin in begins]
            return jnp.concatenate(cut, axis=2)

        keys = (routes * pairs + pair_rank).reshape(pairs)
        x_line, dense, last_unit, slot = start(
            layer_input, slices, unit_of(w_gate_up, chips - 1), keys, chips, head_number, 1
        )
        x_line, w_gate_up = lax.optimization_barrier((x_line, w_gate_up))
        units = [across(unit_of(w_gate_up, mask), chips, mask) for mask in range(chips - 1)]
        units.append(last_unit)
        dense = dense.reshape(width, loc_columns + LANES)
    else:
        parts = w_gate_up.reshape(loc_experts, slice_rows, 2, chips, hidden).transpose(3, 2, 1, 0, 4)
        parts = parts.reshape(chips, 2, slice_rows, loc_experts * hidden)
        piled = jnp.zeros((chips, 2, 2, slice_rows, loc_experts * hidden), bf16)
        for mask in range(chips):
            piece = lax.dynamic_index_in_dim(parts, chip ^ mask, 0, keepdims=False)
            piece = across(piece, chips, mask)
            other = sibling(piece)
            piled = lax.dynamic_update_slice(piled, piece[None, None], (chip ^ mask, core, 0, 0, 0))
            piled = lax.dynamic_update_slice(piled, other[None, None], (chip ^ mask, 1 - core, 0, 0, 0))
        piled = piled.transpose(2, 0, 1, 3, 4).reshape(2, width, loc_experts * hidden)
        expert_gate, expert_up = piled[0], piled[1]
        down_other = sibling(w_down)
        expert_down = (
            jnp.where(
                core == 0,
                jnp.concatenate([w_down, down_other], axis=1),
                jnp.concatenate([down_other, w_down], axis=1),
            )
        ).reshape(loc_experts * hidden, width)

        lined = line_exchange(slices, head_number, 1)
        dense = gather(
            lined.reshape(head_number * dense_rows, loc_columns + LANES), chips, 1, True, 2
        ).reshape(width, loc_columns + LANES)
        x_line = line_exchange(layer_input.reshape(tokens_present, width), head_number, 3, True)

    if not fused:
        grad_all = lax.all_gather(cots, ("chip", "head"), axis=0, tiled=True)
        dense_out = lax.all_gather(output_weight, ("chip", "core", "head"), axis=0, tiled=True)

    dense_qkv = dense[:, :loc_columns]
    dense_router = dense[:, loc_columns : loc_columns + EXPERTS]
    gain_attn = dense[:, loc_columns + EXPERTS].astype(f32)
    gain_ffn = dense[:, loc_columns + EXPERTS + 1].astype(f32)

    x_line = x_line.reshape(line_tokens, width).astype(f32)
    normed_line = x_line * lax.rsqrt(jnp.mean(x_line * x_line, axis=1, keepdims=True) + epsilon)
    first_line = (normed_line * gain_attn).astype(bf16)

    def to_blocks(value):
        columns = value.shape[1:]
        if fused:
            return value.reshape((sequence_batch, blk) + columns)
        return (
            value.reshape((head_number, sequence_batch, token_rows) + columns)
            .swapaxes(0, 1)
            .reshape((sequence_batch, blk) + columns)
        )

    def to_lines(value):
        columns = value.shape[2:]
        if fused:
            return value.reshape((line_tokens,) + columns)
        return (
            value.reshape((sequence_batch, head_number, token_rows) + columns)
            .swapaxes(0, 1)
            .reshape((line_tokens,) + columns)
        )

    q_start = seq_index * blk
    q_pos = q_start + jnp.arange(blk, dtype=jnp.int32)
    cosine, sine = rope_tables(q_pos, HEAD_WIDTH)
    projected = to_blocks(jnp.dot(first_line, dense_qkv, preferred_element_type=f32)).reshape(
        sequence_batch, blk, key_value_location, query_group + 2, HEAD_WIDTH
    )
    turned = rotate(projected[:, :, :, : query_group + 1], cosine, sine)
    query_rows = turned[:, :, :, :query_group].astype(bf16)
    keys_values = (
        jnp.stack([turned[:, :, :, query_group], projected[:, :, :, query_group + 1]], axis=3)
        .astype(bf16)
        .reshape(sequence_batch * blk, key_value_location * 2 * HEAD_WIDTH)
    )
    kv_columns = key_value_location * 2 * HEAD_WIDTH
    pairs_here = sequence_batch * key_value_location
    group_columns = key_value_location * query_group * HEAD_WIDTH
    queries = (
        (query_rows.astype(f32) * scale)
        .astype(bf16)
        .transpose(0, 2, 3, 1, 4)
        .reshape(pairs_here, query_group * blk, HEAD_WIDTH)
    )
    key_seg = segments[:, None, :].astype(f32)
    q_seg = lax.dynamic_slice_in_dim(segments, q_start, blk, 1)
    query_seg = jnp.tile(q_seg[:, None, :].astype(f32), (1, 1, query_group))
    lines, kv_all, out_turned, lse, *beside = attend(
        queries,
        keys_values.reshape(sequence_batch, blk, kv_columns),
        key_seg,
        query_seg,
        [(cots, False), (output_weight, True)] if fused else [],
        chips,
        head_number,
        query_group,
        4,
    )
    if fused:
        grad_all = beside[0].reshape(group_tokens, width)
        dense_out = beside[1].reshape(QUERY_HEADS * HEAD_WIDTH, width)
    mixed_heads = lines.transpose(1, 0, 2).reshape(tokens_present, QUERY_HEADS * HEAD_WIDTH)
    tokens = layer_input.reshape(tokens_present, width).astype(f32)
    middle = tokens + jnp.dot(mixed_heads, dense_out, preferred_element_type=f32)
    inverse_two = lax.rsqrt(jnp.mean(middle * middle, axis=1, keepdims=True) + epsilon)
    normed_two = middle * inverse_two
    second_input = (normed_two * gain_ffn).astype(bf16)
    router_logits = jnp.dot(second_input, dense_router, preferred_element_type=f32)
    route_flat = routes.reshape(tokens_present, top)
    hot = route_flat[:, :, None] == jnp.arange(EXPERTS, dtype=jnp.int32)[None, None, :]
    chosen = jnp.sum(jnp.where(hot, router_logits[:, None, :], 0.0), axis=2)
    gates = jax.nn.softmax(chosen, axis=-1)
    if not fused:
        expert_of = route_flat.reshape(pairs)
        rank = pair_rank.reshape(pairs)
        slot = jnp.sum(
            (expert_of[None, :] == expert_of[:, None]) & (rank[None, :] < rank[:, None]),
            axis=1,
            dtype=jnp.int32,
        )
    kept = (slot < CAP).reshape(tokens_present, top).astype(f32)
    weights_pair = gates * kept
    spread = jnp.sum(jnp.where(hot, weights_pair[:, :, None], 0.0), axis=1)
    spread_high = spread.astype(bf16)
    spread_low = (spread - spread_high.astype(f32)).astype(bf16)
    pad = jnp.zeros((tokens_present, LOW - EXPERTS), bf16)
    payload = jnp.concatenate([second_input, spread_high, pad, spread_low, pad], axis=1)
    if fused:
        back, moe_part, keep_up, other_up, keep_down, other_down = expert_turn(
            payload, grad_all, units, w_down, head_number, 6
        )
        down_share = keep_down.astype(f32) + other_down.astype(f32)
    else:
        x_all = gather(payload, chips, head_number, False, 6).reshape(group_tokens, columns)
        moe_part, back_part, d_gate_w, d_up_w, d_down_w = experts(
            x_all, grad_all, expert_gate, expert_up, expert_down, hidden
        )
        back_part = back_part.reshape(chips, head_number, tokens_present, columns)
        back = scatter_sum(back_part, chips, head_number, False, 7)
        moe = lax.psum_scatter(moe_part, ("chip", "head"), scatter_dimension=0, tiled=True)
        grads = jnp.stack([d_gate_w, d_up_w]).reshape(2, chips, 2, slice_rows, loc_experts * hidden)
        keep = lax.dynamic_index_in_dim(grads, core, 2, keepdims=False)
        give = lax.dynamic_index_in_dim(grads, 1 - core, 2, keepdims=False)
        shared = (keep.astype(f32) + sibling(give).astype(f32)).astype(bf16)
        piled = jnp.zeros((chips, 2, slice_rows, loc_experts * hidden), bf16)
        for mask in range(chips):
            piece = across(lax.dynamic_index_in_dim(shared, chip ^ mask, 1, keepdims=False), chips, mask)
            piled = lax.dynamic_update_slice(piled, piece[None], (chip ^ mask, 0, 0, 0))
        up_share = (
            piled.reshape(chips, 2, slice_rows, loc_experts, hidden)
            .transpose(3, 2, 1, 0, 4)
            .astype(f32)
            .reshape(loc_experts, slice_rows, 2 * FF)
        )
        d_down_w = d_down_w.reshape(loc_experts, 2, hidden // 2, width)
        keep = lax.dynamic_index_in_dim(d_down_w, core, 1, keepdims=False)
        give = lax.dynamic_index_in_dim(d_down_w, 1 - core, 1, keepdims=False)
        down_share = keep.astype(f32) + sibling(give).astype(f32)

    grad_out = cotangent.reshape(tokens_present, width).astype(f32)
    d_kept = back[:, width : width + EXPERTS]
    grad_gate = jnp.sum(jnp.where(hot, d_kept[:, None, :], 0.0), axis=2) * kept
    grad_chosen = gates * (grad_gate - jnp.sum(gates * grad_gate, axis=1, keepdims=True))
    grad_logits = jnp.sum(jnp.where(hot, grad_chosen[:, :, None], 0.0), axis=1)
    grad_router = jnp.dot(second_input.astype(f32).T, grad_logits, precision=HIGH_PRECISION)
    grad_second = back[:, :width] + jnp.dot(
        grad_logits, dense_router.astype(f32).T, precision=HIGH_PRECISION
    )
    grad_gain_ffn = jnp.sum(grad_second * normed_two, axis=0)
    scaled_two = grad_second * gain_ffn
    grad_mid = grad_out + inverse_two * (
        scaled_two - normed_two * jnp.mean(scaled_two * normed_two, axis=1, keepdims=True)
    )
    grad_attn = grad_mid.astype(bf16)
    grad_dense_out = jnp.dot(mixed_heads.T, grad_attn, preferred_element_type=f32)
    grad_dense_out = grad_dense_out.astype(bf16)
    if not fused:
        out_share = lax.psum_scatter(
            grad_dense_out, ("chip", "core", "head"), scatter_dimension=0, tiled=True
        ).astype(f32)
    grad_heads = (
        jnp.dot(grad_attn, dense_out.T, preferred_element_type=f32)
        .astype(bf16)
        .reshape(tokens_present, head_number, group_columns)
        .transpose(1, 0, 2)
    )
    grad_q, grad_kv, *beside = attend_back(
        queries,
        kv_all,
        key_seg,
        query_seg,
        out_turned,
        lse,
        grad_heads,
        [
            (moe_part.reshape(chips, head_number, tokens_present, width), False),
            (grad_dense_out.reshape(chips, 2, head_number, dense_rows, width), True),
        ]
        if fused
        else [],
        [keep_up, other_up] if fused else [],
        head_number,
        query_group,
        8,
    )
    if fused:
        moe, out_share, *shared = beside
        pieces = [across(shared[mask], chips, mask) for mask in range(chips)]
    grad_q = grad_q.reshape(
        sequence_batch, key_value_location, query_group, blk, HEAD_WIDTH
    ).transpose(0, 3, 1, 2, 4)
    grad_kv = grad_kv.reshape(sequence_batch, blk, key_value_location, 2, HEAD_WIDTH)
    grad_proj = jnp.concatenate([grad_q.astype(bf16), grad_kv.astype(bf16)], axis=3).astype(f32)
    unturned = rotate(grad_proj[:, :, :, : query_group + 1], cosine, -sine)
    grad_qkv = to_lines(
        jnp.concatenate([unturned, grad_proj[:, :, :, query_group + 1 :]], axis=3)
        .reshape(sequence_batch, blk, loc_columns)
        .astype(bf16)
    )
    grad_first_part = jnp.dot(grad_qkv, dense_qkv.T, preferred_element_type=f32)
    grad_gain_attn = jnp.sum(grad_first_part * normed_line, axis=0)
    extras = jnp.concatenate(
        [
            grad_router,
            grad_gain_attn[:, None],
            grad_gain_ffn[:, None],
            jnp.zeros((width, LANES - EXPERTS - 2), f32),
        ],
        axis=1,
    ).astype(bf16)
    if fused:
        x_again, gain_again, grad_qkv = lax.optimization_barrier((x_line, gain_attn, grad_qkv))
        scale_again = lax.rsqrt(jnp.mean(x_again * x_again, axis=1, keepdims=True) + epsilon)
        first_line = (x_again * scale_again * gain_again).astype(bf16)
        grad_first, sums = end(
            grad_first_part.astype(bf16).reshape(sequence_batch, head_number, token_rows, width),
            first_line,
            grad_qkv,
            extras,
            chips,
            head_number,
            13,
        )
        pieces, grad_first, sums = lax.optimization_barrier((pieces, grad_first, sums))
        up_share = place_units(pieces, hidden)
        up_share, grad_first, sums, moe, down_share = lax.optimization_barrier(
            (up_share, grad_first, sums, moe, down_share)
        )
        grad_first = jnp.sum(grad_first.astype(f32), axis=0).reshape(tokens_present, width)
        sums = sums.astype(f32)
    else:
        grad_first = jnp.sum(
            line_exchange(
                grad_first_part.astype(bf16).reshape(head_number, tokens_present, width),
                head_number,
                10,
            ).astype(f32),
            axis=0,
        )
        grad_dense_qkv = jnp.dot(first_line.T, grad_qkv, preferred_element_type=f32)
        sums = jnp.concatenate([grad_dense_qkv.astype(bf16), extras], axis=1)
        sums = scatter_sum(
            sums.reshape(chips, 2, head_number * dense_rows, loc_columns + LANES), chips, 1, True, 11
        )
        sums = line_exchange(
            sums.reshape(head_number, dense_rows, loc_columns + LANES), head_number, 12
        )
    inverse_one = lax.rsqrt(jnp.mean(tokens * tokens, axis=1, keepdims=True) + epsilon)
    normed_one = tokens * inverse_one
    scaled_one = grad_first * gain_attn
    grad_input = grad_mid + inverse_one * (
        scaled_one - normed_one * jnp.mean(scaled_one * normed_one, axis=1, keepdims=True)
    )
    mixed_out = (middle + moe.astype(f32)).astype(bf16)
    mixed_out = mixed_out.reshape(sequence_batch, token_rows, width)
    qkv_share = sums[:, :, :loc_columns].transpose(1, 0, 2).reshape(dense_rows, -1)
    extra = jnp.sum(sums[:, :, loc_columns:], axis=0)
    return (
        mixed_out,
        grad_input.reshape(sequence_batch, token_rows, width),
        qkv_share,
        out_share,
        extra[:, :EXPERTS],
        extra[:, EXPERTS],
        extra[:, EXPERTS + 1],
        up_share,
        down_share,
    )


def solution(mesh):
    grid = mesh.devices
    seq, heads = grid.shape
    split = Mesh(grid.reshape(seq // 2, 2, heads), ("chip", "core", "head"))
    places = ("chip", "core", "head")
    inner = ("chip", "core")
    placed = (
        P(None, places, None),
        P(),
        P(None, places, None),
        P(None, places, None),
        P(places, None),
        P(places, None),
        P(places, None),
        P(places),
        P(places),
        P("head", inner, None),
        P("head", inner, None),
        P(None, places, None),
    )
    return jax.shard_map(
        per_device,
        mesh=split,
        in_specs=placed,
        out_specs=(
            P(None, places, None),
            P(None, places, None),
            P(places, None),
            P(places, None),
            P(places, None),
            P(places),
            P(places),
            P("head", inner, None),
            P("head", inner, None),
        ),
        check_vma=False,
    )
```
